32 devices in a mesh: parts: 2 (over x), wide: 16 (over z, y, core).
Axes of the slice: x: 2, y: 2, z: 4, core: 2. Of those that a mesh axis runs over, the one named last changes fastest.
Arguments:
- a_rows: bfloat16 [40960, 2048], P(('parts', 'wide')), parts along dimension 0, may hold values from -6 to 6
- xa_panel: bfloat16 [4096, 256], P(('parts', 'wide')), parts along dimension 0, may hold values from -0.125 to 0.125
- za_panel: bfloat16 [4096, 256], P(('parts', 'wide')), parts along dimension 0, may hold values from -0.125 to 0.125
- send_order: int32 [32, 1280], P(('parts', 'wide')), parts along dimension 0, may hold values from 0 to 1279, each once within a row
- recv_order: int32 [32, 1280], P(('parts', 'wide')), parts along dimension 0, may hold values from 0 to 1279, each once within a row
- shift: float32 [128], P('parts'), parts along dimension 0, may hold values from 1 to 8
- resident: bfloat16 [40960, 1024], P(('parts', 'wide')), parts along dimension 0, may hold values from -6 to 6
Outputs:
- factored: float32 [40960, 256], P(('parts', 'wide')), parts along dimension 0
- updated: bfloat16 [40960, 1024], P(('parts', 'wide')), parts along dimension 0
- pivots: float32 [128], P('parts'), parts along dimension 0
The draws below stay inside these ranges and needn't reach their ends.
There are 2 independent parts, one for each index of `parts`. The reference program is written for one: setup_inputs(seed, part) draws one part's arguments, and reference() takes and returns one part's arrays. A program takes and returns all parts, laid end to end along the dimension named above; each array names one. Nothing has to cross between parts.
Inputs may be any that keep to these rules, and one draw needn't show every extreme that they name: Each row of send_order is a permutation of the local constraint rows. Each row of recv_order is a permutation of the received slots.
All inputs are finite; a program needn't handle non-finite values.
Results may differ from the reference program's by a relative error of at most 0.0004.
Values may be sent and summed in bfloat16 or wider, within the bound.
No kernel may reach another device: no remote copies, remote signals or barrier semaphores. Data moves between devices by JAX's collectives and lax.ppermute only.
A program may use at most 64 MiB of HBM per device.

```python
import math
import jax
import jax.numpy as jnp
from jax import lax

NV = 2048
COLS = 256
PANEL = 64
RES = 1024
R_DEV = 1280
M_ROWS = 20480
N_WIDE = 16


def block_scale(own_key, shape, cuts, low, largest):
    def one(dim, blocks):
        draws = jax.random.uniform(jax.random.fold_in(jax.random.fold_in(own_key, 6), dim), (blocks,), jnp.float32, low / len(cuts), largest / len(cuts))
        return jnp.repeat(jnp.exp(draws), shape[dim] // blocks).reshape((-1,) + (1,) * (len(shape) - dim - 1))

    loudness = one(*cuts[0])
    for cut in cuts[1:]:
        loudness = loudness * one(*cut)
    return loudness


def normal_values(rng, shape, scale, limit, pieces=(), kind=jnp.bfloat16):
    level = block_scale(rng, shape, pieces, -0.22, 0.18) if pieces else 1.0
    values = jax.random.normal(rng, shape, jnp.float32) * scale * level
    return jnp.minimum(jnp.maximum(values, -limit), limit).astype(kind)


def setup_inputs(seed: int = 0, part: int = 0) -> dict:
    key_list = jax.random.split(jax.random.key(seed), 8)
    own_keys = jax.random.split(jax.random.fold_in(key_list[7], part), 8)
    a_rows = normal_values(own_keys[0], (M_ROWS, NV), 1.0, 6.0, ((0, 16),))
    xa_panel = normal_values(own_keys[1], (NV, COLS), NV ** -0.5, 0.125, ((0, 16),))
    za_panel = normal_values(own_keys[2], (NV, COLS), NV ** -0.5, 0.125, ((0, 16),))
    send_order = jax.vmap(lambda own: jax.random.permutation(own, R_DEV))(jax.random.split(own_keys[3], N_WIDE)).reshape((N_WIDE, R_DEV)).astype(jnp.int32)
    recv_order = jax.vmap(lambda own: jax.random.permutation(own, R_DEV))(jax.random.split(own_keys[4], N_WIDE)).reshape((N_WIDE, R_DEV)).astype(jnp.int32)
    shift = jnp.clip(jnp.exp(jax.random.uniform(own_keys[5], (PANEL,), jnp.float32, math.log(1.0), math.log(8.0))), 1.0, 8.0)
    resident = normal_values(own_keys[6], (M_ROWS, RES), 1.0, 6.0, ((0, 16),))
    return dict(a_rows=a_rows, xa_panel=xa_panel, za_panel=za_panel, send_order=send_order, recv_order=recv_order, shift=shift, resident=resident)


def factor(block, shift):
    extent = block.shape[0]
    positions = jnp.arange(extent)
    mirrored = jnp.tril(block) + jnp.tril(block, -1).T
    magnitude = jnp.sum(jnp.abs(mirrored), axis=1)
    is_diag = positions[:, None] == positions[None, :]
    work = jnp.where(is_diag, (shift + magnitude)[:, None], mirrored)

    def step(column_index, carry):
        matrix, lower, pivots = carry
        column = lax.dynamic_slice_in_dim(matrix, column_index, 1, 1)[:, 0]
        pivot = jnp.sum(jnp.where(positions == column_index, column, 0.0))
        below = jnp.where(positions > column_index, column / pivot, 0.0)
        matrix = matrix - pivot * below[:, None] * below[None, :]
        unit = jnp.where(positions == column_index, 1.0, 0.0)
        lower = lower + (below + unit)[:, None] * unit[None, :]
        pivots = pivots + unit * pivot
        return (matrix, lower, pivots)
    start = (work, jnp.zeros_like(work), jnp.zeros_like(shift))
    matrix, lower, pivots = lax.fori_loop(0, extent, step, start)
    return (lower, pivots)

def to_global(stored):
    width = stored.shape[1]
    return stored.reshape(N_WIDE, R_DEV // PANEL, PANEL, width).transpose(1, 0, 2, 3).reshape(N_WIDE * R_DEV, width)

def to_stored(globe):
    width = globe.shape[1]
    return globe.reshape(R_DEV // PANEL, N_WIDE, PANEL, width).transpose(1, 0, 2, 3).reshape(N_WIDE * R_DEV, width)

def reference(a_rows, xa_panel, za_panel, send_order, recv_order, shift, resident):
    first = jnp.dot(a_rows.astype(jnp.float32), xa_panel.astype(jnp.float32), preferred_element_type=jnp.float32)
    second = jnp.dot(a_rows.astype(jnp.float32), za_panel.astype(jnp.float32), preferred_element_type=jnp.float32)
    schur = first * second
    slot_rows = R_DEV // N_WIDE
    per_device = schur.reshape(N_WIDE, R_DEV, COLS)
    sent = jnp.take_along_axis(per_device, send_order[:, :, None], axis=1)
    buffers = sent.reshape(N_WIDE, N_WIDE, slot_rows, COLS).transpose(1, 0, 2, 3).reshape(N_WIDE, R_DEV, COLS)
    stored = jnp.take_along_axis(buffers, recv_order[:, :, None], axis=1).reshape(N_WIDE * R_DEV, COLS)
    globe = to_global(stored)
    lower, pivots = factor(globe[:PANEL, :PANEL], shift)
    identity = jnp.eye(PANEL, dtype=lower.dtype)
    inverse = lax.linalg.triangular_solve(lower, identity, left_side=True, lower=True, unit_diagonal=True)
    scaled = jnp.dot(globe[:, :PANEL], inverse.T, precision=lax.Precision.HIGHEST)
    panel = jnp.concatenate([lower, (scaled / pivots[None, :])[PANEL:]], axis=0)
    tail = scaled[PANEL:COLS + RES]
    update = jnp.dot(panel, tail.T, precision=lax.Precision.HIGHEST)
    keep = (jnp.arange(N_WIDE * R_DEV) >= PANEL)[:, None]
    formed = globe[:, PANEL:] - jnp.where(keep, update[:, :COLS - PANEL], 0.0)
    factored = to_stored(jnp.concatenate([panel, formed], axis=1))
    resident_glob = to_global(resident).astype(jnp.float32)
    updated = to_stored((resident_glob - jnp.where(keep, update[:, COLS - PANEL:], 0.0)).astype(jnp.bfloat16))
    return (factored, updated, pivots)
```

```python
import functools

import jax
import jax.numpy as jnp
from jax import lax
from jax.experimental import pallas as pl
from jax.experimental.pallas import tpu as pltpu
from jax.sharding import PartitionSpec as P

PANEL = 64
LANES = 128
F32 = jnp.float32
BF16 = jnp.bfloat16
VMEM_BYTES = 48 * 1024 * 1024


def params():
    return pltpu.CompilerParams(vmem_limit_bytes=VMEM_BYTES)


def lane_ids(shape):
    return lax.broadcasted_iota(jnp.int32, shape, len(shape) - 1)


def split(x, count):
    terms = []
    for _ in range(count):
        term = x.astype(BF16)
        terms.append(term)
        x = x - term.astype(F32)
    return terms


def swap_halves(x):
    return pltpu.roll(x, LANES // 2, 1)


def one_hot(index_row, width):
    chunks = []
    step = LANES
    for start in range(0, index_row.shape[1], step):
        piece = jnp.broadcast_to(index_row[:, start : start + step], (step, step))
        at = jnp.transpose(piece)
        lanes = lane_ids((step, step))
        chunks.append(
            jnp.concatenate(
                [(at == lanes + column).astype(F32).astype(BF16) for column in range(0, width, step)],
                axis=1,
            )
        )
    return jnp.concatenate(chunks, axis=0) if len(chunks) > 1 else chunks[0]


def doubling(x, axis, masks):
    size = lax.axis_size(axis)
    held = x[None]
    offsets = [0]
    for number, mask in enumerate(masks):
        other = lax.ppermute(held, axis, [(i, i ^ mask) for i in range(size)])
        offsets = offsets + [offset ^ mask for offset in offsets]
        if number == len(masks) - 1:
            return (held, other), offsets
        held = jnp.concatenate([held, other], axis=0)
    return (held,), offsets


def order_kernel(order_ref, a_ref, out_ref, picks_ref):
    rows = a_ref.shape[0]

    @pl.when(pl.program_id(0) == 0)
    def _():
        for start in range(0, rows, LANES):
            picks_ref[start : start + LANES, :] = one_hot(order_ref[:, start : start + LANES], rows)

    out_ref[...] = jnp.dot(picks_ref[...], a_ref[...], preferred_element_type=F32).astype(BF16)


def order_rows(order, a_rows):
    rows, depth = a_rows.shape
    block = 256
    return pl.pallas_call(
        order_kernel,
        grid=(depth // block,),
        in_specs=[
            pl.BlockSpec((1, rows), lambda i: (0, 0)),
            pl.BlockSpec((rows, block), lambda i: (0, i)),
        ],
        out_specs=pl.BlockSpec((rows, block), lambda i: (0, i)),
        out_shape=jax.ShapeDtypeStruct((rows, depth), BF16),
        scratch_shapes=[pltpu.VMEM((rows, rows), BF16)],
        compiler_params=params(),
        cost_estimate=pl.CostEstimate(
            flops=2 * rows * rows * depth, bytes_accessed=4 * rows * depth, transcendentals=0
        ),
        name="order_rows",
    )(order, a_rows)


def assemble(my_index, offsets, parts, panel_ref):
    position = 0
    for part in parts:
        for number in range(part.shape[0]):
            depth = part.shape[1]
            start = pl.multiple_of((my_index ^ offsets[position]) * depth, depth)
            panel_ref[pl.ds(start, depth), :] = part[number]
            position += 1


def lead_product_kernel(offsets, my_ref, low_ref, high_ref, first_ref, second_ref, out_ref, panel_ref):
    @pl.when(pl.program_id(0) == 0)
    def _():
        assemble(my_ref[0], offsets, (first_ref, second_ref), panel_ref)

    panel = panel_ref[...]
    low = jnp.dot(low_ref[...], panel, preferred_element_type=F32)
    high = jnp.dot(high_ref[...], panel, preferred_element_type=F32)
    low = low * swap_halves(low)
    high = high * swap_halves(high)
    out_ref[...] = jnp.where(lane_ids(low.shape) < PANEL, low, high)


def rest_product_kernel(offsets, my_ref, low_ref, high_ref, first_ref, second_ref, out_ref, panel_ref):
    @pl.when(pl.program_id(0) == 0)
    def _():
        assemble(my_ref[0], offsets, (first_ref, second_ref), panel_ref)

    panel = panel_ref[...]
    low = jnp.dot(low_ref[...], panel, preferred_element_type=F32)
    high = jnp.dot(high_ref[...], panel, preferred_element_type=F32)
    out_ref[:, :LANES] = low[:, :LANES] * low[:, LANES : 2 * LANES]
    out_ref[:, LANES : 2 * LANES] = high[:, :LANES] * high[:, LANES : 2 * LANES]
    low = low[:, 2 * LANES :]
    high = high[:, 2 * LANES :]
    low = low * swap_halves(low)
    high = high * swap_halves(high)
    out_ref[:, 2 * LANES :] = jnp.where(lane_ids(low.shape) < PANEL, low, high)


def products(kernel, name, my_index, ordered, parts, offsets, width):
    rows, depth = ordered.shape
    half = rows // 2
    steps = 2
    block = half // steps
    return pl.pallas_call(
        functools.partial(kernel, offsets),
        grid=(steps,),
        in_specs=[
            pl.BlockSpec(memory_space=pltpu.SMEM),
            pl.BlockSpec((block, depth), lambda i: (i, 0)),
            pl.BlockSpec((block, depth), lambda i: (i + steps, 0)),
            pl.BlockSpec(parts[0].shape, lambda i: (0, 0, 0)),
            pl.BlockSpec(parts[1].shape, lambda i: (0, 0, 0)),
        ],
        out_specs=pl.BlockSpec((block, width), lambda i: (i, 0)),
        out_shape=jax.ShapeDtypeStruct((half, width), F32),
        scratch_shapes=[pltpu.VMEM((depth, width), BF16)],
        compiler_params=params(),
        cost_estimate=pl.CostEstimate(
            flops=2 * rows * depth * width, bytes_accessed=2 * rows * depth, transcendentals=0
        ),
        name=name,
    )(my_index, ordered, ordered, *parts)


def narrow_terms(x, terms_ref, start):
    half = x.shape[0]
    first, second, third = (term.astype(F32) for term in split(x, 3))
    near = lane_ids(x.shape) < PANEL
    terms_ref[:half, start : start + LANES] = jnp.where(near, first, swap_halves(second)).astype(BF16)
    terms_ref[half:, start : start + LANES] = jnp.where(near, swap_halves(first), second).astype(BF16)
    terms_ref[:half, start + LANES : start + 2 * LANES] = third.astype(BF16)
    terms_ref[half:, start + LANES : start + 2 * LANES] = swap_halves(third).astype(BF16)


def stored_kernel(index_ref, arrived_ref, out_ref, terms_ref):
    @pl.when(pl.program_id(0) == 0)
    def _():
        narrow_terms(arrived_ref[...], terms_ref, 0)

    picks = one_hot(index_ref[...], terms_ref.shape[0])
    got = jnp.dot(picks, terms_ref[...], preferred_element_type=F32)
    near = got[:, :LANES]
    whole = (near + swap_halves(near)) + got[:, LANES:]
    out_ref[...] = whole[:, :PANEL]


def stored_rows(index, arrived, count, name):
    half = arrived.shape[0]
    block = min(count, 256)
    if block % LANES:
        block = LANES
    steps = -(-count // block)
    return pl.pallas_call(
        stored_kernel,
        grid=(steps,),
        in_specs=[
            pl.BlockSpec((1, block), lambda i: (0, i)),
            pl.BlockSpec((half, LANES), lambda i: (0, 0)),
        ],
        out_specs=pl.BlockSpec((block, PANEL), lambda i: (i, 0)),
        out_shape=jax.ShapeDtypeStruct((steps * block, PANEL), F32),
        scratch_shapes=[pltpu.VMEM((2 * half, 2 * LANES), BF16)],
        compiler_params=params(),
        cost_estimate=pl.CostEstimate(
            flops=2 * steps * block * 2 * half * 2 * LANES, bytes_accessed=4 * half * LANES, transcendentals=0
        ),
        name=name,
    )(index, arrived)


def eliminate(block, shift_row):
    rows = lax.broadcasted_iota(jnp.int32, (PANEL, PANEL), 0)
    columns = lax.broadcasted_iota(jnp.int32, (PANEL, PANEL), 1)
    flipped = jnp.transpose(block)
    mirrored = jnp.where(rows >= columns, block, flipped)
    diagonal = shift_row + jnp.sum(jnp.abs(mirrored), axis=0, keepdims=True)
    unit = (rows == columns).astype(F32)
    work = jnp.where(rows == columns, diagonal, mirrored)
    work = jnp.concatenate([work, unit], axis=1)
    height = 8
    groups = [work[start : start + height] for start in range(0, PANEL, height)]
    sublanes = lax.broadcasted_iota(jnp.int32, (height, LANES), 0)
    scaled_rows = []
    for k in range(PANEL):
        home, offset = divmod(k, height)
        row = groups[home][offset : offset + 1, :]
        row = row / row[:, k : k + 1]
        scaled_rows.append(row)
        for g in range(home, PANEL // height):
            column = jnp.broadcast_to(groups[g][:, k : k + 1], (height, LANES))
            if g == home:
                column = jnp.where(sublanes > offset, column, 0.0)
            groups[g] = groups[g] - column * row
    final = jnp.concatenate(groups, axis=0)
    scaled = jnp.concatenate(scaled_rows, axis=0)
    upper = jnp.where(columns >= rows, scaled[:, :PANEL], 0.0)
    pivots = jnp.sum(jnp.where(rows == columns, final[:, :PANEL], 0.0), axis=0, keepdims=True)
    return upper, final[:, PANEL:], pivots


def exact(lhs, rhs, dims):
    return lax.dot_general(lhs, rhs, (dims, ((), ())), precision=lax.Precision.HIGHEST, preferred_element_type=F32)


def update_kernel(
    offsets,
    blocks_held,
    columns,
    my_ref,
    first_ref,
    second_ref,
    lead_ref,
    shift_ref,
    resident_ref,
    near_ref,
    far_ref,
    pivots_ref,
    leading_ref,
    tail_ref,
    inverse_ref,
    lower_ref,
):
    my_index = my_ref[0]
    step = pl.program_id(0)
    needed = tail_ref.shape[1]

    @pl.when(step == 0)
    def _():
        size = len(offsets)
        position = 0
        packed = blocks_held * PANEL // 2
        part_rows = PANEL // 2
        for part in (first_ref, second_ref):
            for number in range(part.shape[0]):
                owner = my_index ^ offsets[position]
                for start in range(0, blocks_held * PANEL, part_rows):
                    held, inner = divmod(start, PANEL)
                    if start < packed:
                        rows = part[number, start : start + part_rows, :PANEL]
                    else:
                        rows = part[number, start - packed : start - packed + part_rows, PANEL:]
                    target = pl.multiple_of((held * size + owner) * PANEL + inner, part_rows)
                    leading_ref[pl.ds(target, part_rows), :] = rows
                position += 1
        upper, inverse, pivots = eliminate(leading_ref[:PANEL, :], shift_ref[...])
        pivots_ref[...] = pivots
        inverse_ref[...] = inverse
        lower_ref[...] = jnp.transpose(upper)
        tail = exact(inverse, leading_ref[:needed, :], ((1,), (1,)))
        high, low, _ = split(tail, 3)
        tail_ref[0:PANEL, :] = high
        tail_ref[PANEL : 2 * PANEL, :] = high
        tail_ref[2 * PANEL : 3 * PANEL, :] = low
        tail_ref[3 * PANEL :, :] = low

    block = lead_ref.shape[0]
    panel = exact(lead_ref[...], inverse_ref[...], ((1,), (1,))) / pivots_ref[...]
    row_ids = lax.broadcasted_iota(jnp.int32, panel.shape, 0)
    top = jnp.logical_and(jnp.logical_and(my_index == 0, step == 0), row_ids < PANEL)
    lower = jnp.concatenate([lower_ref[...], jnp.zeros((block - PANEL, PANEL), F32)], axis=0)
    used = jnp.where(top, 0.0, panel)
    high, low = (term.astype(F32) for term in split(used, 2))
    pair = jnp.concatenate([high, low], axis=1).astype(BF16)
    factors = jnp.concatenate([pair, pair], axis=1)
    update = jnp.dot(factors, tail_ref[...], preferred_element_type=F32)
    shown = jnp.concatenate([jnp.where(top, lower, panel), jnp.zeros_like(panel)], axis=1)
    near_ref[:, :LANES] = jnp.where(lane_ids(shown.shape) < PANEL, shown, -update[:, :LANES])
    near_ref[:, LANES:] = -update[:, LANES:columns]
    far_ref[...] = (resident_ref[...].astype(F32) - update[:, columns:]).astype(BF16)


def updates(my_index, parts, offsets, lead, shift, resident, blocks_held, columns):
    rows, width = resident.shape
    needed = columns + width
    steps = 5
    block = rows // steps
    held_rows = len(offsets) * blocks_held * PANEL
    return pl.pallas_call(
        functools.partial(update_kernel, offsets, blocks_held, columns),
        grid=(steps,),
        in_specs=[
            pl.BlockSpec(memory_space=pltpu.SMEM),
            pl.BlockSpec(parts[0].shape, lambda i: (0, 0, 0)),
            pl.BlockSpec(parts[1].shape, lambda i: (0, 0, 0)),
            pl.BlockSpec((block, PANEL), lambda i: (i, 0)),
            pl.BlockSpec((1, PANEL), lambda i: (0, 0)),
            pl.BlockSpec((block, width), lambda i: (i, 0)),
        ],
        out_specs=[
            pl.BlockSpec((block, columns), lambda i: (i, 0)),
            pl.BlockSpec((block, width), lambda i: (i, 0)),
            pl.BlockSpec((1, PANEL), lambda i: (0, 0)),
        ],
        out_shape=[
            jax.ShapeDtypeStruct((rows, columns), F32),
            jax.ShapeDtypeStruct((rows, width), BF16),
            jax.ShapeDtypeStruct((1, PANEL), F32),
        ],
        scratch_shapes=[
            pltpu.VMEM((held_rows, PANEL), F32),
            pltpu.VMEM((4 * PANEL, needed), BF16),
            pltpu.VMEM((PANEL, PANEL), F32),
            pltpu.VMEM((PANEL, PANEL), F32),
        ],
        compiler_params=params(),
        cost_estimate=pl.CostEstimate(
            flops=2 * rows * needed * 4 * PANEL, bytes_accessed=4 * rows * (columns + width), transcendentals=0
        ),
        name="factor_and_update",
    )(my_index, *parts, lead, shift, resident)


def formed_kernel(index_ref, arrived_ref, near_ref, out_ref, terms_ref):
    half = arrived_ref.shape[0]

    @pl.when(pl.program_id(0) == 0)
    def _():
        for side in range(2):
            rows = slice(side * half, (side + 1) * half)
            for number, term in enumerate(split(arrived_ref[:, side * LANES : (side + 1) * LANES], 3)):
                terms_ref[rows, number * LANES : (number + 1) * LANES] = term
        narrow_terms(arrived_ref[:, 2 * LANES :], terms_ref, 3 * LANES)

    picks = one_hot(index_ref[...], terms_ref.shape[0])
    got = jnp.dot(picks, terms_ref[...], preferred_element_type=F32)
    wide = (got[:, :LANES] + got[:, LANES : 2 * LANES]) + got[:, 2 * LANES : 3 * LANES]
    near = got[:, 3 * LANES : 4 * LANES]
    narrow = (near + swap_halves(near)) + swap_halves(got[:, 4 * LANES :])
    held = near_ref[:, :LANES]
    out_ref[:, :LANES] = jnp.where(lane_ids(held.shape) < PANEL, held, narrow + held)
    out_ref[:, LANES:] = wide + near_ref[:, LANES:]


def formed_columns(index, arrived, near):
    rows, columns = near.shape
    half, width = arrived.shape
    steps = 5
    block = rows // steps
    return pl.pallas_call(
        formed_kernel,
        grid=(steps,),
        in_specs=[
            pl.BlockSpec((1, block), lambda i: (0, i)),
            pl.BlockSpec((half, width), lambda i: (0, 0)),
            pl.BlockSpec((block, columns), lambda i: (i, 0)),
        ],
        out_specs=pl.BlockSpec((block, columns), lambda i: (i, 0)),
        out_shape=jax.ShapeDtypeStruct((rows, columns), F32),
        scratch_shapes=[pltpu.VMEM((rows, 5 * LANES), BF16)],
        compiler_params=params(),
        cost_estimate=pl.CostEstimate(
            flops=2 * rows * rows * 5 * LANES, bytes_accessed=8 * rows * columns, transcendentals=0
        ),
        name="formed_columns",
    )(index, arrived, near)


def on_device(a_rows, xa_panel, za_panel, send_order, recv_order, shift, resident):
    rows = a_rows.shape[0]
    columns = xa_panel.shape[1]
    group = lax.axis_size("wide")
    my_index = lax.axis_index("wide").astype(jnp.int32).reshape(1)
    masks = [1 << bit for bit in reversed(range(group.bit_length() - 1))]
    share = rows // group
    half = rows // 2

    lead_panel = jnp.concatenate([xa_panel[:, :PANEL], za_panel[:, :PANEL]], axis=1)
    rest_panel = jnp.concatenate(
        [
            xa_panel[:, 2 * PANEL :],
            za_panel[:, 2 * PANEL :],
            xa_panel[:, PANEL : 2 * PANEL],
            za_panel[:, PANEL : 2 * PANEL],
        ],
        axis=1,
    )
    lead_parts, offsets = doubling(lead_panel, "wide", masks)
    rest_parts, _ = doubling(rest_panel, "wide", masks)

    send = send_order.reshape(group, 2, share // 2).transpose(1, 0, 2).reshape(1, rows)
    source, slot = recv_order // share, recv_order % share
    index = (slot // (share // 2)) * half + source * (share // 2) + slot % (share // 2)

    ordered = order_rows(send, a_rows)
    lead_out = products(
        lead_product_kernel, "lead_products", my_index, ordered, lead_parts, offsets, 2 * PANEL
    )
    lead_in = lax.all_to_all(
        lead_out.reshape(group, half // group, -1), "wide", split_axis=0, concat_axis=0, tiled=True
    ).reshape(half, -1)
    rest_out = products(
        rest_product_kernel, "rest_products", my_index, ordered, rest_parts, offsets, rest_panel.shape[1]
    )
    rest_in = lax.all_to_all(
        rest_out.reshape(group, half // group, -1), "wide", split_axis=0, concat_axis=0, tiled=True
    ).reshape(half, -1)

    needed = columns + resident.shape[1]
    blocks_held = -(-needed // (PANEL * group))
    held = blocks_held * PANEL
    first_rows = stored_rows(index, lead_in, held, "leading_rows")
    packed = jnp.concatenate([first_rows[: held // 2], first_rows[held // 2 : held]], axis=1)
    leading_parts, _ = doubling(packed, "wide", masks)
    lead = stored_rows(index, lead_in, rows, "stored_rows")
    near, updated, pivots = updates(
        my_index, leading_parts, offsets, lead, shift[None, :], resident, blocks_held, columns
    )
    factored = formed_columns(index, rest_in, near)
    return (factored, updated, pivots[0])


def solution(mesh):
    placed = (
        P(("parts", "wide"), None),
        P(("parts", "wide"), None),
        P(("parts", "wide"), None),
        P(("parts", "wide"), None),
        P(("parts", "wide"), None),
        P("parts"),
        P(("parts", "wide"), None),
    )
    return jax.shard_map(
        on_device,
        mesh=mesh,
        in_specs=placed,
        out_specs=(P(("parts", "wide"), None), P(("parts", "wide"), None), P("parts")),
        check_vma=False,
    )
```

```python
import functools

import jax
import jax.numpy as jnp
from jax import lax
from jax.experimental import pallas as pl
from jax.experimental.pallas import tpu as pltpu
from jax.sharding import PartitionSpec as P

PANEL = 64
LANES = 128
F32 = jnp.float32
BF16 = jnp.bfloat16
VMEM_BYTES = 48 * 1024 * 1024


def params():
    return pltpu.CompilerParams(vmem_limit_bytes=VMEM_BYTES)


def lane_ids(shape):
    return lax.broadcasted_iota(jnp.int32, shape, len(shape) - 1)


def split(x, count):
    terms = []
    for _ in range(count):
        term = x.astype(BF16)
        terms.append(term)
        x = x - term.astype(F32)
    return terms


def swap_halves(x):
    return pltpu.roll(x, LANES // 2, 1)


def one_hot(index_row, width):
    chunks = []
    step = LANES
    for start in range(0, index_row.shape[1], step):
        piece = jnp.broadcast_to(index_row[:, start : start + step], (step, step))
        at = jnp.transpose(piece)
        lanes = lane_ids((step, step))
        chunks.append(
            jnp.concatenate(
                [(at == lanes + column).astype(F32).astype(BF16) for column in range(0, width, step)],
                axis=1,
            )
        )
    return jnp.concatenate(chunks, axis=0) if len(chunks) > 1 else chunks[0]


def after(x, *earlier):
    return lax.optimization_barrier((x, *earlier))[0]


def exchange(held, offsets, masks, axis):
    size = lax.axis_size(axis)
    combined = [0]
    for mask in masks:
        combined += [other ^ mask for other in combined]
    parts = [held] + [lax.ppermute(held, axis, [(i, i ^ mask) for i in range(size)]) for mask in combined[1:]]
    offsets = [offset ^ mask for mask in combined for offset in offsets]
    return parts, offsets


def join(parts):
    return jnp.concatenate(parts, axis=0)


def phases(size, narrow):
    bits = [1 << bit for bit in reversed(range(size.bit_length() - 1))]
    groups = [bits[start : start + 2] for start in range(0, len(bits), 2)]
    if not narrow:
        groups = groups[:-1] + [[bit] for bit in groups[-1]]
    return groups


def order_kernel(order_ref, a_ref, out_ref, picks_ref):
    rows = a_ref.shape[0]

    @pl.when(pl.program_id(0) == 0)
    def _():
        for start in range(0, rows, LANES):
            picks_ref[start : start + LANES, :] = one_hot(order_ref[:, start : start + LANES], rows)

    got = jnp.dot(picks_ref[...], a_ref[...], preferred_element_type=F32).astype(BF16)
    out_ref[0] = got[: rows // 2]
    out_ref[1] = got[rows // 2 :]


def order_rows(order, a_rows, first, width):
    rows = a_rows.shape[0]
    block = 256
    skip = first // block
    return pl.pallas_call(
        order_kernel,
        grid=(width // block,),
        in_specs=[
            pl.BlockSpec((1, rows), lambda i: (0, 0)),
            pl.BlockSpec((rows, block), lambda i: (0, i + skip)),
        ],
        out_specs=pl.BlockSpec((2, rows // 2, block), lambda i: (0, 0, i)),
        out_shape=jax.ShapeDtypeStruct((2, rows // 2, width), BF16),
        scratch_shapes=[pltpu.VMEM((rows, rows), BF16)],
        compiler_params=params(),
        cost_estimate=pl.CostEstimate(
            flops=2 * rows * rows * width, bytes_accessed=4 * rows * width, transcendentals=0
        ),
        name="order_rows",
    )(order, a_rows)


def panels_kernel(xa_ref, za_ref, lead_ref, rest_ref):
    lead_ref[0] = jnp.concatenate([xa_ref[:, :PANEL], za_ref[:, :PANEL]], axis=1)
    rest_ref[0, :, :LANES] = xa_ref[:, 2 * PANEL :]
    rest_ref[0, :, LANES : 2 * LANES] = za_ref[:, 2 * PANEL :]
    rest_ref[0, :, 2 * LANES :] = jnp.concatenate(
        [xa_ref[:, PANEL : 2 * PANEL], za_ref[:, PANEL : 2 * PANEL]], axis=1
    )


def split_panels(xa_panel, za_panel):
    depth = xa_panel.shape[0]
    return pl.pallas_call(
        panels_kernel,
        out_shape=[
            jax.ShapeDtypeStruct((1, depth, LANES), BF16),
            jax.ShapeDtypeStruct((1, depth, 3 * LANES), BF16),
        ],
        compiler_params=params(),
        name="split_panels",
    )(xa_panel, za_panel)


def assemble(my_index, offsets, parts, panel_ref):
    position = 0
    for part in parts:
        for number in range(part.shape[0]):
            depth = part.shape[1]
            start = pl.multiple_of((my_index ^ offsets[position]) * depth, depth)
            panel_ref[pl.ds(start, depth), :] = part[number]
            position += 1


def ordered_products(pieces, panel_ref, side):
    total = None
    start = 0
    for piece in pieces:
        depth = piece.shape[2]
        product = jnp.dot(piece[side], panel_ref[start : start + depth, :], preferred_element_type=F32)
        total = product if total is None else total + product
        start += depth
    return total


def lead_product_kernel(offsets, count, my_ref, *refs):
    pieces, parts, (out_ref, panel_ref) = refs[:count], refs[count:-2], refs[-2:]

    @pl.when(pl.program_id(0) == 0)
    def _():
        assemble(my_ref[0], offsets, parts, panel_ref)

    low = ordered_products(pieces, panel_ref, 0)
    high = ordered_products(pieces, panel_ref, 1)
    low = low * swap_halves(low)
    high = high * swap_halves(high)
    out_ref[...] = jnp.where(lane_ids(low.shape) < PANEL, low, high)


def rest_product_kernel(offsets, count, my_ref, *refs):
    pieces, parts, (out_ref, panel_ref) = refs[:count], refs[count:-2], refs[-2:]

    @pl.when(pl.program_id(0) == 0)
    def _():
        assemble(my_ref[0], offsets, parts, panel_ref)

    low = ordered_products(pieces, panel_ref, 0)
    high = ordered_products(pieces, panel_ref, 1)
    out_ref[:, :LANES] = low[:, :LANES] * low[:, LANES : 2 * LANES]
    out_ref[:, LANES : 2 * LANES] = high[:, :LANES] * high[:, LANES : 2 * LANES]
    low = low[:, 2 * LANES :]
    high = high[:, 2 * LANES :]
    low = low * swap_halves(low)
    high = high * swap_halves(high)
    out_ref[:, 2 * LANES :] = jnp.where(lane_ids(low.shape) < PANEL, low, high)


def products(kernel, name, my_index, pieces, parts, offsets, width):
    half = pieces[0].shape[1]
    depth = sum(piece.shape[2] for piece in pieces)
    steps = 4
    block = half // steps
    return pl.pallas_call(
        functools.partial(kernel, offsets, len(pieces)),
        grid=(steps,),
        in_specs=[pl.BlockSpec(memory_space=pltpu.SMEM)]
        + [pl.BlockSpec((2, block, piece.shape[2]), lambda i: (0, i, 0)) for piece in pieces]
        + [pl.BlockSpec(part.shape, lambda i: (0, 0, 0)) for part in parts],
        out_specs=pl.BlockSpec((block, width), lambda i: (i, 0)),
        out_shape=jax.ShapeDtypeStruct((half, width), F32),
        scratch_shapes=[pltpu.VMEM((depth, width), BF16)],
        compiler_params=params(),
        cost_estimate=pl.CostEstimate(
            flops=4 * half * depth * width, bytes_accessed=4 * half * depth, transcendentals=0
        ),
        name=name,
    )(my_index, *pieces, *parts)


def narrow_terms(x, terms_ref, start):
    half = x.shape[0]
    first, second, third = (term.astype(F32) for term in split(x, 3))
    near = lane_ids(x.shape) < PANEL
    terms_ref[:half, start : start + LANES] = jnp.where(near, first, swap_halves(second)).astype(BF16)
    terms_ref[half:, start : start + LANES] = jnp.where(near, swap_halves(first), second).astype(BF16)
    terms_ref[:half, start + LANES : start + 2 * LANES] = third.astype(BF16)
    terms_ref[half:, start + LANES : start + 2 * LANES] = swap_halves(third).astype(BF16)


def stored_kernel(index_ref, arrived_ref, out_ref, terms_ref):
    @pl.when(pl.program_id(0) == 0)
    def _():
        narrow_terms(arrived_ref[...], terms_ref, 0)

    picks = one_hot(index_ref[...], terms_ref.shape[0])
    got = jnp.dot(picks, terms_ref[...], preferred_element_type=F32)
    near = got[:, :LANES]
    whole = (near + swap_halves(near)) + got[:, LANES:]
    out_ref[...] = whole[:, :PANEL]


def stored_rows(index, arrived, count, name):
    half = arrived.shape[0]
    block = min(count, 256)
    if block % LANES:
        block = LANES
    steps = -(-count // block)
    return pl.pallas_call(
        stored_kernel,
        grid=(steps,),
        in_specs=[
            pl.BlockSpec((1, block), lambda i: (0, i)),
            pl.BlockSpec((half, LANES), lambda i: (0, 0)),
        ],
        out_specs=pl.BlockSpec((block, PANEL), lambda i: (i, 0)),
        out_shape=jax.ShapeDtypeStruct((steps * block, PANEL), F32),
        scratch_shapes=[pltpu.VMEM((2 * half, 2 * LANES), BF16)],
        compiler_params=params(),
        cost_estimate=pl.CostEstimate(
            flops=2 * steps * block * 2 * half * 2 * LANES, bytes_accessed=4 * half * LANES, transcendentals=0
        ),
        name=name,
    )(index, arrived)


def eliminate(block, shift_row):
    rows = lax.broadcasted_iota(jnp.int32, (PANEL, PANEL), 0)
    columns = lax.broadcasted_iota(jnp.int32, (PANEL, PANEL), 1)
    flipped = jnp.transpose(block)
    mirrored = jnp.where(rows >= columns, block, flipped)
    diagonal = shift_row + jnp.sum(jnp.abs(mirrored), axis=0, keepdims=True)
    unit = (rows == columns).astype(F32)
    work = jnp.where(rows == columns, diagonal, mirrored)
    work = jnp.concatenate([work, unit], axis=1)
    height = 8
    groups = [work[start : start + height] for start in range(0, PANEL, height)]
    sublanes = lax.broadcasted_iota(jnp.int32, (height, LANES), 0)
    scaled_rows = []
    for k in range(PANEL):
        home, offset = divmod(k, height)
        row = groups[home][offset : offset + 1, :]
        row = row / row[:, k : k + 1]
        scaled_rows.append(row)
        for g in range(home, PANEL // height):
            column = jnp.broadcast_to(groups[g][:, k : k + 1], (height, LANES))
            if g == home:
                column = jnp.where(sublanes > offset, column, 0.0)
            groups[g] = groups[g] - column * row
    final = jnp.concatenate(groups, axis=0)
    scaled = jnp.concatenate(scaled_rows, axis=0)
    upper = jnp.where(columns >= rows, scaled[:, :PANEL], 0.0)
    pivots = jnp.sum(jnp.where(rows == columns, final[:, :PANEL], 0.0), axis=0, keepdims=True)
    return upper, final[:, PANEL:], pivots


def exact(lhs, rhs, dims):
    return lax.dot_general(lhs, rhs, (dims, ((), ())), precision=lax.Precision.HIGHEST, preferred_element_type=F32)


def update_kernel(
    offsets,
    blocks_held,
    columns,
    my_ref,
    lead_ref,
    shift_ref,
    resident_ref,
    *refs,
):
    parts = refs[:-7]
    near_ref, far_ref, pivots_ref, leading_ref, tail_ref, inverse_ref, lower_ref = refs[-7:]
    my_index = my_ref[0]
    step = pl.program_id(0)
    needed = tail_ref.shape[1]

    @pl.when(step == 0)
    def _():
        size = len(offsets)
        position = 0
        packed = blocks_held * PANEL // 2
        part_rows = PANEL // 2
        for part in parts:
            for number in range(part.shape[0]):
                owner = my_index ^ offsets[position]
                for start in range(0, blocks_held * PANEL, part_rows):
                    held, inner = divmod(start, PANEL)
                    if start < packed:
                        rows = part[number, start : start + part_rows, :PANEL]
                    else:
                        rows = part[number, start - packed : start - packed + part_rows, PANEL:]
                    target = pl.multiple_of((held * size + owner) * PANEL + inner, part_rows)
                    leading_ref[pl.ds(target, part_rows), :] = rows
                position += 1
        upper, inverse, pivots = eliminate(leading_ref[:PANEL, :], shift_ref[...])
        pivots_ref[...] = pivots
        inverse_ref[...] = inverse
        lower_ref[...] = jnp.transpose(upper)
        tail = exact(inverse, leading_ref[:needed, :], ((1,), (1,)))
        high, low, _ = split(tail, 3)
        tail_ref[0:PANEL, :] = high
        tail_ref[PANEL : 2 * PANEL, :] = high
        tail_ref[2 * PANEL : 3 * PANEL, :] = low
        tail_ref[3 * PANEL :, :] = low

    block = lead_ref.shape[0]
    panel = exact(lead_ref[...], inverse_ref[...], ((1,), (1,))) / pivots_ref[...]
    row_ids = lax.broadcasted_iota(jnp.int32, panel.shape, 0)
    top = jnp.logical_and(jnp.logical_and(my_index == 0, step == 0), row_ids < PANEL)
    lower = jnp.concatenate([lower_ref[...], jnp.zeros((block - PANEL, PANEL), F32)], axis=0)
    used = jnp.where(top, 0.0, panel)
    high, low = (term.astype(F32) for term in split(used, 2))
    pair = jnp.concatenate([high, low], axis=1).astype(BF16)
    factors = jnp.concatenate([pair, pair], axis=1)
    update = jnp.dot(factors, tail_ref[...], preferred_element_type=F32)
    shown = jnp.concatenate([jnp.where(top, lower, panel), jnp.zeros_like(panel)], axis=1)
    near_ref[:, :LANES] = jnp.where(lane_ids(shown.shape) < PANEL, shown, -update[:, :LANES])
    near_ref[:, LANES:] = -update[:, LANES:columns]
    far_ref[...] = (resident_ref[...].astype(F32) - update[:, columns:]).astype(BF16)


def updates(my_index, parts, offsets, lead, shift, resident, blocks_held, columns):
    rows, width = resident.shape
    needed = columns + width
    steps = 5
    block = rows // steps
    held_rows = len(offsets) * blocks_held * PANEL
    return pl.pallas_call(
        functools.partial(update_kernel, offsets, blocks_held, columns),
        grid=(steps,),
        in_specs=[
            pl.BlockSpec(memory_space=pltpu.SMEM),
            pl.BlockSpec((block, PANEL), lambda i: (i, 0)),
            pl.BlockSpec((1, PANEL), lambda i: (0, 0)),
            pl.BlockSpec((block, width), lambda i: (i, 0)),
        ]
        + [pl.BlockSpec(part.shape, lambda i: (0, 0, 0)) for part in parts],
        out_specs=[
            pl.BlockSpec((block, columns), lambda i: (i, 0)),
            pl.BlockSpec((block, width), lambda i: (i, 0)),
            pl.BlockSpec((1, PANEL), lambda i: (0, 0)),
        ],
        out_shape=[
            jax.ShapeDtypeStruct((rows, columns), F32),
            jax.ShapeDtypeStruct((rows, width), BF16),
            jax.ShapeDtypeStruct((1, PANEL), F32),
        ],
        scratch_shapes=[
            pltpu.VMEM((held_rows, PANEL), F32),
            pltpu.VMEM((4 * PANEL, needed), BF16),
            pltpu.VMEM((PANEL, PANEL), F32),
            pltpu.VMEM((PANEL, PANEL), F32),
        ],
        compiler_params=params(),
        cost_estimate=pl.CostEstimate(
            flops=2 * rows * needed * 4 * PANEL, bytes_accessed=4 * rows * (columns + width), transcendentals=0
        ),
        name="factor_and_update",
    )(my_index, lead, shift, resident, *parts)


def formed_kernel(index_ref, arrived_ref, near_ref, out_ref, terms_ref):
    half = arrived_ref.shape[0]

    @pl.when(pl.program_id(0) == 0)
    def _():
        for side in range(2):
            rows = slice(side * half, (side + 1) * half)
            for number, term in enumerate(split(arrived_ref[:, side * LANES : (side + 1) * LANES], 3)):
                terms_ref[rows, number * LANES : (number + 1) * LANES] = term
        narrow_terms(arrived_ref[:, 2 * LANES :], terms_ref, 3 * LANES)

    picks = one_hot(index_ref[...], terms_ref.shape[0])
    got = jnp.dot(picks, terms_ref[...], preferred_element_type=F32)
    wide = (got[:, :LANES] + got[:, LANES : 2 * LANES]) + got[:, 2 * LANES : 3 * LANES]
    near = got[:, 3 * LANES : 4 * LANES]
    narrow = (near + swap_halves(near)) + swap_halves(got[:, 4 * LANES :])
    held = near_ref[:, :LANES]
    out_ref[:, :LANES] = jnp.where(lane_ids(held.shape) < PANEL, held, narrow + held)
    out_ref[:, LANES:] = wide + near_ref[:, LANES:]


def formed_columns(index, arrived, near):
    rows, columns = near.shape
    half, width = arrived.shape
    steps = 5
    block = rows // steps
    return pl.pallas_call(
        formed_kernel,
        grid=(steps,),
        in_specs=[
            pl.BlockSpec((1, block), lambda i: (0, i)),
            pl.BlockSpec((half, width), lambda i: (0, 0)),
            pl.BlockSpec((block, columns), lambda i: (i, 0)),
        ],
        out_specs=pl.BlockSpec((block, columns), lambda i: (i, 0)),
        out_shape=jax.ShapeDtypeStruct((rows, columns), F32),
        scratch_shapes=[pltpu.VMEM((rows, 5 * LANES), BF16)],
        compiler_params=params(),
        cost_estimate=pl.CostEstimate(
            flops=2 * rows * rows * 5 * LANES, bytes_accessed=8 * rows * columns, transcendentals=0
        ),
        name="formed_columns",
    )(index, arrived, near)


def on_device(a_rows, xa_panel, za_panel, send_order, recv_order, shift, resident):
    rows, depth = a_rows.shape
    columns = xa_panel.shape[1]
    group = lax.axis_size("wide")
    my_index = lax.axis_index("wide").astype(jnp.int32).reshape(1)
    share = rows // group
    half = rows // 2
    narrow = phases(group, True)
    wide = phases(group, False)

    send = send_order.reshape(group, 2, share // 2).transpose(1, 0, 2).reshape(1, rows)
    source, slot = recv_order // share, recv_order % share
    index = (slot // (share // 2)) * half + source * (share // 2) + slot % (share // 2)

    lead_panel, rest_panel = split_panels(xa_panel, za_panel)
    lead_parts, offsets = exchange(lead_panel, [0], narrow[0], "wide")
    rest_parts, rest_offsets = exchange(rest_panel, [0], wide[0], "wide")
    pieces = []
    for number, masks in enumerate(narrow[1:]):
        if number < 1:
            pieces.append(order_rows(send, a_rows, 0, depth // 2))
        lead_parts, offsets = exchange(after(join(lead_parts), *pieces), offsets, masks, "wide")
    pieces.append(order_rows(send, a_rows, depth // 2, depth // 2))

    lead_out = products(
        lead_product_kernel, "lead_products", my_index, pieces, lead_parts, offsets, 2 * PANEL
    )
    lead_in = lax.all_to_all(
        lead_out.reshape(group, half // group, -1), "wide", split_axis=0, concat_axis=0, tiled=True
    ).reshape(half, -1)
    rest_parts = [after(join(rest_parts), lead_out)]
    for masks in wide[1:]:
        rest_parts, rest_offsets = exchange(join(rest_parts), rest_offsets, masks, "wide")

    needed = columns + resident.shape[1]
    blocks_held = -(-needed // (PANEL * group))
    held = blocks_held * PANEL
    first_rows = stored_rows(index, lead_in, held, "leading_rows")
    packed = jnp.concatenate([first_rows[: held // 2], first_rows[held // 2 : held]], axis=1)
    leading_parts, leading_offsets = [packed[None]], [0]
    for masks in narrow:
        leading_parts, leading_offsets = exchange(join(leading_parts), leading_offsets, masks, "wide")
    lead = stored_rows(index, lead_in, rows, "stored_rows")

    rest_out = products(
        rest_product_kernel, "rest_products", my_index, pieces, rest_parts, rest_offsets, 6 * PANEL
    )
    rest_in = lax.all_to_all(
        after(rest_out, *leading_parts).reshape(group, half // group, -1),
        "wide",
        split_axis=0,
        concat_axis=0,
        tiled=True,
    ).reshape(half, -1)
    near, updated, pivots = updates(
        my_index, leading_parts, leading_offsets, after(lead, rest_out), shift[None, :], resident, blocks_held, columns
    )
    factored = formed_columns(index, rest_in, near)
    return (factored, updated, pivots[0])


def solution(mesh):
    placed = (
        P(("parts", "wide"), None),
        P(("parts", "wide"), None),
        P(("parts", "wide"), None),
        P(("parts", "wide"), None),
        P(("parts", "wide"), None),
        P("parts"),
        P(("parts", "wide"), None),
    )
    return jax.shard_map(
        on_device,
        mesh=mesh,
        in_specs=placed,
        out_specs=(P(("parts", "wide"), None), P(("parts", "wide"), None), P("parts")),
        check_vma=False,
    )
```

```python
import functools

import jax
import jax.numpy as jnp
from jax import lax
from jax.experimental import pallas as pl
from jax.experimental.pallas import tpu as pltpu
from jax.sharding import PartitionSpec as P

PANEL = 64
LANES = 128
F32 = jnp.float32
BF16 = jnp.bfloat16
MIB = 1024 * 1024


def params(mebibytes=24):
    return pltpu.CompilerParams(vmem_limit_bytes=mebibytes * MIB)


def lane_ids(shape):
    return lax.broadcasted_iota(jnp.int32, shape, len(shape) - 1)


def split(x, count):
    terms = []
    for _ in range(count):
        term = x.astype(BF16)
        terms.append(term)
        x = x - term.astype(F32)
    return terms


def swap_halves(x):
    return pltpu.roll(x, LANES // 2, 1)


def one_hot(index_row, width):
    chunks = []
    step = LANES
    for start in range(0, index_row.shape[1], step):
        piece = jnp.broadcast_to(index_row[:, start : start + step], (step, step))
        at = jnp.transpose(piece)
        lanes = lane_ids((step, step))
        chunks.append(
            jnp.concatenate(
                [(at == lanes + column).astype(F32).astype(BF16) for column in range(0, width, step)],
                axis=1,
            )
        )
    return jnp.concatenate(chunks, axis=0) if len(chunks) > 1 else chunks[0]


def after(x, *earlier):
    return lax.optimization_barrier((x, *earlier))[0]


def exchange(held, offsets, masks, axis):
    size = lax.axis_size(axis)
    combined = [0]
    for mask in masks:
        combined += [other ^ mask for other in combined]
    parts = [held] + [lax.ppermute(held, axis, [(i, i ^ mask) for i in range(size)]) for mask in combined[1:]]
    offsets = [offset ^ mask for mask in combined for offset in offsets]
    return parts, offsets


def join(parts):
    return jnp.concatenate(parts, axis=0)


def gather(x, masks, axis):
    parts, offsets = [x], [0]
    for group in masks:
        parts, offsets = exchange(join(parts), offsets, group, axis)
    return parts, offsets


def phases(size):
    bits = [1 << bit for bit in reversed(range(size.bit_length() - 1))]
    pairs = [bits[start : start + 2] for start in range(0, len(bits), 2)]
    far = [bits[start : start + 2] for start in range(0, len(bits) - 2, 2)]
    return pairs, far + [bits[-2:-1], bits[-1:]], [bits[-2:-1]] + far + [bits[-1:]]


def picks_kernel(send_ref, index_ref, send_picks_ref, index_picks_ref):
    width = send_picks_ref.shape[1]
    send_picks_ref[...] = one_hot(send_ref[...], width)
    index_picks_ref[...] = one_hot(index_ref[...], width)


def order_picks(send, index):
    rows = send.shape[1]
    block = LANES
    return pl.pallas_call(
        picks_kernel,
        grid=(rows // block,),
        in_specs=[pl.BlockSpec((1, block), lambda i: (0, i))] * 2,
        out_specs=[pl.BlockSpec((block, rows), lambda i: (i, 0))] * 2,
        out_shape=[jax.ShapeDtypeStruct((rows, rows), BF16)] * 2,
        compiler_params=params(8),
        cost_estimate=pl.CostEstimate(flops=4 * rows * rows, bytes_accessed=4 * rows * rows, transcendentals=0),
        name="order_picks",
    )(send, index)


def panels_kernel(xa_hbm, za_hbm, lead_ref, near_ref, far_ref, xa_ref, za_ref, sems):
    copies = [
        pltpu.make_async_copy(xa_hbm, xa_ref, sems.at[0]),
        pltpu.make_async_copy(za_hbm, za_ref, sems.at[1]),
    ]
    for copy in copies:
        copy.start()
    for copy in copies:
        copy.wait()
    lead_ref[0] = jnp.concatenate([xa_ref[:, :PANEL], za_ref[:, :PANEL]], axis=1)
    near_ref[0] = jnp.concatenate([xa_ref[:, PANEL : 2 * PANEL], za_ref[:, PANEL : 2 * PANEL]], axis=1)
    far_ref[0, :, :LANES] = xa_ref[:, LANES:]
    far_ref[0, :, LANES:] = za_ref[:, LANES:]


def split_panels(xa_panel, za_panel):
    depth, columns = xa_panel.shape
    return pl.pallas_call(
        panels_kernel,
        in_specs=[pl.BlockSpec(memory_space=pl.ANY)] * 2,
        out_shape=[
            jax.ShapeDtypeStruct((1, depth, LANES), BF16),
            jax.ShapeDtypeStruct((1, depth, LANES), BF16),
            jax.ShapeDtypeStruct((1, depth, 2 * (columns - LANES)), BF16),
        ],
        scratch_shapes=[
            pltpu.VMEM((depth, columns), BF16),
            pltpu.VMEM((depth, columns), BF16),
            pltpu.SemaphoreType.DMA((2,)),
        ],
        compiler_params=params(8),
        name="split_panels",
    )(xa_panel, za_panel)


def assemble(my_index, offsets, parts, panel_ref):
    position = 0
    for part in parts:
        for number in range(part.shape[0]):
            depth = part.shape[1]
            start = pl.multiple_of((my_index ^ offsets[position]) * depth, depth)
            panel_ref[pl.ds(start, depth), :] = part[number]
            position += 1


def whole_sum(got):
    pair = got[:, :LANES]
    return (pair + swap_halves(pair)) + got[:, LANES:]


def lead_product_kernel(offsets, my_ref, a_ref, picks_ref, *refs):
    parts, (out_ref, panel_ref, terms_ref) = refs[:-3], refs[-3:]
    assemble(my_ref[0], offsets, parts, panel_ref)
    rows = a_ref.shape[0]
    block = 256
    for start in range(0, rows, block):
        both = jnp.dot(a_ref[start : start + block, :], panel_ref[...], preferred_element_type=F32)
        first, second, third = (term.astype(F32) for term in split(both * swap_halves(both), 3))
        near = lane_ids(both.shape) < PANEL
        terms_ref[start : start + block, :LANES] = jnp.where(near, first, second).astype(BF16)
        terms_ref[start : start + block, LANES:] = third.astype(BF16)
    half = rows // 2
    block = half // 2
    for start in range(0, half, block):
        low = jnp.dot(picks_ref[start : start + block, :], terms_ref[...], preferred_element_type=F32)
        high = jnp.dot(picks_ref[half + start : half + start + block, :], terms_ref[...], preferred_element_type=F32)
        low, high = whole_sum(low), whole_sum(high)
        out_ref[start : start + block, :] = jnp.where(lane_ids(low.shape) < PANEL, low, high)


def lead_products(my_index, a_rows, picks, parts, offsets):
    rows, depth = a_rows.shape
    return pl.pallas_call(
        functools.partial(lead_product_kernel, offsets),
        in_specs=[pl.BlockSpec(memory_space=pltpu.SMEM)] + [pl.BlockSpec(memory_space=pltpu.VMEM)] * (2 + len(parts)),
        out_specs=pl.BlockSpec(memory_space=pltpu.VMEM),
        out_shape=jax.ShapeDtypeStruct((rows // 2, LANES), F32),
        scratch_shapes=[pltpu.VMEM((depth, LANES), BF16), pltpu.VMEM((rows, 2 * LANES), BF16)],
        compiler_params=params(),
        cost_estimate=pl.CostEstimate(
            flops=2 * rows * (depth + 2 * rows) * LANES, bytes_accessed=2 * rows * depth, transcendentals=0
        ),
        name="lead_products",
    )(my_index, a_rows, picks, *parts)


BIAS = 128


def rest_product_kernel(near_offsets, far_offsets, near_count, my_ref, a_ref, picks_ref, *refs):
    parts, (out_ref, panel_ref, terms_ref) = refs[:-3], refs[-3:]
    assemble(my_ref[0], near_offsets, parts[:near_count], panel_ref.at[:, :LANES])
    assemble(my_ref[0], far_offsets, parts[near_count:], panel_ref.at[:, LANES:])
    rows = a_ref.shape[0]
    block = 256
    for start in range(0, rows, block):
        both = jnp.dot(a_ref[start : start + block, :], panel_ref[...], preferred_element_type=F32)
        near = both[:, :LANES]
        near = near * swap_halves(near)
        far = both[:, LANES : 2 * LANES] * both[:, 2 * LANES :]
        largest = jnp.max(jnp.maximum(jnp.abs(near), jnp.abs(far)), axis=1, keepdims=True)
        largest = jnp.maximum(largest, 1e-30)
        exponent = jnp.floor(jnp.log2(largest)) + 1.0
        far = jnp.floor(far * jnp.exp2(15.0 - exponent) + 0.5)
        far = jnp.minimum(jnp.maximum(far, -32767.0), 32767.0)
        near = jnp.floor(near * jnp.exp2(23.0 - exponent) + 0.5)
        near = jnp.minimum(jnp.maximum(near, -8388607.0), 8388607.0)
        far_top = jnp.floor(far * (1 / 256))
        near_top = jnp.floor(near * (1 / 65536))
        near = near - near_top * 65536.0
        near_middle = jnp.floor(near * (1 / 256))
        low_lanes = lane_ids(near.shape) < PANEL
        rows_here = slice(start, start + block)
        terms_ref[rows_here, :LANES] = far_top.astype(BF16)
        terms_ref[rows_here, LANES : 2 * LANES] = (far - far_top * 256.0).astype(BF16)
        terms_ref[rows_here, 2 * LANES : 3 * LANES] = jnp.where(low_lanes, near_top, near_middle).astype(BF16)
        terms_ref[rows_here, 3 * LANES :] = jnp.where(low_lanes, near - near_middle * 256.0, exponent).astype(BF16)

    def coded(start, size):
        got = jnp.dot(picks_ref[start : start + size, :], terms_ref[...], preferred_element_type=F32)
        far = got[:, :LANES] * 256.0 + got[:, LANES : 2 * LANES]
        tops, lows = got[:, 2 * LANES : 3 * LANES], got[:, 3 * LANES :]
        low_lanes = lane_ids(tops.shape) < PANEL
        tops = tops * jnp.where(low_lanes, 65536.0, 256.0)
        swapped = swap_halves(lows)
        near = tops + swap_halves(tops) + jnp.where(low_lanes, lows, swapped)
        exponent = jnp.where(low_lanes, swapped, lows)
        near = near.astype(jnp.int32) * 256 + (exponent.astype(jnp.int32) + BIAS)
        return far.astype(jnp.int32), near

    half = rows // 2
    block = half // 2
    for start in range(0, half, block):
        far_low, near_low = coded(start, block)
        far_high, near_high = coded(half + start, block)
        out_ref[start : start + block, :LANES] = far_low * 65536 + (far_high & 65535)
        out_ref[start : start + block, LANES:] = jnp.where(lane_ids(near_low.shape) < PANEL, near_low, near_high)


def rest_products(my_index, a_rows, picks, near_parts, near_offsets, far_parts, far_offsets):
    rows, depth = a_rows.shape
    parts = [*near_parts, *far_parts]
    return pl.pallas_call(
        functools.partial(rest_product_kernel, near_offsets, far_offsets, len(near_parts)),
        in_specs=[pl.BlockSpec(memory_space=pltpu.SMEM)] + [pl.BlockSpec(memory_space=pltpu.VMEM)] * (2 + len(parts)),
        out_specs=pl.BlockSpec(memory_space=pltpu.VMEM),
        out_shape=jax.ShapeDtypeStruct((rows // 2, 2 * LANES), jnp.int32),
        scratch_shapes=[pltpu.VMEM((depth, 3 * LANES), BF16), pltpu.VMEM((rows, 4 * LANES), BF16)],
        compiler_params=params(),
        cost_estimate=pl.CostEstimate(
            flops=2 * rows * (3 * depth + 4 * rows) * LANES, bytes_accessed=2 * rows * depth, transcendentals=0
        ),
        name="rest_products",
    )(my_index, a_rows, picks, *parts)


def packed_terms(x, terms_ref, start):
    half = x.shape[0]
    first, second, third = (term.astype(F32) for term in split(x, 3))
    near = lane_ids(x.shape) < PANEL
    other = swap_halves(third)
    terms_ref[:half, start : start + LANES] = jnp.where(near, first, swap_halves(second)).astype(BF16)
    terms_ref[half:, start : start + LANES] = jnp.where(near, swap_halves(first), second).astype(BF16)
    terms_ref[:half, start + LANES : start + 2 * LANES] = jnp.where(near, third, other).astype(BF16)
    terms_ref[half:, start + LANES : start + 2 * LANES] = jnp.where(near, other, third).astype(BF16)


def leading_kernel(held, picks_ref, arrived_ref, out_ref, terms_ref):
    packed_terms(arrived_ref[...], terms_ref, 0)
    got = whole_sum(jnp.dot(picks_ref[:held, :], terms_ref[...], preferred_element_type=F32))
    first, second = got[: held // 2], got[held // 2 :]
    out_ref[0] = jnp.where(lane_ids(first.shape) < PANEL, first, second)


def leading_rows(picks, arrived, held):
    rows = picks.shape[0]
    return pl.pallas_call(
        functools.partial(leading_kernel, held),
        in_specs=[pl.BlockSpec(memory_space=pltpu.VMEM)] * 2,
        out_specs=pl.BlockSpec(memory_space=pltpu.VMEM),
        out_shape=jax.ShapeDtypeStruct((1, held // 2, LANES), F32),
        scratch_shapes=[pltpu.VMEM((rows, 2 * LANES), BF16)],
        compiler_params=params(16),
        cost_estimate=pl.CostEstimate(
            flops=4 * held * rows * LANES, bytes_accessed=2 * rows * LANES, transcendentals=0
        ),
        name="leading_rows",
    )(picks, arrived)


def stored_kernel(picks_ref, arrived_ref, out_ref, terms_ref):
    packed_terms(arrived_ref[...], terms_ref, 0)
    rows = picks_ref.shape[0]
    block = 256
    for start in range(0, rows, block):
        got = jnp.dot(picks_ref[start : start + block, :], terms_ref[...], preferred_element_type=F32)
        out_ref[start : start + block, :] = whole_sum(got)[:, :PANEL]


def stored_rows(picks, arrived):
    rows = picks.shape[0]
    return pl.pallas_call(
        stored_kernel,
        in_specs=[pl.BlockSpec(memory_space=pltpu.VMEM)] * 2,
        out_specs=pl.BlockSpec(memory_space=pltpu.VMEM),
        out_shape=jax.ShapeDtypeStruct((rows, PANEL), F32),
        scratch_shapes=[pltpu.VMEM((rows, 2 * LANES), BF16)],
        compiler_params=params(16),
        cost_estimate=pl.CostEstimate(
            flops=4 * rows * rows * LANES, bytes_accessed=2 * rows * rows, transcendentals=0
        ),
        name="stored_rows",
    )(picks, arrived)


def eliminate(block, shift_row):
    rows = lax.broadcasted_iota(jnp.int32, (PANEL, PANEL), 0)
    columns = lax.broadcasted_iota(jnp.int32, (PANEL, PANEL), 1)
    flipped = jnp.transpose(block)
    mirrored = jnp.where(rows >= columns, block, flipped)
    diagonal = shift_row + jnp.sum(jnp.abs(mirrored), axis=0, keepdims=True)
    unit = (rows == columns).astype(F32)
    work = jnp.where(rows == columns, diagonal, mirrored)
    work = jnp.concatenate([work, unit], axis=1)
    height = 8
    groups = [work[start : start + height] for start in range(0, PANEL, height)]
    sublanes = lax.broadcasted_iota(jnp.int32, (height, LANES), 0)
    scaled_rows = []
    for k in range(PANEL):
        home, offset = divmod(k, height)
        row = groups[home][offset : offset + 1, :]
        row = row / row[:, k : k + 1]
        scaled_rows.append(row)
        for g in range(home, PANEL // height):
            column = jnp.broadcast_to(groups[g][:, k : k + 1], (height, LANES))
            if g == home:
                column = jnp.where(sublanes > offset, column, 0.0)
            groups[g] = groups[g] - column * row
    final = jnp.concatenate(groups, axis=0)
    scaled = jnp.concatenate(scaled_rows, axis=0)
    upper = jnp.where(columns >= rows, scaled[:, :PANEL], 0.0)
    pivots = jnp.sum(jnp.where(rows == columns, final[:, :PANEL], 0.0), axis=0, keepdims=True)
    return upper, final[:, PANEL:], pivots


def exact(lhs, rhs, dims):
    return lax.dot_general(lhs, rhs, (dims, ((), ())), precision=lax.Precision.HIGHEST, preferred_element_type=F32)


def update_kernel(
    offsets,
    blocks_held,
    columns,
    my_ref,
    lead_ref,
    shift_ref,
    resident_ref,
    *refs,
):
    parts = refs[:-7]
    near_ref, far_ref, pivots_ref, leading_ref, tail_ref, inverse_ref, lower_ref = refs[-7:]
    my_index = my_ref[0]
    step = pl.program_id(0)
    needed = tail_ref.shape[1]

    @pl.when(step == 0)
    def _():
        size = len(offsets)
        position = 0
        packed = blocks_held * PANEL // 2
        part_rows = PANEL // 2
        for part in parts:
            for number in range(part.shape[0]):
                owner = my_index ^ offsets[position]
                for start in range(0, blocks_held * PANEL, part_rows):
                    held, inner = divmod(start, PANEL)
                    if start < packed:
                        rows = part[number, start : start + part_rows, :PANEL]
                    else:
                        rows = part[number, start - packed : start - packed + part_rows, PANEL:]
                    target = pl.multiple_of((held * size + owner) * PANEL + inner, part_rows)
                    leading_ref[pl.ds(target, part_rows), :] = rows
                position += 1
        upper, inverse, pivots = eliminate(leading_ref[:PANEL, :], shift_ref[...])
        pivots_ref[...] = pivots
        inverse_ref[...] = inverse
        lower_ref[...] = jnp.transpose(upper)
        tail = exact(inverse, leading_ref[:needed, :], ((1,), (1,)))
        high, low, _ = split(tail, 3)
        tail_ref[0:PANEL, :] = high
        tail_ref[PANEL : 2 * PANEL, :] = high
        tail_ref[2 * PANEL : 3 * PANEL, :] = low
        tail_ref[3 * PANEL :, :] = low

    block = lead_ref.shape[0]
    panel = exact(lead_ref[...], inverse_ref[...], ((1,), (1,))) / pivots_ref[...]
    row_ids = lax.broadcasted_iota(jnp.int32, panel.shape, 0)
    top = jnp.logical_and(jnp.logical_and(my_index == 0, step == 0), row_ids < PANEL)
    lower = jnp.concatenate([lower_ref[...], jnp.zeros((block - PANEL, PANEL), F32)], axis=0)
    used = jnp.where(top, 0.0, panel)
    high, low = (term.astype(F32) for term in split(used, 2))
    pair = jnp.concatenate([high, low], axis=1).astype(BF16)
    factors = jnp.concatenate([pair, pair], axis=1)
    update = jnp.dot(factors, tail_ref[...], preferred_element_type=F32)
    shown = jnp.concatenate([jnp.where(top, lower, panel), jnp.zeros_like(panel)], axis=1)
    near_ref[:, :LANES] = jnp.where(lane_ids(shown.shape) < PANEL, shown, -update[:, :LANES])
    near_ref[:, LANES:] = -update[:, LANES:columns]
    far_ref[...] = (resident_ref[...].astype(F32) - update[:, columns:]).astype(BF16)


def updates(my_index, parts, offsets, lead, shift, resident, blocks_held, columns):
    rows, width = resident.shape
    needed = columns + width
    steps = 5
    block = rows // steps
    held_rows = len(offsets) * blocks_held * PANEL
    return pl.pallas_call(
        functools.partial(update_kernel, offsets, blocks_held, columns),
        grid=(steps,),
        in_specs=[
            pl.BlockSpec(memory_space=pltpu.SMEM),
            pl.BlockSpec((block, PANEL), lambda i: (i, 0)),
            pl.BlockSpec((1, PANEL), lambda i: (0, 0)),
            pl.BlockSpec((block, width), lambda i: (i, 0)),
        ]
        + [pl.BlockSpec(part.shape, lambda i: (0, 0, 0)) for part in parts],
        out_specs=[
            pl.BlockSpec((block, columns), lambda i: (i, 0)),
            pl.BlockSpec((block, width), lambda i: (i, 0)),
            pl.BlockSpec((1, PANEL), lambda i: (0, 0)),
        ],
        out_shape=[
            jax.ShapeDtypeStruct((rows, columns), F32),
            jax.ShapeDtypeStruct((rows, width), BF16),
            jax.ShapeDtypeStruct((1, PANEL), F32),
        ],
        scratch_shapes=[
            pltpu.VMEM((held_rows, PANEL), F32),
            pltpu.VMEM((4 * PANEL, needed), BF16),
            pltpu.VMEM((PANEL, PANEL), F32),
            pltpu.VMEM((PANEL, PANEL), F32),
        ],
        compiler_params=params(),
        cost_estimate=pl.CostEstimate(
            flops=2 * rows * needed * 4 * PANEL, bytes_accessed=4 * rows * (columns + width), transcendentals=0
        ),
        name="factor_and_update",
    )(my_index, lead, shift, resident, *parts)


def formed_kernel(picks_ref, arrived_ref, near_ref, out_ref, terms_ref):
    half = arrived_ref.shape[0]

    @pl.when(pl.program_id(0) == 0)
    def _():
        words = arrived_ref[:, LANES:]
        low_lanes = lane_ids(words.shape) < PANEL
        exponent = ((words & 255) - BIAS).astype(F32)
        other = swap_halves(exponent)
        packed_terms((words >> 8).astype(F32) * jnp.exp2(exponent - 23.0), terms_ref, 2 * LANES)
        words = arrived_ref[:, :LANES]
        low = (words >> 16).astype(F32) * jnp.exp2(jnp.where(low_lanes, exponent, other) - 15.0)
        high = ((words << 16) >> 16).astype(F32) * jnp.exp2(jnp.where(low_lanes, other, exponent) - 15.0)
        for side, values in enumerate((low, high)):
            first, second = split(values, 2)
            terms_ref[side * half : (side + 1) * half, :LANES] = first
            terms_ref[side * half : (side + 1) * half, LANES : 2 * LANES] = second

    got = jnp.dot(picks_ref[...], terms_ref[...], preferred_element_type=F32)
    narrow = whole_sum(got[:, 2 * LANES :])
    held = near_ref[:, :LANES]
    out_ref[:, :LANES] = jnp.where(lane_ids(held.shape) < PANEL, held, narrow + held)
    out_ref[:, LANES:] = (got[:, :LANES] + got[:, LANES : 2 * LANES]) + near_ref[:, LANES:]


def formed_columns(picks, arrived, near):
    rows, columns = near.shape
    half, width = arrived.shape
    steps = 5
    block = rows // steps
    return pl.pallas_call(
        formed_kernel,
        grid=(steps,),
        in_specs=[
            pl.BlockSpec((block, rows), lambda i: (i, 0)),
            pl.BlockSpec((half, width), lambda i: (0, 0)),
            pl.BlockSpec((block, columns), lambda i: (i, 0)),
        ],
        out_specs=pl.BlockSpec((block, columns), lambda i: (i, 0)),
        out_shape=jax.ShapeDtypeStruct((rows, columns), F32),
        scratch_shapes=[pltpu.VMEM((rows, 4 * LANES), BF16)],
        compiler_params=params(),
        cost_estimate=pl.CostEstimate(
            flops=8 * rows * rows * LANES, bytes_accessed=8 * rows * columns, transcendentals=0
        ),
        name="formed_columns",
    )(picks, arrived, near)


def swap_rows(x, group):
    rows, width = x.shape
    return lax.all_to_all(
        x.reshape(group, rows // group, width), "wide", split_axis=0, concat_axis=0, tiled=True
    ).reshape(rows, width)


def on_device(a_rows, xa_panel, za_panel, send_order, recv_order, shift, resident):
    rows = a_rows.shape[0]
    columns = xa_panel.shape[1]
    group = lax.axis_size("wide")
    my_index = lax.axis_index("wide").astype(jnp.int32).reshape(1)
    share = rows // group
    half = rows // 2
    few, far_first, second_first = phases(group)

    send = send_order.reshape(group, 2, share // 2).transpose(1, 0, 2).reshape(1, rows)
    source, slot = recv_order // share, recv_order % share
    index = (slot // (share // 2)) * half + source * (share // 2) + slot % (share // 2)
    send_picks, index_picks = order_picks(send, index)

    lead_panel, near_panel, far_panel = split_panels(xa_panel, za_panel)
    lead_parts, lead_offsets = gather(lead_panel, few, "wide")
    near_parts, near_offsets = gather(near_panel, second_first, "wide")
    far_parts, far_offsets = gather(far_panel, far_first, "wide")

    lead_out = lead_products(my_index, a_rows, send_picks, lead_parts, lead_offsets)
    lead_in = swap_rows(lead_out, group)

    needed = columns + resident.shape[1]
    blocks_held = -(-needed // (PANEL * group))
    packed = leading_rows(index_picks, lead_in, blocks_held * PANEL)
    leading_parts, leading_offsets = exchange(packed, [0], few[0], "wide")
    lead = stored_rows(index_picks, lead_in)
    for masks in few[1:]:
        leading_parts, leading_offsets = exchange(
            after(join(leading_parts), lead), leading_offsets, masks, "wide"
        )

    rest_out = rest_products(my_index, a_rows, send_picks, near_parts, near_offsets, far_parts, far_offsets)
    rest_in = swap_rows(after(rest_out, *leading_parts), group)
    near, updated, pivots = updates(
        my_index,
        leading_parts,
        leading_offsets,
        after(lead, rest_out),
        shift[None, :],
        resident,
        blocks_held,
        columns,
    )
    factored = formed_columns(index_picks, rest_in, near)
    return (factored, updated, pivots[0])


def solution(mesh):
    placed = (
        P(("parts", "wide"), None),
        P(("parts", "wide"), None),
        P(("parts", "wide"), None),
        P(("parts", "wide"), None),
        P(("parts", "wide"), None),
        P("parts"),
        P(("parts", "wide"), None),
    )
    return jax.shard_map(
        on_device,
        mesh=mesh,
        in_specs=placed,
        out_specs=(P(("parts", "wide"), None), P(("parts", "wide"), None), P("parts")),
        check_vma=False,
    )
```

```python
import functools

import jax
import jax.numpy as jnp
from jax import lax
from jax.experimental import pallas as pl
from jax.experimental.pallas import tpu as pltpu
from jax.sharding import PartitionSpec as P

PANEL = 64
LANES = 128
F32 = jnp.float32
BF16 = jnp.bfloat16
MIB = 1024 * 1024


def params(mebibytes=60):
    return pltpu.CompilerParams(vmem_limit_bytes=mebibytes * MIB)


def lane_ids(shape):
    return lax.broadcasted_iota(jnp.int32, shape, len(shape) - 1)


def split(x, count):
    terms = []
    for _ in range(count):
        term = x.astype(BF16)
        terms.append(term)
        x = x - term.astype(F32)
    return terms


def swap_halves(x):
    return pltpu.roll(x, LANES // 2, 1)


def one_hot(index_row, width):
    chunks = []
    step = LANES
    for start in range(0, index_row.shape[1], step):
        piece = jnp.broadcast_to(index_row[:, start : start + step], (step, step))
        at = jnp.transpose(piece)
        lanes = lane_ids((step, step))
        chunks.append(
            jnp.concatenate(
                [(at == lanes + column).astype(F32).astype(BF16) for column in range(0, width, step)],
                axis=1,
            )
        )
    return jnp.concatenate(chunks, axis=0) if len(chunks) > 1 else chunks[0]


def after(x, *earlier):
    return lax.optimization_barrier((x, *earlier))[0]


def exchange(held, masks, axis):
    size = lax.axis_size(axis)
    combined = [0]
    for mask in masks:
        combined += [other ^ mask for other in combined]
    parts = list(held)
    for mask in combined[1:]:
        parts += [lax.ppermute(part, axis, [(i, i ^ mask) for i in range(size)]) for part in held]
    return parts


def offsets_of(phases):
    offsets = [0]
    for masks in phases:
        combined = [0]
        for mask in masks:
            combined += [other ^ mask for other in combined]
        offsets = [offset ^ mask for mask in combined for offset in offsets]
    return offsets


def join(parts):
    return [jnp.concatenate(parts, axis=0)]


def phases_of(size):
    bits = [1 << bit for bit in reversed(range(size.bit_length() - 1))]
    pairs = [bits[start : start + 2] for start in range(0, len(bits), 2)]
    singles = [bits[start : start + 2] for start in range(0, len(bits) - 2, 2)]
    return pairs, singles + [bits[-2:-1], bits[-1:]]


def picks_kernel(send_ref, index_ref, send_picks_ref, index_picks_ref):
    width = send_picks_ref.shape[1]
    send_picks_ref[...] = one_hot(send_ref[...], width)
    index_picks_ref[...] = one_hot(index_ref[...], width)


def order_picks(send, index):
    rows = send.shape[1]
    block = LANES
    return pl.pallas_call(
        picks_kernel,
        grid=(rows // block,),
        in_specs=[pl.BlockSpec((1, block), lambda i: (0, i))] * 2,
        out_specs=[pl.BlockSpec((block, rows), lambda i: (i, 0))] * 2,
        out_shape=[jax.ShapeDtypeStruct((rows, rows), BF16)] * 2,
        compiler_params=params(),
        cost_estimate=pl.CostEstimate(flops=4 * rows * rows, bytes_accessed=4 * rows * rows, transcendentals=0),
        name="order_picks",
    )(send, index)


def panels_kernel(xa_hbm, za_hbm, lead_ref, rest_ref, xa_ref, za_ref, sems):
    copies = [
        pltpu.make_async_copy(xa_hbm, xa_ref, sems.at[0]),
        pltpu.make_async_copy(za_hbm, za_ref, sems.at[1]),
    ]
    for copy in copies:
        copy.start()
    for copy in copies:
        copy.wait()
    lead_ref[0] = jnp.concatenate([xa_ref[:, :PANEL], za_ref[:, :PANEL]], axis=1)
    rest_ref[0, :, :LANES] = jnp.concatenate([xa_ref[:, PANEL:LANES], za_ref[:, PANEL:LANES]], axis=1)
    rest_ref[0, :, LANES : 2 * LANES] = xa_ref[:, LANES:]
    rest_ref[0, :, 2 * LANES :] = za_ref[:, LANES:]


def split_panels(xa_panel, za_panel):
    depth, columns = xa_panel.shape
    return pl.pallas_call(
        panels_kernel,
        in_specs=[pl.BlockSpec(memory_space=pl.ANY)] * 2,
        out_shape=[
            jax.ShapeDtypeStruct((1, depth, LANES), BF16),
            jax.ShapeDtypeStruct((1, depth, 2 * columns - LANES), BF16),
        ],
        scratch_shapes=[
            pltpu.VMEM((depth, columns), BF16),
            pltpu.VMEM((depth, columns), BF16),
            pltpu.SemaphoreType.DMA((2,)),
        ],
        compiler_params=params(),
        name="split_panels",
    )(xa_panel, za_panel)


def assemble(my_index, offsets, parts, panel_ref):
    position = 0
    for part in parts:
        for number in range(part.shape[0]):
            depth = part.shape[1]
            start = pl.multiple_of((my_index ^ offsets[position]) * depth, depth)
            panel_ref[pl.ds(start, depth), :] = part[number]
            position += 1


def whole_sum(got):
    pair = got[:, :LANES]
    return (pair + swap_halves(pair)) + got[:, LANES:]


A_BLOCK = 256


def fetches(pairs, sems):
    copies = [pltpu.make_async_copy(source, target, sems.at[i]) for i, (source, target) in enumerate(pairs)]
    for copy in copies:
        copy.start()
    return copies


def row_blocks(a_hbm, a_ref, picks_hbm, picks_ref, sems):
    starts = range(0, a_ref.shape[0], A_BLOCK)
    pairs = [(a_hbm.at[pl.ds(start, A_BLOCK), :], a_ref.at[pl.ds(start, A_BLOCK), :]) for start in starts]
    return starts, fetches(pairs + [(picks_hbm, picks_ref)], sems)


def lead_product_kernel(offsets, my_ref, a_hbm, picks_hbm, *refs):
    parts, (out_ref, a_ref, picks_ref, panel_ref, terms_ref, sems) = refs[:-6], refs[-6:]
    starts, copies = row_blocks(a_hbm, a_ref, picks_hbm, picks_ref, sems)
    assemble(my_ref[0], offsets, parts, panel_ref)
    rows = a_ref.shape[0]
    for start, copy in zip(starts, copies):
        copy.wait()
        both = jnp.dot(a_ref[start : start + A_BLOCK, :], panel_ref[...], preferred_element_type=F32)
        first, second, third = (term.astype(F32) for term in split(both * swap_halves(both), 3))
        near = lane_ids(both.shape) < PANEL
        terms_ref[start : start + A_BLOCK, :LANES] = jnp.where(near, first, second).astype(BF16)
        terms_ref[start : start + A_BLOCK, LANES:] = third.astype(BF16)
    copies[-1].wait()
    half = rows // 2
    block = half // 2
    for start in range(0, half, block):
        low = jnp.dot(picks_ref[start : start + block, :], terms_ref[...], preferred_element_type=F32)
        high = jnp.dot(picks_ref[half + start : half + start + block, :], terms_ref[...], preferred_element_type=F32)
        low, high = whole_sum(low), whole_sum(high)
        out_ref[start : start + block, :] = jnp.where(lane_ids(low.shape) < PANEL, low, high)


def product_call(kernel, name, my_index, a_rows, picks, parts, width, terms, out_shape):
    rows, depth = a_rows.shape
    anywhere = pl.BlockSpec(memory_space=pl.ANY)
    return pl.pallas_call(
        kernel,
        in_specs=[pl.BlockSpec(memory_space=pltpu.SMEM), anywhere, anywhere]
        + [pl.BlockSpec(memory_space=pltpu.VMEM)] * len(parts),
        out_specs=pl.BlockSpec(memory_space=pltpu.VMEM),
        out_shape=out_shape,
        scratch_shapes=[
            pltpu.VMEM((rows, depth), BF16),
            pltpu.VMEM((rows, rows), BF16),
            pltpu.VMEM((depth, width), BF16),
            pltpu.VMEM((rows, terms), BF16),
            pltpu.SemaphoreType.DMA((rows // A_BLOCK + 1,)),
        ],
        compiler_params=params(),
        cost_estimate=pl.CostEstimate(
            flops=2 * rows * (depth * width + rows * terms), bytes_accessed=2 * rows * (depth + rows), transcendentals=0
        ),
        name=name,
    )(my_index, a_rows, picks, *parts)


def lead_products(my_index, a_rows, picks, parts, offsets):
    return product_call(
        functools.partial(lead_product_kernel, offsets),
        "lead_products",
        my_index,
        a_rows,
        picks,
        parts,
        LANES,
        2 * LANES,
        jax.ShapeDtypeStruct((a_rows.shape[0] // 2, LANES), F32),
    )


BIAS = 128


def rest_product_kernel(offsets, my_ref, a_hbm, picks_hbm, *refs):
    parts, (out_ref, a_ref, picks_ref, panel_ref, terms_ref, sems) = refs[:-6], refs[-6:]
    starts, copies = row_blocks(a_hbm, a_ref, picks_hbm, picks_ref, sems)
    assemble(my_ref[0], offsets, parts, panel_ref)
    rows = a_ref.shape[0]
    block = A_BLOCK
    for start, copy in zip(starts, copies):
        copy.wait()
        both = jnp.dot(a_ref[start : start + block, :], panel_ref[...], preferred_element_type=F32)
        near = both[:, :LANES]
        near = near * swap_halves(near)
        far = both[:, LANES : 2 * LANES] * both[:, 2 * LANES :]
        largest = jnp.max(jnp.maximum(jnp.abs(near), jnp.abs(far)), axis=1, keepdims=True)
        largest = jnp.maximum(largest, 1e-30)
        exponent = jnp.floor(jnp.log2(largest)) + 1.0
        far = jnp.floor(far * jnp.exp2(15.0 - exponent) + 0.5)
        far = jnp.minimum(jnp.maximum(far, -32767.0), 32767.0)
        near = jnp.floor(near * jnp.exp2(23.0 - exponent) + 0.5)
        near = jnp.minimum(jnp.maximum(near, -8388607.0), 8388607.0)
        far_top = jnp.floor(far * (1 / 256))
        near_top = jnp.floor(near * (1 / 65536))
        near = near - near_top * 65536.0
        near_middle = jnp.floor(near * (1 / 256))
        low_lanes = lane_ids(near.shape) < PANEL
        rows_here = slice(start, start + block)
        terms_ref[rows_here, :LANES] = far_top.astype(BF16)
        terms_ref[rows_here, LANES : 2 * LANES] = (far - far_top * 256.0).astype(BF16)
        terms_ref[rows_here, 2 * LANES : 3 * LANES] = jnp.where(low_lanes, near_top, near_middle).astype(BF16)
        terms_ref[rows_here, 3 * LANES :] = jnp.where(low_lanes, near - near_middle * 256.0, exponent).astype(BF16)

    copies[-1].wait()

    def coded(start, size):
        got = jnp.dot(picks_ref[start : start + size, :], terms_ref[...], preferred_element_type=F32)
        far = got[:, :LANES] * 256.0 + got[:, LANES : 2 * LANES]
        tops, lows = got[:, 2 * LANES : 3 * LANES], got[:, 3 * LANES :]
        low_lanes = lane_ids(tops.shape) < PANEL
        tops = tops * jnp.where(low_lanes, 65536.0, 256.0)
        swapped = swap_halves(lows)
        near = tops + swap_halves(tops) + jnp.where(low_lanes, lows, swapped)
        exponent = jnp.where(low_lanes, swapped, lows)
        near = near.astype(jnp.int32) * 256 + (exponent.astype(jnp.int32) + BIAS)
        return far.astype(jnp.int32), near

    half = rows // 2
    block = half // 2
    for start in range(0, half, block):
        far_low, near_low = coded(start, block)
        far_high, near_high = coded(half + start, block)
        out_ref[start : start + block, :LANES] = far_low * 65536 + (far_high & 65535)
        out_ref[start : start + block, LANES:] = jnp.where(lane_ids(near_low.shape) < PANEL, near_low, near_high)


def rest_products(my_index, a_rows, picks, parts, offsets):
    return product_call(
        functools.partial(rest_product_kernel, offsets),
        "rest_products",
        my_index,
        a_rows,
        picks,
        parts,
        3 * LANES,
        4 * LANES,
        jax.ShapeDtypeStruct((a_rows.shape[0] // 2, 2 * LANES), jnp.int32),
    )


def packed_terms(x, terms_ref, start):
    half = x.shape[0]
    first, second, third = (term.astype(F32) for term in split(x, 3))
    near = lane_ids(x.shape) < PANEL
    other = swap_halves(third)
    terms_ref[:half, start : start + LANES] = jnp.where(near, first, swap_halves(second)).astype(BF16)
    terms_ref[half:, start : start + LANES] = jnp.where(near, swap_halves(first), second).astype(BF16)
    terms_ref[:half, start + LANES : start + 2 * LANES] = jnp.where(near, third, other).astype(BF16)
    terms_ref[half:, start + LANES : start + 2 * LANES] = jnp.where(near, other, third).astype(BF16)


def leading_kernel(picks_ref, arrived_ref, out_ref, terms_ref):
    packed_terms(arrived_ref[...], terms_ref, 0)
    got = whole_sum(jnp.dot(picks_ref[...], terms_ref[...], preferred_element_type=F32))
    half = got.shape[0] // 2
    first, second = got[:half], got[half:]
    out_ref[0] = jnp.where(lane_ids(first.shape) < PANEL, first, second)


def leading_rows(picks, arrived, held):
    rows = picks.shape[0]
    half = rows // 2
    return pl.pallas_call(
        leading_kernel,
        grid=(1,),
        in_specs=[
            pl.BlockSpec((held, rows), lambda i: (0, 0)),
            pl.BlockSpec((half, LANES), lambda i: (0, 0)),
        ],
        out_specs=pl.BlockSpec((1, held // 2, LANES), lambda i: (0, 0, 0)),
        out_shape=jax.ShapeDtypeStruct((1, held // 2, LANES), F32),
        scratch_shapes=[pltpu.VMEM((rows, 2 * LANES), BF16)],
        compiler_params=params(),
        cost_estimate=pl.CostEstimate(
            flops=4 * held * rows * LANES, bytes_accessed=2 * rows * LANES, transcendentals=0
        ),
        name="leading_rows",
    )(picks, arrived)


def stored_kernel(picks_ref, arrived_ref, out_ref, terms_ref):
    @pl.when(pl.program_id(0) == 0)
    def _():
        packed_terms(arrived_ref[...], terms_ref, 0)

    got = jnp.dot(picks_ref[...], terms_ref[...], preferred_element_type=F32)
    out_ref[...] = whole_sum(got)[:, :PANEL]


def stored_rows(picks, arrived):
    rows = picks.shape[0]
    half = rows // 2
    block = A_BLOCK
    return pl.pallas_call(
        stored_kernel,
        grid=(rows // block,),
        in_specs=[
            pl.BlockSpec((block, rows), lambda i: (i, 0)),
            pl.BlockSpec((half, LANES), lambda i: (0, 0)),
        ],
        out_specs=pl.BlockSpec((block, PANEL), lambda i: (i, 0)),
        out_shape=jax.ShapeDtypeStruct((rows, PANEL), F32),
        scratch_shapes=[pltpu.VMEM((rows, 2 * LANES), BF16)],
        compiler_params=params(),
        cost_estimate=pl.CostEstimate(
            flops=4 * rows * rows * LANES, bytes_accessed=2 * rows * rows, transcendentals=0
        ),
        name="stored_rows",
    )(picks, arrived)


def eliminate(block, shift_row):
    rows = lax.broadcasted_iota(jnp.int32, (PANEL, PANEL), 0)
    columns = lax.broadcasted_iota(jnp.int32, (PANEL, PANEL), 1)
    flipped = jnp.transpose(block)
    mirrored = jnp.where(rows >= columns, block, flipped)
    diagonal = shift_row + jnp.sum(jnp.abs(mirrored), axis=0, keepdims=True)
    unit = (rows == columns).astype(F32)
    work = jnp.where(rows == columns, diagonal, mirrored)
    work = jnp.concatenate([work, unit], axis=1)
    height = 8
    groups = [work[start : start + height] for start in range(0, PANEL, height)]
    sublanes = lax.broadcasted_iota(jnp.int32, (height, LANES), 0)
    scaled_rows = []
    for k in range(PANEL):
        home, offset = divmod(k, height)
        row = groups[home][offset : offset + 1, :]
        row = row / row[:, k : k + 1]
        scaled_rows.append(row)
        for g in range(home, PANEL // height):
            column = jnp.broadcast_to(groups[g][:, k : k + 1], (height, LANES))
            if g == home:
                column = jnp.where(sublanes > offset, column, 0.0)
            groups[g] = groups[g] - column * row
    final = jnp.concatenate(groups, axis=0)
    scaled = jnp.concatenate(scaled_rows, axis=0)
    upper = jnp.where(columns >= rows, scaled[:, :PANEL], 0.0)
    pivots = jnp.sum(jnp.where(rows == columns, final[:, :PANEL], 0.0), axis=0, keepdims=True)
    return upper, final[:, PANEL:], pivots


def exact(lhs, rhs, dims):
    return lax.dot_general(lhs, rhs, (dims, ((), ())), precision=lax.Precision.HIGHEST, preferred_element_type=F32)


def update_kernel(
    offsets,
    blocks_held,
    columns,
    my_ref,
    lead_ref,
    shift_ref,
    resident_ref,
    *refs,
):
    parts = refs[:-7]
    near_ref, far_ref, pivots_ref, leading_ref, tail_ref, inverse_ref, lower_ref = refs[-7:]
    my_index = my_ref[0]
    step = pl.program_id(0)
    needed = tail_ref.shape[1]

    @pl.when(step == 0)
    def _():
        size = len(offsets)
        position = 0
        packed = blocks_held * PANEL // 2
        part_rows = PANEL // 2
        for part in parts:
            for number in range(part.shape[0]):
                owner = my_index ^ offsets[position]
                for start in range(0, blocks_held * PANEL, part_rows):
                    held, inner = divmod(start, PANEL)
                    if start < packed:
                        rows = part[number, start : start + part_rows, :PANEL]
                    else:
                        rows = part[number, start - packed : start - packed + part_rows, PANEL:]
                    target = pl.multiple_of((held * size + owner) * PANEL + inner, part_rows)
                    leading_ref[pl.ds(target, part_rows), :] = rows
                position += 1
        upper, inverse, pivots = eliminate(leading_ref[:PANEL, :], shift_ref[...])
        pivots_ref[...] = pivots
        inverse_ref[...] = inverse
        lower_ref[...] = jnp.transpose(upper)
        tail = exact(inverse, leading_ref[:needed, :], ((1,), (1,)))
        high, low, _ = split(tail, 3)
        tail_ref[0:PANEL, :] = high
        tail_ref[PANEL : 2 * PANEL, :] = high
        tail_ref[2 * PANEL : 3 * PANEL, :] = low
        tail_ref[3 * PANEL :, :] = low

    block = lead_ref.shape[0]
    panel = exact(lead_ref[...], inverse_ref[...], ((1,), (1,))) / pivots_ref[...]
    row_ids = lax.broadcasted_iota(jnp.int32, panel.shape, 0)
    top = jnp.logical_and(jnp.logical_and(my_index == 0, step == 0), row_ids < PANEL)
    lower = jnp.concatenate([lower_ref[...], jnp.zeros((block - PANEL, PANEL), F32)], axis=0)
    used = jnp.where(top, 0.0, panel)
    high, low = (term.astype(F32) for term in split(used, 2))
    pair = jnp.concatenate([high, low], axis=1).astype(BF16)
    factors = jnp.concatenate([pair, pair], axis=1)
    update = jnp.dot(factors, tail_ref[...], preferred_element_type=F32)
    shown = jnp.concatenate([jnp.where(top, lower, panel), jnp.zeros_like(panel)], axis=1)
    near_ref[:, :LANES] = jnp.where(lane_ids(shown.shape) < PANEL, shown, -update[:, :LANES])
    near_ref[:, LANES:] = -update[:, LANES:columns]
    far_ref[...] = (resident_ref[...].astype(F32) - update[:, columns:]).astype(BF16)


def updates(my_index, parts, offsets, lead, shift, resident, blocks_held, columns):
    rows, width = resident.shape
    needed = columns + width
    steps = 5
    block = rows // steps
    held_rows = len(offsets) * blocks_held * PANEL
    return pl.pallas_call(
        functools.partial(update_kernel, offsets, blocks_held, columns),
        grid=(steps,),
        in_specs=[
            pl.BlockSpec(memory_space=pltpu.SMEM),
            pl.BlockSpec((block, PANEL), lambda i: (i, 0)),
            pl.BlockSpec((1, PANEL), lambda i: (0, 0)),
            pl.BlockSpec((block, width), lambda i: (i, 0)),
        ]
        + [pl.BlockSpec(part.shape, lambda i: (0, 0, 0)) for part in parts],
        out_specs=[
            pl.BlockSpec((block, columns), lambda i: (i, 0)),
            pl.BlockSpec((block, width), lambda i: (i, 0)),
            pl.BlockSpec((1, PANEL), lambda i: (0, 0)),
        ],
        out_shape=[
            jax.ShapeDtypeStruct((rows, columns), F32),
            jax.ShapeDtypeStruct((rows, width), BF16),
            jax.ShapeDtypeStruct((1, PANEL), F32),
        ],
        scratch_shapes=[
            pltpu.VMEM((held_rows, PANEL), F32),
            pltpu.VMEM((4 * PANEL, needed), BF16),
            pltpu.VMEM((PANEL, PANEL), F32),
            pltpu.VMEM((PANEL, PANEL), F32),
        ],
        compiler_params=params(),
        cost_estimate=pl.CostEstimate(
            flops=2 * rows * needed * 4 * PANEL, bytes_accessed=4 * rows * (columns + width), transcendentals=0
        ),
        name="factor_and_update",
    )(my_index, lead, shift, resident, *parts)


def formed_kernel(picks_ref, arrived_ref, near_ref, out_ref, terms_ref):
    half = arrived_ref.shape[0]

    @pl.when(pl.program_id(0) == 0)
    def _():
        words = arrived_ref[:, LANES:]
        low_lanes = lane_ids(words.shape) < PANEL
        exponent = ((words & 255) - BIAS).astype(F32)
        other = swap_halves(exponent)
        packed_terms((words >> 8).astype(F32) * jnp.exp2(exponent - 23.0), terms_ref, 2 * LANES)
        words = arrived_ref[:, :LANES]
        low = (words >> 16).astype(F32) * jnp.exp2(jnp.where(low_lanes, exponent, other) - 15.0)
        high = ((words << 16) >> 16).astype(F32) * jnp.exp2(jnp.where(low_lanes, other, exponent) - 15.0)
        for side, values in enumerate((low, high)):
            first, second = split(values, 2)
            terms_ref[side * half : (side + 1) * half, :LANES] = first
            terms_ref[side * half : (side + 1) * half, LANES : 2 * LANES] = second

    got = jnp.dot(picks_ref[...], terms_ref[...], preferred_element_type=F32)
    narrow = whole_sum(got[:, 2 * LANES :])
    held = near_ref[:, :LANES]
    out_ref[:, :LANES] = jnp.where(lane_ids(held.shape) < PANEL, held, narrow + held)
    out_ref[:, LANES:] = (got[:, :LANES] + got[:, LANES : 2 * LANES]) + near_ref[:, LANES:]


def formed_columns(picks, arrived, near):
    rows, columns = near.shape
    half, width = arrived.shape
    steps = 5
    block = rows // steps
    return pl.pallas_call(
        formed_kernel,
        grid=(steps,),
        in_specs=[
            pl.BlockSpec((block, rows), lambda i: (i, 0)),
            pl.BlockSpec((half, width), lambda i: (0, 0)),
            pl.BlockSpec((block, columns), lambda i: (i, 0)),
        ],
        out_specs=pl.BlockSpec((block, columns), lambda i: (i, 0)),
        out_shape=jax.ShapeDtypeStruct((rows, columns), F32),
        scratch_shapes=[pltpu.VMEM((rows, 4 * LANES), BF16)],
        compiler_params=params(),
        cost_estimate=pl.CostEstimate(
            flops=8 * rows * rows * LANES, bytes_accessed=8 * rows * columns, transcendentals=0
        ),
        name="formed_columns",
    )(picks, arrived, near)


def swap_rows(x, group):
    rows, width = x.shape
    return lax.all_to_all(
        x.reshape(group, rows // group, width), "wide", split_axis=0, concat_axis=0, tiled=True
    ).reshape(rows, width)


def on_device(a_rows, xa_panel, za_panel, send_order, recv_order, shift, resident):
    rows = a_rows.shape[0]
    columns = xa_panel.shape[1]
    group = lax.axis_size("wide")
    my_index = lax.axis_index("wide").astype(jnp.int32).reshape(1)
    share = rows // group
    half = rows // 2
    few, apart = phases_of(group)

    send = send_order.reshape(group, 2, share // 2).transpose(1, 0, 2).reshape(1, rows)
    source, slot = recv_order // share, recv_order % share
    index = (slot // (share // 2)) * half + source * (share // 2) + slot % (share // 2)
    send_picks, index_picks = order_picks(send, index)

    lead_panel, rest_panel = split_panels(xa_panel, za_panel)
    lead_parts = [lead_panel]
    for masks in few:
        lead_parts = exchange(join(lead_parts), masks, "wide")
    rest_parts = [rest_panel]
    for masks in apart[:-1]:
        rest_parts = exchange(join(rest_parts), masks, "wide")
    rest_parts = exchange(rest_parts, apart[-1], "wide")

    lead_out = lead_products(my_index, a_rows, send_picks, lead_parts, offsets_of(few))
    lead_in = swap_rows(lead_out, group)

    needed = columns + resident.shape[1]
    blocks_held = -(-needed // (PANEL * group))
    leading_parts = exchange([leading_rows(index_picks, lead_in, blocks_held * PANEL)], few[0], "wide")
    lead = stored_rows(index_picks, lead_in)
    for masks in few[1:]:
        leading_parts = exchange([after(join(leading_parts)[0], lead)], masks, "wide")

    rest_out = rest_products(my_index, a_rows, send_picks, rest_parts, offsets_of(apart))
    rest_in = swap_rows(after(rest_out, *leading_parts), group)
    near, updated, pivots = updates(
        my_index,
        leading_parts,
        offsets_of(few),
        after(lead, rest_out),
        shift[None, :],
        resident,
        blocks_held,
        columns,
    )
    factored = formed_columns(index_picks, rest_in, near)
    return (factored, updated, pivots[0])


def solution(mesh):
    placed = (
        P(("parts", "wide"), None),
        P(("parts", "wide"), None),
        P(("parts", "wide"), None),
        P(("parts", "wide"), None),
        P(("parts", "wide"), None),
        P("parts"),
        P(("parts", "wide"), None),
    )
    return jax.shard_map(
        on_device,
        mesh=mesh,
        in_specs=placed,
        out_specs=(P(("parts", "wide"), None), P(("parts", "wide"), None), P("parts")),
        check_vma=False,
    )
```

```python
import functools

import jax
import jax.numpy as jnp
from jax import lax
from jax.experimental import pallas as pl
from jax.experimental.pallas import tpu as pltpu
from jax.sharding import PartitionSpec as P

PANEL = 64
LANES = 128
A_BLOCK = 256
F32 = jnp.float32
BF16 = jnp.bfloat16
MIB = 1024 * 1024


def params(mebibytes=12):
    return pltpu.CompilerParams(vmem_limit_bytes=mebibytes * MIB)


def lane_ids(shape):
    return lax.broadcasted_iota(jnp.int32, shape, len(shape) - 1)


def split(x, count):
    terms = []
    for _ in range(count):
        term = x.astype(BF16)
        terms.append(term)
        x = x - term.astype(F32)
    return terms


def swap_halves(x):
    return pltpu.roll(x, LANES // 2, 1)


def as_column(index_row):
    return jnp.transpose(jnp.broadcast_to(index_row, (LANES, LANES)))


def picks_of(at, width):
    lanes = lane_ids(at.shape)
    return jnp.concatenate(
        [(at == lanes + column).astype(F32).astype(BF16) for column in range(0, width, LANES)], axis=1
    )


def one_hot(index_row, width):
    chunks = [
        picks_of(as_column(index_row[:, start : start + LANES]), width)
        for start in range(0, index_row.shape[1], LANES)
    ]
    return jnp.concatenate(chunks, axis=0) if len(chunks) > 1 else chunks[0]


def packed_order(share, half, slot):
    part = share // 2
    return (slot % share) // part * half + slot // share * part + slot % part


def fill_order(order_ref, at_ref, share):
    rows = order_ref.shape[1]
    height = 8
    for start in range(0, rows, LANES):
        column = as_column(order_ref[:, start : start + LANES])
        if not share:
            at_ref[start : start + LANES, :] = column
            continue
        for inner in range(0, LANES, height):
            place = packed_order(share, rows // 2, start + inner)
            at_ref[place : place + height, :] = column[inner : inner + height]


def after(x, *earlier):
    return lax.optimization_barrier((x, *earlier))[0]


def exchange(held, masks, axis):
    size = lax.axis_size(axis)
    combined = [0]
    for mask in masks:
        combined += [other ^ mask for other in combined]
    parts = list(held)
    for mask in combined[1:]:
        parts += [lax.ppermute(part, axis, [(i, i ^ mask) for i in range(size)]) for part in held]
    return parts


def offsets_of(phases):
    offsets = [0]
    for masks in phases:
        combined = [0]
        for mask in masks:
            combined += [other ^ mask for other in combined]
        offsets = [offset ^ mask for mask in combined for offset in offsets]
    return offsets


def join(parts):
    return [jnp.concatenate(parts, axis=0)]


def phases_of(size):
    bits = [1 << bit for bit in reversed(range(size.bit_length() - 1))]
    pairs = [bits[start : start + 2] for start in range(0, len(bits), 2)]
    singles = [bits[start : start + 2] for start in range(0, len(bits) - 2, 2)]
    return pairs, singles + [bits[-2:-1], bits[-1:]]


def picks_kernel(share, order_ref, a_hbm, picks_ref, copy_ref, at_ref, sem):
    copy = pltpu.make_async_copy(a_hbm, copy_ref, sem)
    copy.start()
    fill_order(order_ref, at_ref, share)
    rows, width = picks_ref.shape
    for start in range(0, rows, A_BLOCK):
        picks_ref[start : start + A_BLOCK, :] = picks_of(at_ref[start : start + A_BLOCK, :], width)
    copy.wait()


def order_picks(order, a_rows, share):
    rows, depth = a_rows.shape
    return pl.pallas_call(
        functools.partial(picks_kernel, share),
        in_specs=[pl.BlockSpec(memory_space=pltpu.VMEM), pl.BlockSpec(memory_space=pl.ANY)],
        out_specs=[pl.BlockSpec(memory_space=pltpu.VMEM)] * 2,
        out_shape=[jax.ShapeDtypeStruct((rows, rows), BF16), jax.ShapeDtypeStruct((rows, depth), BF16)],
        scratch_shapes=[pltpu.VMEM((rows, LANES), jnp.int32), pltpu.SemaphoreType.DMA],
        compiler_params=params(),
        cost_estimate=pl.CostEstimate(flops=4 * rows * rows, bytes_accessed=4 * rows * depth, transcendentals=0),
        name="order_picks",
    )(order, a_rows)


def panels_kernel(my_ref, xa_hbm, za_hbm, lead_ref, rest_ref, xa_ref, za_ref, sems):
    copies = [
        pltpu.make_async_copy(xa_hbm, xa_ref, sems.at[0]),
        pltpu.make_async_copy(za_hbm, za_ref, sems.at[1]),
    ]
    for copy in copies:
        copy.start()
    for copy in copies:
        copy.wait()
    lead_ref[0] = jnp.concatenate([xa_ref[:, :PANEL], za_ref[:, :PANEL]], axis=1)
    rest_ref[0, :, :LANES] = jnp.concatenate([xa_ref[:, PANEL:LANES], za_ref[:, PANEL:LANES]], axis=1)
    rest_ref[0, :, LANES : 2 * LANES] = xa_ref[:, LANES:]
    rest_ref[0, :, 2 * LANES :] = za_ref[:, LANES:]


def split_panels(my_index, xa_panel, za_panel):
    depth, columns = xa_panel.shape
    return pl.pallas_call(
        panels_kernel,
        in_specs=[pl.BlockSpec(memory_space=pltpu.SMEM)] + [pl.BlockSpec(memory_space=pl.ANY)] * 2,
        out_shape=[
            jax.ShapeDtypeStruct((1, depth, LANES), BF16),
            jax.ShapeDtypeStruct((1, depth, 2 * columns - LANES), BF16),
        ],
        scratch_shapes=[
            pltpu.VMEM((depth, columns), BF16),
            pltpu.VMEM((depth, columns), BF16),
            pltpu.SemaphoreType.DMA((2,)),
        ],
        compiler_params=params(),
        name="split_panels",
    )(my_index, xa_panel, za_panel)


def assemble(my_index, offsets, parts, panel_ref):
    position = 0
    for part in parts:
        for number in range(part.shape[0]):
            depth = part.shape[1]
            start = pl.multiple_of((my_index ^ offsets[position]) * depth, depth)
            panel_ref[pl.ds(start, depth), :] = part[number]
            position += 1


def whole_sum(got):
    pair = got[:, :LANES]
    return (pair + swap_halves(pair)) + got[:, LANES:]


def lead_product_kernel(offsets, my_ref, a_ref, picks_ref, *refs):
    parts, (out_ref, panel_ref, terms_ref) = refs[:-3], refs[-3:]
    assemble(my_ref[0], offsets, parts, panel_ref)
    rows = a_ref.shape[0]
    for start in range(0, rows, A_BLOCK):
        both = jnp.dot(a_ref[start : start + A_BLOCK, :], panel_ref[...], preferred_element_type=F32)
        first, second, third = (term.astype(F32) for term in split(both * swap_halves(both), 3))
        near = lane_ids(both.shape) < PANEL
        terms_ref[start : start + A_BLOCK, :LANES] = jnp.where(near, first, second).astype(BF16)
        terms_ref[start : start + A_BLOCK, LANES:] = third.astype(BF16)
    half = rows // 2
    block = half // 2
    for start in range(0, half, block):
        low = jnp.dot(picks_ref[start : start + block, :], terms_ref[...], preferred_element_type=F32)
        high = jnp.dot(picks_ref[half + start : half + start + block, :], terms_ref[...], preferred_element_type=F32)
        low, high = whole_sum(low), whole_sum(high)
        out_ref[start : start + block, :] = jnp.where(lane_ids(low.shape) < PANEL, low, high)


def lead_products(my_index, a_rows, picks, parts, offsets):
    rows, depth = a_rows.shape
    return pl.pallas_call(
        functools.partial(lead_product_kernel, offsets),
        in_specs=[pl.BlockSpec(memory_space=pltpu.SMEM)] + [pl.BlockSpec(memory_space=pltpu.VMEM)] * (2 + len(parts)),
        out_specs=pl.BlockSpec(memory_space=pltpu.VMEM),
        out_shape=jax.ShapeDtypeStruct((rows // 2, LANES), F32),
        scratch_shapes=[pltpu.VMEM((depth, LANES), BF16), pltpu.VMEM((rows, 2 * LANES), BF16)],
        compiler_params=params(),
        cost_estimate=pl.CostEstimate(
            flops=2 * rows * (depth + 2 * rows) * LANES, bytes_accessed=2 * rows * depth, transcendentals=0
        ),
        name="lead_products",
    )(my_index, a_rows, picks, *parts)


BIAS = 128


def rest_product_kernel(offsets, share, my_ref, order_ref, a_hbm, *refs):
    parts, (out_ref, a_ref, at_ref, panel_ref, terms_ref, sems) = refs[:-6], refs[-6:]
    rows = a_ref.shape[0]
    block = A_BLOCK
    starts = range(0, rows, block)
    copies = [
        pltpu.make_async_copy(a_hbm.at[pl.ds(start, block), :], a_ref.at[pl.ds(start, block), :], sems.at[i])
        for i, start in enumerate(starts)
    ]
    for copy in copies[:2]:
        copy.start()
    fill_order(order_ref, at_ref, share)
    assemble(my_ref[0], offsets, parts, panel_ref)
    for i, start in enumerate(starts):
        copies[i].wait()
        if i + 2 < len(copies):
            copies[i + 2].start()
        both = jnp.dot(a_ref[start : start + block, :], panel_ref[...], preferred_element_type=F32)
        near = both[:, :LANES]
        near = near * swap_halves(near)
        far = both[:, LANES : 2 * LANES] * both[:, 2 * LANES :]
        largest = jnp.max(jnp.maximum(jnp.abs(near), jnp.abs(far)), axis=1, keepdims=True)
        largest = jnp.maximum(largest, 1e-30)
        exponent = jnp.floor(jnp.log2(largest)) + 1.0
        far = jnp.floor(far * jnp.exp2(15.0 - exponent) + 0.5)
        far = jnp.minimum(jnp.maximum(far, -32767.0), 32767.0)
        near = jnp.floor(near * jnp.exp2(23.0 - exponent) + 0.5)
        near = jnp.minimum(jnp.maximum(near, -8388607.0), 8388607.0)
        far_top = jnp.floor(far * (1 / 256))
        near_top = jnp.floor(near * (1 / 65536))
        near = near - near_top * 65536.0
        near_middle = jnp.floor(near * (1 / 256))
        low_lanes = lane_ids(near.shape) < PANEL
        rows_here = slice(start, start + block)
        terms_ref[rows_here, :LANES] = far_top.astype(BF16)
        terms_ref[rows_here, LANES : 2 * LANES] = (far - far_top * 256.0).astype(BF16)
        terms_ref[rows_here, 2 * LANES : 3 * LANES] = jnp.where(low_lanes, near_top, near_middle).astype(BF16)
        terms_ref[rows_here, 3 * LANES :] = jnp.where(low_lanes, near - near_middle * 256.0, exponent).astype(BF16)


    def coded(start, size):
        picks = picks_of(at_ref[start : start + size, :], rows)
        got = jnp.dot(picks, terms_ref[...], preferred_element_type=F32)
        far = got[:, :LANES] * 256.0 + got[:, LANES : 2 * LANES]
        tops, lows = got[:, 2 * LANES : 3 * LANES], got[:, 3 * LANES :]
        low_lanes = lane_ids(tops.shape) < PANEL
        tops = tops * jnp.where(low_lanes, 65536.0, 256.0)
        swapped = swap_halves(lows)
        near = tops + swap_halves(tops) + jnp.where(low_lanes, lows, swapped)
        exponent = jnp.where(low_lanes, swapped, lows)
        near = near.astype(jnp.int32) * 256 + (exponent.astype(jnp.int32) + BIAS)
        return far.astype(jnp.int32), near

    half = rows // 2
    block = half // 2
    for start in range(0, half, block):
        far_low, near_low = coded(start, block)
        far_high, near_high = coded(half + start, block)
        out_ref[start : start + block, :LANES] = far_low * 65536 + (far_high & 65535)
        out_ref[start : start + block, LANES:] = jnp.where(lane_ids(near_low.shape) < PANEL, near_low, near_high)


def rest_products(my_index, order, a_rows, parts, offsets, share):
    rows, depth = a_rows.shape
    return pl.pallas_call(
        functools.partial(rest_product_kernel, offsets, share),
        in_specs=[
            pl.BlockSpec(memory_space=pltpu.SMEM),
            pl.BlockSpec(memory_space=pltpu.VMEM),
            pl.BlockSpec(memory_space=pl.ANY),
        ]
        + [pl.BlockSpec(memory_space=pltpu.VMEM)] * len(parts),
        out_specs=pl.BlockSpec(memory_space=pltpu.VMEM),
        out_shape=jax.ShapeDtypeStruct((rows // 2, 2 * LANES), jnp.int32),
        scratch_shapes=[
            pltpu.VMEM((rows, depth), BF16),
            pltpu.VMEM((rows, LANES), jnp.int32),
            pltpu.VMEM((depth, 3 * LANES), BF16),
            pltpu.VMEM((rows, 4 * LANES), BF16),
            pltpu.SemaphoreType.DMA((rows // A_BLOCK,)),
        ],
        compiler_params=params(24),
        cost_estimate=pl.CostEstimate(
            flops=2 * rows * (3 * depth + 4 * rows) * LANES, bytes_accessed=2 * rows * depth, transcendentals=0
        ),
        name="rest_products",
    )(my_index, order, a_rows, *parts)


def packed_terms(x, terms_ref, start):
    half = x.shape[0]
    first, second, third = (term.astype(F32) for term in split(x, 3))
    near = lane_ids(x.shape) < PANEL
    other = swap_halves(third)
    terms_ref[:half, start : start + LANES] = jnp.where(near, first, swap_halves(second)).astype(BF16)
    terms_ref[half:, start : start + LANES] = jnp.where(near, swap_halves(first), second).astype(BF16)
    terms_ref[:half, start + LANES : start + 2 * LANES] = jnp.where(near, third, other).astype(BF16)
    terms_ref[half:, start + LANES : start + 2 * LANES] = jnp.where(near, other, third).astype(BF16)


def leading_kernel(held, index_ref, arrived_ref, out_ref, terms_ref):
    packed_terms(arrived_ref[...], terms_ref, 0)
    width = -(-held // LANES) * LANES
    picks = one_hot(index_ref[:, :width], terms_ref.shape[0])
    got = whole_sum(jnp.dot(picks, terms_ref[...], preferred_element_type=F32))
    first, second = got[: held // 2], got[held // 2 : held]
    out_ref[0] = jnp.where(lane_ids(first.shape) < PANEL, first, second)


def leading_rows(index, arrived, held):
    rows = index.shape[1]
    return pl.pallas_call(
        functools.partial(leading_kernel, held),
        in_specs=[pl.BlockSpec(memory_space=pltpu.VMEM)] * 2,
        out_specs=pl.BlockSpec(memory_space=pltpu.VMEM),
        out_shape=jax.ShapeDtypeStruct((1, held // 2, LANES), F32),
        scratch_shapes=[pltpu.VMEM((rows, 2 * LANES), BF16)],
        compiler_params=params(),
        cost_estimate=pl.CostEstimate(
            flops=4 * held * rows * LANES, bytes_accessed=2 * rows * LANES, transcendentals=0
        ),
        name="leading_rows",
    )(index, arrived)


def stored_kernel(index_ref, arrived_ref, out_ref, terms_ref):
    packed_terms(arrived_ref[...], terms_ref, 0)
    rows = out_ref.shape[0]
    for start in range(0, rows, A_BLOCK):
        picks = one_hot(index_ref[:, start : start + A_BLOCK], rows)
        got = jnp.dot(picks, terms_ref[...], preferred_element_type=F32)
        out_ref[start : start + A_BLOCK, :] = whole_sum(got)[:, :PANEL]


def stored_rows(index, arrived):
    rows = index.shape[1]
    return pl.pallas_call(
        stored_kernel,
        in_specs=[pl.BlockSpec(memory_space=pltpu.VMEM)] * 2,
        out_specs=pl.BlockSpec(memory_space=pltpu.VMEM),
        out_shape=jax.ShapeDtypeStruct((rows, PANEL), F32),
        scratch_shapes=[pltpu.VMEM((rows, 2 * LANES), BF16)],
        compiler_params=params(),
        cost_estimate=pl.CostEstimate(
            flops=4 * rows * rows * LANES, bytes_accessed=2 * rows * rows, transcendentals=0
        ),
        name="stored_rows",
    )(index, arrived)


def eliminate(block, shift_row):
    rows = lax.broadcasted_iota(jnp.int32, (PANEL, PANEL), 0)
    columns = lax.broadcasted_iota(jnp.int32, (PANEL, PANEL), 1)
    flipped = jnp.transpose(block)
    mirrored = jnp.where(rows >= columns, block, flipped)
    diagonal = shift_row + jnp.sum(jnp.abs(mirrored), axis=0, keepdims=True)
    unit = (rows == columns).astype(F32)
    work = jnp.where(rows == columns, diagonal, mirrored)
    work = jnp.concatenate([work, unit], axis=1)
    height = 8
    groups = [work[start : start + height] for start in range(0, PANEL, height)]
    sublanes = lax.broadcasted_iota(jnp.int32, (height, LANES), 0)
    scaled_rows = []
    for k in range(PANEL):
        home, offset = divmod(k, height)
        row = groups[home][offset : offset + 1, :]
        row = row / row[:, k : k + 1]
        scaled_rows.append(row)
        for g in range(home, PANEL // height):
            column = jnp.broadcast_to(groups[g][:, k : k + 1], (height, LANES))
            if g == home:
                column = jnp.where(sublanes > offset, column, 0.0)
            groups[g] = groups[g] - column * row
    final = jnp.concatenate(groups, axis=0)
    scaled = jnp.concatenate(scaled_rows, axis=0)
    upper = jnp.where(columns >= rows, scaled[:, :PANEL], 0.0)
    pivots = jnp.sum(jnp.where(rows == columns, final[:, :PANEL], 0.0), axis=0, keepdims=True)
    return upper, final[:, PANEL:], pivots


def exact(lhs, rhs, dims):
    return lax.dot_general(lhs, rhs, (dims, ((), ())), precision=lax.Precision.HIGHEST, preferred_element_type=F32)


def update_kernel(offsets, blocks_held, columns, my_ref, lead_ref, shift_ref, resident_hbm, *refs):
    parts = refs[:-10]
    near_hbm, far_hbm, pivots_ref, leading_ref, tail_ref, resident_ref, near_ref, far_ref, sem, sems = refs[-10:]
    fetch = pltpu.make_async_copy(resident_hbm, resident_ref, sem)
    fetch.start()
    my_index = my_ref[0]
    size = len(offsets)
    position = 0
    packed = blocks_held * PANEL // 2
    part_rows = PANEL // 2
    for part in parts:
        for number in range(part.shape[0]):
            owner = my_index ^ offsets[position]
            for start in range(0, blocks_held * PANEL, part_rows):
                held, inner = divmod(start, PANEL)
                if start < packed:
                    rows = part[number, start : start + part_rows, :PANEL]
                else:
                    rows = part[number, start - packed : start - packed + part_rows, PANEL:]
                target = pl.multiple_of((held * size + owner) * PANEL + inner, part_rows)
                leading_ref[pl.ds(target, part_rows), :] = rows
            position += 1
    upper, inverse, pivots = eliminate(leading_ref[:PANEL, :], shift_ref[...])
    pivots_ref[...] = pivots
    lower = jnp.transpose(upper)
    needed = tail_ref.shape[1]
    tail = exact(inverse, leading_ref[:needed, :], ((1,), (1,)))
    high, low = split(tail, 2)
    tail_ref[0:PANEL, :] = high
    tail_ref[PANEL : 2 * PANEL, :] = high
    tail_ref[2 * PANEL : 3 * PANEL, :] = low
    tail_ref[3 * PANEL :, :] = low
    fetch.wait()

    block = A_BLOCK
    stores = []
    for number, start in enumerate(range(0, lead_ref.shape[0], block)):
        rows_here = slice(start, start + block)
        panel = exact(lead_ref[rows_here, :], inverse, ((1,), (1,))) / pivots
        shown = used = panel
        if start == 0:
            row_ids = lax.broadcasted_iota(jnp.int32, panel.shape, 0)
            top = jnp.logical_and(my_index == 0, row_ids < PANEL)
            used = jnp.where(top, 0.0, panel)
            filled = jnp.concatenate([lower, jnp.zeros((block - PANEL, PANEL), F32)], axis=0)
            shown = jnp.where(top, filled, panel)
        high, low = (term.astype(F32) for term in split(used, 2))
        pair = jnp.concatenate([high, low], axis=1).astype(BF16)
        factors = jnp.concatenate([pair, pair], axis=1)
        update = jnp.dot(factors, tail_ref[...], preferred_element_type=F32)
        shown = jnp.concatenate([shown, jnp.zeros_like(shown)], axis=1)
        near_ref[rows_here, :LANES] = jnp.where(lane_ids(shown.shape) < PANEL, shown, -update[:, :LANES])
        near_ref[rows_here, LANES:] = -update[:, LANES:columns]
        far_ref[rows_here, :] = (resident_ref[rows_here, :].astype(F32) - update[:, columns:]).astype(BF16)
        for which, (source, target) in enumerate(((near_ref, near_hbm), (far_ref, far_hbm))):
            store = pltpu.make_async_copy(
                source.at[pl.ds(start, block), :], target.at[pl.ds(start, block), :], sems.at[which, number]
            )
            store.start()
            stores.append(store)
    for store in stores:
        store.wait()


def updates(my_index, parts, offsets, lead, shift, resident, blocks_held, columns):
    rows, width = resident.shape
    needed = columns + width
    held_rows = len(offsets) * blocks_held * PANEL
    vmem = pl.BlockSpec(memory_space=pltpu.VMEM)
    anywhere = pl.BlockSpec(memory_space=pl.ANY)
    return pl.pallas_call(
        functools.partial(update_kernel, offsets, blocks_held, columns),
        in_specs=[pl.BlockSpec(memory_space=pltpu.SMEM), vmem, vmem, anywhere] + [vmem] * len(parts),
        out_specs=[anywhere, anywhere, vmem],
        out_shape=[
            jax.ShapeDtypeStruct((rows, columns), F32),
            jax.ShapeDtypeStruct((rows, width), BF16),
            jax.ShapeDtypeStruct((1, PANEL), F32),
        ],
        scratch_shapes=[
            pltpu.VMEM((held_rows, PANEL), F32),
            pltpu.VMEM((4 * PANEL, needed), BF16),
            pltpu.VMEM((rows, width), BF16),
            pltpu.VMEM((rows, columns), F32),
            pltpu.VMEM((rows, width), BF16),
            pltpu.SemaphoreType.DMA,
            pltpu.SemaphoreType.DMA((2, rows // A_BLOCK)),
        ],
        compiler_params=params(28),
        cost_estimate=pl.CostEstimate(
            flops=2 * rows * needed * 4 * PANEL, bytes_accessed=4 * rows * (columns + width), transcendentals=0
        ),
        name="factor_and_update",
    )(my_index, lead, shift, resident, *parts)


def formed_kernel(index_ref, arrived_ref, near_ref, out_ref, terms_ref):
    half = arrived_ref.shape[0]

    @pl.when(pl.program_id(0) == 0)
    def _():
        words = arrived_ref[:, LANES:]
        low_lanes = lane_ids(words.shape) < PANEL
        exponent = ((words & 255) - BIAS).astype(F32)
        other = swap_halves(exponent)
        packed_terms((words >> 8).astype(F32) * jnp.exp2(exponent - 23.0), terms_ref, 2 * LANES)
        words = arrived_ref[:, :LANES]
        low = (words >> 16).astype(F32) * jnp.exp2(jnp.where(low_lanes, exponent, other) - 15.0)
        high = ((words << 16) >> 16).astype(F32) * jnp.exp2(jnp.where(low_lanes, other, exponent) - 15.0)
        for side, values in enumerate((low, high)):
            first, second = split(values, 2)
            terms_ref[side * half : (side + 1) * half, :LANES] = first
            terms_ref[side * half : (side + 1) * half, LANES : 2 * LANES] = second

    picks = one_hot(index_ref[...], terms_ref.shape[0])
    got = jnp.dot(picks, terms_ref[...], preferred_element_type=F32)
    narrow = whole_sum(got[:, 2 * LANES :])
    held = near_ref[:, :LANES]
    out_ref[:, :LANES] = jnp.where(lane_ids(held.shape) < PANEL, held, narrow + held)
    out_ref[:, LANES:] = (got[:, :LANES] + got[:, LANES : 2 * LANES]) + near_ref[:, LANES:]


def formed_columns(index, arrived, near):
    rows, columns = near.shape
    half, width = arrived.shape
    steps = 5
    block = rows // steps
    return pl.pallas_call(
        formed_kernel,
        grid=(steps,),
        in_specs=[
            pl.BlockSpec((1, block), lambda i: (0, i)),
            pl.BlockSpec((half, width), lambda i: (0, 0)),
            pl.BlockSpec((block, columns), lambda i: (i, 0)),
        ],
        out_specs=pl.BlockSpec((block, columns), lambda i: (i, 0)),
        out_shape=jax.ShapeDtypeStruct((rows, columns), F32),
        scratch_shapes=[pltpu.VMEM((rows, 4 * LANES), BF16)],
        compiler_params=params(),
        cost_estimate=pl.CostEstimate(
            flops=8 * rows * rows * LANES, bytes_accessed=8 * rows * columns, transcendentals=0
        ),
        name="formed_columns",
    )(index, arrived, near)


def swap_rows(x, group):
    rows, width = x.shape
    return lax.all_to_all(
        x.reshape(group, rows // group, width), "wide", split_axis=0, concat_axis=0, tiled=True
    ).reshape(rows, width)


def on_device(a_rows, xa_panel, za_panel, send_order, recv_order, shift, resident):
    rows = a_rows.shape[0]
    columns = xa_panel.shape[1]
    group = lax.axis_size("wide")
    my_index = lax.axis_index("wide").astype(jnp.int32).reshape(1)
    share = rows // group
    half = rows // 2
    few, apart = phases_of(group)

    order, packing = send_order, share
    if share % 16:
        order = send_order.reshape(group, 2, share // 2).transpose(1, 0, 2).reshape(1, rows)
        packing = 0
    source, slot = recv_order // share, recv_order % share
    index = (slot // (share // 2)) * half + source * (share // 2) + slot % (share // 2)

    lead_panel, rest_panel = split_panels(my_index, xa_panel, za_panel)
    send_picks, a_copy = order_picks(order, a_rows, packing)
    lead_parts = exchange([lead_panel], few[0], "wide")
    for masks in few[1:]:
        lead_parts = exchange([after(join(lead_parts)[0], send_picks)], masks, "wide")
    rest_parts = exchange([after(rest_panel, lead_parts[0])], apart[0], "wide")

    lead_out = lead_products(my_index, a_copy, send_picks, lead_parts, offsets_of(few))
    lead_in = swap_rows(lead_out, group)

    rest_parts = [after(join(rest_parts)[0], lead_in)]
    for masks in apart[1:-1]:
        rest_parts = exchange(join(rest_parts), masks, "wide")
    rest_parts = exchange(rest_parts, apart[-1], "wide")

    needed = columns + resident.shape[1]
    blocks_held = -(-needed // (PANEL * group))
    leading_parts = exchange([leading_rows(index, lead_in, blocks_held * PANEL)], few[0], "wide")
    lead = stored_rows(index, lead_in)
    for masks in few[1:]:
        leading_parts = exchange([after(join(leading_parts)[0], lead)], masks, "wide")

    rest_out = rest_products(my_index, order, a_rows, rest_parts, offsets_of(apart), packing)
    rest_in = swap_rows(after(rest_out, *leading_parts), group)
    near, updated, pivots = updates(
        my_index,
        leading_parts,
        offsets_of(few),
        after(lead, rest_out),
        shift[None, :],
        resident,
        blocks_held,
        columns,
    )
    factored = formed_columns(index, rest_in, near)
    return (factored, updated, pivots[0])


def solution(mesh):
    placed = (
        P(("parts", "wide"), None),
        P(("parts", "wide"), None),
        P(("parts", "wide"), None),
        P(("parts", "wide"), None),
        P(("parts", "wide"), None),
        P("parts"),
        P(("parts", "wide"), None),
    )
    return jax.shard_map(
        on_device,
        mesh=mesh,
        in_specs=placed,
        out_specs=(P(("parts", "wide"), None), P(("parts", "wide"), None), P("parts")),
        check_vma=False,
    )
```

```python
import functools

import jax
import jax.numpy as jnp
from jax import lax
from jax.experimental import pallas as pl
from jax.experimental.pallas import tpu as pltpu
from jax.sharding import PartitionSpec as P

PANEL = 64
LANES = 128
A_BLOCK = 256
F32 = jnp.float32
BF16 = jnp.bfloat16
MIB = 1024 * 1024


def params(mebibytes=12):
    return pltpu.CompilerParams(vmem_limit_bytes=mebibytes * MIB)


def lane_ids(shape):
    return lax.broadcasted_iota(jnp.int32, shape, len(shape) - 1)


def split(x, count):
    terms = []
    for _ in range(count):
        term = x.astype(BF16)
        terms.append(term)
        x = x - term.astype(F32)
    return terms


def swap_halves(x):
    return pltpu.roll(x, LANES // 2, 1)


def as_column(index_row):
    return jnp.transpose(jnp.broadcast_to(index_row, (LANES, LANES)))


def picks_of(at, width):
    lanes = lane_ids(at.shape)
    return jnp.concatenate(
        [(at == lanes + column).astype(F32).astype(BF16) for column in range(0, width, LANES)], axis=1
    )


def one_hot(index_row, width):
    chunks = [
        picks_of(as_column(index_row[:, start : start + LANES]), width)
        for start in range(0, index_row.shape[1], LANES)
    ]
    return jnp.concatenate(chunks, axis=0) if len(chunks) > 1 else chunks[0]


def packed_order(share, half, slot):
    part = share // 2
    return (slot % share) // part * half + slot // share * part + slot % part


def fill_order(order_ref, at_ref, share):
    rows = order_ref.shape[1]
    height = 8
    for start in range(0, rows, LANES):
        column = as_column(order_ref[:, start : start + LANES])
        if not share:
            at_ref[start : start + LANES, :] = column
            continue
        for inner in range(0, LANES, height):
            place = packed_order(share, rows // 2, start + inner)
            at_ref[place : place + height, :] = column[inner : inner + height]


def after(x, *earlier):
    return lax.optimization_barrier((x, *earlier))[0]


def exchange(held, masks, axis):
    size = lax.axis_size(axis)
    combined = [0]
    for mask in masks:
        combined += [other ^ mask for other in combined]
    parts = list(held)
    for mask in combined[1:]:
        parts += [lax.ppermute(part, axis, [(i, i ^ mask) for i in range(size)]) for part in held]
    return parts


def offsets_of(phases):
    offsets = [0]
    for masks in phases:
        combined = [0]
        for mask in masks:
            combined += [other ^ mask for other in combined]
        offsets = [offset ^ mask for mask in combined for offset in offsets]
    return offsets


def join(parts):
    return [jnp.concatenate(parts, axis=0)]


def phases_of(size):
    bits = [1 << bit for bit in reversed(range(size.bit_length() - 1))]
    pairs = [bits[start : start + 2] for start in range(0, len(bits), 2)]
    singles = [bits[start : start + 2] for start in range(0, len(bits) - 2, 2)]
    return pairs, singles + [bits[-2:-1], bits[-1:]]


def picks_kernel(share, order_ref, a_hbm, picks_ref, copy_ref, at_ref, sem):
    copy = pltpu.make_async_copy(a_hbm, copy_ref, sem)
    copy.start()
    fill_order(order_ref, at_ref, share)
    rows, width = picks_ref.shape
    for start in range(0, rows, A_BLOCK):
        picks_ref[start : start + A_BLOCK, :] = picks_of(at_ref[start : start + A_BLOCK, :], width)
    copy.wait()


def order_picks(order, a_rows, share):
    rows, depth = a_rows.shape
    return pl.pallas_call(
        functools.partial(picks_kernel, share),
        in_specs=[pl.BlockSpec(memory_space=pltpu.VMEM), pl.BlockSpec(memory_space=pl.ANY)],
        out_specs=[pl.BlockSpec(memory_space=pltpu.VMEM)] * 2,
        out_shape=[jax.ShapeDtypeStruct((rows, rows), BF16), jax.ShapeDtypeStruct((rows, depth), BF16)],
        scratch_shapes=[pltpu.VMEM((rows, LANES), jnp.int32), pltpu.SemaphoreType.DMA],
        compiler_params=params(),
        cost_estimate=pl.CostEstimate(flops=4 * rows * rows, bytes_accessed=4 * rows * depth, transcendentals=0),
        name="order_picks",
    )(order, a_rows)


def panels_kernel(my_ref, xa_hbm, za_hbm, lead_ref, rest_ref, xa_ref, za_ref, sems):
    copies = [
        pltpu.make_async_copy(xa_hbm, xa_ref, sems.at[0]),
        pltpu.make_async_copy(za_hbm, za_ref, sems.at[1]),
    ]
    for copy in copies:
        copy.start()
    for copy in copies:
        copy.wait()
    lead_ref[0] = jnp.concatenate([xa_ref[:, :PANEL], za_ref[:, :PANEL]], axis=1)
    rest_ref[0, :, :LANES] = jnp.concatenate([xa_ref[:, PANEL:LANES], za_ref[:, PANEL:LANES]], axis=1)
    rest_ref[0, :, LANES : 2 * LANES] = xa_ref[:, LANES:]
    rest_ref[0, :, 2 * LANES :] = za_ref[:, LANES:]


def split_panels(my_index, xa_panel, za_panel):
    depth, columns = xa_panel.shape
    return pl.pallas_call(
        panels_kernel,
        in_specs=[pl.BlockSpec(memory_space=pltpu.SMEM)] + [pl.BlockSpec(memory_space=pl.ANY)] * 2,
        out_shape=[
            jax.ShapeDtypeStruct((1, depth, LANES), BF16),
            jax.ShapeDtypeStruct((1, depth, 2 * columns - LANES), BF16),
        ],
        scratch_shapes=[
            pltpu.VMEM((depth, columns), BF16),
            pltpu.VMEM((depth, columns), BF16),
            pltpu.SemaphoreType.DMA((2,)),
        ],
        compiler_params=params(60),
        name="split_panels",
    )(my_index, xa_panel, za_panel)


def assemble(my_index, offsets, parts, panel_ref):
    position = 0
    for part in parts:
        for number in range(part.shape[0]):
            depth = part.shape[1]
            start = pl.multiple_of((my_index ^ offsets[position]) * depth, depth)
            panel_ref[pl.ds(start, depth), :] = part[number]
            position += 1


def whole_sum(got):
    pair = got[:, :LANES]
    return (pair + swap_halves(pair)) + got[:, LANES:]


def lead_product_kernel(offsets, my_ref, a_ref, picks_ref, *refs):
    parts, (out_ref, panel_ref, terms_ref) = refs[:-3], refs[-3:]
    assemble(my_ref[0], offsets, parts, panel_ref)
    rows = a_ref.shape[0]
    for start in range(0, rows, A_BLOCK):
        both = jnp.dot(a_ref[start : start + A_BLOCK, :], panel_ref[...], preferred_element_type=F32)
        first, second, third = (term.astype(F32) for term in split(both * swap_halves(both), 3))
        near = lane_ids(both.shape) < PANEL
        terms_ref[start : start + A_BLOCK, :LANES] = jnp.where(near, first, second).astype(BF16)
        terms_ref[start : start + A_BLOCK, LANES:] = third.astype(BF16)
    half = rows // 2
    block = half // 2
    for start in range(0, half, block):
        low = jnp.dot(picks_ref[start : start + block, :], terms_ref[...], preferred_element_type=F32)
        high = jnp.dot(picks_ref[half + start : half + start + block, :], terms_ref[...], preferred_element_type=F32)
        low, high = whole_sum(low), whole_sum(high)
        out_ref[start : start + block, :] = jnp.where(lane_ids(low.shape) < PANEL, low, high)


def lead_products(my_index, a_rows, picks, parts, offsets):
    rows, depth = a_rows.shape
    return pl.pallas_call(
        functools.partial(lead_product_kernel, offsets),
        in_specs=[pl.BlockSpec(memory_space=pltpu.SMEM)] + [pl.BlockSpec(memory_space=pltpu.VMEM)] * (2 + len(parts)),
        out_specs=pl.BlockSpec(memory_space=pltpu.VMEM),
        out_shape=jax.ShapeDtypeStruct((rows // 2, LANES), F32),
        scratch_shapes=[pltpu.VMEM((depth, LANES), BF16), pltpu.VMEM((rows, 2 * LANES), BF16)],
        compiler_params=params(),
        cost_estimate=pl.CostEstimate(
            flops=2 * rows * (depth + 2 * rows) * LANES, bytes_accessed=2 * rows * depth, transcendentals=0
        ),
        name="lead_products",
    )(my_index, a_rows, picks, *parts)


BIAS = 128


def rest_product_kernel(offsets, share, my_ref, order_ref, a_hbm, *refs):
    parts, (out_ref, a_ref, at_ref, panel_ref, terms_ref, sems) = refs[:-6], refs[-6:]
    rows = a_ref.shape[0]
    block = A_BLOCK
    starts = range(0, rows, block)
    copies = [
        pltpu.make_async_copy(a_hbm.at[pl.ds(start, block), :], a_ref.at[pl.ds(start, block), :], sems.at[i])
        for i, start in enumerate(starts)
    ]
    for copy in copies[:2]:
        copy.start()
    fill_order(order_ref, at_ref, share)
    assemble(my_ref[0], offsets, parts, panel_ref)
    for i, start in enumerate(starts):
        copies[i].wait()
        if i + 2 < len(copies):
            copies[i + 2].start()
        both = jnp.dot(a_ref[start : start + block, :], panel_ref[...], preferred_element_type=F32)
        near = both[:, :LANES]
        near = near * swap_halves(near)
        far = both[:, LANES : 2 * LANES] * both[:, 2 * LANES :]
        largest = jnp.max(jnp.maximum(jnp.abs(near), jnp.abs(far)), axis=1, keepdims=True)
        largest = jnp.maximum(largest, 1e-30)
        exponent = jnp.floor(jnp.log2(largest)) + 1.0
        far = jnp.floor(far * jnp.exp2(15.0 - exponent) + 0.5)
        far = jnp.minimum(jnp.maximum(far, -32767.0), 32767.0)
        near = jnp.floor(near * jnp.exp2(23.0 - exponent) + 0.5)
        near = jnp.minimum(jnp.maximum(near, -8388607.0), 8388607.0)
        far_top = jnp.floor(far * (1 / 256))
        near_top = jnp.floor(near * (1 / 65536))
        near = near - near_top * 65536.0
        near_middle = jnp.floor(near * (1 / 256))
        low_lanes = lane_ids(near.shape) < PANEL
        rows_here = slice(start, start + block)
        terms_ref[rows_here, :LANES] = far_top.astype(BF16)
        terms_ref[rows_here, LANES : 2 * LANES] = (far - far_top * 256.0).astype(BF16)
        terms_ref[rows_here, 2 * LANES : 3 * LANES] = jnp.where(low_lanes, near_top, near_middle).astype(BF16)
        terms_ref[rows_here, 3 * LANES :] = jnp.where(low_lanes, near - near_middle * 256.0, exponent).astype(BF16)


    def coded(start, size):
        picks = picks_of(at_ref[start : start + size, :], rows)
        got = jnp.dot(picks, terms_ref[...], preferred_element_type=F32)
        far = got[:, :LANES] * 256.0 + got[:, LANES : 2 * LANES]
        tops, lows = got[:, 2 * LANES : 3 * LANES], got[:, 3 * LANES :]
        low_lanes = lane_ids(tops.shape) < PANEL
        tops = tops * jnp.where(low_lanes, 65536.0, 256.0)
        swapped = swap_halves(lows)
        near = tops + swap_halves(tops) + jnp.where(low_lanes, lows, swapped)
        exponent = jnp.where(low_lanes, swapped, lows)
        near = near.astype(jnp.int32) * 256 + (exponent.astype(jnp.int32) + BIAS)
        return far.astype(jnp.int32), near

    half = rows // 2
    block = half // 2
    for start in range(0, half, block):
        far_low, near_low = coded(start, block)
        far_high, near_high = coded(half + start, block)
        out_ref[start : start + block, :LANES] = far_low * 65536 + (far_high & 65535)
        out_ref[start : start + block, LANES:] = jnp.where(lane_ids(near_low.shape) < PANEL, near_low, near_high)


def rest_products(my_index, order, a_rows, parts, offsets, share):
    rows, depth = a_rows.shape
    return pl.pallas_call(
        functools.partial(rest_product_kernel, offsets, share),
        in_specs=[
            pl.BlockSpec(memory_space=pltpu.SMEM),
            pl.BlockSpec(memory_space=pltpu.VMEM),
            pl.BlockSpec(memory_space=pl.ANY),
        ]
        + [pl.BlockSpec(memory_space=pltpu.VMEM)] * len(parts),
        out_specs=pl.BlockSpec(memory_space=pltpu.VMEM),
        out_shape=jax.ShapeDtypeStruct((rows // 2, 2 * LANES), jnp.int32),
        scratch_shapes=[
            pltpu.VMEM((rows, depth), BF16),
            pltpu.VMEM((rows, LANES), jnp.int32),
            pltpu.VMEM((depth, 3 * LANES), BF16),
            pltpu.VMEM((rows, 4 * LANES), BF16),
            pltpu.SemaphoreType.DMA((rows // A_BLOCK,)),
        ],
        compiler_params=params(60),
        cost_estimate=pl.CostEstimate(
            flops=2 * rows * (3 * depth + 4 * rows) * LANES, bytes_accessed=2 * rows * depth, transcendentals=0
        ),
        name="rest_products",
    )(my_index, order, a_rows, *parts)


def packed_terms(x, terms_ref, start):
    half = x.shape[0]
    first, second, third = (term.astype(F32) for term in split(x, 3))
    near = lane_ids(x.shape) < PANEL
    other = swap_halves(third)
    terms_ref[:half, start : start + LANES] = jnp.where(near, first, swap_halves(second)).astype(BF16)
    terms_ref[half:, start : start + LANES] = jnp.where(near, swap_halves(first), second).astype(BF16)
    terms_ref[:half, start + LANES : start + 2 * LANES] = jnp.where(near, third, other).astype(BF16)
    terms_ref[half:, start + LANES : start + 2 * LANES] = jnp.where(near, other, third).astype(BF16)


def leading_kernel(held, index_ref, arrived_ref, out_ref, terms_ref):
    packed_terms(arrived_ref[...], terms_ref, 0)
    width = -(-held // LANES) * LANES
    picks = one_hot(index_ref[:, :width], terms_ref.shape[0])
    got = whole_sum(jnp.dot(picks, terms_ref[...], preferred_element_type=F32))
    first, second = got[: held // 2], got[held // 2 : held]
    out_ref[0] = jnp.where(lane_ids(first.shape) < PANEL, first, second)


def leading_rows(index, arrived, held):
    rows = index.shape[1]
    return pl.pallas_call(
        functools.partial(leading_kernel, held),
        in_specs=[pl.BlockSpec(memory_space=pltpu.VMEM)] * 2,
        out_specs=pl.BlockSpec(memory_space=pltpu.VMEM),
        out_shape=jax.ShapeDtypeStruct((1, held // 2, LANES), F32),
        scratch_shapes=[pltpu.VMEM((rows, 2 * LANES), BF16)],
        compiler_params=params(),
        cost_estimate=pl.CostEstimate(
            flops=4 * held * rows * LANES, bytes_accessed=2 * rows * LANES, transcendentals=0
        ),
        name="leading_rows",
    )(index, arrived)


def eliminate(block, shift_row):
    rows = lax.broadcasted_iota(jnp.int32, (PANEL, PANEL), 0)
    columns = lax.broadcasted_iota(jnp.int32, (PANEL, PANEL), 1)
    flipped = jnp.transpose(block)
    mirrored = jnp.where(rows >= columns, block, flipped)
    diagonal = shift_row + jnp.sum(jnp.abs(mirrored), axis=0, keepdims=True)
    unit = (rows == columns).astype(F32)
    work = jnp.where(rows == columns, diagonal, mirrored)
    work = jnp.concatenate([work, unit], axis=1)
    height = 8
    groups = [work[start : start + height] for start in range(0, PANEL, height)]
    sublanes = lax.broadcasted_iota(jnp.int32, (height, LANES), 0)
    scaled_rows = []
    for k in range(PANEL):
        home, offset = divmod(k, height)
        row = groups[home][offset : offset + 1, :]
        row = row / row[:, k : k + 1]
        scaled_rows.append(row)
        for g in range(home, PANEL // height):
            column = jnp.broadcast_to(groups[g][:, k : k + 1], (height, LANES))
            if g == home:
                column = jnp.where(sublanes > offset, column, 0.0)
            groups[g] = groups[g] - column * row
    final = jnp.concatenate(groups, axis=0)
    scaled = jnp.concatenate(scaled_rows, axis=0)
    upper = jnp.where(columns >= rows, scaled[:, :PANEL], 0.0)
    pivots = jnp.sum(jnp.where(rows == columns, final[:, :PANEL], 0.0), axis=0, keepdims=True)
    return upper, final[:, PANEL:], pivots


def exact(lhs, rhs, dims):
    return lax.dot_general(lhs, rhs, (dims, ((), ())), precision=lax.Precision.HIGHEST, preferred_element_type=F32)


def update_kernel(offsets, blocks_held, columns, my_ref, index_ref, arrived_ref, shift_ref, resident_hbm, *refs):
    parts = refs[:-12]
    near_hbm, far_hbm, pivots_ref, leading_ref, tail_ref, resident_ref, terms_ref, lead_ref = refs[-12:-4]
    near_ref, far_ref, sem, sems = refs[-4:]
    fetch = pltpu.make_async_copy(resident_hbm, resident_ref, sem)
    fetch.start()
    my_index = my_ref[0]
    size = len(offsets)
    position = 0
    packed = blocks_held * PANEL // 2
    part_rows = PANEL // 2
    for part in parts:
        for number in range(part.shape[0]):
            owner = my_index ^ offsets[position]
            for start in range(0, blocks_held * PANEL, part_rows):
                held, inner = divmod(start, PANEL)
                if start < packed:
                    rows = part[number, start : start + part_rows, :PANEL]
                else:
                    rows = part[number, start - packed : start - packed + part_rows, PANEL:]
                target = pl.multiple_of((held * size + owner) * PANEL + inner, part_rows)
                leading_ref[pl.ds(target, part_rows), :] = rows
            position += 1
    upper, inverse, pivots = eliminate(leading_ref[:PANEL, :], shift_ref[...])
    pivots_ref[...] = pivots
    lower = jnp.transpose(upper)
    needed = tail_ref.shape[1]
    tail = exact(inverse, leading_ref[:needed, :], ((1,), (1,)))
    high, low = split(tail, 2)
    tail_ref[0:PANEL, :] = high
    tail_ref[PANEL : 2 * PANEL, :] = high
    tail_ref[2 * PANEL : 3 * PANEL, :] = low
    tail_ref[3 * PANEL :, :] = low

    block = A_BLOCK
    packed_terms(arrived_ref[...], terms_ref, 0)
    for start in range(0, lead_ref.shape[0], block):
        picks = one_hot(index_ref[:, start : start + block], lead_ref.shape[0])
        got = jnp.dot(picks, terms_ref[...], preferred_element_type=F32)
        lead_ref[start : start + block, :] = whole_sum(got)[:, :PANEL]
    fetch.wait()
    stores = []
    for number, start in enumerate(range(0, lead_ref.shape[0], block)):
        rows_here = slice(start, start + block)
        panel = exact(lead_ref[rows_here, :], inverse, ((1,), (1,))) / pivots
        shown = used = panel
        if start == 0:
            row_ids = lax.broadcasted_iota(jnp.int32, panel.shape, 0)
            top = jnp.logical_and(my_index == 0, row_ids < PANEL)
            used = jnp.where(top, 0.0, panel)
            filled = jnp.concatenate([lower, jnp.zeros((block - PANEL, PANEL), F32)], axis=0)
            shown = jnp.where(top, filled, panel)
        high, low = (term.astype(F32) for term in split(used, 2))
        pair = jnp.concatenate([high, low], axis=1).astype(BF16)
        factors = jnp.concatenate([pair, pair], axis=1)
        update = jnp.dot(factors, tail_ref[...], preferred_element_type=F32)
        shown = jnp.concatenate([shown, jnp.zeros_like(shown)], axis=1)
        near_ref[rows_here, :LANES] = jnp.where(lane_ids(shown.shape) < PANEL, shown, -update[:, :LANES])
        near_ref[rows_here, LANES:] = -update[:, LANES:columns]
        far_ref[rows_here, :] = (resident_ref[rows_here, :].astype(F32) - update[:, columns:]).astype(BF16)
        for which, (source, target) in enumerate(((near_ref, near_hbm), (far_ref, far_hbm))):
            store = pltpu.make_async_copy(
                source.at[pl.ds(start, block), :], target.at[pl.ds(start, block), :], sems.at[which, number]
            )
            store.start()
            stores.append(store)
    for store in stores:
        store.wait()


def updates(my_index, parts, offsets, index, arrived, shift, resident, blocks_held, columns):
    rows, width = resident.shape
    needed = columns + width
    held_rows = len(offsets) * blocks_held * PANEL
    vmem = pl.BlockSpec(memory_space=pltpu.VMEM)
    anywhere = pl.BlockSpec(memory_space=pl.ANY)
    return pl.pallas_call(
        functools.partial(update_kernel, offsets, blocks_held, columns),
        in_specs=[pl.BlockSpec(memory_space=pltpu.SMEM), vmem, vmem, vmem, anywhere] + [vmem] * len(parts),
        out_specs=[anywhere, anywhere, vmem],
        out_shape=[
            jax.ShapeDtypeStruct((rows, columns), F32),
            jax.ShapeDtypeStruct((rows, width), BF16),
            jax.ShapeDtypeStruct((1, PANEL), F32),
        ],
        scratch_shapes=[
            pltpu.VMEM((held_rows, PANEL), F32),
            pltpu.VMEM((4 * PANEL, needed), BF16),
            pltpu.VMEM((rows, width), BF16),
            pltpu.VMEM((rows, 2 * LANES), BF16),
            pltpu.VMEM((rows, PANEL), F32),
            pltpu.VMEM((rows, columns), F32),
            pltpu.VMEM((rows, width), BF16),
            pltpu.SemaphoreType.DMA,
            pltpu.SemaphoreType.DMA((2, rows // A_BLOCK)),
        ],
        compiler_params=params(60),
        cost_estimate=pl.CostEstimate(
            flops=2 * rows * needed * 4 * PANEL, bytes_accessed=4 * rows * (columns + width), transcendentals=0
        ),
        name="factor_and_update",
    )(my_index, index, arrived, shift, resident, *parts)


def formed_kernel(index_ref, arrived_ref, near_ref, out_ref, terms_ref):
    half = arrived_ref.shape[0]

    @pl.when(pl.program_id(0) == 0)
    def _():
        words = arrived_ref[:, LANES:]
        low_lanes = lane_ids(words.shape) < PANEL
        exponent = ((words & 255) - BIAS).astype(F32)
        other = swap_halves(exponent)
        packed_terms((words >> 8).astype(F32) * jnp.exp2(exponent - 23.0), terms_ref, 2 * LANES)
        words = arrived_ref[:, :LANES]
        low = (words >> 16).astype(F32) * jnp.exp2(jnp.where(low_lanes, exponent, other) - 15.0)
        high = ((words << 16) >> 16).astype(F32) * jnp.exp2(jnp.where(low_lanes, other, exponent) - 15.0)
        for side, values in enumerate((low, high)):
            first, second = split(values, 2)
            terms_ref[side * half : (side + 1) * half, :LANES] = first
            terms_ref[side * half : (side + 1) * half, LANES : 2 * LANES] = second

    picks = one_hot(index_ref[...], terms_ref.shape[0])
    got = jnp.dot(picks, terms_ref[...], preferred_element_type=F32)
    narrow = whole_sum(got[:, 2 * LANES :])
    held = near_ref[:, :LANES]
    out_ref[:, :LANES] = jnp.where(lane_ids(held.shape) < PANEL, held, narrow + held)
    out_ref[:, LANES:] = (got[:, :LANES] + got[:, LANES : 2 * LANES]) + near_ref[:, LANES:]


def formed_columns(index, arrived, near):
    rows, columns = near.shape
    half, width = arrived.shape
    steps = 5
    block = rows // steps
    return pl.pallas_call(
        formed_kernel,
        grid=(steps,),
        in_specs=[
            pl.BlockSpec((1, block), lambda i: (0, i)),
            pl.BlockSpec((half, width), lambda i: (0, 0)),
            pl.BlockSpec((block, columns), lambda i: (i, 0)),
        ],
        out_specs=pl.BlockSpec((block, columns), lambda i: (i, 0)),
        out_shape=jax.ShapeDtypeStruct((rows, columns), F32),
        scratch_shapes=[pltpu.VMEM((rows, 4 * LANES), BF16)],
        compiler_params=params(60),
        cost_estimate=pl.CostEstimate(
            flops=8 * rows * rows * LANES, bytes_accessed=8 * rows * columns, transcendentals=0
        ),
        name="formed_columns",
    )(index, arrived, near)


def swap_rows(x, group):
    rows, width = x.shape
    return lax.all_to_all(
        x.reshape(group, rows // group, width), "wide", split_axis=0, concat_axis=0, tiled=True
    ).reshape(rows, width)


def on_device(a_rows, xa_panel, za_panel, send_order, recv_order, shift, resident):
    rows = a_rows.shape[0]
    columns = xa_panel.shape[1]
    group = lax.axis_size("wide")
    my_index = lax.axis_index("wide").astype(jnp.int32).reshape(1)
    share = rows // group
    half = rows // 2
    few, apart = phases_of(group)

    order, packing = send_order, share
    if share % 16:
        order = send_order.reshape(group, 2, share // 2).transpose(1, 0, 2).reshape(1, rows)
        packing = 0
    source, slot = recv_order // share, recv_order % share
    index = (slot // (share // 2)) * half + source * (share // 2) + slot % (share // 2)

    lead_panel, rest_panel = split_panels(my_index, xa_panel, za_panel)
    send_picks, a_copy = order_picks(order, a_rows, packing)
    lead_parts = exchange([lead_panel], few[0], "wide")
    for masks in few[1:]:
        lead_parts = exchange([after(join(lead_parts)[0], send_picks)], masks, "wide")
    rest_parts = exchange([after(rest_panel, lead_parts[0])], apart[0], "wide")

    lead_out = lead_products(my_index, a_copy, send_picks, lead_parts, offsets_of(few))
    lead_in = swap_rows(after(lead_out, *rest_parts), group)

    rest_parts = list(lax.optimization_barrier((*rest_parts, lead_out))[:-1])
    for masks in apart[1:-1]:
        rest_parts = exchange(join(rest_parts), masks, "wide")

    needed = columns + resident.shape[1]
    blocks_held = -(-needed // (PANEL * group))
    packed = leading_rows(index, lead_in, blocks_held * PANEL)
    leading_parts = [packed]
    for masks in few:
        leading_parts = exchange(join(leading_parts), masks, "wide")
    rest_parts = list(lax.optimization_barrier((*rest_parts, packed))[:-1])
    rest_parts = exchange(rest_parts, apart[-1], "wide")

    rest_out = rest_products(my_index, order, a_rows, rest_parts, offsets_of(apart), packing)
    rest_in = swap_rows(after(rest_out, *leading_parts), group)
    near, updated, pivots = updates(
        my_index,
        leading_parts,
        offsets_of(few),
        index,
        after(lead_in, rest_out),
        shift[None, :],
        resident,
        blocks_held,
        columns,
    )
    factored = formed_columns(index, rest_in, near)
    return (factored, updated, pivots[0])


def solution(mesh):
    placed = (
        P(("parts", "wide"), None),
        P(("parts", "wide"), None),
        P(("parts", "wide"), None),
        P(("parts", "wide"), None),
        P(("parts", "wide"), None),
        P("parts"),
        P(("parts", "wide"), None),
    )
    return jax.shard_map(
        on_device,
        mesh=mesh,
        in_specs=placed,
        out_specs=(P(("parts", "wide"), None), P(("parts", "wide"), None), P("parts")),
        check_vma=False,
    )
```

```python
import functools

import jax
import jax.numpy as jnp
from jax import lax
from jax.experimental import pallas as pl
from jax.experimental.pallas import tpu as pltpu
from jax.sharding import PartitionSpec as P

PANEL = 64
LANES = 128
A_BLOCK = 256
F32 = jnp.float32
BF16 = jnp.bfloat16
MIB = 1024 * 1024


def params(mebibytes=12):
    return pltpu.CompilerParams(vmem_limit_bytes=mebibytes * MIB)


def lane_ids(shape):
    return lax.broadcasted_iota(jnp.int32, shape, len(shape) - 1)


def split(x, count):
    terms = []
    for _ in range(count):
        term = x.astype(BF16)
        terms.append(term)
        x = x - term.astype(F32)
    return terms


def swap_halves(x):
    return pltpu.roll(x, LANES // 2, 1)


def as_column(index_row):
    return jnp.transpose(jnp.broadcast_to(index_row, (LANES, LANES)))


def picks_of(at, width):
    lanes = lane_ids(at.shape)
    return jnp.concatenate(
        [(at == lanes + column).astype(F32).astype(BF16) for column in range(0, width, LANES)], axis=1
    )


def one_hot(index_row, width):
    chunks = [
        picks_of(as_column(index_row[:, start : start + LANES]), width)
        for start in range(0, index_row.shape[1], LANES)
    ]
    return jnp.concatenate(chunks, axis=0) if len(chunks) > 1 else chunks[0]


def packed_order(share, half, slot):
    part = share // 2
    return (slot % share) // part * half + slot // share * part + slot % part


def fill_order(order_ref, at_ref, share):
    rows = order_ref.shape[1]
    height = 8
    for start in range(0, rows, LANES):
        column = as_column(order_ref[:, start : start + LANES])
        if not share:
            at_ref[start : start + LANES, :] = column
            continue
        for inner in range(0, LANES, height):
            place = packed_order(share, rows // 2, start + inner)
            at_ref[place : place + height, :] = column[inner : inner + height]


def after(x, *earlier):
    return lax.optimization_barrier((x, *earlier))[0]


def exchange(held, masks, axis):
    size = lax.axis_size(axis)
    combined = [0]
    for mask in masks:
        combined += [other ^ mask for other in combined]
    parts = list(held)
    for mask in combined[1:]:
        parts += [lax.ppermute(part, axis, [(i, i ^ mask) for i in range(size)]) for part in held]
    return parts


def offsets_of(phases):
    offsets = [0]
    for masks in phases:
        combined = [0]
        for mask in masks:
            combined += [other ^ mask for other in combined]
        offsets = [offset ^ mask for mask in combined for offset in offsets]
    return offsets


def join(parts):
    return [jnp.concatenate(parts, axis=0)]


def phases_of(size):
    bits = [1 << bit for bit in reversed(range(size.bit_length() - 1))]
    pairs = [bits[start : start + 2] for start in range(0, len(bits), 2)]
    singles = [bits[start : start + 2] for start in range(0, len(bits) - 2, 2)]
    return pairs, singles + [bits[-2:-1], bits[-1:]]


def picks_kernel(share, order_ref, a_hbm, picks_ref, copy_ref, at_ref, sem):
    copy = pltpu.make_async_copy(a_hbm, copy_ref, sem)
    copy.start()
    fill_order(order_ref, at_ref, share)
    rows, width = picks_ref.shape
    for start in range(0, rows, A_BLOCK):
        picks_ref[start : start + A_BLOCK, :] = picks_of(at_ref[start : start + A_BLOCK, :], width)
    copy.wait()


def order_picks(order, a_rows, share):
    rows, depth = a_rows.shape
    return pl.pallas_call(
        functools.partial(picks_kernel, share),
        in_specs=[pl.BlockSpec(memory_space=pltpu.VMEM), pl.BlockSpec(memory_space=pl.ANY)],
        out_specs=[pl.BlockSpec(memory_space=pltpu.VMEM)] * 2,
        out_shape=[jax.ShapeDtypeStruct((rows, rows), BF16), jax.ShapeDtypeStruct((rows, depth), BF16)],
        scratch_shapes=[pltpu.VMEM((rows, LANES), jnp.int32), pltpu.SemaphoreType.DMA],
        compiler_params=params(),
        cost_estimate=pl.CostEstimate(flops=4 * rows * rows, bytes_accessed=4 * rows * depth, transcendentals=0),
        name="order_picks",
    )(order, a_rows)


def panels_kernel(my_ref, xa_hbm, za_hbm, lead_ref, rest_ref, xa_ref, za_ref, sems):
    copies = [
        pltpu.make_async_copy(xa_hbm, xa_ref, sems.at[0]),
        pltpu.make_async_copy(za_hbm, za_ref, sems.at[1]),
    ]
    for copy in copies:
        copy.start()
    for copy in copies:
        copy.wait()
    lead_ref[0] = jnp.concatenate([xa_ref[:, :PANEL], za_ref[:, :PANEL]], axis=1)
    rest_ref[0, :, :LANES] = jnp.concatenate([xa_ref[:, PANEL:LANES], za_ref[:, PANEL:LANES]], axis=1)
    rest_ref[0, :, LANES : 2 * LANES] = xa_ref[:, LANES:]
    rest_ref[0, :, 2 * LANES :] = za_ref[:, LANES:]


def split_panels(my_index, xa_panel, za_panel):
    depth, columns = xa_panel.shape
    return pl.pallas_call(
        panels_kernel,
        in_specs=[pl.BlockSpec(memory_space=pltpu.SMEM)] + [pl.BlockSpec(memory_space=pl.ANY)] * 2,
        out_shape=[
            jax.ShapeDtypeStruct((1, depth, LANES), BF16),
            jax.ShapeDtypeStruct((1, depth, 2 * columns - LANES), BF16),
        ],
        scratch_shapes=[
            pltpu.VMEM((depth, columns), BF16),
            pltpu.VMEM((depth, columns), BF16),
            pltpu.SemaphoreType.DMA((2,)),
        ],
        compiler_params=params(60),
        name="split_panels",
    )(my_index, xa_panel, za_panel)


def assemble(my_index, offsets, parts, panel_ref):
    position = 0
    for part in parts:
        for number in range(part.shape[0]):
            depth = part.shape[1]
            start = pl.multiple_of((my_index ^ offsets[position]) * depth, depth)
            panel_ref[pl.ds(start, depth), :] = part[number]
            position += 1


def whole_sum(got):
    pair = got[:, :LANES]
    return (pair + swap_halves(pair)) + got[:, LANES:]


def lead_product_kernel(offsets, my_ref, a_ref, picks_ref, *refs):
    parts, (out_ref, panel_ref, terms_ref) = refs[:-3], refs[-3:]
    assemble(my_ref[0], offsets, parts, panel_ref)
    rows = a_ref.shape[0]
    for start in range(0, rows, A_BLOCK):
        both = jnp.dot(a_ref[start : start + A_BLOCK, :], panel_ref[...], preferred_element_type=F32)
        first, second, third = (term.astype(F32) for term in split(both * swap_halves(both), 3))
        near = lane_ids(both.shape) < PANEL
        terms_ref[start : start + A_BLOCK, :LANES] = jnp.where(near, first, second).astype(BF16)
        terms_ref[start : start + A_BLOCK, LANES:] = third.astype(BF16)
    half = rows // 2
    block = half // 2
    for start in range(0, half, block):
        low = jnp.dot(picks_ref[start : start + block, :], terms_ref[...], preferred_element_type=F32)
        high = jnp.dot(picks_ref[half + start : half + start + block, :], terms_ref[...], preferred_element_type=F32)
        low, high = whole_sum(low), whole_sum(high)
        out_ref[start : start + block, :] = jnp.where(lane_ids(low.shape) < PANEL, low, high)


def lead_products(my_index, a_rows, picks, parts, offsets):
    rows, depth = a_rows.shape
    return pl.pallas_call(
        functools.partial(lead_product_kernel, offsets),
        in_specs=[pl.BlockSpec(memory_space=pltpu.SMEM)] + [pl.BlockSpec(memory_space=pltpu.VMEM)] * (2 + len(parts)),
        out_specs=pl.BlockSpec(memory_space=pltpu.VMEM),
        out_shape=jax.ShapeDtypeStruct((rows // 2, LANES), F32),
        scratch_shapes=[pltpu.VMEM((depth, LANES), BF16), pltpu.VMEM((rows, 2 * LANES), BF16)],
        compiler_params=params(),
        cost_estimate=pl.CostEstimate(
            flops=2 * rows * (depth + 2 * rows) * LANES, bytes_accessed=2 * rows * depth, transcendentals=0
        ),
        name="lead_products",
    )(my_index, a_rows, picks, *parts)


BIAS = 128


def rest_product_kernel(offsets, share, my_ref, order_ref, a_hbm, *refs):
    parts, (out_ref, a_ref, at_ref, panel_ref, terms_ref, sems, part_sems) = refs[:-7], refs[-7:]
    rows = a_ref.shape[0]
    block = A_BLOCK
    starts = range(0, rows, block)
    copies = [
        pltpu.make_async_copy(a_hbm.at[pl.ds(start, block), :], a_ref.at[pl.ds(start, block), :], sems.at[i])
        for i, start in enumerate(starts)
    ]
    fetches = []
    for part in parts:
        for number in range(part.shape[0]):
            depth = part.shape[1]
            position = len(fetches)
            place = pl.multiple_of((my_ref[0] ^ offsets[position]) * depth, depth)
            fetches.append(
                pltpu.make_async_copy(part.at[number], panel_ref.at[pl.ds(place, depth), :], part_sems.at[position])
            )
    for copy in fetches + copies[:2]:
        copy.start()
    fill_order(order_ref, at_ref, share)
    for copy in fetches:
        copy.wait()
    for i, start in enumerate(starts):
        copies[i].wait()
        if i + 2 < len(copies):
            copies[i + 2].start()
        both = jnp.dot(a_ref[start : start + block, :], panel_ref[...], preferred_element_type=F32)
        near = both[:, :LANES]
        near = near * swap_halves(near)
        far = both[:, LANES : 2 * LANES] * both[:, 2 * LANES :]
        largest = jnp.max(jnp.maximum(jnp.abs(near), jnp.abs(far)), axis=1, keepdims=True)
        largest = jnp.maximum(largest, 1e-30)
        exponent = jnp.floor(jnp.log2(largest)) + 1.0
        far = jnp.floor(far * jnp.exp2(15.0 - exponent) + 0.5)
        far = jnp.minimum(jnp.maximum(far, -32767.0), 32767.0)
        near = jnp.floor(near * jnp.exp2(23.0 - exponent) + 0.5)
        near = jnp.minimum(jnp.maximum(near, -8388607.0), 8388607.0)
        far_top = jnp.floor(far * (1 / 256))
        near_top = jnp.floor(near * (1 / 65536))
        near = near - near_top * 65536.0
        near_middle = jnp.floor(near * (1 / 256))
        low_lanes = lane_ids(near.shape) < PANEL
        rows_here = slice(start, start + block)
        terms_ref[rows_here, :LANES] = far_top.astype(BF16)
        terms_ref[rows_here, LANES : 2 * LANES] = (far - far_top * 256.0).astype(BF16)
        terms_ref[rows_here, 2 * LANES : 3 * LANES] = jnp.where(low_lanes, near_top, near_middle).astype(BF16)
        terms_ref[rows_here, 3 * LANES :] = jnp.where(low_lanes, near - near_middle * 256.0, exponent).astype(BF16)


    def coded(start, size):
        picks = picks_of(at_ref[start : start + size, :], rows)
        got = jnp.dot(picks, terms_ref[...], preferred_element_type=F32)
        far = got[:, :LANES] * 256.0 + got[:, LANES : 2 * LANES]
        tops, lows = got[:, 2 * LANES : 3 * LANES], got[:, 3 * LANES :]
        low_lanes = lane_ids(tops.shape) < PANEL
        tops = tops * jnp.where(low_lanes, 65536.0, 256.0)
        swapped = swap_halves(lows)
        near = tops + swap_halves(tops) + jnp.where(low_lanes, lows, swapped)
        exponent = jnp.where(low_lanes, swapped, lows)
        near = near.astype(jnp.int32) * 256 + (exponent.astype(jnp.int32) + BIAS)
        return far.astype(jnp.int32), near

    half = rows // 2
    block = half // 2
    for start in range(0, half, block):
        far_low, near_low = coded(start, block)
        far_high, near_high = coded(half + start, block)
        out_ref[start : start + block, :LANES] = far_low * 65536 + (far_high & 65535)
        out_ref[start : start + block, LANES:] = jnp.where(lane_ids(near_low.shape) < PANEL, near_low, near_high)


def rest_products(my_index, order, a_rows, parts, offsets, share):
    rows, depth = a_rows.shape
    return pl.pallas_call(
        functools.partial(rest_product_kernel, offsets, share),
        in_specs=[
            pl.BlockSpec(memory_space=pltpu.SMEM),
            pl.BlockSpec(memory_space=pltpu.VMEM),
            pl.BlockSpec(memory_space=pl.ANY),
        ]
        + [pl.BlockSpec(memory_space=pl.ANY)] * len(parts),
        out_specs=pl.BlockSpec(memory_space=pltpu.VMEM),
        out_shape=jax.ShapeDtypeStruct((rows // 2, 2 * LANES), jnp.int32),
        scratch_shapes=[
            pltpu.VMEM((rows, depth), BF16),
            pltpu.VMEM((rows, LANES), jnp.int32),
            pltpu.VMEM((depth, 3 * LANES), BF16),
            pltpu.VMEM((rows, 4 * LANES), BF16),
            pltpu.SemaphoreType.DMA((rows // A_BLOCK,)),
            pltpu.SemaphoreType.DMA((len(offsets),)),
        ],
        compiler_params=params(60),
        cost_estimate=pl.CostEstimate(
            flops=2 * rows * (3 * depth + 4 * rows) * LANES, bytes_accessed=2 * rows * depth, transcendentals=0
        ),
        name="rest_products",
    )(my_index, order, a_rows, *parts)


def packed_terms(x, terms_ref, start):
    half = x.shape[0]
    first, second, third = (term.astype(F32) for term in split(x, 3))
    near = lane_ids(x.shape) < PANEL
    other = swap_halves(third)
    terms_ref[:half, start : start + LANES] = jnp.where(near, first, swap_halves(second)).astype(BF16)
    terms_ref[half:, start : start + LANES] = jnp.where(near, swap_halves(first), second).astype(BF16)
    terms_ref[:half, start + LANES : start + 2 * LANES] = jnp.where(near, third, other).astype(BF16)
    terms_ref[half:, start + LANES : start + 2 * LANES] = jnp.where(near, other, third).astype(BF16)


def leading_kernel(held, index_ref, arrived_ref, out_ref, terms_ref):
    packed_terms(arrived_ref[...], terms_ref, 0)
    width = -(-held // LANES) * LANES
    picks = one_hot(index_ref[:, :width], terms_ref.shape[0])
    got = whole_sum(jnp.dot(picks, terms_ref[...], preferred_element_type=F32))
    first, second = got[: held // 2], got[held // 2 : held]
    out_ref[0] = jnp.where(lane_ids(first.shape) < PANEL, first, second)


def leading_rows(index, arrived, held):
    rows = index.shape[1]
    return pl.pallas_call(
        functools.partial(leading_kernel, held),
        in_specs=[pl.BlockSpec(memory_space=pltpu.VMEM)] * 2,
        out_specs=pl.BlockSpec(memory_space=pltpu.VMEM),
        out_shape=jax.ShapeDtypeStruct((1, held // 2, LANES), F32),
        scratch_shapes=[pltpu.VMEM((rows, 2 * LANES), BF16)],
        compiler_params=params(),
        cost_estimate=pl.CostEstimate(
            flops=4 * held * rows * LANES, bytes_accessed=2 * rows * LANES, transcendentals=0
        ),
        name="leading_rows",
    )(index, arrived)


def eliminate(block, shift_row):
    rows = lax.broadcasted_iota(jnp.int32, (PANEL, PANEL), 0)
    columns = lax.broadcasted_iota(jnp.int32, (PANEL, PANEL), 1)
    flipped = jnp.transpose(block)
    mirrored = jnp.where(rows >= columns, block, flipped)
    diagonal = shift_row + jnp.sum(jnp.abs(mirrored), axis=0, keepdims=True)
    unit = (rows == columns).astype(F32)
    work = jnp.where(rows == columns, diagonal, mirrored)
    work = jnp.concatenate([work, unit], axis=1)
    height = 8
    groups = [work[start : start + height] for start in range(0, PANEL, height)]
    sublanes = lax.broadcasted_iota(jnp.int32, (height, LANES), 0)
    scaled_rows = []
    for k in range(PANEL):
        home, offset = divmod(k, height)
        row = groups[home][offset : offset + 1, :]
        row = row / row[:, k : k + 1]
        scaled_rows.append(row)
        for g in range(home, PANEL // height):
            column = jnp.broadcast_to(groups[g][:, k : k + 1], (height, LANES))
            if g == home:
                column = jnp.where(sublanes > offset, column, 0.0)
            groups[g] = groups[g] - column * row
    final = jnp.concatenate(groups, axis=0)
    scaled = jnp.concatenate(scaled_rows, axis=0)
    upper = jnp.where(columns >= rows, scaled[:, :PANEL], 0.0)
    pivots = jnp.sum(jnp.where(rows == columns, final[:, :PANEL], 0.0), axis=0, keepdims=True)
    return upper, final[:, PANEL:], pivots


def exact(lhs, rhs, dims):
    return lax.dot_general(lhs, rhs, (dims, ((), ())), precision=lax.Precision.HIGHEST, preferred_element_type=F32)


def update_kernel(offsets, blocks_held, columns, my_ref, index_ref, arrived_ref, shift_ref, resident_hbm, *refs):
    parts = refs[:-12]
    near_hbm, far_hbm, pivots_ref, leading_ref, tail_ref, resident_ref, terms_ref, lead_ref = refs[-12:-4]
    near_ref, far_ref, sem, sems = refs[-4:]
    fetch = pltpu.make_async_copy(resident_hbm, resident_ref, sem)
    fetch.start()
    my_index = my_ref[0]
    size = len(offsets)
    position = 0
    packed = blocks_held * PANEL // 2
    part_rows = PANEL // 2
    for part in parts:
        for number in range(part.shape[0]):
            owner = my_index ^ offsets[position]
            for start in range(0, blocks_held * PANEL, part_rows):
                held, inner = divmod(start, PANEL)
                if start < packed:
                    rows = part[number, start : start + part_rows, :PANEL]
                else:
                    rows = part[number, start - packed : start - packed + part_rows, PANEL:]
                target = pl.multiple_of((held * size + owner) * PANEL + inner, part_rows)
                leading_ref[pl.ds(target, part_rows), :] = rows
            position += 1
    upper, inverse, pivots = eliminate(leading_ref[:PANEL, :], shift_ref[...])
    pivots_ref[...] = pivots
    lower = jnp.transpose(upper)
    needed = tail_ref.shape[1]
    tail = exact(inverse, leading_ref[:needed, :], ((1,), (1,)))
    high, low = split(tail, 2)
    tail_ref[0:PANEL, :] = high
    tail_ref[PANEL : 2 * PANEL, :] = high
    tail_ref[2 * PANEL : 3 * PANEL, :] = low
    tail_ref[3 * PANEL :, :] = low

    block = A_BLOCK
    packed_terms(arrived_ref[...], terms_ref, 0)
    for start in range(0, lead_ref.shape[0], block):
        picks = one_hot(index_ref[:, start : start + block], lead_ref.shape[0])
        got = jnp.dot(picks, terms_ref[...], preferred_element_type=F32)
        lead_ref[start : start + block, :] = whole_sum(got)[:, :PANEL]
    fetch.wait()
    stores = []
    for number, start in enumerate(range(0, lead_ref.shape[0], block)):
        rows_here = slice(start, start + block)
        panel = exact(lead_ref[rows_here, :], inverse, ((1,), (1,))) / pivots
        shown = used = panel
        if start == 0:
            row_ids = lax.broadcasted_iota(jnp.int32, panel.shape, 0)
            top = jnp.logical_and(my_index == 0, row_ids < PANEL)
            used = jnp.where(top, 0.0, panel)
            filled = jnp.concatenate([lower, jnp.zeros((block - PANEL, PANEL), F32)], axis=0)
            shown = jnp.where(top, filled, panel)
        high, low = (term.astype(F32) for term in split(used, 2))
        pair = jnp.concatenate([high, low], axis=1).astype(BF16)
        factors = jnp.concatenate([pair, pair], axis=1)
        update = jnp.dot(factors, tail_ref[...], preferred_element_type=F32)
        shown = jnp.concatenate([shown, jnp.zeros_like(shown)], axis=1)
        near_ref[rows_here, :LANES] = jnp.where(lane_ids(shown.shape) < PANEL, shown, -update[:, :LANES])
        near_ref[rows_here, LANES:] = -update[:, LANES:columns]
        far_ref[rows_here, :] = (resident_ref[rows_here, :].astype(F32) - update[:, columns:]).astype(BF16)
        for which, (source, target) in enumerate(((near_ref, near_hbm), (far_ref, far_hbm))):
            store = pltpu.make_async_copy(
                source.at[pl.ds(start, block), :], target.at[pl.ds(start, block), :], sems.at[which, number]
            )
            store.start()
            stores.append(store)
    for store in stores:
        store.wait()


def updates(my_index, parts, offsets, index, arrived, shift, resident, blocks_held, columns):
    rows, width = resident.shape
    needed = columns + width
    held_rows = len(offsets) * blocks_held * PANEL
    vmem = pl.BlockSpec(memory_space=pltpu.VMEM)
    anywhere = pl.BlockSpec(memory_space=pl.ANY)
    return pl.pallas_call(
        functools.partial(update_kernel, offsets, blocks_held, columns),
        in_specs=[pl.BlockSpec(memory_space=pltpu.SMEM), vmem, vmem, vmem, anywhere] + [vmem] * len(parts),
        out_specs=[anywhere, anywhere, vmem],
        out_shape=[
            jax.ShapeDtypeStruct((rows, columns), F32),
            jax.ShapeDtypeStruct((rows, width), BF16),
            jax.ShapeDtypeStruct((1, PANEL), F32),
        ],
        scratch_shapes=[
            pltpu.VMEM((held_rows, PANEL), F32),
            pltpu.VMEM((4 * PANEL, needed), BF16),
            pltpu.VMEM((rows, width), BF16),
            pltpu.VMEM((rows, 2 * LANES), BF16),
            pltpu.VMEM((rows, PANEL), F32),
            pltpu.VMEM((rows, columns), F32),
            pltpu.VMEM((rows, width), BF16),
            pltpu.SemaphoreType.DMA,
            pltpu.SemaphoreType.DMA((2, rows // A_BLOCK)),
        ],
        compiler_params=params(60),
        cost_estimate=pl.CostEstimate(
            flops=2 * rows * needed * 4 * PANEL, bytes_accessed=4 * rows * (columns + width), transcendentals=0
        ),
        name="factor_and_update",
    )(my_index, index, arrived, shift, resident, *parts)


def formed_kernel(index_ref, arrived_ref, near_ref, out_ref, terms_ref):
    half = arrived_ref.shape[0]

    @pl.when(pl.program_id(0) == 0)
    def _():
        words = arrived_ref[:, LANES:]
        low_lanes = lane_ids(words.shape) < PANEL
        exponent = ((words & 255) - BIAS).astype(F32)
        other = swap_halves(exponent)
        packed_terms((words >> 8).astype(F32) * jnp.exp2(exponent - 23.0), terms_ref, 2 * LANES)
        words = arrived_ref[:, :LANES]
        low = (words >> 16).astype(F32) * jnp.exp2(jnp.where(low_lanes, exponent, other) - 15.0)
        high = ((words << 16) >> 16).astype(F32) * jnp.exp2(jnp.where(low_lanes, other, exponent) - 15.0)
        for side, values in enumerate((low, high)):
            first, second = split(values, 2)
            terms_ref[side * half : (side + 1) * half, :LANES] = first
            terms_ref[side * half : (side + 1) * half, LANES : 2 * LANES] = second

    picks = one_hot(index_ref[...], terms_ref.shape[0])
    got = jnp.dot(picks, terms_ref[...], preferred_element_type=F32)
    narrow = whole_sum(got[:, 2 * LANES :])
    held = near_ref[:, :LANES]
    out_ref[:, :LANES] = jnp.where(lane_ids(held.shape) < PANEL, held, narrow + held)
    out_ref[:, LANES:] = (got[:, :LANES] + got[:, LANES : 2 * LANES]) + near_ref[:, LANES:]


def formed_columns(index, arrived, near):
    rows, columns = near.shape
    half, width = arrived.shape
    steps = 5
    block = rows // steps
    return pl.pallas_call(
        formed_kernel,
        grid=(steps,),
        in_specs=[
            pl.BlockSpec((1, block), lambda i: (0, i)),
            pl.BlockSpec((half, width), lambda i: (0, 0)),
            pl.BlockSpec((block, columns), lambda i: (i, 0)),
        ],
        out_specs=pl.BlockSpec((block, columns), lambda i: (i, 0)),
        out_shape=jax.ShapeDtypeStruct((rows, columns), F32),
        scratch_shapes=[pltpu.VMEM((rows, 4 * LANES), BF16)],
        compiler_params=params(60),
        cost_estimate=pl.CostEstimate(
            flops=8 * rows * rows * LANES, bytes_accessed=8 * rows * columns, transcendentals=0
        ),
        name="formed_columns",
    )(index, arrived, near)


def swap_rows(x, group):
    rows, width = x.shape
    return lax.all_to_all(
        x.reshape(group, rows // group, width), "wide", split_axis=0, concat_axis=0, tiled=True
    ).reshape(rows, width)


def on_device(a_rows, xa_panel, za_panel, send_order, recv_order, shift, resident):
    rows = a_rows.shape[0]
    columns = xa_panel.shape[1]
    group = lax.axis_size("wide")
    my_index = lax.axis_index("wide").astype(jnp.int32).reshape(1)
    share = rows // group
    half = rows // 2
    few, apart = phases_of(group)

    order, packing = send_order, share
    if share % 16:
        order = send_order.reshape(group, 2, share // 2).transpose(1, 0, 2).reshape(1, rows)
        packing = 0
    source, slot = recv_order // share, recv_order % share
    index = (slot // (share // 2)) * half + source * (share // 2) + slot % (share // 2)

    lead_panel, rest_panel = split_panels(my_index, xa_panel, za_panel)
    send_picks, a_copy = order_picks(order, a_rows, packing)
    lead_parts = [lead_panel]
    for masks in few:
        lead_parts = exchange(join(lead_parts), masks, "wide")
    rest_parts = [rest_panel]
    for masks in apart[:-1]:
        rest_parts = exchange(join(rest_parts), masks, "wide")
    rest_parts = exchange(rest_parts, apart[-1], "wide")

    lead_out = lead_products(my_index, a_copy, send_picks, lead_parts, offsets_of(few))
    lead_in = swap_rows(lead_out, group)
    rest_out = rest_products(my_index, order, a_rows, rest_parts, offsets_of(apart), packing)

    needed = columns + resident.shape[1]
    blocks_held = -(-needed // (PANEL * group))
    packed = leading_rows(index, after(lead_in, rest_out), blocks_held * PANEL)
    leading_parts = [packed]
    for masks in few:
        leading_parts = exchange(join(leading_parts), masks, "wide")
    rest_in = swap_rows(after(rest_out, *leading_parts), group)
    near, updated, pivots = updates(
        my_index,
        leading_parts,
        offsets_of(few),
        index,
        lead_in,
        shift[None, :],
        resident,
        blocks_held,
        columns,
    )
    factored = formed_columns(index, rest_in, near)
    return (factored, updated, pivots[0])


def solution(mesh):
    placed = (
        P(("parts", "wide"), None),
        P(("parts", "wide"), None),
        P(("parts", "wide"), None),
        P(("parts", "wide"), None),
        P(("parts", "wide"), None),
        P("parts"),
        P(("parts", "wide"), None),
    )
    return jax.shard_map(
        on_device,
        mesh=mesh,
        in_specs=placed,
        out_specs=(P(("parts", "wide"), None), P(("parts", "wide"), None), P("parts")),
        check_vma=False,
    )
```

```python
import functools

import jax
import jax.numpy as jnp
from jax import lax
from jax.experimental import pallas as pl
from jax.experimental.pallas import tpu as pltpu
from jax.sharding import PartitionSpec as P

PANEL = 64
LANES = 128
A_BLOCK = 256
F32 = jnp.float32
BF16 = jnp.bfloat16
MIB = 1024 * 1024


def params(mebibytes=12):
    return pltpu.CompilerParams(vmem_limit_bytes=mebibytes * MIB)


def lane_ids(shape):
    return lax.broadcasted_iota(jnp.int32, shape, len(shape) - 1)


def split(x, count):
    terms = []
    for _ in range(count):
        term = x.astype(BF16)
        terms.append(term)
        x = x - term.astype(F32)
    return terms


def swap_halves(x):
    return pltpu.roll(x, LANES // 2, 1)


def as_column(index_row):
    return jnp.transpose(jnp.broadcast_to(index_row, (LANES, LANES)))


def picks_of(at, width):
    lanes = lane_ids(at.shape)
    return jnp.concatenate(
        [(at == lanes + column).astype(F32).astype(BF16) for column in range(0, width, LANES)], axis=1
    )


def one_hot(index_row, width):
    chunks = [
        picks_of(as_column(index_row[:, start : start + LANES]), width)
        for start in range(0, index_row.shape[1], LANES)
    ]
    return jnp.concatenate(chunks, axis=0) if len(chunks) > 1 else chunks[0]


def packed_order(share, half, slot):
    part = share // 2
    return (slot % share) // part * half + slot // share * part + slot % part


def fill_order(order_ref, at_ref, share):
    rows = order_ref.shape[1]
    height = 8
    for start in range(0, rows, LANES):
        column = as_column(order_ref[:, start : start + LANES])
        if not share:
            at_ref[start : start + LANES, :] = column
            continue
        for inner in range(0, LANES, height):
            place = packed_order(share, rows // 2, start + inner)
            at_ref[place : place + height, :] = column[inner : inner + height]


def exchange(held, masks, axis):
    size = lax.axis_size(axis)
    combined = [0]
    for mask in masks:
        combined += [other ^ mask for other in combined]
    parts = list(held)
    for mask in combined[1:]:
        parts += [lax.ppermute(part, axis, [(i, i ^ mask) for i in range(size)]) for part in held]
    return parts


def offsets_of(phases):
    offsets = [0]
    for masks in phases:
        combined = [0]
        for mask in masks:
            combined += [other ^ mask for other in combined]
        offsets = [offset ^ mask for mask in combined for offset in offsets]
    return offsets


def join(parts):
    return [jnp.concatenate(parts, axis=0)]


def phases_of(size):
    bits = [1 << bit for bit in reversed(range(size.bit_length() - 1))]
    return [bits[start : start + 2] for start in range(0, len(bits), 2)], [[bit] for bit in bits]


def tied(parts, *earlier):
    return list(lax.optimization_barrier((*parts, *earlier))[: len(parts)])


def picks_kernel(share, order_ref, a_hbm, picks_ref, copy_ref, at_ref, sem):
    copy = pltpu.make_async_copy(a_hbm, copy_ref, sem)
    copy.start()
    fill_order(order_ref, at_ref, share)
    rows, width = picks_ref.shape
    for start in range(0, rows, A_BLOCK):
        picks_ref[start : start + A_BLOCK, :] = picks_of(at_ref[start : start + A_BLOCK, :], width)
    copy.wait()


def order_picks(order, a_rows, share):
    rows, depth = a_rows.shape
    return pl.pallas_call(
        functools.partial(picks_kernel, share),
        in_specs=[pl.BlockSpec(memory_space=pltpu.VMEM), pl.BlockSpec(memory_space=pl.ANY)],
        out_specs=[pl.BlockSpec(memory_space=pltpu.VMEM)] * 2,
        out_shape=[jax.ShapeDtypeStruct((rows, rows), BF16), jax.ShapeDtypeStruct((rows, depth), BF16)],
        scratch_shapes=[pltpu.VMEM((rows, LANES), jnp.int32), pltpu.SemaphoreType.DMA],
        compiler_params=params(),
        cost_estimate=pl.CostEstimate(flops=4 * rows * rows, bytes_accessed=4 * rows * depth, transcendentals=0),
        name="order_picks",
    )(order, a_rows)


def panels_kernel(my_ref, xa_hbm, za_hbm, lead_ref, rest_ref, xa_ref, za_ref, sems):
    copies = [
        pltpu.make_async_copy(xa_hbm, xa_ref, sems.at[0]),
        pltpu.make_async_copy(za_hbm, za_ref, sems.at[1]),
    ]
    for copy in copies:
        copy.start()
    for copy in copies:
        copy.wait()
    lead_ref[0] = jnp.concatenate([xa_ref[:, :PANEL], za_ref[:, :PANEL]], axis=1)
    rest_ref[0, :, :LANES] = jnp.concatenate([xa_ref[:, PANEL:LANES], za_ref[:, PANEL:LANES]], axis=1)
    rest_ref[0, :, LANES : 2 * LANES] = xa_ref[:, LANES:]
    rest_ref[0, :, 2 * LANES :] = za_ref[:, LANES:]


def split_panels(my_index, xa_panel, za_panel):
    depth, columns = xa_panel.shape
    return pl.pallas_call(
        panels_kernel,
        in_specs=[pl.BlockSpec(memory_space=pltpu.SMEM)] + [pl.BlockSpec(memory_space=pl.ANY)] * 2,
        out_shape=[
            jax.ShapeDtypeStruct((1, depth, LANES), BF16),
            jax.ShapeDtypeStruct((1, depth, 2 * columns - LANES), BF16),
        ],
        scratch_shapes=[
            pltpu.VMEM((depth, columns), BF16),
            pltpu.VMEM((depth, columns), BF16),
            pltpu.SemaphoreType.DMA((2,)),
        ],
        compiler_params=params(60),
        name="split_panels",
    )(my_index, xa_panel, za_panel)


def assemble(my_index, offsets, parts, panel_ref):
    position = 0
    for part in parts:
        for number in range(part.shape[0]):
            depth = part.shape[1]
            start = pl.multiple_of((my_index ^ offsets[position]) * depth, depth)
            panel_ref[pl.ds(start, depth), :] = part[number]
            position += 1


def whole_sum(got):
    pair = got[:, :LANES]
    return (pair + swap_halves(pair)) + got[:, LANES:]


def lead_product_kernel(offsets, my_ref, a_ref, picks_ref, *refs):
    parts, (out_ref, panel_ref, terms_ref) = refs[:-3], refs[-3:]
    assemble(my_ref[0], offsets, parts, panel_ref)
    rows = a_ref.shape[0]
    for start in range(0, rows, A_BLOCK):
        both = jnp.dot(a_ref[start : start + A_BLOCK, :], panel_ref[...], preferred_element_type=F32)
        first, second, third = (term.astype(F32) for term in split(both * swap_halves(both), 3))
        near = lane_ids(both.shape) < PANEL
        terms_ref[start : start + A_BLOCK, :LANES] = jnp.where(near, first, second).astype(BF16)
        terms_ref[start : start + A_BLOCK, LANES:] = third.astype(BF16)
    half = rows // 2
    block = half // 2
    for start in range(0, half, block):
        low = jnp.dot(picks_ref[start : start + block, :], terms_ref[...], preferred_element_type=F32)
        high = jnp.dot(picks_ref[half + start : half + start + block, :], terms_ref[...], preferred_element_type=F32)
        low, high = whole_sum(low), whole_sum(high)
        out_ref[start : start + block, :] = jnp.where(lane_ids(low.shape) < PANEL, low, high)


def lead_products(my_index, a_rows, picks, parts, offsets):
    rows, depth = a_rows.shape
    return pl.pallas_call(
        functools.partial(lead_product_kernel, offsets),
        in_specs=[pl.BlockSpec(memory_space=pltpu.SMEM)] + [pl.BlockSpec(memory_space=pltpu.VMEM)] * (2 + len(parts)),
        out_specs=pl.BlockSpec(memory_space=pltpu.VMEM),
        out_shape=jax.ShapeDtypeStruct((rows // 2, LANES), F32),
        scratch_shapes=[pltpu.VMEM((depth, LANES), BF16), pltpu.VMEM((rows, 2 * LANES), BF16)],
        compiler_params=params(),
        cost_estimate=pl.CostEstimate(
            flops=2 * rows * (depth + 2 * rows) * LANES, bytes_accessed=2 * rows * depth, transcendentals=0
        ),
        name="lead_products",
    )(my_index, a_rows, picks, *parts)


BIAS = 128


def rest_product_kernel(offsets, share, my_ref, order_ref, a_hbm, *refs):
    parts, (out_ref, a_ref, at_ref, picks_ref, panel_ref, terms_ref, sems, part_sems) = refs[:-8], refs[-8:]
    rows = a_ref.shape[0]
    block = A_BLOCK
    starts = range(0, rows, block)
    copies = [
        pltpu.make_async_copy(a_hbm.at[pl.ds(start, block), :], a_ref.at[pl.ds(start, block), :], sems.at[i])
        for i, start in enumerate(starts)
    ]
    fetches = []
    for part in parts:
        for number in range(part.shape[0]):
            depth = part.shape[1]
            position = len(fetches)
            place = pl.multiple_of((my_ref[0] ^ offsets[position]) * depth, depth)
            fetches.append(
                pltpu.make_async_copy(part.at[number], panel_ref.at[pl.ds(place, depth), :], part_sems.at[position])
            )
    for copy in fetches + copies[:2]:
        copy.start()
    fill_order(order_ref, at_ref, share)
    for start in starts:
        picks_ref[start : start + block, :] = picks_of(at_ref[start : start + block, :], rows)
    for copy in fetches:
        copy.wait()

    def product(i):
        copies[i].wait()
        if i + 2 < len(copies):
            copies[i + 2].start()
        return jnp.dot(a_ref[starts[i] : starts[i] + block, :], panel_ref[...], preferred_element_type=F32)

    later = product(0)
    for i, start in enumerate(starts):
        both = later
        if i + 1 < len(starts):
            later = product(i + 1)
        near = both[:, :LANES]
        near = near * swap_halves(near)
        far = both[:, LANES : 2 * LANES] * both[:, 2 * LANES :]
        largest = jnp.max(jnp.maximum(jnp.abs(near), jnp.abs(far)), axis=1, keepdims=True)
        largest = jnp.maximum(largest, 1e-30)
        exponent = jnp.floor(jnp.log2(largest)) + 1.0
        far = jnp.floor(far * jnp.exp2(15.0 - exponent) + 0.5)
        far = jnp.minimum(jnp.maximum(far, -32767.0), 32767.0)
        near = jnp.floor(near * jnp.exp2(23.0 - exponent) + 0.5)
        near = jnp.minimum(jnp.maximum(near, -8388607.0), 8388607.0)
        far_top = jnp.floor(far * (1 / 256))
        near_top = jnp.floor(near * (1 / 65536))
        near = near - near_top * 65536.0
        near_middle = jnp.floor(near * (1 / 256))
        low_lanes = lane_ids(near.shape) < PANEL
        rows_here = slice(start, start + block)
        terms_ref[rows_here, :LANES] = far_top.astype(BF16)
        terms_ref[rows_here, LANES : 2 * LANES] = (far - far_top * 256.0).astype(BF16)
        terms_ref[rows_here, 2 * LANES : 3 * LANES] = jnp.where(low_lanes, near_top, near_middle).astype(BF16)
        terms_ref[rows_here, 3 * LANES :] = jnp.where(low_lanes, near - near_middle * 256.0, exponent).astype(BF16)


    def coded(start, size):
        got = jnp.dot(picks_ref[start : start + size, :], terms_ref[...], preferred_element_type=F32)
        far = got[:, :LANES] * 256.0 + got[:, LANES : 2 * LANES]
        tops, lows = got[:, 2 * LANES : 3 * LANES], got[:, 3 * LANES :]
        low_lanes = lane_ids(tops.shape) < PANEL
        tops = tops * jnp.where(low_lanes, 65536.0, 256.0)
        swapped = swap_halves(lows)
        near = tops + swap_halves(tops) + jnp.where(low_lanes, lows, swapped)
        exponent = jnp.where(low_lanes, swapped, lows)
        near = near.astype(jnp.int32) * 256 + (exponent.astype(jnp.int32) + BIAS)
        return far.astype(jnp.int32), near

    half = rows // 2
    block = half // 2
    for start in range(0, half, block):
        far_low, near_low = coded(start, block)
        far_high, near_high = coded(half + start, block)
        out_ref[start : start + block, :LANES] = far_low * 65536 + (far_high & 65535)
        out_ref[start : start + block, LANES:] = jnp.where(lane_ids(near_low.shape) < PANEL, near_low, near_high)


def rest_products(my_index, order, a_rows, parts, offsets, share):
    rows, depth = a_rows.shape
    return pl.pallas_call(
        functools.partial(rest_product_kernel, offsets, share),
        in_specs=[
            pl.BlockSpec(memory_space=pltpu.SMEM),
            pl.BlockSpec(memory_space=pltpu.VMEM),
            pl.BlockSpec(memory_space=pl.ANY),
        ]
        + [pl.BlockSpec(memory_space=pl.ANY)] * len(parts),
        out_specs=pl.BlockSpec(memory_space=pltpu.VMEM),
        out_shape=jax.ShapeDtypeStruct((rows // 2, 2 * LANES), jnp.int32),
        scratch_shapes=[
            pltpu.VMEM((rows, depth), BF16),
            pltpu.VMEM((rows, LANES), jnp.int32),
            pltpu.VMEM((rows, rows), BF16),
            pltpu.VMEM((depth, 3 * LANES), BF16),
            pltpu.VMEM((rows, 4 * LANES), BF16),
            pltpu.SemaphoreType.DMA((rows // A_BLOCK,)),
            pltpu.SemaphoreType.DMA((len(offsets),)),
        ],
        compiler_params=params(60),
        cost_estimate=pl.CostEstimate(
            flops=2 * rows * (3 * depth + 4 * rows) * LANES, bytes_accessed=2 * rows * depth, transcendentals=0
        ),
        name="rest_products",
    )(my_index, order, a_rows, *parts)


def packed_terms(x, terms_ref, start):
    half = x.shape[0]
    first, second, third = (term.astype(F32) for term in split(x, 3))
    near = lane_ids(x.shape) < PANEL
    other = swap_halves(third)
    terms_ref[:half, start : start + LANES] = jnp.where(near, first, swap_halves(second)).astype(BF16)
    terms_ref[half:, start : start + LANES] = jnp.where(near, swap_halves(first), second).astype(BF16)
    terms_ref[:half, start + LANES : start + 2 * LANES] = jnp.where(near, third, other).astype(BF16)
    terms_ref[half:, start + LANES : start + 2 * LANES] = jnp.where(near, other, third).astype(BF16)


def leading_kernel(held, index_ref, arrived_ref, out_ref, terms_ref):
    packed_terms(arrived_ref[...], terms_ref, 0)
    width = -(-held // LANES) * LANES
    picks = one_hot(index_ref[:, :width], terms_ref.shape[0])
    got = whole_sum(jnp.dot(picks, terms_ref[...], preferred_element_type=F32))
    first, second = got[: held // 2], got[held // 2 : held]
    out_ref[0] = jnp.where(lane_ids(first.shape) < PANEL, first, second)


def leading_rows(index, arrived, held):
    rows = index.shape[1]
    return pl.pallas_call(
        functools.partial(leading_kernel, held),
        in_specs=[pl.BlockSpec(memory_space=pltpu.VMEM)] * 2,
        out_specs=pl.BlockSpec(memory_space=pltpu.VMEM),
        out_shape=jax.ShapeDtypeStruct((1, held // 2, LANES), F32),
        scratch_shapes=[pltpu.VMEM((rows, 2 * LANES), BF16)],
        compiler_params=params(),
        cost_estimate=pl.CostEstimate(
            flops=4 * held * rows * LANES, bytes_accessed=2 * rows * LANES, transcendentals=0
        ),
        name="leading_rows",
    )(index, arrived)


def eliminate(block, shift_row):
    rows = lax.broadcasted_iota(jnp.int32, (PANEL, PANEL), 0)
    columns = lax.broadcasted_iota(jnp.int32, (PANEL, PANEL), 1)
    flipped = jnp.transpose(block)
    mirrored = jnp.where(rows >= columns, block, flipped)
    diagonal = shift_row + jnp.sum(jnp.abs(mirrored), axis=0, keepdims=True)
    unit = (rows == columns).astype(F32)
    work = jnp.where(rows == columns, diagonal, mirrored)
    work = jnp.concatenate([work, unit], axis=1)
    height = 8
    groups = [work[start : start + height] for start in range(0, PANEL, height)]
    sublanes = lax.broadcasted_iota(jnp.int32, (height, LANES), 0)
    scaled_rows = []
    for k in range(PANEL):
        home, offset = divmod(k, height)
        row = groups[home][offset : offset + 1, :]
        row = row / row[:, k : k + 1]
        scaled_rows.append(row)
        for g in range(home, PANEL // height):
            column = jnp.broadcast_to(groups[g][:, k : k + 1], (height, LANES))
            if g == home:
                column = jnp.where(sublanes > offset, column, 0.0)
            groups[g] = groups[g] - column * row
    final = jnp.concatenate(groups, axis=0)
    scaled = jnp.concatenate(scaled_rows, axis=0)
    upper = jnp.where(columns >= rows, scaled[:, :PANEL], 0.0)
    pivots = jnp.sum(jnp.where(rows == columns, final[:, :PANEL], 0.0), axis=0, keepdims=True)
    return upper, final[:, PANEL:], pivots


def exact(lhs, rhs, dims):
    return lax.dot_general(lhs, rhs, (dims, ((), ())), precision=lax.Precision.HIGHEST, preferred_element_type=F32)


def update_kernel(offsets, blocks_held, columns, my_ref, index_ref, arrived_ref, shift_ref, resident_hbm, *refs):
    parts = refs[:-12]
    near_hbm, far_hbm, pivots_ref, leading_ref, tail_ref, resident_ref, terms_ref, lead_ref = refs[-12:-4]
    near_ref, far_ref, sem, sems = refs[-4:]
    fetch = pltpu.make_async_copy(resident_hbm, resident_ref, sem)
    fetch.start()
    my_index = my_ref[0]
    size = len(offsets)
    position = 0
    packed = blocks_held * PANEL // 2
    part_rows = PANEL // 2
    for part in parts:
        for number in range(part.shape[0]):
            owner = my_index ^ offsets[position]
            for start in range(0, blocks_held * PANEL, part_rows):
                held, inner = divmod(start, PANEL)
                if start < packed:
                    rows = part[number, start : start + part_rows, :PANEL]
                else:
                    rows = part[number, start - packed : start - packed + part_rows, PANEL:]
                target = pl.multiple_of((held * size + owner) * PANEL + inner, part_rows)
                leading_ref[pl.ds(target, part_rows), :] = rows
            position += 1
    upper, inverse, pivots = eliminate(leading_ref[:PANEL, :], shift_ref[...])
    pivots_ref[...] = pivots
    lower = jnp.transpose(upper)
    needed = tail_ref.shape[1]
    tail = exact(inverse, leading_ref[:needed, :], ((1,), (1,)))
    high, low = split(tail, 2)
    tail_ref[0:PANEL, :] = high
    tail_ref[PANEL : 2 * PANEL, :] = high
    tail_ref[2 * PANEL : 3 * PANEL, :] = low
    tail_ref[3 * PANEL :, :] = low

    block = A_BLOCK
    packed_terms(arrived_ref[...], terms_ref, 0)
    for start in range(0, lead_ref.shape[0], block):
        picks = one_hot(index_ref[:, start : start + block], lead_ref.shape[0])
        got = jnp.dot(picks, terms_ref[...], preferred_element_type=F32)
        lead_ref[start : start + block, :] = whole_sum(got)[:, :PANEL]
    fetch.wait()
    stores = []
    for number, start in enumerate(range(0, lead_ref.shape[0], block)):
        rows_here = slice(start, start + block)
        panel = exact(lead_ref[rows_here, :], inverse, ((1,), (1,))) / pivots
        shown = used = panel
        if start == 0:
            row_ids = lax.broadcasted_iota(jnp.int32, panel.shape, 0)
            top = jnp.logical_and(my_index == 0, row_ids < PANEL)
            used = jnp.where(top, 0.0, panel)
            filled = jnp.concatenate([lower, jnp.zeros((block - PANEL, PANEL), F32)], axis=0)
            shown = jnp.where(top, filled, panel)
        high, low = (term.astype(F32) for term in split(used, 2))
        pair = jnp.concatenate([high, low], axis=1).astype(BF16)
        factors = jnp.concatenate([pair, pair], axis=1)
        update = jnp.dot(factors, tail_ref[...], preferred_element_type=F32)
        shown = jnp.concatenate([shown, jnp.zeros_like(shown)], axis=1)
        near_ref[rows_here, :LANES] = jnp.where(lane_ids(shown.shape) < PANEL, shown, -update[:, :LANES])
        near_ref[rows_here, LANES:] = -update[:, LANES:columns]
        far_ref[rows_here, :] = (resident_ref[rows_here, :].astype(F32) - update[:, columns:]).astype(BF16)
        for which, (source, target) in enumerate(((near_ref, near_hbm), (far_ref, far_hbm))):
            store = pltpu.make_async_copy(
                source.at[pl.ds(start, block), :], target.at[pl.ds(start, block), :], sems.at[which, number]
            )
            store.start()
            stores.append(store)
    for store in stores:
        store.wait()


def updates(my_index, parts, offsets, index, arrived, shift, resident, blocks_held, columns):
    rows, width = resident.shape
    needed = columns + width
    held_rows = len(offsets) * blocks_held * PANEL
    vmem = pl.BlockSpec(memory_space=pltpu.VMEM)
    anywhere = pl.BlockSpec(memory_space=pl.ANY)
    return pl.pallas_call(
        functools.partial(update_kernel, offsets, blocks_held, columns),
        in_specs=[pl.BlockSpec(memory_space=pltpu.SMEM), vmem, vmem, vmem, anywhere] + [vmem] * len(parts),
        out_specs=[anywhere, anywhere, vmem],
        out_shape=[
            jax.ShapeDtypeStruct((rows, columns), F32),
            jax.ShapeDtypeStruct((rows, width), BF16),
            jax.ShapeDtypeStruct((1, PANEL), F32),
        ],
        scratch_shapes=[
            pltpu.VMEM((held_rows, PANEL), F32),
            pltpu.VMEM((4 * PANEL, needed), BF16),
            pltpu.VMEM((rows, width), BF16),
            pltpu.VMEM((rows, 2 * LANES), BF16),
            pltpu.VMEM((rows, PANEL), F32),
            pltpu.VMEM((rows, columns), F32),
            pltpu.VMEM((rows, width), BF16),
            pltpu.SemaphoreType.DMA,
            pltpu.SemaphoreType.DMA((2, rows // A_BLOCK)),
        ],
        compiler_params=params(60),
        cost_estimate=pl.CostEstimate(
            flops=2 * rows * needed * 4 * PANEL, bytes_accessed=4 * rows * (columns + width), transcendentals=0
        ),
        name="factor_and_update",
    )(my_index, index, arrived, shift, resident, *parts)


def formed_kernel(index_ref, arrived_ref, near_ref, out_ref, terms_ref):
    half = arrived_ref.shape[0]

    @pl.when(pl.program_id(0) == 0)
    def _():
        words = arrived_ref[:, LANES:]
        low_lanes = lane_ids(words.shape) < PANEL
        exponent = ((words & 255) - BIAS).astype(F32)
        other = swap_halves(exponent)
        packed_terms((words >> 8).astype(F32) * jnp.exp2(exponent - 23.0), terms_ref, 2 * LANES)
        words = arrived_ref[:, :LANES]
        low = (words >> 16).astype(F32) * jnp.exp2(jnp.where(low_lanes, exponent, other) - 15.0)
        high = ((words << 16) >> 16).astype(F32) * jnp.exp2(jnp.where(low_lanes, other, exponent) - 15.0)
        for side, values in enumerate((low, high)):
            first, second = split(values, 2)
            terms_ref[side * half : (side + 1) * half, :LANES] = first
            terms_ref[side * half : (side + 1) * half, LANES : 2 * LANES] = second

    picks = one_hot(index_ref[...], terms_ref.shape[0])
    got = jnp.dot(picks, terms_ref[...], preferred_element_type=F32)
    narrow = whole_sum(got[:, 2 * LANES :])
    held = near_ref[:, :LANES]
    out_ref[:, :LANES] = jnp.where(lane_ids(held.shape) < PANEL, held, narrow + held)
    out_ref[:, LANES:] = (got[:, :LANES] + got[:, LANES : 2 * LANES]) + near_ref[:, LANES:]


def formed_columns(index, arrived, near):
    rows, columns = near.shape
    half, width = arrived.shape
    steps = 5
    block = rows // steps
    return pl.pallas_call(
        formed_kernel,
        grid=(steps,),
        in_specs=[
            pl.BlockSpec((1, block), lambda i: (0, i)),
            pl.BlockSpec((half, width), lambda i: (0, 0)),
            pl.BlockSpec((block, columns), lambda i: (i, 0)),
        ],
        out_specs=pl.BlockSpec((block, columns), lambda i: (i, 0)),
        out_shape=jax.ShapeDtypeStruct((rows, columns), F32),
        scratch_shapes=[pltpu.VMEM((rows, 4 * LANES), BF16)],
        compiler_params=params(32),
        cost_estimate=pl.CostEstimate(
            flops=8 * rows * rows * LANES, bytes_accessed=8 * rows * columns, transcendentals=0
        ),
        name="formed_columns",
    )(index, arrived, near)


def swap_rows(x, group):
    rows, width = x.shape
    return lax.all_to_all(
        x.reshape(group, rows // group, width), "wide", split_axis=0, concat_axis=0, tiled=True
    ).reshape(rows, width)


def on_device(a_rows, xa_panel, za_panel, send_order, recv_order, shift, resident):
    rows = a_rows.shape[0]
    columns = xa_panel.shape[1]
    group = lax.axis_size("wide")
    my_index = lax.axis_index("wide").astype(jnp.int32).reshape(1)
    share = rows // group
    half = rows // 2
    few, apart = phases_of(group)

    order, packing = send_order, share
    if share % 16:
        order = send_order.reshape(group, 2, share // 2).transpose(1, 0, 2).reshape(1, rows)
        packing = 0
    source, slot = recv_order // share, recv_order % share
    index = (slot // (share // 2)) * half + source * (share // 2) + slot % (share // 2)

    lead_panel, rest_panel = split_panels(my_index, xa_panel, za_panel)
    send_picks, a_copy = order_picks(order, a_rows, packing)
    lead_parts = [lead_panel]
    for masks in few:
        lead_parts = exchange(join(lead_parts), masks, "wide")
    rest_parts = [rest_panel]
    for number, masks in enumerate(apart[:-2]):
        rest_parts = exchange(join(rest_parts), masks, "wide")
        if number == 0:
            lead_parts = tied(lead_parts, *rest_parts)

    lead_out = lead_products(my_index, a_copy, send_picks, lead_parts, offsets_of(few))
    lead_in = swap_rows(tied([lead_out], *rest_parts)[0], group)
    rest_parts = exchange(join(tied(rest_parts, lead_out)), apart[-2], "wide")

    needed = columns + resident.shape[1]
    blocks_held = -(-needed // (PANEL * group))
    leading_parts = [leading_rows(index, lead_in, blocks_held * PANEL)]
    for masks in few:
        leading_parts = exchange(join(leading_parts), masks, "wide")
        if masks is few[0]:
            rest_parts = exchange(tied(rest_parts, *leading_parts), apart[-1], "wide")
    rest_out = rest_products(my_index, order, a_rows, rest_parts, offsets_of(apart), packing)
    rest_in = swap_rows(tied([rest_out], *leading_parts)[0], group)
    near, updated, pivots = updates(
        my_index,
        leading_parts,
        offsets_of(few),
        index,
        tied([lead_in], rest_out)[0],
        shift[None, :],
        resident,
        blocks_held,
        columns,
    )
    factored = formed_columns(index, rest_in, near)
    return (factored, updated, pivots[0])


def solution(mesh):
    placed = (
        P(("parts", "wide"), None),
        P(("parts", "wide"), None),
        P(("parts", "wide"), None),
        P(("parts", "wide"), None),
        P(("parts", "wide"), None),
        P("parts"),
        P(("parts", "wide"), None),
    )
    return jax.shard_map(
        on_device,
        mesh=mesh,
        in_specs=placed,
        out_specs=(P(("parts", "wide"), None), P(("parts", "wide"), None), P("parts")),
        check_vma=False,
    )
```

```python
import functools

import jax
import jax.numpy as jnp
from jax import lax
from jax.experimental import pallas as pl
from jax.experimental.pallas import tpu as pltpu
from jax.sharding import PartitionSpec as P

PANEL = 64
LANES = 128
A_BLOCK = 256
F32 = jnp.float32
BF16 = jnp.bfloat16
MIB = 1024 * 1024


def params(mebibytes=12):
    return pltpu.CompilerParams(vmem_limit_bytes=mebibytes * MIB)


def lane_ids(shape):
    return lax.broadcasted_iota(jnp.int32, shape, len(shape) - 1)


def split(x, count):
    terms = []
    for _ in range(count):
        term = x.astype(BF16)
        terms.append(term)
        x = x - term.astype(F32)
    return terms


def swap_halves(x):
    return pltpu.roll(x, LANES // 2, 1)


def as_column(index_row):
    return jnp.transpose(jnp.broadcast_to(index_row, (LANES, LANES)))


def picks_of(at, width):
    lanes = lane_ids(at.shape)
    return jnp.concatenate(
        [(at == lanes + column).astype(F32).astype(BF16) for column in range(0, width, LANES)], axis=1
    )


def one_hot(index_row, width):
    chunks = [
        picks_of(as_column(index_row[:, start : start + LANES]), width)
        for start in range(0, index_row.shape[1], LANES)
    ]
    return jnp.concatenate(chunks, axis=0) if len(chunks) > 1 else chunks[0]


def packed_order(share, half, slot):
    part = share // 2
    return (slot % share) // part * half + slot // share * part + slot % part


def fill_order(order_ref, at_ref, share):
    rows = order_ref.shape[1]
    height = 8
    for start in range(0, rows, LANES):
        column = as_column(order_ref[:, start : start + LANES])
        if not share:
            at_ref[start : start + LANES, :] = column
            continue
        for inner in range(0, LANES, height):
            place = packed_order(share, rows // 2, start + inner)
            at_ref[place : place + height, :] = column[inner : inner + height]


def exchange(held, masks, axis):
    size = lax.axis_size(axis)
    combined = [0]
    for mask in masks:
        combined += [other ^ mask for other in combined]
    parts = list(held)
    for mask in combined[1:]:
        parts += [lax.ppermute(part, axis, [(i, i ^ mask) for i in range(size)]) for part in held]
    return parts


def offsets_of(phases):
    offsets = [0]
    for masks in phases:
        combined = [0]
        for mask in masks:
            combined += [other ^ mask for other in combined]
        offsets = [offset ^ mask for mask in combined for offset in offsets]
    return offsets


def join(parts):
    return [jnp.concatenate(parts, axis=0)]


def phases_of(size):
    bits = [1 << bit for bit in reversed(range(size.bit_length() - 1))]
    return [bits[start : start + 2] for start in range(0, len(bits), 2)], [[bit] for bit in bits]


def tied(parts, *earlier):
    return list(lax.optimization_barrier((*parts, *earlier))[: len(parts)])


def picks_kernel(share, order_ref, a_hbm, picks_ref, copy_ref, at_ref, sem):
    copy = pltpu.make_async_copy(a_hbm, copy_ref, sem)
    copy.start()
    fill_order(order_ref, at_ref, share)
    rows, width = picks_ref.shape
    for start in range(0, rows, A_BLOCK):
        picks_ref[start : start + A_BLOCK, :] = picks_of(at_ref[start : start + A_BLOCK, :], width)
    copy.wait()


def order_picks(order, a_rows, share):
    rows, depth = a_rows.shape
    return pl.pallas_call(
        functools.partial(picks_kernel, share),
        in_specs=[pl.BlockSpec(memory_space=pltpu.VMEM), pl.BlockSpec(memory_space=pl.ANY)],
        out_specs=[pl.BlockSpec(memory_space=pltpu.VMEM)] * 2,
        out_shape=[jax.ShapeDtypeStruct((rows, rows), BF16), jax.ShapeDtypeStruct((rows, depth), BF16)],
        scratch_shapes=[pltpu.VMEM((rows, LANES), jnp.int32), pltpu.SemaphoreType.DMA],
        compiler_params=params(),
        cost_estimate=pl.CostEstimate(flops=4 * rows * rows, bytes_accessed=4 * rows * depth, transcendentals=0),
        name="order_picks",
    )(order, a_rows)


def panels_kernel(my_ref, xa_hbm, za_hbm, lead_ref, rest_ref, xa_ref, za_ref, sems):
    copies = [
        pltpu.make_async_copy(xa_hbm, xa_ref, sems.at[0]),
        pltpu.make_async_copy(za_hbm, za_ref, sems.at[1]),
    ]
    for copy in copies:
        copy.start()
    for copy in copies:
        copy.wait()
    lead_ref[0] = jnp.concatenate([xa_ref[:, :PANEL], za_ref[:, :PANEL]], axis=1)
    rest_ref[0, :, :LANES] = jnp.concatenate([xa_ref[:, PANEL:LANES], za_ref[:, PANEL:LANES]], axis=1)
    rest_ref[0, :, LANES : 2 * LANES] = xa_ref[:, LANES:]
    rest_ref[0, :, 2 * LANES :] = za_ref[:, LANES:]


def split_panels(my_index, xa_panel, za_panel):
    depth, columns = xa_panel.shape
    return pl.pallas_call(
        panels_kernel,
        in_specs=[pl.BlockSpec(memory_space=pltpu.SMEM)] + [pl.BlockSpec(memory_space=pl.ANY)] * 2,
        out_shape=[
            jax.ShapeDtypeStruct((1, depth, LANES), BF16),
            jax.ShapeDtypeStruct((1, depth, 2 * columns - LANES), BF16),
        ],
        scratch_shapes=[
            pltpu.VMEM((depth, columns), BF16),
            pltpu.VMEM((depth, columns), BF16),
            pltpu.SemaphoreType.DMA((2,)),
        ],
        compiler_params=params(),
        name="split_panels",
    )(my_index, xa_panel, za_panel)


def assemble(my_index, offsets, parts, panel_ref):
    position = 0
    for part in parts:
        for number in range(part.shape[0]):
            depth = part.shape[1]
            start = pl.multiple_of((my_index ^ offsets[position]) * depth, depth)
            panel_ref[pl.ds(start, depth), :] = part[number]
            position += 1


def whole_sum(got):
    pair = got[:, :LANES]
    return (pair + swap_halves(pair)) + got[:, LANES:]


def lead_product_kernel(offsets, my_ref, a_ref, picks_ref, *refs):
    parts, (out_ref, panel_ref, terms_ref) = refs[:-3], refs[-3:]
    assemble(my_ref[0], offsets, parts, panel_ref)
    rows = a_ref.shape[0]
    for start in range(0, rows, A_BLOCK):
        both = jnp.dot(a_ref[start : start + A_BLOCK, :], panel_ref[...], preferred_element_type=F32)
        first, second, third = (term.astype(F32) for term in split(both * swap_halves(both), 3))
        near = lane_ids(both.shape) < PANEL
        terms_ref[start : start + A_BLOCK, :LANES] = jnp.where(near, first, second).astype(BF16)
        terms_ref[start : start + A_BLOCK, LANES:] = third.astype(BF16)
    half = rows // 2
    block = half // 2
    for start in range(0, half, block):
        low = jnp.dot(picks_ref[start : start + block, :], terms_ref[...], preferred_element_type=F32)
        high = jnp.dot(picks_ref[half + start : half + start + block, :], terms_ref[...], preferred_element_type=F32)
        low, high = whole_sum(low), whole_sum(high)
        out_ref[start : start + block, :] = jnp.where(lane_ids(low.shape) < PANEL, low, high)


def lead_products(my_index, a_rows, picks, parts, offsets):
    rows, depth = a_rows.shape
    return pl.pallas_call(
        functools.partial(lead_product_kernel, offsets),
        in_specs=[pl.BlockSpec(memory_space=pltpu.SMEM)] + [pl.BlockSpec(memory_space=pltpu.VMEM)] * (2 + len(parts)),
        out_specs=pl.BlockSpec(memory_space=pltpu.VMEM),
        out_shape=jax.ShapeDtypeStruct((rows // 2, LANES), F32),
        scratch_shapes=[pltpu.VMEM((depth, LANES), BF16), pltpu.VMEM((rows, 2 * LANES), BF16)],
        compiler_params=params(),
        cost_estimate=pl.CostEstimate(
            flops=2 * rows * (depth + 2 * rows) * LANES, bytes_accessed=2 * rows * depth, transcendentals=0
        ),
        name="lead_products",
    )(my_index, a_rows, picks, *parts)


BIAS = 128


def rest_product_kernel(offsets, share, my_ref, order_ref, a_hbm, *refs):
    parts, (out_ref, a_ref, at_ref, picks_ref, panel_ref, terms_ref, sems, part_sems) = refs[:-8], refs[-8:]
    rows = a_ref.shape[0]
    block = A_BLOCK
    starts = range(0, rows, block)
    copies = [
        pltpu.make_async_copy(a_hbm.at[pl.ds(start, block), :], a_ref.at[pl.ds(start, block), :], sems.at[i])
        for i, start in enumerate(starts)
    ]
    fetches = []
    for part in parts:
        for number in range(part.shape[0]):
            depth = part.shape[1]
            position = len(fetches)
            place = pl.multiple_of((my_ref[0] ^ offsets[position]) * depth, depth)
            fetches.append(
                pltpu.make_async_copy(part.at[number], panel_ref.at[pl.ds(place, depth), :], part_sems.at[position])
            )
    for copy in fetches + copies[:2]:
        copy.start()
    fill_order(order_ref, at_ref, share)
    for start in starts:
        picks_ref[start : start + block, :] = picks_of(at_ref[start : start + block, :], rows)
    for copy in fetches:
        copy.wait()

    def product(i):
        copies[i].wait()
        if i + 2 < len(copies):
            copies[i + 2].start()
        return jnp.dot(a_ref[starts[i] : starts[i] + block, :], panel_ref[...], preferred_element_type=F32)

    later = product(0)
    for i, start in enumerate(starts):
        both = later
        if i + 1 < len(starts):
            later = product(i + 1)
        near = both[:, :LANES]
        near = near * swap_halves(near)
        far = both[:, LANES : 2 * LANES] * both[:, 2 * LANES :]
        largest = jnp.max(jnp.maximum(jnp.abs(near), jnp.abs(far)), axis=1, keepdims=True)
        largest = jnp.maximum(largest, 1e-30)
        exponent = jnp.floor(jnp.log2(largest)) + 1.0
        scale = jnp.exp2(15.0 - exponent)
        far = jnp.floor(far * scale + 0.5)
        far = jnp.minimum(jnp.maximum(far, -32767.0), 32767.0)
        near = jnp.floor(near * (scale * 256.0) + 0.5)
        near = jnp.minimum(jnp.maximum(near, -8388607.0), 8388607.0)
        far_top = jnp.floor(far * (1 / 256))
        near_top = jnp.floor(near * (1 / 65536))
        near = near - near_top * 65536.0
        near_middle = jnp.floor(near * (1 / 256))
        low_lanes = lane_ids(near.shape) < PANEL
        rows_here = slice(start, start + block)
        terms_ref[rows_here, :LANES] = far_top.astype(BF16)
        terms_ref[rows_here, LANES : 2 * LANES] = (far - far_top * 256.0).astype(BF16)
        terms_ref[rows_here, 2 * LANES : 3 * LANES] = jnp.where(low_lanes, near_top, near_middle).astype(BF16)
        terms_ref[rows_here, 3 * LANES :] = jnp.where(low_lanes, near - near_middle * 256.0, exponent).astype(BF16)


    def coded(start, size):
        got = jnp.dot(picks_ref[start : start + size, :], terms_ref[...], preferred_element_type=F32)
        far = got[:, :LANES] * 256.0 + got[:, LANES : 2 * LANES]
        tops, lows = got[:, 2 * LANES : 3 * LANES], got[:, 3 * LANES :]
        low_lanes = lane_ids(tops.shape) < PANEL
        tops = tops * jnp.where(low_lanes, 65536.0, 256.0)
        swapped = swap_halves(lows)
        near = tops + swap_halves(tops) + jnp.where(low_lanes, lows, swapped)
        exponent = jnp.where(low_lanes, swapped, lows)
        near = near.astype(jnp.int32) * 256 + (exponent.astype(jnp.int32) + BIAS)
        return far.astype(jnp.int32), near

    half = rows // 2
    block = half // 2
    for start in range(0, half, block):
        far_low, near_low = coded(start, block)
        far_high, near_high = coded(half + start, block)
        out_ref[start : start + block, :LANES] = far_low * 65536 + (far_high & 65535)
        out_ref[start : start + block, LANES:] = jnp.where(lane_ids(near_low.shape) < PANEL, near_low, near_high)


def rest_products(my_index, order, a_rows, parts, offsets, share):
    rows, depth = a_rows.shape
    return pl.pallas_call(
        functools.partial(rest_product_kernel, offsets, share),
        in_specs=[
            pl.BlockSpec(memory_space=pltpu.SMEM),
            pl.BlockSpec(memory_space=pltpu.VMEM),
            pl.BlockSpec(memory_space=pl.ANY),
        ]
        + [pl.BlockSpec(memory_space=pl.ANY)] * len(parts),
        out_specs=pl.BlockSpec(memory_space=pltpu.VMEM),
        out_shape=jax.ShapeDtypeStruct((rows // 2, 2 * LANES), jnp.int32),
        scratch_shapes=[
            pltpu.VMEM((rows, depth), BF16),
            pltpu.VMEM((rows, LANES), jnp.int32),
            pltpu.VMEM((rows, rows), BF16),
            pltpu.VMEM((depth, 3 * LANES), BF16),
            pltpu.VMEM((rows, 4 * LANES), BF16),
            pltpu.SemaphoreType.DMA((rows // A_BLOCK,)),
            pltpu.SemaphoreType.DMA((len(offsets),)),
        ],
        compiler_params=params(58),
        cost_estimate=pl.CostEstimate(
            flops=2 * rows * (3 * depth + 4 * rows) * LANES, bytes_accessed=2 * rows * depth, transcendentals=0
        ),
        name="rest_products",
    )(my_index, order, a_rows, *parts)


def packed_terms(x, terms_ref, start):
    half = x.shape[0]
    first, second, third = (term.astype(F32) for term in split(x, 3))
    near = lane_ids(x.shape) < PANEL
    other = swap_halves(third)
    terms_ref[:half, start : start + LANES] = jnp.where(near, first, swap_halves(second)).astype(BF16)
    terms_ref[half:, start : start + LANES] = jnp.where(near, swap_halves(first), second).astype(BF16)
    terms_ref[:half, start + LANES : start + 2 * LANES] = jnp.where(near, third, other).astype(BF16)
    terms_ref[half:, start + LANES : start + 2 * LANES] = jnp.where(near, other, third).astype(BF16)


def leading_kernel(held, index_ref, arrived_ref, out_ref, terms_ref):
    packed_terms(arrived_ref[...], terms_ref, 0)
    width = -(-held // LANES) * LANES
    picks = one_hot(index_ref[:, :width], terms_ref.shape[0])
    got = whole_sum(jnp.dot(picks, terms_ref[...], preferred_element_type=F32))
    first, second = got[: held // 2], got[held // 2 : held]
    out_ref[0] = jnp.where(lane_ids(first.shape) < PANEL, first, second)


def leading_rows(index, arrived, held):
    rows = index.shape[1]
    return pl.pallas_call(
        functools.partial(leading_kernel, held),
        in_specs=[pl.BlockSpec(memory_space=pltpu.VMEM)] * 2,
        out_specs=pl.BlockSpec(memory_space=pltpu.VMEM),
        out_shape=jax.ShapeDtypeStruct((1, held // 2, LANES), F32),
        scratch_shapes=[pltpu.VMEM((rows, 2 * LANES), BF16)],
        compiler_params=params(),
        cost_estimate=pl.CostEstimate(
            flops=4 * held * rows * LANES, bytes_accessed=2 * rows * LANES, transcendentals=0
        ),
        name="leading_rows",
    )(index, arrived)


def eliminate(block, shift_row):
    rows = lax.broadcasted_iota(jnp.int32, (PANEL, PANEL), 0)
    columns = lax.broadcasted_iota(jnp.int32, (PANEL, PANEL), 1)
    flipped = jnp.transpose(block)
    mirrored = jnp.where(rows >= columns, block, flipped)
    diagonal = shift_row + jnp.sum(jnp.abs(mirrored), axis=0, keepdims=True)
    unit = (rows == columns).astype(F32)
    work = jnp.where(rows == columns, diagonal, mirrored)
    work = jnp.concatenate([work, unit], axis=1)
    height = 8
    groups = [work[start : start + height] for start in range(0, PANEL, height)]
    sublanes = lax.broadcasted_iota(jnp.int32, (height, LANES), 0)
    scaled_rows = []
    for k in range(PANEL):
        home, offset = divmod(k, height)
        row = groups[home][offset : offset + 1, :]
        row = row / row[:, k : k + 1]
        scaled_rows.append(row)
        for g in range(home, PANEL // height):
            column = jnp.broadcast_to(groups[g][:, k : k + 1], (height, LANES))
            if g == home:
                column = jnp.where(sublanes > offset, column, 0.0)
            groups[g] = groups[g] - column * row
    final = jnp.concatenate(groups, axis=0)
    scaled = jnp.concatenate(scaled_rows, axis=0)
    upper = jnp.where(columns >= rows, scaled[:, :PANEL], 0.0)
    pivots = jnp.sum(jnp.where(rows == columns, final[:, :PANEL], 0.0), axis=0, keepdims=True)
    return upper, final[:, PANEL:], pivots


def exact(lhs, rhs, dims):
    return lax.dot_general(lhs, rhs, (dims, ((), ())), precision=lax.Precision.HIGHEST, preferred_element_type=F32)


def update_kernel(offsets, blocks_held, columns, my_ref, index_ref, arrived_ref, shift_ref, resident_hbm, *refs):
    parts = refs[:-12]
    near_hbm, far_hbm, pivots_ref, leading_ref, tail_ref, resident_ref, terms_ref, lead_ref = refs[-12:-4]
    near_ref, far_ref, sem, sems = refs[-4:]
    fetch = pltpu.make_async_copy(resident_hbm, resident_ref, sem)
    fetch.start()
    my_index = my_ref[0]
    size = len(offsets)
    position = 0
    packed = blocks_held * PANEL // 2
    part_rows = PANEL // 2
    for part in parts:
        for number in range(part.shape[0]):
            owner = my_index ^ offsets[position]
            for start in range(0, blocks_held * PANEL, part_rows):
                held, inner = divmod(start, PANEL)
                if start < packed:
                    rows = part[number, start : start + part_rows, :PANEL]
                else:
                    rows = part[number, start - packed : start - packed + part_rows, PANEL:]
                target = pl.multiple_of((held * size + owner) * PANEL + inner, part_rows)
                leading_ref[pl.ds(target, part_rows), :] = rows
            position += 1
    upper, inverse, pivots = eliminate(leading_ref[:PANEL, :], shift_ref[...])
    pivots_ref[...] = pivots
    lower = jnp.transpose(upper)
    needed = tail_ref.shape[1]
    tail = exact(inverse, leading_ref[:needed, :], ((1,), (1,)))
    high, low = split(tail, 2)
    tail_ref[0:PANEL, :] = high
    tail_ref[PANEL : 2 * PANEL, :] = high
    tail_ref[2 * PANEL : 3 * PANEL, :] = low
    tail_ref[3 * PANEL :, :] = low

    block = A_BLOCK
    packed_terms(arrived_ref[...], terms_ref, 0)
    for start in range(0, lead_ref.shape[0], block):
        picks = one_hot(index_ref[:, start : start + block], lead_ref.shape[0])
        got = jnp.dot(picks, terms_ref[...], preferred_element_type=F32)
        lead_ref[start : start + block, :] = whole_sum(got)[:, :PANEL]
    fetch.wait()
    stores = []
    for number, start in enumerate(range(0, lead_ref.shape[0], block)):
        rows_here = slice(start, start + block)
        panel = exact(lead_ref[rows_here, :], inverse, ((1,), (1,))) / pivots
        shown = used = panel
        if start == 0:
            row_ids = lax.broadcasted_iota(jnp.int32, panel.shape, 0)
            top = jnp.logical_and(my_index == 0, row_ids < PANEL)
            used = jnp.where(top, 0.0, panel)
            filled = jnp.concatenate([lower, jnp.zeros((block - PANEL, PANEL), F32)], axis=0)
            shown = jnp.where(top, filled, panel)
        high, low = (term.astype(F32) for term in split(used, 2))
        pair = jnp.concatenate([high, low], axis=1).astype(BF16)
        factors = jnp.concatenate([pair, pair], axis=1)
        update = jnp.dot(factors, tail_ref[...], preferred_element_type=F32)
        shown = jnp.concatenate([shown, jnp.zeros_like(shown)], axis=1)
        near_ref[rows_here, :LANES] = jnp.where(lane_ids(shown.shape) < PANEL, shown, -update[:, :LANES])
        near_ref[rows_here, LANES:] = -update[:, LANES:columns]
        far_ref[rows_here, :] = (resident_ref[rows_here, :].astype(F32) - update[:, columns:]).astype(BF16)
        for which, (source, target) in enumerate(((near_ref, near_hbm), (far_ref, far_hbm))):
            store = pltpu.make_async_copy(
                source.at[pl.ds(start, block), :], target.at[pl.ds(start, block), :], sems.at[which, number]
            )
            store.start()
            stores.append(store)
    for store in stores:
        store.wait()


def updates(my_index, parts, offsets, index, arrived, shift, resident, blocks_held, columns):
    rows, width = resident.shape
    needed = columns + width
    held_rows = len(offsets) * blocks_held * PANEL
    vmem = pl.BlockSpec(memory_space=pltpu.VMEM)
    anywhere = pl.BlockSpec(memory_space=pl.ANY)
    return pl.pallas_call(
        functools.partial(update_kernel, offsets, blocks_held, columns),
        in_specs=[pl.BlockSpec(memory_space=pltpu.SMEM), vmem, vmem, vmem, anywhere] + [vmem] * len(parts),
        out_specs=[anywhere, anywhere, vmem],
        out_shape=[
            jax.ShapeDtypeStruct((rows, columns), F32),
            jax.ShapeDtypeStruct((rows, width), BF16),
            jax.ShapeDtypeStruct((1, PANEL), F32),
        ],
        scratch_shapes=[
            pltpu.VMEM((held_rows, PANEL), F32),
            pltpu.VMEM((4 * PANEL, needed), BF16),
            pltpu.VMEM((rows, width), BF16),
            pltpu.VMEM((rows, 2 * LANES), BF16),
            pltpu.VMEM((rows, PANEL), F32),
            pltpu.VMEM((rows, columns), F32),
            pltpu.VMEM((rows, width), BF16),
            pltpu.SemaphoreType.DMA,
            pltpu.SemaphoreType.DMA((2, rows // A_BLOCK)),
        ],
        compiler_params=params(60),
        cost_estimate=pl.CostEstimate(
            flops=2 * rows * needed * 4 * PANEL, bytes_accessed=4 * rows * (columns + width), transcendentals=0
        ),
        name="factor_and_update",
    )(my_index, index, arrived, shift, resident, *parts)


def formed_kernel(index_ref, arrived_ref, near_hbm, out_hbm, near_ref, terms_ref, out_ref, in_sems, out_sems):
    half = arrived_ref.shape[0]
    block = A_BLOCK
    starts = range(0, near_ref.shape[0], block)

    def rows_of(ref, start):
        return ref.at[pl.ds(start, block), :]

    fetches = [
        pltpu.make_async_copy(rows_of(near_hbm, start), rows_of(near_ref, start), in_sems.at[i])
        for i, start in enumerate(starts)
    ]
    for fetch in fetches:
        fetch.start()
    words = arrived_ref[:, LANES:]
    low_lanes = lane_ids(words.shape) < PANEL
    exponent = ((words & 255) - BIAS).astype(F32)
    scale = jnp.exp2(exponent - 15.0)
    other = swap_halves(scale)
    packed_terms((words >> 8).astype(F32) * (scale * (1 / 256)), terms_ref, 2 * LANES)
    words = arrived_ref[:, :LANES]
    low = (words >> 16).astype(F32) * jnp.where(low_lanes, scale, other)
    high = ((words << 16) >> 16).astype(F32) * jnp.where(low_lanes, other, scale)
    for side, values in enumerate((low, high)):
        first, second = split(values, 2)
        terms_ref[side * half : (side + 1) * half, :LANES] = first
        terms_ref[side * half : (side + 1) * half, LANES : 2 * LANES] = second

    stores = []
    for i, start in enumerate(starts):
        rows_here = slice(start, start + block)
        picks = one_hot(index_ref[:, rows_here], terms_ref.shape[0])
        got = jnp.dot(picks, terms_ref[...], preferred_element_type=F32)
        narrow = whole_sum(got[:, 2 * LANES :])
        fetches[i].wait()
        held = near_ref[rows_here, :LANES]
        out_ref[rows_here, :LANES] = jnp.where(lane_ids(held.shape) < PANEL, held, narrow + held)
        out_ref[rows_here, LANES:] = (got[:, :LANES] + got[:, LANES : 2 * LANES]) + near_ref[rows_here, LANES:]
        store = pltpu.make_async_copy(rows_of(out_ref, start), rows_of(out_hbm, start), out_sems.at[i])
        store.start()
        stores.append(store)
    for store in stores:
        store.wait()


def formed_columns(index, arrived, near):
    rows, columns = near.shape
    vmem = pl.BlockSpec(memory_space=pltpu.VMEM)
    anywhere = pl.BlockSpec(memory_space=pl.ANY)
    return pl.pallas_call(
        formed_kernel,
        in_specs=[vmem, vmem, anywhere],
        out_specs=anywhere,
        out_shape=jax.ShapeDtypeStruct((rows, columns), F32),
        input_output_aliases={2: 0},
        scratch_shapes=[
            pltpu.VMEM((rows, columns), F32),
            pltpu.VMEM((rows, 4 * LANES), BF16),
            pltpu.VMEM((rows, columns), F32),
            pltpu.SemaphoreType.DMA((rows // A_BLOCK,)),
            pltpu.SemaphoreType.DMA((rows // A_BLOCK,)),
        ],
        compiler_params=params(32),
        cost_estimate=pl.CostEstimate(
            flops=8 * rows * rows * LANES, bytes_accessed=8 * rows * columns, transcendentals=0
        ),
        name="formed_columns",
    )(index, arrived, near)


def swap_rows(x, group):
    rows, width = x.shape
    return lax.all_to_all(
        x.reshape(group, rows // group, width), "wide", split_axis=0, concat_axis=0, tiled=True
    ).reshape(rows, width)


def on_device(a_rows, xa_panel, za_panel, send_order, recv_order, shift, resident):
    rows = a_rows.shape[0]
    columns = xa_panel.shape[1]
    group = lax.axis_size("wide")
    my_index = lax.axis_index("wide").astype(jnp.int32).reshape(1)
    share = rows // group
    half = rows // 2
    few, apart = phases_of(group)

    order, packing = send_order, share
    if share % 16:
        order = send_order.reshape(group, 2, share // 2).transpose(1, 0, 2).reshape(1, rows)
        packing = 0
    source, slot = recv_order // share, recv_order % share
    index = (slot // (share // 2)) * half + source * (share // 2) + slot % (share // 2)

    lead_panel, rest_panel = split_panels(my_index, xa_panel, za_panel)
    send_picks, a_copy = order_picks(order, a_rows, packing)
    lead_parts = exchange([lead_panel], few[0], "wide")
    for masks in few[1:]:
        lead_parts = exchange(tied(join(lead_parts), send_picks), masks, "wide")
    rest_parts = tied([rest_panel], send_picks)
    for masks in apart[:-2]:
        rest_parts = exchange(join(rest_parts), masks, "wide")
        rest_parts = tied(rest_parts, lead_parts[-2])
    rest_parts = join(rest_parts)
    lead_out = lead_products(my_index, a_copy, send_picks, tied(lead_parts, *rest_parts), offsets_of(few))
    rest_parts = exchange(rest_parts, apart[-2], "wide")
    lead_in = swap_rows(lead_out, group)
    rest_parts = exchange(tied(rest_parts, lead_out), apart[-1], "wide")
    rest_out = rest_products(my_index, order, a_rows, rest_parts, offsets_of(apart), packing)

    needed = columns + resident.shape[1]
    blocks_held = -(-needed // (PANEL * group))
    leading_parts = [leading_rows(index, tied([lead_in], rest_out)[0], blocks_held * PANEL)]
    for masks in few:
        leading_parts = exchange(join(leading_parts), masks, "wide")
    rest_in = swap_rows(tied([rest_out], leading_parts[-2])[0], group)
    near, updated, pivots = updates(
        my_index,
        leading_parts,
        offsets_of(few),
        index,
        lead_in,
        shift[None, :],
        resident,
        blocks_held,
        columns,
    )
    factored = formed_columns(index, rest_in, near)
    return (factored, updated, pivots[0])


def solution(mesh):
    placed = (
        P(("parts", "wide"), None),
        P(("parts", "wide"), None),
        P(("parts", "wide"), None),
        P(("parts", "wide"), None),
        P(("parts", "wide"), None),
        P("parts"),
        P(("parts", "wide"), None),
    )
    return jax.shard_map(
        on_device,
        mesh=mesh,
        in_specs=placed,
        out_specs=(P(("parts", "wide"), None), P(("parts", "wide"), None), P("parts")),
        check_vma=False,
    )
```

```python
import functools

import jax
import jax.numpy as jnp
from jax import lax
from jax.experimental import pallas as pl
from jax.experimental.pallas import tpu as pltpu
from jax.sharding import PartitionSpec as P

PANEL = 64
LANES = 128
A_BLOCK = 640
F32 = jnp.float32
BF16 = jnp.bfloat16
MIB = 1024 * 1024


def params(mebibytes=12):
    return pltpu.CompilerParams(vmem_limit_bytes=mebibytes * MIB)


def in_hbm(x):
    return pltpu.with_memory_space_constraint(x, pltpu.HBM)


def lane_ids(shape):
    return lax.broadcasted_iota(jnp.int32, shape, len(shape) - 1)


def split(x, count):
    terms = []
    for _ in range(count):
        term = x.astype(BF16)
        terms.append(term)
        x = x - term.astype(F32)
    return terms


def swap_halves(x):
    return pltpu.roll(x, LANES // 2, 1)


def as_column(index_row):
    return jnp.transpose(jnp.broadcast_to(index_row, (LANES, LANES)))


def picks_of(at, width):
    lanes = lane_ids(at.shape)
    return jnp.concatenate(
        [(at == lanes + column).astype(F32).astype(BF16) for column in range(0, width, LANES)], axis=1
    )


def one_hot(index_row, width):
    chunks = [
        picks_of(as_column(index_row[:, start : start + LANES]), width)
        for start in range(0, index_row.shape[1], LANES)
    ]
    return jnp.concatenate(chunks, axis=0) if len(chunks) > 1 else chunks[0]


def packed_order(share, half, slot):
    part = share // 2
    return (slot % share) // part * half + slot // share * part + slot % part


def fill_order(order_ref, at_ref, share):
    rows = order_ref.shape[1]
    height = 8
    for start in range(0, rows, LANES):
        column = as_column(order_ref[:, start : start + LANES])
        if not share:
            at_ref[start : start + LANES, :] = column
            continue
        for inner in range(0, LANES, height):
            place = packed_order(share, rows // 2, start + inner)
            at_ref[place : place + height, :] = column[inner : inner + height]


def exchange(held, masks, axis):
    size = lax.axis_size(axis)
    combined = [0]
    for mask in masks:
        combined += [other ^ mask for other in combined]
    parts = list(held)
    for mask in combined[1:]:
        parts += [lax.ppermute(part, axis, [(i, i ^ mask) for i in range(size)]) for part in held]
    return parts


def offsets_of(phases):
    offsets = [0]
    for masks in phases:
        combined = [0]
        for mask in masks:
            combined += [other ^ mask for other in combined]
        offsets = [offset ^ mask for mask in combined for offset in offsets]
    return offsets


def join(parts):
    return [jnp.concatenate(parts, axis=0)]


def phases_of(size):
    bits = [1 << bit for bit in reversed(range(size.bit_length() - 1))]
    return [bits[start : start + 2] for start in range(0, len(bits), 2)], [[bit] for bit in bits]


def tied(parts, *earlier):
    return list(lax.optimization_barrier((*parts, *earlier))[: len(parts)])


def picks_kernel(share, order_hbm, a_hbm, picks_ref, copy_ref, order_ref, at_ref, sems):
    fetch = pltpu.make_async_copy(order_hbm, order_ref, sems.at[0])
    copy = pltpu.make_async_copy(a_hbm, copy_ref, sems.at[1])
    fetch.start()
    copy.start()
    fetch.wait()
    fill_order(order_ref, at_ref, share)
    rows, width = picks_ref.shape
    for start in range(0, rows, A_BLOCK):
        picks_ref[start : start + A_BLOCK, :] = picks_of(at_ref[start : start + A_BLOCK, :], width)
    copy.wait()


def order_picks(order, a_rows, share):
    rows, depth = a_rows.shape
    return pl.pallas_call(
        functools.partial(picks_kernel, share),
        in_specs=[pl.BlockSpec(memory_space=pltpu.HBM)] * 2,
        out_specs=[pl.BlockSpec(memory_space=pltpu.VMEM)] * 2,
        out_shape=[jax.ShapeDtypeStruct((rows, rows), BF16), jax.ShapeDtypeStruct((rows, depth), BF16)],
        scratch_shapes=[
            pltpu.VMEM((1, rows), jnp.int32),
            pltpu.VMEM((rows, LANES), jnp.int32),
            pltpu.SemaphoreType.DMA((2,)),
        ],
        compiler_params=params(),
        cost_estimate=pl.CostEstimate(flops=4 * rows * rows, bytes_accessed=4 * rows * depth, transcendentals=0),
        name="order_picks",
    )(in_hbm(order), in_hbm(a_rows))


def panels_kernel(my_ref, xa_hbm, za_hbm, lead_ref, rest_ref, xa_ref, za_ref, sems):
    copies = [
        pltpu.make_async_copy(xa_hbm, xa_ref, sems.at[0]),
        pltpu.make_async_copy(za_hbm, za_ref, sems.at[1]),
    ]
    for copy in copies:
        copy.start()
    for copy in copies:
        copy.wait()
    lead_ref[0] = jnp.concatenate([xa_ref[:, :PANEL], za_ref[:, :PANEL]], axis=1)
    rest_ref[0, :, :LANES] = jnp.concatenate([xa_ref[:, PANEL:LANES], za_ref[:, PANEL:LANES]], axis=1)
    rest_ref[0, :, LANES : 2 * LANES] = xa_ref[:, LANES:]
    rest_ref[0, :, 2 * LANES :] = za_ref[:, LANES:]


def split_panels(my_index, xa_panel, za_panel):
    depth, columns = xa_panel.shape
    return pl.pallas_call(
        panels_kernel,
        in_specs=[pl.BlockSpec(memory_space=pltpu.SMEM)] + [pl.BlockSpec(memory_space=pltpu.HBM)] * 2,
        out_shape=[
            jax.ShapeDtypeStruct((1, depth, LANES), BF16),
            jax.ShapeDtypeStruct((1, depth, 2 * columns - LANES), BF16),
        ],
        scratch_shapes=[
            pltpu.VMEM((depth, columns), BF16),
            pltpu.VMEM((depth, columns), BF16),
            pltpu.SemaphoreType.DMA((2,)),
        ],
        compiler_params=params(),
        name="split_panels",
    )(my_index, in_hbm(xa_panel), in_hbm(za_panel))


def assemble(my_index, offsets, parts, panel_ref):
    position = 0
    for part in parts:
        for number in range(part.shape[0]):
            depth = part.shape[1]
            start = pl.multiple_of((my_index ^ offsets[position]) * depth, depth)
            panel_ref[pl.ds(start, depth), :] = part[number]
            position += 1


def whole_sum(got):
    pair = got[:, :LANES]
    return (pair + swap_halves(pair)) + got[:, LANES:]


def lead_product_kernel(offsets, my_ref, a_ref, picks_ref, *refs):
    parts, (out_ref, panel_ref, terms_ref) = refs[:-3], refs[-3:]
    assemble(my_ref[0], offsets, parts, panel_ref)
    rows = a_ref.shape[0]
    for start in range(0, rows, A_BLOCK):
        both = jnp.dot(a_ref[start : start + A_BLOCK, :], panel_ref[...], preferred_element_type=F32)
        first, second, third = (term.astype(F32) for term in split(both * swap_halves(both), 3))
        near = lane_ids(both.shape) < PANEL
        terms_ref[start : start + A_BLOCK, :LANES] = jnp.where(near, first, second).astype(BF16)
        terms_ref[start : start + A_BLOCK, LANES:] = third.astype(BF16)
    half = rows // 2
    block = half // 2
    for start in range(0, half, block):
        low = jnp.dot(picks_ref[start : start + block, :], terms_ref[...], preferred_element_type=F32)
        high = jnp.dot(picks_ref[half + start : half + start + block, :], terms_ref[...], preferred_element_type=F32)
        low, high = whole_sum(low), whole_sum(high)
        out_ref[start : start + block, :] = jnp.where(lane_ids(low.shape) < PANEL, low, high)


def lead_products(my_index, a_rows, picks, parts, offsets):
    rows, depth = a_rows.shape
    return pl.pallas_call(
        functools.partial(lead_product_kernel, offsets),
        in_specs=[pl.BlockSpec(memory_space=pltpu.SMEM)] + [pl.BlockSpec(memory_space=pltpu.VMEM)] * (2 + len(parts)),
        out_specs=pl.BlockSpec(memory_space=pltpu.VMEM),
        out_shape=jax.ShapeDtypeStruct((rows // 2, LANES), F32),
        scratch_shapes=[pltpu.VMEM((depth, LANES), BF16), pltpu.VMEM((rows, 2 * LANES), BF16)],
        compiler_params=params(),
        cost_estimate=pl.CostEstimate(
            flops=2 * rows * (depth + 2 * rows) * LANES, bytes_accessed=2 * rows * depth, transcendentals=0
        ),
        name="lead_products",
    )(my_index, a_rows, picks, *parts)


BIAS = 128


def rest_product_kernel(offsets, share, my_ref, order_ref, a_hbm, *refs):
    parts, (out_ref, a_ref, at_ref, picks_ref, panel_ref, terms_ref, sems, part_sems) = refs[:-8], refs[-8:]
    rows = a_ref.shape[0]
    block = A_BLOCK
    starts = range(0, rows, block)
    copies = [
        pltpu.make_async_copy(a_hbm.at[pl.ds(start, block), :], a_ref.at[pl.ds(start, block), :], sems.at[i])
        for i, start in enumerate(starts)
    ]
    fetches = []
    for part in parts:
        for number in range(part.shape[0]):
            depth = part.shape[1]
            position = len(fetches)
            place = pl.multiple_of((my_ref[0] ^ offsets[position]) * depth, depth)
            fetches.append(
                pltpu.make_async_copy(part.at[number], panel_ref.at[pl.ds(place, depth), :], part_sems.at[position])
            )
    for copy in fetches + copies[:2]:
        copy.start()
    fill_order(order_ref, at_ref, share)
    for start in starts:
        picks_ref[start : start + block, :] = picks_of(at_ref[start : start + block, :], rows)
    for copy in fetches:
        copy.wait()

    def product(i):
        copies[i].wait()
        if i + 2 < len(copies):
            copies[i + 2].start()
        return jnp.dot(a_ref[starts[i] : starts[i] + block, :], panel_ref[...], preferred_element_type=F32)

    later = product(0)
    for i, start in enumerate(starts):
        both = later
        if i + 1 < len(starts):
            later = product(i + 1)
        near = both[:, :LANES]
        near = near * swap_halves(near)
        far = both[:, LANES : 2 * LANES] * both[:, 2 * LANES :]
        largest = jnp.max(jnp.maximum(jnp.abs(near), jnp.abs(far)), axis=1, keepdims=True)
        largest = jnp.maximum(largest, 1e-30)
        exponent = jnp.floor(jnp.log2(largest)) + 1.0
        scale = jnp.exp2(15.0 - exponent)
        far = jnp.floor(far * scale + 0.5)
        far = jnp.minimum(jnp.maximum(far, -32767.0), 32767.0)
        near = jnp.floor(near * (scale * 256.0) + 0.5)
        near = jnp.minimum(jnp.maximum(near, -8388607.0), 8388607.0)
        far_top = jnp.floor(far * (1 / 256))
        near_top = jnp.floor(near * (1 / 65536))
        near = near - near_top * 65536.0
        near_middle = jnp.floor(near * (1 / 256))
        low_lanes = lane_ids(near.shape) < PANEL
        rows_here = slice(start, start + block)
        terms_ref[rows_here, :LANES] = far_top.astype(BF16)
        terms_ref[rows_here, LANES : 2 * LANES] = (far - far_top * 256.0).astype(BF16)
        terms_ref[rows_here, 2 * LANES : 3 * LANES] = jnp.where(low_lanes, near_top, near_middle).astype(BF16)
        terms_ref[rows_here, 3 * LANES :] = jnp.where(low_lanes, near - near_middle * 256.0, exponent).astype(BF16)


    def coded(start, size):
        got = jnp.dot(picks_ref[start : start + size, :], terms_ref[...], preferred_element_type=F32)
        far = got[:, :LANES] * 256.0 + got[:, LANES : 2 * LANES]
        tops, lows = got[:, 2 * LANES : 3 * LANES], got[:, 3 * LANES :]
        low_lanes = lane_ids(tops.shape) < PANEL
        tops = tops * jnp.where(low_lanes, 65536.0, 256.0)
        swapped = swap_halves(lows)
        near = tops + swap_halves(tops) + jnp.where(low_lanes, lows, swapped)
        exponent = jnp.where(low_lanes, swapped, lows)
        near = near.astype(jnp.int32) * 256 + (exponent.astype(jnp.int32) + BIAS)
        return far.astype(jnp.int32), near

    half = rows // 2
    block = half // 2
    for start in range(0, half, block):
        far_low, near_low = coded(start, block)
        far_high, near_high = coded(half + start, block)
        out_ref[start : start + block, :LANES] = far_low * 65536 + (far_high & 65535)
        out_ref[start : start + block, LANES:] = jnp.where(lane_ids(near_low.shape) < PANEL, near_low, near_high)


def rest_products(my_index, order, a_rows, parts, offsets, share):
    rows, depth = a_rows.shape
    return pl.pallas_call(
        functools.partial(rest_product_kernel, offsets, share),
        in_specs=[
            pl.BlockSpec(memory_space=pltpu.SMEM),
            pl.BlockSpec(memory_space=pltpu.VMEM),
            pl.BlockSpec(memory_space=pltpu.HBM),
        ]
        + [pl.BlockSpec(memory_space=pl.ANY)] * len(parts),
        out_specs=pl.BlockSpec(memory_space=pltpu.VMEM),
        out_shape=jax.ShapeDtypeStruct((rows // 2, 2 * LANES), jnp.int32),
        scratch_shapes=[
            pltpu.VMEM((rows, depth), BF16),
            pltpu.VMEM((rows, LANES), jnp.int32),
            pltpu.VMEM((rows, rows), BF16),
            pltpu.VMEM((depth, 3 * LANES), BF16),
            pltpu.VMEM((rows, 4 * LANES), BF16),
            pltpu.SemaphoreType.DMA((rows // A_BLOCK,)),
            pltpu.SemaphoreType.DMA((len(offsets),)),
        ],
        compiler_params=params(32),
        cost_estimate=pl.CostEstimate(
            flops=2 * rows * (3 * depth + 4 * rows) * LANES, bytes_accessed=2 * rows * depth, transcendentals=0
        ),
        name="rest_products",
    )(my_index, order, in_hbm(a_rows), *parts)


def packed_terms(x, terms_ref, start):
    half = x.shape[0]
    first, second, third = (term.astype(F32) for term in split(x, 3))
    near = lane_ids(x.shape) < PANEL
    other = swap_halves(third)
    terms_ref[:half, start : start + LANES] = jnp.where(near, first, swap_halves(second)).astype(BF16)
    terms_ref[half:, start : start + LANES] = jnp.where(near, swap_halves(first), second).astype(BF16)
    terms_ref[:half, start + LANES : start + 2 * LANES] = jnp.where(near, third, other).astype(BF16)
    terms_ref[half:, start + LANES : start + 2 * LANES] = jnp.where(near, other, third).astype(BF16)


def leading_kernel(held, index_ref, arrived_ref, out_ref, terms_ref):
    packed_terms(arrived_ref[...], terms_ref, 0)
    width = -(-held // LANES) * LANES
    picks = one_hot(index_ref[:, :width], terms_ref.shape[0])
    got = whole_sum(jnp.dot(picks, terms_ref[...], preferred_element_type=F32))
    first, second = got[: held // 2], got[held // 2 : held]
    out_ref[0] = jnp.where(lane_ids(first.shape) < PANEL, first, second)


def leading_rows(index, arrived, held):
    rows = index.shape[1]
    return pl.pallas_call(
        functools.partial(leading_kernel, held),
        in_specs=[pl.BlockSpec(memory_space=pltpu.VMEM)] * 2,
        out_specs=pl.BlockSpec(memory_space=pltpu.VMEM),
        out_shape=jax.ShapeDtypeStruct((1, held // 2, LANES), F32),
        scratch_shapes=[pltpu.VMEM((rows, 2 * LANES), BF16)],
        compiler_params=params(),
        cost_estimate=pl.CostEstimate(
            flops=4 * held * rows * LANES, bytes_accessed=2 * rows * LANES, transcendentals=0
        ),
        name="leading_rows",
    )(index, arrived)


def eliminate(block, shift_row):
    rows = lax.broadcasted_iota(jnp.int32, (PANEL, PANEL), 0)
    columns = lax.broadcasted_iota(jnp.int32, (PANEL, PANEL), 1)
    flipped = jnp.transpose(block)
    mirrored = jnp.where(rows >= columns, block, flipped)
    diagonal = shift_row + jnp.sum(jnp.abs(mirrored), axis=0, keepdims=True)
    unit = (rows == columns).astype(F32)
    work = jnp.where(rows == columns, diagonal, mirrored)
    work = jnp.concatenate([work, unit], axis=1)
    height = 8
    groups = [work[start : start + height] for start in range(0, PANEL, height)]
    sublanes = lax.broadcasted_iota(jnp.int32, (height, LANES), 0)
    scaled_rows = []
    for k in range(PANEL):
        home, offset = divmod(k, height)
        row = groups[home][offset : offset + 1, :]
        row = row / row[:, k : k + 1]
        scaled_rows.append(row)
        for g in range(home, PANEL // height):
            column = jnp.broadcast_to(groups[g][:, k : k + 1], (height, LANES))
            if g == home:
                column = jnp.where(sublanes > offset, column, 0.0)
            groups[g] = groups[g] - column * row
    final = jnp.concatenate(groups, axis=0)
    scaled = jnp.concatenate(scaled_rows, axis=0)
    upper = jnp.where(columns >= rows, scaled[:, :PANEL], 0.0)
    pivots = jnp.sum(jnp.where(rows == columns, final[:, :PANEL], 0.0), axis=0, keepdims=True)
    return upper, final[:, PANEL:], pivots


def exact(lhs, rhs, dims):
    return lax.dot_general(lhs, rhs, (dims, ((), ())), precision=lax.Precision.HIGHEST, preferred_element_type=F32)


def update_kernel(offsets, blocks_held, columns, my_ref, index_ref, arrived_ref, shift_ref, resident_hbm, *refs):
    parts = refs[:-12]
    near_hbm, far_hbm, pivots_ref, leading_ref, tail_ref, resident_ref, terms_ref, lead_ref = refs[-12:-4]
    near_ref, far_ref, sem, sems = refs[-4:]
    fetch = pltpu.make_async_copy(resident_hbm, resident_ref, sem)
    fetch.start()
    my_index = my_ref[0]
    size = len(offsets)
    position = 0
    packed = blocks_held * PANEL // 2
    part_rows = PANEL // 2
    for part in parts:
        for number in range(part.shape[0]):
            owner = my_index ^ offsets[position]
            for start in range(0, blocks_held * PANEL, part_rows):
                held, inner = divmod(start, PANEL)
                if start < packed:
                    rows = part[number, start : start + part_rows, :PANEL]
                else:
                    rows = part[number, start - packed : start - packed + part_rows, PANEL:]
                target = pl.multiple_of((held * size + owner) * PANEL + inner, part_rows)
                leading_ref[pl.ds(target, part_rows), :] = rows
            position += 1
    upper, inverse, pivots = eliminate(leading_ref[:PANEL, :], shift_ref[...])
    pivots_ref[...] = pivots
    lower = jnp.transpose(upper)
    needed = tail_ref.shape[1]
    tail = exact(inverse, leading_ref[:needed, :], ((1,), (1,)))
    high, low = split(tail, 2)
    tail_ref[0:PANEL, :] = high
    tail_ref[PANEL : 2 * PANEL, :] = high
    tail_ref[2 * PANEL : 3 * PANEL, :] = low
    tail_ref[3 * PANEL :, :] = low

    block = A_BLOCK
    packed_terms(arrived_ref[...], terms_ref, 0)
    for start in range(0, lead_ref.shape[0], block):
        picks = one_hot(index_ref[:, start : start + block], lead_ref.shape[0])
        got = jnp.dot(picks, terms_ref[...], preferred_element_type=F32)
        lead_ref[start : start + block, :] = whole_sum(got)[:, :PANEL]
    fetch.wait()
    stores = []
    for number, start in enumerate(range(0, lead_ref.shape[0], block)):
        rows_here = slice(start, start + block)
        panel = exact(lead_ref[rows_here, :], inverse, ((1,), (1,))) / pivots
        shown = used = panel
        if start == 0:
            row_ids = lax.broadcasted_iota(jnp.int32, panel.shape, 0)
            top = jnp.logical_and(my_index == 0, row_ids < PANEL)
            used = jnp.where(top, 0.0, panel)
            filled = jnp.concatenate([lower, jnp.zeros((block - PANEL, PANEL), F32)], axis=0)
            shown = jnp.where(top, filled, panel)
        high, low = (term.astype(F32) for term in split(used, 2))
        pair = jnp.concatenate([high, low], axis=1).astype(BF16)
        factors = jnp.concatenate([pair, pair], axis=1)
        update = jnp.dot(factors, tail_ref[...], preferred_element_type=F32)
        shown = jnp.concatenate([shown, jnp.zeros_like(shown)], axis=1)
        near_ref[rows_here, :LANES] = jnp.where(lane_ids(shown.shape) < PANEL, shown, -update[:, :LANES])
        near_ref[rows_here, LANES:] = -update[:, LANES:columns]
        far_ref[rows_here, :] = (resident_ref[rows_here, :].astype(F32) - update[:, columns:]).astype(BF16)
        for which, (source, target) in enumerate(((near_ref, near_hbm), (far_ref, far_hbm))):
            store = pltpu.make_async_copy(
                source.at[pl.ds(start, block), :], target.at[pl.ds(start, block), :], sems.at[which, number]
            )
            store.start()
            stores.append(store)
    for store in stores:
        store.wait()


def updates(my_index, parts, offsets, index, arrived, shift, resident, blocks_held, columns):
    rows, width = resident.shape
    needed = columns + width
    held_rows = len(offsets) * blocks_held * PANEL
    vmem = pl.BlockSpec(memory_space=pltpu.VMEM)
    anywhere = pl.BlockSpec(memory_space=pltpu.HBM)
    return pl.pallas_call(
        functools.partial(update_kernel, offsets, blocks_held, columns),
        in_specs=[pl.BlockSpec(memory_space=pltpu.SMEM), vmem, vmem, vmem, anywhere] + [vmem] * len(parts),
        out_specs=[anywhere, anywhere, vmem],
        out_shape=[
            pltpu.HBM((rows, columns), F32),
            pltpu.HBM((rows, width), BF16),
            jax.ShapeDtypeStruct((1, PANEL), F32),
        ],
        scratch_shapes=[
            pltpu.VMEM((held_rows, PANEL), F32),
            pltpu.VMEM((4 * PANEL, needed), BF16),
            pltpu.VMEM((rows, width), BF16),
            pltpu.VMEM((rows, 2 * LANES), BF16),
            pltpu.VMEM((rows, PANEL), F32),
            pltpu.VMEM((rows, columns), F32),
            pltpu.VMEM((rows, width), BF16),
            pltpu.SemaphoreType.DMA,
            pltpu.SemaphoreType.DMA((2, rows // A_BLOCK)),
        ],
        compiler_params=params(32),
        cost_estimate=pl.CostEstimate(
            flops=2 * rows * needed * 4 * PANEL, bytes_accessed=4 * rows * (columns + width), transcendentals=0
        ),
        name="factor_and_update",
    )(my_index, index, arrived, shift, in_hbm(resident), *parts)


def formed_kernel(index_ref, arrived_ref, near_hbm, out_hbm, near_ref, terms_ref, out_ref, in_sems, out_sems):
    half = arrived_ref.shape[0]
    block = A_BLOCK
    starts = range(0, near_ref.shape[0], block)

    def rows_of(ref, start):
        return ref.at[pl.ds(start, block), :]

    fetches = [
        pltpu.make_async_copy(rows_of(near_hbm, start), rows_of(near_ref, start), in_sems.at[i])
        for i, start in enumerate(starts)
    ]
    for fetch in fetches:
        fetch.start()
    words = arrived_ref[:, LANES:]
    low_lanes = lane_ids(words.shape) < PANEL
    exponent = ((words & 255) - BIAS).astype(F32)
    scale = jnp.exp2(exponent - 15.0)
    other = swap_halves(scale)
    packed_terms((words >> 8).astype(F32) * (scale * (1 / 256)), terms_ref, 2 * LANES)
    words = arrived_ref[:, :LANES]
    low = (words >> 16).astype(F32) * jnp.where(low_lanes, scale, other)
    high = ((words << 16) >> 16).astype(F32) * jnp.where(low_lanes, other, scale)
    for side, values in enumerate((low, high)):
        first, second = split(values, 2)
        terms_ref[side * half : (side + 1) * half, :LANES] = first
        terms_ref[side * half : (side + 1) * half, LANES : 2 * LANES] = second

    stores = []
    for i, start in enumerate(starts):
        rows_here = slice(start, start + block)
        picks = one_hot(index_ref[:, rows_here], terms_ref.shape[0])
        got = jnp.dot(picks, terms_ref[...], preferred_element_type=F32)
        narrow = whole_sum(got[:, 2 * LANES :])
        fetches[i].wait()
        held = near_ref[rows_here, :LANES]
        out_ref[rows_here, :LANES] = jnp.where(lane_ids(held.shape) < PANEL, held, narrow + held)
        out_ref[rows_here, LANES:] = (got[:, :LANES] + got[:, LANES : 2 * LANES]) + near_ref[rows_here, LANES:]
        store = pltpu.make_async_copy(rows_of(out_ref, start), rows_of(out_hbm, start), out_sems.at[i])
        store.start()
        stores.append(store)
    for store in stores:
        store.wait()


def formed_columns(index, arrived, near):
    rows, columns = near.shape
    vmem = pl.BlockSpec(memory_space=pltpu.VMEM)
    anywhere = pl.BlockSpec(memory_space=pltpu.HBM)
    return pl.pallas_call(
        formed_kernel,
        in_specs=[vmem, vmem, anywhere],
        out_specs=anywhere,
        out_shape=pltpu.HBM((rows, columns), F32),
        input_output_aliases={2: 0},
        scratch_shapes=[
            pltpu.VMEM((rows, columns), F32),
            pltpu.VMEM((rows, 4 * LANES), BF16),
            pltpu.VMEM((rows, columns), F32),
            pltpu.SemaphoreType.DMA((rows // A_BLOCK,)),
            pltpu.SemaphoreType.DMA((rows // A_BLOCK,)),
        ],
        compiler_params=params(32),
        cost_estimate=pl.CostEstimate(
            flops=8 * rows * rows * LANES, bytes_accessed=8 * rows * columns, transcendentals=0
        ),
        name="formed_columns",
    )(index, arrived, near)


def swap_rows(x, group):
    rows, width = x.shape
    return lax.all_to_all(
        x.reshape(group, rows // group, width), "wide", split_axis=0, concat_axis=0, tiled=True
    ).reshape(rows, width)


def on_device(a_rows, xa_panel, za_panel, send_order, recv_order, shift, resident):
    rows = a_rows.shape[0]
    columns = xa_panel.shape[1]
    group = lax.axis_size("wide")
    my_index = lax.axis_index("wide").astype(jnp.int32).reshape(1)
    share = rows // group
    half = rows // 2
    few, apart = phases_of(group)

    order, packing = send_order, share
    if share % 16:
        order = send_order.reshape(group, 2, share // 2).transpose(1, 0, 2).reshape(1, rows)
        packing = 0
    source, slot = recv_order // share, recv_order % share
    index = (slot // (share // 2)) * half + source * (share // 2) + slot % (share // 2)

    lead_panel, rest_panel = split_panels(my_index, xa_panel, za_panel)
    send_picks, a_copy = order_picks(order, a_rows, packing)
    lead_parts = [lead_panel]
    for masks in few:
        lead_parts = exchange(join(lead_parts), masks, "wide")
    rest_parts = [rest_panel]
    for number, masks in enumerate(apart[:-2]):
        rest_parts = exchange(join(rest_parts), masks, "wide")
        if number == 0:
            lead_parts = tied(lead_parts, *rest_parts)

    lead_out = lead_products(my_index, a_copy, send_picks, lead_parts, offsets_of(few))
    lead_in = swap_rows(tied([lead_out], *rest_parts)[0], group)
    rest_parts = exchange(join(tied(rest_parts, lead_out)), apart[-2], "wide")

    needed = columns + resident.shape[1]
    blocks_held = -(-needed // (PANEL * group))
    leading_parts = [leading_rows(index, lead_in, blocks_held * PANEL)]
    for masks in few:
        leading_parts = exchange(join(leading_parts), masks, "wide")
        if masks is few[0]:
            rest_parts = exchange(tied(rest_parts, *leading_parts), apart[-1], "wide")
    rest_out = rest_products(my_index, order, a_rows, rest_parts, offsets_of(apart), packing)
    rest_in = swap_rows(tied([rest_out], *leading_parts)[0], group)
    near, updated, pivots = updates(
        my_index,
        leading_parts,
        offsets_of(few),
        index,
        tied([lead_in], rest_out)[0],
        shift[None, :],
        resident,
        blocks_held,
        columns,
    )
    factored = formed_columns(index, rest_in, near)
    return (factored, updated, pivots[0])


def solution(mesh):
    placed = (
        P(("parts", "wide"), None),
        P(("parts", "wide"), None),
        P(("parts", "wide"), None),
        P(("parts", "wide"), None),
        P(("parts", "wide"), None),
        P("parts"),
        P(("parts", "wide"), None),
    )
    return jax.shard_map(
        on_device,
        mesh=mesh,
        in_specs=placed,
        out_specs=(P(("parts", "wide"), None), P(("parts", "wide"), None), P("parts")),
        check_vma=False,
    )
```

```python
import functools

import jax
import jax.numpy as jnp
from jax import lax
from jax.experimental import pallas as pl
from jax.experimental.pallas import tpu as pltpu
from jax.sharding import PartitionSpec as P

PANEL = 64
LANES = 128
A_BLOCK = 640
CHUNK = 64
STORE_BLOCK = 256
F32 = jnp.float32
BF16 = jnp.bfloat16
MIB = 1024 * 1024


def params(mebibytes=12):
    return pltpu.CompilerParams(vmem_limit_bytes=mebibytes * MIB)


def in_hbm(x):
    return pltpu.with_memory_space_constraint(x, pltpu.HBM)


def lane_ids(shape):
    return lax.broadcasted_iota(jnp.int32, shape, len(shape) - 1)


def split(x, count):
    terms = []
    for _ in range(count):
        term = x.astype(BF16)
        terms.append(term)
        x = x - term.astype(F32)
    return terms


def swap_halves(x):
    return pltpu.roll(x, LANES // 2, 1)


def as_column(index_row):
    return jnp.transpose(jnp.broadcast_to(index_row, (LANES, LANES)))


def picks_of(at, width):
    lanes = lane_ids(at.shape)
    return jnp.concatenate(
        [(at == lanes + column).astype(F32).astype(BF16) for column in range(0, width, LANES)], axis=1
    )


def fill_picks(at_ref, picks_ref):
    rows, width = picks_ref.shape
    for start in range(0, rows, LANES):
        picks_ref[start : start + LANES, :] = picks_of(at_ref[start : start + LANES, :], width)


def one_hot(index_row, width):
    chunks = [
        picks_of(as_column(index_row[:, start : start + LANES]), width)
        for start in range(0, index_row.shape[1], LANES)
    ]
    return jnp.concatenate(chunks, axis=0) if len(chunks) > 1 else chunks[0]


def packed_order(share, half, slot):
    part = share // 2
    return (slot % share) // part * half + slot // share * part + slot % part


def fill_order(order_ref, at_ref, share):
    rows = order_ref.shape[1]
    height = 8
    for start in range(0, rows, LANES):
        column = as_column(order_ref[:, start : start + LANES])
        if not share:
            at_ref[start : start + LANES, :] = column
            continue
        for inner in range(0, LANES, height):
            place = packed_order(share, rows // 2, start + inner)
            at_ref[place : place + height, :] = column[inner : inner + height]


def exchange(held, masks, axis):
    size = lax.axis_size(axis)
    combined = [0]
    for mask in masks:
        combined += [other ^ mask for other in combined]
    parts = list(held)
    for mask in combined[1:]:
        parts += [lax.ppermute(part, axis, [(i, i ^ mask) for i in range(size)]) for part in held]
    return parts


def offsets_of(phases):
    offsets = [0]
    for masks in phases:
        combined = [0]
        for mask in masks:
            combined += [other ^ mask for other in combined]
        offsets = [offset ^ mask for mask in combined for offset in offsets]
    return offsets


def join(parts):
    return [jnp.concatenate(parts, axis=0)]


def phases_of(size):
    bits = [1 << bit for bit in reversed(range(size.bit_length() - 1))]
    return [bits[start : start + 2] for start in range(0, len(bits), 2)], [[bit] for bit in bits]


def tied(parts, *earlier):
    return list(lax.optimization_barrier((*parts, *earlier))[: len(parts)])


def picks_kernel(share, order_hbm, a_hbm, picks_ref, copy_ref, order_ref, at_ref, sems):
    fetch = pltpu.make_async_copy(order_hbm, order_ref, sems.at[0])
    copy = pltpu.make_async_copy(a_hbm, copy_ref, sems.at[1])
    fetch.start()
    copy.start()
    fetch.wait()
    fill_order(order_ref, at_ref, share)
    fill_picks(at_ref, picks_ref)
    copy.wait()


def order_picks(order, a_rows, share):
    rows, depth = a_rows.shape
    return pl.pallas_call(
        functools.partial(picks_kernel, share),
        in_specs=[pl.BlockSpec(memory_space=pltpu.HBM)] * 2,
        out_specs=[pl.BlockSpec(memory_space=pltpu.VMEM)] * 2,
        out_shape=[jax.ShapeDtypeStruct((rows, rows), BF16), jax.ShapeDtypeStruct((rows, depth), BF16)],
        scratch_shapes=[
            pltpu.VMEM((1, rows), jnp.int32),
            pltpu.VMEM((rows, LANES), jnp.int32),
            pltpu.SemaphoreType.DMA((2,)),
        ],
        compiler_params=params(),
        cost_estimate=pl.CostEstimate(flops=4 * rows * rows, bytes_accessed=4 * rows * depth, transcendentals=0),
        name="order_picks",
    )(in_hbm(order), in_hbm(a_rows))


def panels_kernel(my_ref, xa_hbm, za_hbm, lead_ref, rest_ref, xa_ref, za_ref, sems):
    copies = [
        pltpu.make_async_copy(xa_hbm, xa_ref, sems.at[0]),
        pltpu.make_async_copy(za_hbm, za_ref, sems.at[1]),
    ]
    for copy in copies:
        copy.start()
    for copy in copies:
        copy.wait()
    lead_ref[0] = jnp.concatenate([xa_ref[:, :PANEL], za_ref[:, :PANEL]], axis=1)
    rest_ref[0, :, :LANES] = jnp.concatenate([xa_ref[:, PANEL:LANES], za_ref[:, PANEL:LANES]], axis=1)
    rest_ref[0, :, LANES : 2 * LANES] = xa_ref[:, LANES:]
    rest_ref[0, :, 2 * LANES :] = za_ref[:, LANES:]


def split_panels(my_index, xa_panel, za_panel):
    depth, columns = xa_panel.shape
    return pl.pallas_call(
        panels_kernel,
        in_specs=[pl.BlockSpec(memory_space=pltpu.SMEM)] + [pl.BlockSpec(memory_space=pltpu.HBM)] * 2,
        out_shape=[
            jax.ShapeDtypeStruct((1, depth, LANES), BF16),
            jax.ShapeDtypeStruct((1, depth, 2 * columns - LANES), BF16),
        ],
        scratch_shapes=[
            pltpu.VMEM((depth, columns), BF16),
            pltpu.VMEM((depth, columns), BF16),
            pltpu.SemaphoreType.DMA((2,)),
        ],
        compiler_params=params(),
        name="split_panels",
    )(my_index, in_hbm(xa_panel), in_hbm(za_panel))


def assemble(my_index, offsets, parts, panel_ref):
    position = 0
    for part in parts:
        for number in range(part.shape[0]):
            depth = part.shape[1]
            start = pl.multiple_of((my_index ^ offsets[position]) * depth, depth)
            panel_ref[pl.ds(start, depth), :] = part[number]
            position += 1


def whole_sum(got):
    pair = got[:, :LANES]
    return (pair + swap_halves(pair)) + got[:, LANES:]


def lead_product_kernel(offsets, my_ref, a_ref, picks_ref, *refs):
    parts, (out_ref, panel_ref, terms_ref, both_ref, got_ref) = refs[:-5], refs[-5:]
    assemble(my_ref[0], offsets, parts, panel_ref)
    rows = a_ref.shape[0]
    half = rows // 2
    near = lane_ids((CHUNK, LANES)) < PANEL
    both_ref[...] = jnp.dot(a_ref[...], panel_ref[...], preferred_element_type=F32)
    for start in range(0, rows, CHUNK):
        here = slice(start, start + CHUNK)
        both = both_ref[here, :]
        first, second, third = (term.astype(F32) for term in split(both * swap_halves(both), 3))
        terms_ref[here, :LANES] = jnp.where(near, first, second).astype(BF16)
        terms_ref[here, LANES:] = third.astype(BF16)
    got_ref[...] = jnp.dot(picks_ref[...], terms_ref[...], preferred_element_type=F32)
    for start in range(0, half, CHUNK):
        low = whole_sum(got_ref[start : start + CHUNK, :])
        high = whole_sum(got_ref[half + start : half + start + CHUNK, :])
        out_ref[start : start + CHUNK, :] = jnp.where(near, low, high)


def lead_products(my_index, a_rows, picks, parts, offsets):
    rows, depth = a_rows.shape
    return pl.pallas_call(
        functools.partial(lead_product_kernel, offsets),
        in_specs=[pl.BlockSpec(memory_space=pltpu.SMEM)] + [pl.BlockSpec(memory_space=pltpu.VMEM)] * (2 + len(parts)),
        out_specs=pl.BlockSpec(memory_space=pltpu.VMEM),
        out_shape=jax.ShapeDtypeStruct((rows // 2, LANES), F32),
        scratch_shapes=[
            pltpu.VMEM((depth, LANES), BF16),
            pltpu.VMEM((rows, 2 * LANES), BF16),
            pltpu.VMEM((rows, LANES), F32),
            pltpu.VMEM((rows, 2 * LANES), F32),
        ],
        compiler_params=params(),
        cost_estimate=pl.CostEstimate(
            flops=2 * rows * (depth + 2 * rows) * LANES, bytes_accessed=2 * rows * depth, transcendentals=0
        ),
        name="lead_products",
    )(my_index, a_rows, picks, *parts)


BIAS = 128


def rest_product_kernel(offsets, share, my_ref, order_ref, a_hbm, *refs):
    parts, refs = refs[:-10], refs[-10:]
    out_ref, a_ref, at_ref, picks_ref, panel_ref, terms_ref, both_ref, got_ref, sems, part_sems = refs
    rows = a_ref.shape[0]
    half = rows // 2
    starts = range(0, rows, A_BLOCK)
    copies = [
        pltpu.make_async_copy(a_hbm.at[pl.ds(start, A_BLOCK), :], a_ref.at[pl.ds(start, A_BLOCK), :], sems.at[i])
        for i, start in enumerate(starts)
    ]
    fetches = []
    for part in parts:
        for number in range(part.shape[0]):
            depth = part.shape[1]
            position = len(fetches)
            place = pl.multiple_of((my_ref[0] ^ offsets[position]) * depth, depth)
            fetches.append(
                pltpu.make_async_copy(part.at[number], panel_ref.at[pl.ds(place, depth), :], part_sems.at[position])
            )
    for copy in fetches + copies:
        copy.start()
    fill_order(order_ref, at_ref, share)
    fill_picks(at_ref, picks_ref)
    for copy in fetches:
        copy.wait()
    for copy, start in zip(copies, starts):
        copy.wait()
        both_ref[start : start + A_BLOCK, :] = jnp.dot(
            a_ref[start : start + A_BLOCK, :], panel_ref[...], preferred_element_type=F32
        )
    low_lanes = lane_ids((CHUNK, LANES)) < PANEL
    for start in range(0, rows, CHUNK):
        here = slice(start, start + CHUNK)
        near = both_ref[here, :LANES]
        near = near * swap_halves(near)
        far = both_ref[here, LANES : 2 * LANES] * both_ref[here, 2 * LANES :]
        largest = jnp.max(jnp.maximum(jnp.abs(near), jnp.abs(far)), axis=1, keepdims=True)
        largest = jnp.maximum(largest, 1e-30)
        exponent = jnp.floor(jnp.log2(largest)) + 1.0
        scale = jnp.exp2(15.0 - exponent)
        far = jnp.floor(far * scale + 0.5)
        far = jnp.minimum(jnp.maximum(far, -32767.0), 32767.0)
        near = jnp.floor(near * (scale * 256.0) + 0.5)
        near = jnp.minimum(jnp.maximum(near, -8388607.0), 8388607.0)
        far_top = jnp.floor(far * (1 / 256))
        near_top = jnp.floor(near * (1 / 65536))
        near = near - near_top * 65536.0
        near_middle = jnp.floor(near * (1 / 256))
        terms_ref[here, :LANES] = far_top.astype(BF16)
        terms_ref[here, LANES : 2 * LANES] = (far - far_top * 256.0).astype(BF16)
        terms_ref[here, 2 * LANES : 3 * LANES] = jnp.where(low_lanes, near_top, near_middle).astype(BF16)
        terms_ref[here, 3 * LANES :] = jnp.where(low_lanes, near - near_middle * 256.0, exponent).astype(BF16)
    got_ref[...] = jnp.dot(picks_ref[...], terms_ref[...], preferred_element_type=F32)

    def coded(start):
        here = slice(start, start + CHUNK)
        far = got_ref[here, :LANES] * 256.0 + got_ref[here, LANES : 2 * LANES]
        tops, lows = got_ref[here, 2 * LANES : 3 * LANES], got_ref[here, 3 * LANES :]
        tops = tops * jnp.where(low_lanes, 65536.0, 256.0)
        swapped = swap_halves(lows)
        near = tops + swap_halves(tops) + jnp.where(low_lanes, lows, swapped)
        exponent = jnp.where(low_lanes, swapped, lows)
        near = near.astype(jnp.int32) * 256 + (exponent.astype(jnp.int32) + BIAS)
        return far.astype(jnp.int32), near

    for start in range(0, half, CHUNK):
        far_low, near_low = coded(start)
        far_high, near_high = coded(half + start)
        out_ref[start : start + CHUNK, :LANES] = far_low * 65536 + (far_high & 65535)
        out_ref[start : start + CHUNK, LANES:] = jnp.where(low_lanes, near_low, near_high)


def rest_products(my_index, order, a_rows, parts, offsets, share):
    rows, depth = a_rows.shape
    return pl.pallas_call(
        functools.partial(rest_product_kernel, offsets, share),
        in_specs=[
            pl.BlockSpec(memory_space=pltpu.SMEM),
            pl.BlockSpec(memory_space=pltpu.VMEM),
            pl.BlockSpec(memory_space=pltpu.HBM),
        ]
        + [pl.BlockSpec(memory_space=pl.ANY)] * len(parts),
        out_specs=pl.BlockSpec(memory_space=pltpu.VMEM),
        out_shape=jax.ShapeDtypeStruct((rows // 2, 2 * LANES), jnp.int32),
        scratch_shapes=[
            pltpu.VMEM((rows, depth), BF16),
            pltpu.VMEM((rows, LANES), jnp.int32),
            pltpu.VMEM((rows, rows), BF16),
            pltpu.VMEM((depth, 3 * LANES), BF16),
            pltpu.VMEM((rows, 4 * LANES), BF16),
            pltpu.VMEM((rows, 3 * LANES), F32),
            pltpu.VMEM((rows, 4 * LANES), F32),
            pltpu.SemaphoreType.DMA((rows // A_BLOCK,)),
            pltpu.SemaphoreType.DMA((len(offsets),)),
        ],
        compiler_params=params(32),
        cost_estimate=pl.CostEstimate(
            flops=2 * rows * (3 * depth + 4 * rows) * LANES, bytes_accessed=2 * rows * depth, transcendentals=0
        ),
        name="rest_products",
    )(my_index, order, in_hbm(a_rows), *parts)


def packed_terms(x, terms_ref, place, start):
    half = terms_ref.shape[0] // 2
    first, second, third = (term.astype(F32) for term in split(x, 3))
    near = lane_ids(x.shape) < PANEL
    other = swap_halves(third)
    low = slice(place, place + x.shape[0])
    high = slice(half + place, half + place + x.shape[0])
    terms_ref[low, start : start + LANES] = jnp.where(near, first, swap_halves(second)).astype(BF16)
    terms_ref[high, start : start + LANES] = jnp.where(near, swap_halves(first), second).astype(BF16)
    terms_ref[low, start + LANES : start + 2 * LANES] = jnp.where(near, third, other).astype(BF16)
    terms_ref[high, start + LANES : start + 2 * LANES] = jnp.where(near, other, third).astype(BF16)


def arrived_terms(arrived_ref, terms_ref):
    for place in range(0, arrived_ref.shape[0], CHUNK):
        packed_terms(arrived_ref[place : place + CHUNK, :], terms_ref, place, 0)


def leading_kernel(held, index_ref, arrived_ref, out_ref, terms_ref):
    arrived_terms(arrived_ref, terms_ref)
    width = -(-held // LANES) * LANES
    picks = one_hot(index_ref[:, :width], terms_ref.shape[0])
    got = whole_sum(jnp.dot(picks, terms_ref[...], preferred_element_type=F32))
    first, second = got[: held // 2], got[held // 2 : held]
    out_ref[0] = jnp.where(lane_ids(first.shape) < PANEL, first, second)


def leading_rows(index, arrived, held):
    rows = index.shape[1]
    return pl.pallas_call(
        functools.partial(leading_kernel, held),
        in_specs=[pl.BlockSpec(memory_space=pltpu.VMEM)] * 2,
        out_specs=pl.BlockSpec(memory_space=pltpu.VMEM),
        out_shape=jax.ShapeDtypeStruct((1, held // 2, LANES), F32),
        scratch_shapes=[pltpu.VMEM((rows, 2 * LANES), BF16)],
        compiler_params=params(),
        cost_estimate=pl.CostEstimate(
            flops=4 * held * rows * LANES, bytes_accessed=2 * rows * LANES, transcendentals=0
        ),
        name="leading_rows",
    )(index, arrived)


def eliminate(block, shift_row):
    rows = lax.broadcasted_iota(jnp.int32, (PANEL, PANEL), 0)
    columns = lax.broadcasted_iota(jnp.int32, (PANEL, PANEL), 1)
    flipped = jnp.transpose(block)
    mirrored = jnp.where(rows >= columns, block, flipped)
    diagonal = shift_row + jnp.sum(jnp.abs(mirrored), axis=0, keepdims=True)
    unit = (rows == columns).astype(F32)
    work = jnp.where(rows == columns, diagonal, mirrored)
    work = jnp.concatenate([work, unit], axis=1)
    height = 8
    groups = [work[start : start + height] for start in range(0, PANEL, height)]
    sublanes = lax.broadcasted_iota(jnp.int32, (height, LANES), 0)
    scaled_rows = []
    for k in range(PANEL):
        home, offset = divmod(k, height)
        row = groups[home][offset : offset + 1, :]
        row = row / row[:, k : k + 1]
        scaled_rows.append(row)
        for g in range(home, PANEL // height):
            column = jnp.broadcast_to(groups[g][:, k : k + 1], (height, LANES))
            if g == home:
                column = jnp.where(sublanes > offset, column, 0.0)
            groups[g] = groups[g] - column * row
    final = jnp.concatenate(groups, axis=0)
    scaled = jnp.concatenate(scaled_rows, axis=0)
    upper = jnp.where(columns >= rows, scaled[:, :PANEL], 0.0)
    pivots = jnp.sum(jnp.where(rows == columns, final[:, :PANEL], 0.0), axis=0, keepdims=True)
    return upper, final[:, PANEL:], pivots


def exact(lhs, rhs, dims):
    return lax.dot_general(lhs, rhs, (dims, ((), ())), precision=lax.Precision.HIGHEST, preferred_element_type=F32)


def update_kernel(offsets, blocks_held, columns, my_ref, index_ref, arrived_ref, shift_ref, resident_hbm, *refs):
    parts = refs[:-12]
    near_hbm, far_hbm, pivots_ref, leading_ref, tail_ref, resident_ref, terms_ref, lead_ref = refs[-12:-4]
    near_ref, far_ref, sem, sems = refs[-4:]
    fetch = pltpu.make_async_copy(resident_hbm, resident_ref, sem)
    fetch.start()
    my_index = my_ref[0]
    size = len(offsets)
    position = 0
    packed = blocks_held * PANEL // 2
    part_rows = PANEL // 2
    for part in parts:
        for number in range(part.shape[0]):
            owner = my_index ^ offsets[position]
            for start in range(0, blocks_held * PANEL, part_rows):
                held, inner = divmod(start, PANEL)
                if start < packed:
                    rows = part[number, start : start + part_rows, :PANEL]
                else:
                    rows = part[number, start - packed : start - packed + part_rows, PANEL:]
                target = pl.multiple_of((held * size + owner) * PANEL + inner, part_rows)
                leading_ref[pl.ds(target, part_rows), :] = rows
            position += 1
    upper, inverse, pivots = eliminate(leading_ref[:PANEL, :], shift_ref[...])
    pivots_ref[...] = pivots
    lower = jnp.transpose(upper)
    needed = tail_ref.shape[1]
    tail = exact(inverse, leading_ref[:needed, :], ((1,), (1,)))
    high, low = split(tail, 2)
    tail_ref[0:PANEL, :] = high
    tail_ref[PANEL : 2 * PANEL, :] = high
    tail_ref[2 * PANEL : 3 * PANEL, :] = low
    tail_ref[3 * PANEL :, :] = low

    block = A_BLOCK
    arrived_terms(arrived_ref, terms_ref)
    for start in range(0, lead_ref.shape[0], block):
        picks = one_hot(index_ref[:, start : start + block], lead_ref.shape[0])
        got = jnp.dot(picks, terms_ref[...], preferred_element_type=F32)
        lead_ref[start : start + block, :] = whole_sum(got)[:, :PANEL]
    fetch.wait()
    stores = []
    for number, start in enumerate(range(0, lead_ref.shape[0], block)):
        rows_here = slice(start, start + block)
        panel = exact(lead_ref[rows_here, :], inverse, ((1,), (1,))) / pivots
        shown = used = panel
        if start == 0:
            row_ids = lax.broadcasted_iota(jnp.int32, panel.shape, 0)
            top = jnp.logical_and(my_index == 0, row_ids < PANEL)
            used = jnp.where(top, 0.0, panel)
            filled = jnp.concatenate([lower, jnp.zeros((block - PANEL, PANEL), F32)], axis=0)
            shown = jnp.where(top, filled, panel)
        high, low = (term.astype(F32) for term in split(used, 2))
        pair = jnp.concatenate([high, low], axis=1).astype(BF16)
        factors = jnp.concatenate([pair, pair], axis=1)
        update = jnp.dot(factors, tail_ref[...], preferred_element_type=F32)
        shown = jnp.concatenate([shown, jnp.zeros_like(shown)], axis=1)
        near_ref[rows_here, :LANES] = jnp.where(lane_ids(shown.shape) < PANEL, shown, -update[:, :LANES])
        near_ref[rows_here, LANES:] = -update[:, LANES:columns]
        far_ref[rows_here, :] = (resident_ref[rows_here, :].astype(F32) - update[:, columns:]).astype(BF16)
        for which, (source, target) in enumerate(((near_ref, near_hbm), (far_ref, far_hbm))):
            store = pltpu.make_async_copy(
                source.at[pl.ds(start, block), :], target.at[pl.ds(start, block), :], sems.at[which, number]
            )
            store.start()
            stores.append(store)
    for store in stores:
        store.wait()


def updates(my_index, parts, offsets, index, arrived, shift, resident, blocks_held, columns):
    rows, width = resident.shape
    needed = columns + width
    held_rows = len(offsets) * blocks_held * PANEL
    vmem = pl.BlockSpec(memory_space=pltpu.VMEM)
    anywhere = pl.BlockSpec(memory_space=pltpu.HBM)
    return pl.pallas_call(
        functools.partial(update_kernel, offsets, blocks_held, columns),
        in_specs=[pl.BlockSpec(memory_space=pltpu.SMEM), vmem, vmem, vmem, anywhere] + [vmem] * len(parts),
        out_specs=[anywhere, anywhere, vmem],
        out_shape=[
            pltpu.HBM((rows, columns), F32),
            pltpu.HBM((rows, width), BF16),
            jax.ShapeDtypeStruct((1, PANEL), F32),
        ],
        scratch_shapes=[
            pltpu.VMEM((held_rows, PANEL), F32),
            pltpu.VMEM((4 * PANEL, needed), BF16),
            pltpu.VMEM((rows, width), BF16),
            pltpu.VMEM((rows, 2 * LANES), BF16),
            pltpu.VMEM((rows, PANEL), F32),
            pltpu.VMEM((rows, columns), F32),
            pltpu.VMEM((rows, width), BF16),
            pltpu.SemaphoreType.DMA,
            pltpu.SemaphoreType.DMA((2, rows // A_BLOCK)),
        ],
        compiler_params=params(32),
        cost_estimate=pl.CostEstimate(
            flops=2 * rows * needed * 4 * PANEL, bytes_accessed=4 * rows * (columns + width), transcendentals=0
        ),
        name="factor_and_update",
    )(my_index, index, arrived, shift, in_hbm(resident), *parts)


def formed_kernel(index_ref, arrived_ref, near_hbm, out_hbm, near_ref, terms_ref, got_ref, out_ref, in_sems, out_sems):
    half = arrived_ref.shape[0]
    block = STORE_BLOCK
    starts = range(0, near_ref.shape[0], block)

    def rows_of(ref, start):
        return ref.at[pl.ds(start, block), :]

    fetches = [
        pltpu.make_async_copy(rows_of(near_hbm, start), rows_of(near_ref, start), in_sems.at[i])
        for i, start in enumerate(starts)
    ]
    for fetch in fetches:
        fetch.start()
    low_lanes = lane_ids((CHUNK, LANES)) < PANEL
    for place in range(0, half, CHUNK):
        words = arrived_ref[place : place + CHUNK, LANES:]
        scale = jnp.exp2(((words & 255) - (BIAS + 15)).astype(F32))
        other = swap_halves(scale)
        packed_terms((words >> 8).astype(F32) * (scale * (1 / 256)), terms_ref, place, 2 * LANES)
        words = arrived_ref[place : place + CHUNK, :LANES]
        low = (words >> 16).astype(F32) * jnp.where(low_lanes, scale, other)
        high = ((words << 16) >> 16).astype(F32) * jnp.where(low_lanes, other, scale)
        for side, values in enumerate((low, high)):
            first, second = split(values, 2)
            here = slice(side * half + place, side * half + place + CHUNK)
            terms_ref[here, :LANES] = first
            terms_ref[here, LANES : 2 * LANES] = second

    stores = []
    for i, start in enumerate(starts):
        rows_here = slice(start, start + block)
        picks = one_hot(index_ref[:, rows_here], terms_ref.shape[0])
        got_ref[rows_here, :] = jnp.dot(picks, terms_ref[...], preferred_element_type=F32)
        fetches[i].wait()
        for place in range(start, start + block, CHUNK):
            here = slice(place, place + CHUNK)
            narrow = whole_sum(got_ref[here, 2 * LANES :])
            held = near_ref[here, :LANES]
            out_ref[here, :LANES] = jnp.where(low_lanes, held, narrow + held)
            out_ref[here, LANES:] = (got_ref[here, :LANES] + got_ref[here, LANES : 2 * LANES]) + near_ref[here, LANES:]
        store = pltpu.make_async_copy(rows_of(out_ref, start), rows_of(out_hbm, start), out_sems.at[i])
        store.start()
        stores.append(store)
    for store in stores:
        store.wait()


def formed_columns(index, arrived, near):
    rows, columns = near.shape
    vmem = pl.BlockSpec(memory_space=pltpu.VMEM)
    anywhere = pl.BlockSpec(memory_space=pltpu.HBM)
    return pl.pallas_call(
        formed_kernel,
        in_specs=[vmem, vmem, anywhere],
        out_specs=anywhere,
        out_shape=pltpu.HBM((rows, columns), F32),
        input_output_aliases={2: 0},
        scratch_shapes=[
            pltpu.VMEM((rows, columns), F32),
            pltpu.VMEM((rows, 4 * LANES), BF16),
            pltpu.VMEM((rows, 4 * LANES), F32),
            pltpu.VMEM((rows, columns), F32),
            pltpu.SemaphoreType.DMA((rows // STORE_BLOCK,)),
            pltpu.SemaphoreType.DMA((rows // STORE_BLOCK,)),
        ],
        compiler_params=params(32),
        cost_estimate=pl.CostEstimate(
            flops=8 * rows * rows * LANES, bytes_accessed=8 * rows * columns, transcendentals=0
        ),
        name="formed_columns",
    )(index, arrived, near)


def swap_rows(x, group):
    rows, width = x.shape
    return lax.all_to_all(
        x.reshape(group, rows // group, width), "wide", split_axis=0, concat_axis=0, tiled=True
    ).reshape(rows, width)


def on_device(a_rows, xa_panel, za_panel, send_order, recv_order, shift, resident):
    rows = a_rows.shape[0]
    columns = xa_panel.shape[1]
    group = lax.axis_size("wide")
    my_index = lax.axis_index("wide").astype(jnp.int32).reshape(1)
    share = rows // group
    half = rows // 2
    few, apart = phases_of(group)

    order, packing = send_order, share
    if share % 16:
        order = send_order.reshape(group, 2, share // 2).transpose(1, 0, 2).reshape(1, rows)
        packing = 0
    source, slot = recv_order // share, recv_order % share
    index = (slot // (share // 2)) * half + source * (share // 2) + slot % (share // 2)

    lead_panel, rest_panel = split_panels(my_index, xa_panel, za_panel)
    send_picks, a_copy = order_picks(order, a_rows, packing)
    lead_parts = join(exchange([lead_panel], few[0], "wide"))
    rest_parts = tied([rest_panel], *lead_parts)
    for masks in few[1:]:
        lead_parts = exchange(join(lead_parts), masks, "wide")
    for number, masks in enumerate(apart[:-2]):
        rest_parts = exchange(join(rest_parts), masks, "wide")
        if number == 0:
            rest_parts = tied(rest_parts, send_picks)
            lead_parts = tied(lead_parts, *rest_parts)

    lead_out = lead_products(my_index, a_copy, send_picks, lead_parts, offsets_of(few))
    lead_in = swap_rows(tied([lead_out], *rest_parts)[0], group)
    rest_parts = exchange(join(tied(rest_parts, lead_out)), apart[-2], "wide")

    needed = columns + resident.shape[1]
    blocks_held = -(-needed // (PANEL * group))
    leading_parts = [leading_rows(index, lead_in, blocks_held * PANEL)]
    for masks in few:
        leading_parts = exchange(join(leading_parts), masks, "wide")
        if masks is few[0]:
            rest_parts = exchange(tied(rest_parts, *leading_parts), apart[-1], "wide")
    rest_out = rest_products(my_index, order, a_rows, rest_parts, offsets_of(apart), packing)
    rest_in = swap_rows(tied([rest_out], *leading_parts)[0], group)
    near, updated, pivots = updates(
        my_index,
        leading_parts,
        offsets_of(few),
        index,
        tied([lead_in], rest_out)[0],
        shift[None, :],
        resident,
        blocks_held,
        columns,
    )
    factored = formed_columns(index, rest_in, near)
    return (factored, updated, pivots[0])


def solution(mesh):
    placed = (
        P(("parts", "wide"), None),
        P(("parts", "wide"), None),
        P(("parts", "wide"), None),
        P(("parts", "wide"), None),
        P(("parts", "wide"), None),
        P("parts"),
        P(("parts", "wide"), None),
    )
    return jax.shard_map(
        on_device,
        mesh=mesh,
        in_specs=placed,
        out_specs=(P(("parts", "wide"), None), P(("parts", "wide"), None), P("parts")),
        check_vma=False,
    )
```

```python
import functools

import jax
import jax.numpy as jnp
from jax import lax
from jax.experimental import pallas as pl
from jax.experimental.pallas import tpu as pltpu
from jax.sharding import PartitionSpec as P

PANEL = 64
LANES = 128
A_BLOCK = 640
DEEP_BLOCK = 256
F32 = jnp.float32
BF16 = jnp.bfloat16
MIB = 1024 * 1024


def params(mebibytes=12):
    return pltpu.CompilerParams(vmem_limit_bytes=mebibytes * MIB)


def in_hbm(x):
    return pltpu.with_memory_space_constraint(x, pltpu.HBM)


def lane_ids(shape):
    return lax.broadcasted_iota(jnp.int32, shape, len(shape) - 1)


def split(x, count):
    terms = []
    for _ in range(count):
        term = x.astype(BF16)
        terms.append(term)
        x = x - term.astype(F32)
    return terms


def swap_halves(x):
    return pltpu.roll(x, LANES // 2, 1)


def as_column(index_row):
    return jnp.transpose(jnp.broadcast_to(index_row, (LANES, LANES)))


def picks_of(at, width):
    lanes = lane_ids(at.shape)
    return jnp.concatenate(
        [(at == lanes + column).astype(F32).astype(BF16) for column in range(0, width, LANES)], axis=1
    )


def fill_picks(at_ref, picks_ref):
    rows, width = picks_ref.shape
    for start in range(0, rows, LANES):
        picks_ref[start : start + LANES, :] = picks_of(at_ref[start : start + LANES, :], width)


def one_hot(index_row, width):
    chunks = [
        picks_of(as_column(index_row[:, start : start + LANES]), width)
        for start in range(0, index_row.shape[1], LANES)
    ]
    return jnp.concatenate(chunks, axis=0) if len(chunks) > 1 else chunks[0]


def packed_order(share, half, slot):
    part = share // 2
    return (slot % share) // part * half + slot // share * part + slot % part


def fill_order(order_ref, at_ref, share):
    rows = order_ref.shape[1]
    height = 8
    for start in range(0, rows, LANES):
        column = as_column(order_ref[:, start : start + LANES])
        if not share:
            at_ref[start : start + LANES, :] = column
            continue
        for inner in range(0, LANES, height):
            place = packed_order(share, rows // 2, start + inner)
            at_ref[place : place + height, :] = column[inner : inner + height]


def exchange(held, masks, axis):
    size = lax.axis_size(axis)
    combined = [0]
    for mask in masks:
        combined += [other ^ mask for other in combined]
    parts = list(held)
    for mask in combined[1:]:
        parts += [lax.ppermute(part, axis, [(i, i ^ mask) for i in range(size)]) for part in held]
    return parts


def offsets_of(phases):
    offsets = [0]
    for masks in phases:
        combined = [0]
        for mask in masks:
            combined += [other ^ mask for other in combined]
        offsets = [offset ^ mask for mask in combined for offset in offsets]
    return offsets


def join(parts):
    return [jnp.concatenate(parts, axis=0)]


def phases_of(size):
    bits = [1 << bit for bit in reversed(range(size.bit_length() - 1))]
    return [bits[start : start + 2] for start in range(0, len(bits), 2)], [[bit] for bit in bits]


def tied(parts, *earlier):
    return list(lax.optimization_barrier((*parts, *earlier))[: len(parts)])


def picks_kernel(share, order_hbm, a_hbm, picks_ref, copy_ref, order_ref, at_ref, sems):
    fetch = pltpu.make_async_copy(order_hbm, order_ref, sems.at[0])
    copy = pltpu.make_async_copy(a_hbm, copy_ref, sems.at[1])
    fetch.start()
    copy.start()
    fetch.wait()
    fill_order(order_ref, at_ref, share)
    fill_picks(at_ref, picks_ref)
    copy.wait()


def order_picks(order, a_rows, share):
    rows, depth = a_rows.shape
    return pl.pallas_call(
        functools.partial(picks_kernel, share),
        in_specs=[pl.BlockSpec(memory_space=pltpu.HBM)] * 2,
        out_specs=[pl.BlockSpec(memory_space=pltpu.VMEM)] * 2,
        out_shape=[jax.ShapeDtypeStruct((rows, rows), BF16), jax.ShapeDtypeStruct((rows, depth), BF16)],
        scratch_shapes=[
            pltpu.VMEM((1, rows), jnp.int32),
            pltpu.VMEM((rows, LANES), jnp.int32),
            pltpu.SemaphoreType.DMA((2,)),
        ],
        compiler_params=params(),
        cost_estimate=pl.CostEstimate(flops=4 * rows * rows, bytes_accessed=4 * rows * depth, transcendentals=0),
        name="order_picks",
    )(in_hbm(order), in_hbm(a_rows))


def panels_kernel(my_ref, xa_hbm, za_hbm, lead_ref, rest_ref, xa_ref, za_ref, sems):
    copies = [
        pltpu.make_async_copy(xa_hbm, xa_ref, sems.at[0]),
        pltpu.make_async_copy(za_hbm, za_ref, sems.at[1]),
    ]
    for copy in copies:
        copy.start()
    for copy in copies:
        copy.wait()
    lead_ref[0] = jnp.concatenate([xa_ref[:, :PANEL], za_ref[:, :PANEL]], axis=1)
    rest_ref[0, :, :LANES] = jnp.concatenate([xa_ref[:, PANEL:LANES], za_ref[:, PANEL:LANES]], axis=1)
    rest_ref[0, :, LANES : 2 * LANES] = xa_ref[:, LANES:]
    rest_ref[0, :, 2 * LANES :] = za_ref[:, LANES:]


def split_panels(my_index, xa_panel, za_panel):
    depth, columns = xa_panel.shape
    return pl.pallas_call(
        panels_kernel,
        in_specs=[pl.BlockSpec(memory_space=pltpu.SMEM)] + [pl.BlockSpec(memory_space=pltpu.HBM)] * 2,
        out_shape=[
            jax.ShapeDtypeStruct((1, depth, LANES), BF16),
            jax.ShapeDtypeStruct((1, depth, 2 * columns - LANES), BF16),
        ],
        scratch_shapes=[
            pltpu.VMEM((depth, columns), BF16),
            pltpu.VMEM((depth, columns), BF16),
            pltpu.SemaphoreType.DMA((2,)),
        ],
        compiler_params=params(),
        name="split_panels",
    )(my_index, in_hbm(xa_panel), in_hbm(za_panel))


def assemble(my_index, offsets, parts, panel_ref):
    position = 0
    for part in parts:
        for number in range(part.shape[0]):
            depth = part.shape[1]
            start = pl.multiple_of((my_index ^ offsets[position]) * depth, depth)
            panel_ref[pl.ds(start, depth), :] = part[number]
            position += 1


def whole_sum(got):
    pair = got[:, :LANES]
    return (pair + swap_halves(pair)) + got[:, LANES:]


def lead_product_kernel(offsets, my_ref, a_ref, picks_ref, *refs):
    parts, (out_ref, panel_ref, terms_ref) = refs[:-3], refs[-3:]
    assemble(my_ref[0], offsets, parts, panel_ref)
    rows = a_ref.shape[0]
    for start in range(0, rows, DEEP_BLOCK):
        both = jnp.dot(a_ref[start : start + DEEP_BLOCK, :], panel_ref[...], preferred_element_type=F32)
        first, second, third = (term.astype(F32) for term in split(both * swap_halves(both), 3))
        near = lane_ids(both.shape) < PANEL
        terms_ref[start : start + DEEP_BLOCK, :LANES] = jnp.where(near, first, second).astype(BF16)
        terms_ref[start : start + DEEP_BLOCK, LANES:] = third.astype(BF16)
    half = rows // 2
    block = half // 2
    for start in range(0, half, block):
        low = jnp.dot(picks_ref[start : start + block, :], terms_ref[...], preferred_element_type=F32)
        high = jnp.dot(picks_ref[half + start : half + start + block, :], terms_ref[...], preferred_element_type=F32)
        low, high = whole_sum(low), whole_sum(high)
        out_ref[start : start + block, :] = jnp.where(lane_ids(low.shape) < PANEL, low, high)


def lead_products(my_index, a_rows, picks, parts, offsets):
    rows, depth = a_rows.shape
    return pl.pallas_call(
        functools.partial(lead_product_kernel, offsets),
        in_specs=[pl.BlockSpec(memory_space=pltpu.SMEM)] + [pl.BlockSpec(memory_space=pltpu.VMEM)] * (2 + len(parts)),
        out_specs=pl.BlockSpec(memory_space=pltpu.VMEM),
        out_shape=jax.ShapeDtypeStruct((rows // 2, LANES), F32),
        scratch_shapes=[pltpu.VMEM((depth, LANES), BF16), pltpu.VMEM((rows, 2 * LANES), BF16)],
        compiler_params=params(),
        cost_estimate=pl.CostEstimate(
            flops=2 * rows * (depth + 2 * rows) * LANES, bytes_accessed=2 * rows * depth, transcendentals=0
        ),
        name="lead_products",
    )(my_index, a_rows, picks, *parts)


BIAS = 128
MARGIN = 0.9995
ROUNDER = 1.5 * 2.0**23


def nearest(x):
    return (x + ROUNDER) - ROUNDER


def rest_product_kernel(offsets, share, my_ref, order_ref, a_hbm, *refs):
    parts, (out_ref, a_ref, at_ref, picks_ref, panel_ref, terms_ref, sems, part_sems) = refs[:-8], refs[-8:]
    rows = a_ref.shape[0]
    half = rows // 2
    block = DEEP_BLOCK
    starts = range(0, rows, block)
    copies = [
        pltpu.make_async_copy(a_hbm.at[pl.ds(start, block), :], a_ref.at[pl.ds(start, block), :], sems.at[i])
        for i, start in enumerate(starts)
    ]
    fetches = []
    for part in parts:
        for number in range(part.shape[0]):
            depth = part.shape[1]
            position = len(fetches)
            place = pl.multiple_of((my_ref[0] ^ offsets[position]) * depth, depth)
            fetches.append(
                pltpu.make_async_copy(part.at[number], panel_ref.at[pl.ds(place, depth), :], part_sems.at[position])
            )
    for copy in fetches + copies[:2]:
        copy.start()
    fill_order(order_ref, at_ref, share)
    fill_picks(at_ref, picks_ref)
    for copy in fetches:
        copy.wait()

    def product(i):
        copies[i].wait()
        if i + 2 < len(copies):
            copies[i + 2].start()
        return jnp.dot(a_ref[starts[i] : starts[i] + block, :], panel_ref[...], preferred_element_type=F32)

    low_lanes = lane_ids((block, LANES)) < PANEL
    later = product(0)
    for i, start in enumerate(starts):
        both = later
        if i + 1 < len(starts):
            later = product(i + 1)
        near = both[:, :LANES]
        near = near * swap_halves(near)
        far = both[:, LANES : 2 * LANES] * both[:, 2 * LANES :]
        largest = jnp.max(jnp.maximum(jnp.abs(near), jnp.abs(far)), axis=1, keepdims=True)
        exponent = jnp.floor(jnp.log2(jnp.maximum(largest, 1e-30))) + 1.0
        scale = jnp.exp2(15.0 - exponent) * MARGIN
        far = nearest(far * scale)
        near = nearest(near * scale)
        far_top = nearest(far * (1 / 256))
        near_top = nearest(near * (1 / 256))
        here = slice(start, start + block)
        terms_ref[here, :LANES] = far_top.astype(BF16)
        terms_ref[here, LANES : 2 * LANES] = (far - far_top * 256.0).astype(BF16)
        terms_ref[here, 2 * LANES : 3 * LANES] = jnp.where(low_lanes, near_top, near - near_top * 256.0).astype(BF16)
        terms_ref[here, 3 * LANES :] = jnp.broadcast_to(exponent, (block, LANES)).astype(BF16)

    def coded(start, size):
        got = jnp.dot(picks_ref[start : start + size, :], terms_ref[...], preferred_element_type=F32)
        far = got[:, :LANES] * 256.0 + got[:, LANES : 2 * LANES]
        pair = got[:, 2 * LANES : 3 * LANES]
        pair = jnp.where(lane_ids(pair.shape) < PANEL, pair * 256.0, pair)
        near = (pair + swap_halves(pair)).astype(jnp.int32) * 65536 + (got[:, 3 * LANES :].astype(jnp.int32) + BIAS)
        return far.astype(jnp.int32), near

    block = half // 2
    for start in range(0, half, block):
        far_low, near_low = coded(start, block)
        far_high, near_high = coded(half + start, block)
        out_ref[start : start + block, :LANES] = far_low * 65536 + (far_high & 65535)
        out_ref[start : start + block, LANES:] = jnp.where(lane_ids(near_low.shape) < PANEL, near_low, near_high)


def rest_products(my_index, order, a_rows, parts, offsets, share):
    rows, depth = a_rows.shape
    return pl.pallas_call(
        functools.partial(rest_product_kernel, offsets, share),
        in_specs=[
            pl.BlockSpec(memory_space=pltpu.SMEM),
            pl.BlockSpec(memory_space=pltpu.VMEM),
            pl.BlockSpec(memory_space=pltpu.HBM),
        ]
        + [pl.BlockSpec(memory_space=pl.ANY)] * len(parts),
        out_specs=pl.BlockSpec(memory_space=pltpu.VMEM),
        out_shape=jax.ShapeDtypeStruct((rows // 2, 2 * LANES), jnp.int32),
        scratch_shapes=[
            pltpu.VMEM((rows, depth), BF16),
            pltpu.VMEM((rows, LANES), jnp.int32),
            pltpu.VMEM((rows, rows), BF16),
            pltpu.VMEM((depth, 3 * LANES), BF16),
            pltpu.VMEM((rows, 4 * LANES), BF16),
            pltpu.SemaphoreType.DMA((rows // DEEP_BLOCK,)),
            pltpu.SemaphoreType.DMA((len(offsets),)),
        ],
        compiler_params=params(32),
        cost_estimate=pl.CostEstimate(
            flops=2 * rows * (3 * depth + 4 * rows) * LANES, bytes_accessed=2 * rows * depth, transcendentals=0
        ),
        name="rest_products",
    )(my_index, order, in_hbm(a_rows), *parts)


def packed_terms(x, terms_ref, start):
    half = x.shape[0]
    first, second, third = (term.astype(F32) for term in split(x, 3))
    near = lane_ids(x.shape) < PANEL
    other = swap_halves(third)
    terms_ref[:half, start : start + LANES] = jnp.where(near, first, swap_halves(second)).astype(BF16)
    terms_ref[half:, start : start + LANES] = jnp.where(near, swap_halves(first), second).astype(BF16)
    terms_ref[:half, start + LANES : start + 2 * LANES] = jnp.where(near, third, other).astype(BF16)
    terms_ref[half:, start + LANES : start + 2 * LANES] = jnp.where(near, other, third).astype(BF16)


def leading_kernel(held, index_ref, arrived_ref, out_ref, terms_ref):
    packed_terms(arrived_ref[...], terms_ref, 0)
    width = -(-held // LANES) * LANES
    picks = one_hot(index_ref[:, :width], terms_ref.shape[0])
    got = whole_sum(jnp.dot(picks, terms_ref[...], preferred_element_type=F32))
    first, second = got[: held // 2], got[held // 2 : held]
    out_ref[0] = jnp.where(lane_ids(first.shape) < PANEL, first, second)


def leading_rows(index, arrived, held):
    rows = index.shape[1]
    return pl.pallas_call(
        functools.partial(leading_kernel, held),
        in_specs=[pl.BlockSpec(memory_space=pltpu.VMEM)] * 2,
        out_specs=pl.BlockSpec(memory_space=pltpu.VMEM),
        out_shape=jax.ShapeDtypeStruct((1, held // 2, LANES), F32),
        scratch_shapes=[pltpu.VMEM((rows, 2 * LANES), BF16)],
        compiler_params=params(),
        cost_estimate=pl.CostEstimate(
            flops=4 * held * rows * LANES, bytes_accessed=2 * rows * LANES, transcendentals=0
        ),
        name="leading_rows",
    )(index, arrived)


def eliminate(block, shift_row):
    rows = lax.broadcasted_iota(jnp.int32, (PANEL, PANEL), 0)
    columns = lax.broadcasted_iota(jnp.int32, (PANEL, PANEL), 1)
    flipped = jnp.transpose(block)
    mirrored = jnp.where(rows >= columns, block, flipped)
    diagonal = shift_row + jnp.sum(jnp.abs(mirrored), axis=0, keepdims=True)
    unit = (rows == columns).astype(F32)
    work = jnp.where(rows == columns, diagonal, mirrored)
    work = jnp.concatenate([work, unit], axis=1)
    height = 8
    groups = [work[start : start + height] for start in range(0, PANEL, height)]
    sublanes = lax.broadcasted_iota(jnp.int32, (height, LANES), 0)
    scaled_rows = []
    for k in range(PANEL):
        home, offset = divmod(k, height)
        row = groups[home][offset : offset + 1, :]
        row = row / row[:, k : k + 1]
        scaled_rows.append(row)
        for g in range(home, PANEL // height):
            column = jnp.broadcast_to(groups[g][:, k : k + 1], (height, LANES))
            if g == home:
                column = jnp.where(sublanes > offset, column, 0.0)
            groups[g] = groups[g] - column * row
    final = jnp.concatenate(groups, axis=0)
    scaled = jnp.concatenate(scaled_rows, axis=0)
    upper = jnp.where(columns >= rows, scaled[:, :PANEL], 0.0)
    pivots = jnp.sum(jnp.where(rows == columns, final[:, :PANEL], 0.0), axis=0, keepdims=True)
    return upper, final[:, PANEL:], pivots


def exact(lhs, rhs, dims):
    return lax.dot_general(lhs, rhs, (dims, ((), ())), precision=lax.Precision.HIGHEST, preferred_element_type=F32)


def update_kernel(offsets, blocks_held, columns, my_ref, index_ref, arrived_ref, shift_ref, resident_hbm, *refs):
    parts = refs[:-12]
    near_hbm, far_hbm, pivots_ref, leading_ref, tail_ref, resident_ref, terms_ref, lead_ref = refs[-12:-4]
    near_ref, far_ref, sem, sems = refs[-4:]
    fetch = pltpu.make_async_copy(resident_hbm, resident_ref, sem)
    fetch.start()
    my_index = my_ref[0]
    size = len(offsets)
    position = 0
    packed = blocks_held * PANEL // 2
    part_rows = PANEL // 2
    for part in parts:
        for number in range(part.shape[0]):
            owner = my_index ^ offsets[position]
            for start in range(0, blocks_held * PANEL, part_rows):
                held, inner = divmod(start, PANEL)
                if start < packed:
                    rows = part[number, start : start + part_rows, :PANEL]
                else:
                    rows = part[number, start - packed : start - packed + part_rows, PANEL:]
                target = pl.multiple_of((held * size + owner) * PANEL + inner, part_rows)
                leading_ref[pl.ds(target, part_rows), :] = rows
            position += 1
    upper, inverse, pivots = eliminate(leading_ref[:PANEL, :], shift_ref[...])
    pivots_ref[...] = pivots
    lower = jnp.transpose(upper)
    needed = tail_ref.shape[1]
    tail = exact(inverse, leading_ref[:needed, :], ((1,), (1,)))
    high, low = split(tail, 2)
    tail_ref[0:PANEL, :] = high
    tail_ref[PANEL : 2 * PANEL, :] = high
    tail_ref[2 * PANEL : 3 * PANEL, :] = low
    tail_ref[3 * PANEL :, :] = low

    block = A_BLOCK
    packed_terms(arrived_ref[...], terms_ref, 0)
    for start in range(0, lead_ref.shape[0], block):
        picks = one_hot(index_ref[:, start : start + block], lead_ref.shape[0])
        got = jnp.dot(picks, terms_ref[...], preferred_element_type=F32)
        lead_ref[start : start + block, :] = whole_sum(got)[:, :PANEL]
    fetch.wait()
    stores = []
    for number, start in enumerate(range(0, lead_ref.shape[0], block)):
        rows_here = slice(start, start + block)
        panel = exact(lead_ref[rows_here, :], inverse, ((1,), (1,))) / pivots
        shown = used = panel
        if start == 0:
            row_ids = lax.broadcasted_iota(jnp.int32, panel.shape, 0)
            top = jnp.logical_and(my_index == 0, row_ids < PANEL)
            used = jnp.where(top, 0.0, panel)
            filled = jnp.concatenate([lower, jnp.zeros((block - PANEL, PANEL), F32)], axis=0)
            shown = jnp.where(top, filled, panel)
        high, low = (term.astype(F32) for term in split(used, 2))
        pair = jnp.concatenate([high, low], axis=1).astype(BF16)
        factors = jnp.concatenate([pair, pair], axis=1)
        update = jnp.dot(factors, tail_ref[...], preferred_element_type=F32)
        shown = jnp.concatenate([shown, jnp.zeros_like(shown)], axis=1)
        near_ref[rows_here, :LANES] = jnp.where(lane_ids(shown.shape) < PANEL, shown, -update[:, :LANES])
        near_ref[rows_here, LANES:] = -update[:, LANES:columns]
        far_ref[rows_here, :] = (resident_ref[rows_here, :].astype(F32) - update[:, columns:]).astype(BF16)
        for which, (source, target) in enumerate(((near_ref, near_hbm), (far_ref, far_hbm))):
            store = pltpu.make_async_copy(
                source.at[pl.ds(start, block), :], target.at[pl.ds(start, block), :], sems.at[which, number]
            )
            store.start()
            stores.append(store)
    for store in stores:
        store.wait()


def updates(my_index, parts, offsets, index, arrived, shift, resident, blocks_held, columns):
    rows, width = resident.shape
    needed = columns + width
    held_rows = len(offsets) * blocks_held * PANEL
    vmem = pl.BlockSpec(memory_space=pltpu.VMEM)
    anywhere = pl.BlockSpec(memory_space=pltpu.HBM)
    return pl.pallas_call(
        functools.partial(update_kernel, offsets, blocks_held, columns),
        in_specs=[pl.BlockSpec(memory_space=pltpu.SMEM), vmem, vmem, vmem, anywhere] + [vmem] * len(parts),
        out_specs=[anywhere, anywhere, vmem],
        out_shape=[
            pltpu.HBM((rows, columns), F32),
            pltpu.HBM((rows, width), BF16),
            jax.ShapeDtypeStruct((1, PANEL), F32),
        ],
        scratch_shapes=[
            pltpu.VMEM((held_rows, PANEL), F32),
            pltpu.VMEM((4 * PANEL, needed), BF16),
            pltpu.VMEM((rows, width), BF16),
            pltpu.VMEM((rows, 2 * LANES), BF16),
            pltpu.VMEM((rows, PANEL), F32),
            pltpu.VMEM((rows, columns), F32),
            pltpu.VMEM((rows, width), BF16),
            pltpu.SemaphoreType.DMA,
            pltpu.SemaphoreType.DMA((2, rows // A_BLOCK)),
        ],
        compiler_params=params(32),
        cost_estimate=pl.CostEstimate(
            flops=2 * rows * needed * 4 * PANEL, bytes_accessed=4 * rows * (columns + width), transcendentals=0
        ),
        name="factor_and_update",
    )(my_index, index, arrived, shift, in_hbm(resident), *parts)


def formed_kernel(index_ref, arrived_ref, near_hbm, out_hbm, near_ref, terms_ref, out_ref, in_sems, out_sems):
    half = arrived_ref.shape[0]
    block = A_BLOCK
    starts = range(0, near_ref.shape[0], block)

    def rows_of(ref, start):
        return ref.at[pl.ds(start, block), :]

    fetches = [
        pltpu.make_async_copy(rows_of(near_hbm, start), rows_of(near_ref, start), in_sems.at[i])
        for i, start in enumerate(starts)
    ]
    for fetch in fetches:
        fetch.start()
    words = arrived_ref[:, LANES:]
    low_lanes = lane_ids(words.shape) < PANEL
    scale = jnp.exp2(((words & 255) - (BIAS + 15)).astype(F32)) * (1 / MARGIN)
    other = swap_halves(scale)
    first, second = (term.astype(F32) for term in split((words >> 16).astype(F32) * scale, 2))
    terms_ref[:half, 2 * LANES :] = jnp.where(low_lanes, first, swap_halves(second)).astype(BF16)
    terms_ref[half:, 2 * LANES :] = jnp.where(low_lanes, swap_halves(first), second).astype(BF16)
    words = arrived_ref[:, :LANES]
    low = (words >> 16).astype(F32) * jnp.where(low_lanes, scale, other)
    high = ((words << 16) >> 16).astype(F32) * jnp.where(low_lanes, other, scale)
    for side, values in enumerate((low, high)):
        first, second = split(values, 2)
        terms_ref[side * half : (side + 1) * half, :LANES] = first
        terms_ref[side * half : (side + 1) * half, LANES : 2 * LANES] = second

    stores = []
    for i, start in enumerate(starts):
        rows_here = slice(start, start + block)
        picks = one_hot(index_ref[:, rows_here], terms_ref.shape[0])
        got = jnp.dot(picks, terms_ref[...], preferred_element_type=F32)
        pair = got[:, 2 * LANES :]
        fetches[i].wait()
        held = near_ref[rows_here, :LANES]
        out_ref[rows_here, :LANES] = jnp.where(
            lane_ids(held.shape) < PANEL, held, (pair + swap_halves(pair)) + held
        )
        out_ref[rows_here, LANES:] = (got[:, :LANES] + got[:, LANES : 2 * LANES]) + near_ref[rows_here, LANES:]
        store = pltpu.make_async_copy(rows_of(out_ref, start), rows_of(out_hbm, start), out_sems.at[i])
        store.start()
        stores.append(store)
    for store in stores:
        store.wait()


def formed_columns(index, arrived, near):
    rows, columns = near.shape
    vmem = pl.BlockSpec(memory_space=pltpu.VMEM)
    anywhere = pl.BlockSpec(memory_space=pltpu.HBM)
    return pl.pallas_call(
        formed_kernel,
        in_specs=[vmem, vmem, anywhere],
        out_specs=anywhere,
        out_shape=pltpu.HBM((rows, columns), F32),
        input_output_aliases={2: 0},
        scratch_shapes=[
            pltpu.VMEM((rows, columns), F32),
            pltpu.VMEM((rows, 3 * LANES), BF16),
            pltpu.VMEM((rows, columns), F32),
            pltpu.SemaphoreType.DMA((rows // A_BLOCK,)),
            pltpu.SemaphoreType.DMA((rows // A_BLOCK,)),
        ],
        compiler_params=params(32),
        cost_estimate=pl.CostEstimate(
            flops=8 * rows * rows * LANES, bytes_accessed=8 * rows * columns, transcendentals=0
        ),
        name="formed_columns",
    )(index, arrived, near)


def swap_rows(x, group):
    rows, width = x.shape
    return lax.all_to_all(
        x.reshape(group, rows // group, width), "wide", split_axis=0, concat_axis=0, tiled=True
    ).reshape(rows, width)


def on_device(a_rows, xa_panel, za_panel, send_order, recv_order, shift, resident):
    rows = a_rows.shape[0]
    columns = xa_panel.shape[1]
    group = lax.axis_size("wide")
    my_index = lax.axis_index("wide").astype(jnp.int32).reshape(1)
    share = rows // group
    half = rows // 2
    few, apart = phases_of(group)

    order, packing = send_order, share
    if share % 16:
        order = send_order.reshape(group, 2, share // 2).transpose(1, 0, 2).reshape(1, rows)
        packing = 0
    source, slot = recv_order // share, recv_order % share
    index = (slot // (share // 2)) * half + source * (share // 2) + slot % (share // 2)

    lead_panel, rest_panel = split_panels(my_index, xa_panel, za_panel)
    send_picks, a_copy = order_picks(order, a_rows, packing)
    lead_parts = [lead_panel]
    for masks in few:
        lead_parts = exchange(join(lead_parts), masks, "wide")
    rest_parts = [rest_panel]
    for number, masks in enumerate(apart[:-2]):
        rest_parts = exchange(join(rest_parts), masks, "wide")
        if number == 0:
            lead_parts = tied(lead_parts, *rest_parts)

    lead_out = lead_products(my_index, a_copy, send_picks, lead_parts, offsets_of(few))
    lead_in = swap_rows(tied([lead_out], *rest_parts)[0], group)
    rest_parts = exchange(join(tied(rest_parts, lead_out)), apart[-2], "wide")

    needed = columns + resident.shape[1]
    blocks_held = -(-needed // (PANEL * group))
    leading_parts = [leading_rows(index, lead_in, blocks_held * PANEL)]
    for masks in few:
        leading_parts = exchange(join(leading_parts), masks, "wide")
        if masks is few[0]:
            rest_parts = exchange(tied(rest_parts, *leading_parts), apart[-1], "wide")
    rest_out = rest_products(my_index, order, a_rows, rest_parts, offsets_of(apart), packing)
    rest_in = swap_rows(tied([rest_out], *leading_parts)[0], group)
    near, updated, pivots = updates(
        my_index,
        leading_parts,
        offsets_of(few),
        index,
        tied([lead_in], rest_out)[0],
        shift[None, :],
        resident,
        blocks_held,
        columns,
    )
    factored = formed_columns(index, rest_in, near)
    return (factored, updated, pivots[0])


def solution(mesh):
    placed = (
        P(("parts", "wide"), None),
        P(("parts", "wide"), None),
        P(("parts", "wide"), None),
        P(("parts", "wide"), None),
        P(("parts", "wide"), None),
        P("parts"),
        P(("parts", "wide"), None),
    )
    return jax.shard_map(
        on_device,
        mesh=mesh,
        in_specs=placed,
        out_specs=(P(("parts", "wide"), None), P(("parts", "wide"), None), P("parts")),
        check_vma=False,
    )
```

```python
import functools

import jax
import jax.numpy as jnp
from jax import lax
from jax.experimental import pallas as pl
from jax.experimental.pallas import tpu as pltpu
from jax.sharding import PartitionSpec as P

PANEL = 64
LANES = 128
A_BLOCK = 640
DEEP_BLOCK = 256
F32 = jnp.float32
BF16 = jnp.bfloat16
MIB = 1024 * 1024


def params(mebibytes=12):
    return pltpu.CompilerParams(vmem_limit_bytes=mebibytes * MIB)


def in_hbm(x):
    return pltpu.with_memory_space_constraint(x, pltpu.HBM)


def lane_ids(shape):
    return lax.broadcasted_iota(jnp.int32, shape, len(shape) - 1)


def split(x, count):
    terms = []
    for _ in range(count):
        term = x.astype(BF16)
        terms.append(term)
        x = x - term.astype(F32)
    return terms


def swap_halves(x):
    return pltpu.roll(x, LANES // 2, 1)


def as_column(index_row):
    return jnp.transpose(jnp.broadcast_to(index_row, (LANES, LANES)))


def picks_of(at, width):
    lanes = lane_ids(at.shape)
    return jnp.concatenate(
        [(at == lanes + column).astype(F32).astype(BF16) for column in range(0, width, LANES)], axis=1
    )


def fill_picks(at_ref, picks_ref):
    rows, width = picks_ref.shape
    for start in range(0, rows, LANES):
        picks_ref[start : start + LANES, :] = picks_of(at_ref[start : start + LANES, :], width)


def one_hot(index_row, width):
    chunks = [
        picks_of(as_column(index_row[:, start : start + LANES]), width)
        for start in range(0, index_row.shape[1], LANES)
    ]
    return jnp.concatenate(chunks, axis=0) if len(chunks) > 1 else chunks[0]


def packed_order(share, half, slot):
    part = share // 2
    return (slot % share) // part * half + slot // share * part + slot % part


def fill_order(order_ref, at_ref, share):
    rows = order_ref.shape[1]
    height = 8
    for start in range(0, rows, LANES):
        column = as_column(order_ref[:, start : start + LANES])
        if not share:
            at_ref[start : start + LANES, :] = column
            continue
        for inner in range(0, LANES, height):
            place = packed_order(share, rows // 2, start + inner)
            at_ref[place : place + height, :] = column[inner : inner + height]


def exchange(held, masks, axis):
    size = lax.axis_size(axis)
    combined = [0]
    for mask in masks:
        combined += [other ^ mask for other in combined]
    parts = list(held)
    for mask in combined[1:]:
        parts += [lax.ppermute(part, axis, [(i, i ^ mask) for i in range(size)]) for part in held]
    return parts


def offsets_of(phases):
    offsets = [0]
    for masks in phases:
        combined = [0]
        for mask in masks:
            combined += [other ^ mask for other in combined]
        offsets = [offset ^ mask for mask in combined for offset in offsets]
    return offsets


def join(parts):
    return [jnp.concatenate(parts, axis=0)]


def phases_of(size):
    bits = [1 << bit for bit in reversed(range(size.bit_length() - 1))]
    return [bits[start : start + 2] for start in range(0, len(bits), 2)], [[bit] for bit in bits]


def tied(parts, *earlier):
    return list(lax.optimization_barrier((*parts, *earlier))[: len(parts)])


def picks_kernel(share, order_hbm, a_hbm, picks_ref, copy_ref, order_ref, at_ref, sems):
    fetch = pltpu.make_async_copy(order_hbm, order_ref, sems.at[0])
    copy = pltpu.make_async_copy(a_hbm, copy_ref, sems.at[1])
    fetch.start()
    copy.start()
    fetch.wait()
    fill_order(order_ref, at_ref, share)
    fill_picks(at_ref, picks_ref)
    copy.wait()


def order_picks(order, a_rows, share):
    rows, depth = a_rows.shape
    return pl.pallas_call(
        functools.partial(picks_kernel, share),
        in_specs=[pl.BlockSpec(memory_space=pltpu.HBM)] * 2,
        out_specs=[pl.BlockSpec(memory_space=pltpu.VMEM)] * 2,
        out_shape=[jax.ShapeDtypeStruct((rows, rows), BF16), jax.ShapeDtypeStruct((rows, depth), BF16)],
        scratch_shapes=[
            pltpu.VMEM((1, rows), jnp.int32),
            pltpu.VMEM((rows, LANES), jnp.int32),
            pltpu.SemaphoreType.DMA((2,)),
        ],
        compiler_params=params(),
        cost_estimate=pl.CostEstimate(flops=4 * rows * rows, bytes_accessed=4 * rows * depth, transcendentals=0),
        name="order_picks",
    )(in_hbm(order), in_hbm(a_rows))


def panels_kernel(my_ref, xa_hbm, za_hbm, lead_ref, rest_ref, xa_ref, za_ref, sems):
    copies = [
        pltpu.make_async_copy(xa_hbm, xa_ref, sems.at[0]),
        pltpu.make_async_copy(za_hbm, za_ref, sems.at[1]),
    ]
    for copy in copies:
        copy.start()
    for copy in copies:
        copy.wait()
    lead_ref[0] = jnp.concatenate([xa_ref[:, :PANEL], za_ref[:, :PANEL]], axis=1)
    rest_ref[0, :, :LANES] = jnp.concatenate([xa_ref[:, PANEL:LANES], za_ref[:, PANEL:LANES]], axis=1)
    rest_ref[0, :, LANES : 2 * LANES] = xa_ref[:, LANES:]
    rest_ref[0, :, 2 * LANES :] = za_ref[:, LANES:]


def split_panels(my_index, xa_panel, za_panel):
    depth, columns = xa_panel.shape
    return pl.pallas_call(
        panels_kernel,
        in_specs=[pl.BlockSpec(memory_space=pltpu.SMEM)] + [pl.BlockSpec(memory_space=pltpu.HBM)] * 2,
        out_shape=[
            jax.ShapeDtypeStruct((1, depth, LANES), BF16),
            jax.ShapeDtypeStruct((1, depth, 2 * columns - LANES), BF16),
        ],
        scratch_shapes=[
            pltpu.VMEM((depth, columns), BF16),
            pltpu.VMEM((depth, columns), BF16),
            pltpu.SemaphoreType.DMA((2,)),
        ],
        compiler_params=params(),
        name="split_panels",
    )(my_index, in_hbm(xa_panel), in_hbm(za_panel))


def assemble(my_index, offsets, parts, panel_ref):
    position = 0
    for part in parts:
        for number in range(part.shape[0]):
            depth = part.shape[1]
            start = pl.multiple_of((my_index ^ offsets[position]) * depth, depth)
            panel_ref[pl.ds(start, depth), :] = part[number]
            position += 1


def whole_sum(got):
    pair = got[:, :LANES]
    return (pair + swap_halves(pair)) + got[:, LANES:]


def lead_product_kernel(offsets, my_ref, a_ref, picks_ref, *refs):
    parts, (out_ref, panel_ref, terms_ref) = refs[:-3], refs[-3:]
    assemble(my_ref[0], offsets, parts, panel_ref)
    rows = a_ref.shape[0]
    for start in range(0, rows, DEEP_BLOCK):
        both = jnp.dot(a_ref[start : start + DEEP_BLOCK, :], panel_ref[...], preferred_element_type=F32)
        first, second, third = (term.astype(F32) for term in split(both * swap_halves(both), 3))
        near = lane_ids(both.shape) < PANEL
        terms_ref[start : start + DEEP_BLOCK, :LANES] = jnp.where(near, first, second).astype(BF16)
        terms_ref[start : start + DEEP_BLOCK, LANES:] = third.astype(BF16)
    half = rows // 2
    block = half // 2
    for start in range(0, half, block):
        low = jnp.dot(picks_ref[start : start + block, :], terms_ref[...], preferred_element_type=F32)
        high = jnp.dot(picks_ref[half + start : half + start + block, :], terms_ref[...], preferred_element_type=F32)
        low, high = whole_sum(low), whole_sum(high)
        out_ref[start : start + block, :] = jnp.where(lane_ids(low.shape) < PANEL, low, high)


def lead_products(my_index, a_rows, picks, parts, offsets):
    rows, depth = a_rows.shape
    return pl.pallas_call(
        functools.partial(lead_product_kernel, offsets),
        in_specs=[pl.BlockSpec(memory_space=pltpu.SMEM)] + [pl.BlockSpec(memory_space=pltpu.VMEM)] * (2 + len(parts)),
        out_specs=pl.BlockSpec(memory_space=pltpu.VMEM),
        out_shape=jax.ShapeDtypeStruct((rows // 2, LANES), F32),
        scratch_shapes=[pltpu.VMEM((depth, LANES), BF16), pltpu.VMEM((rows, 2 * LANES), BF16)],
        compiler_params=params(),
        cost_estimate=pl.CostEstimate(
            flops=2 * rows * (depth + 2 * rows) * LANES, bytes_accessed=2 * rows * depth, transcendentals=0
        ),
        name="lead_products",
    )(my_index, a_rows, picks, *parts)


BIAS = 128
MARGIN = 0.9995
ROUNDER = 1.5 * 2.0**23


def nearest(x):
    return (x + ROUNDER) - ROUNDER


def rest_product_kernel(offsets, share, my_ref, order_ref, a_hbm, *refs):
    parts, (out_ref, a_ref, at_ref, picks_ref, panel_ref, terms_ref, sems) = refs[:-7], refs[-7:]
    rows = a_ref.shape[0]
    half = rows // 2
    block = DEEP_BLOCK
    starts = range(0, rows, block)
    copies = [
        pltpu.make_async_copy(a_hbm.at[pl.ds(start, block), :], a_ref.at[pl.ds(start, block), :], sems.at[i])
        for i, start in enumerate(starts)
    ]
    for copy in copies[:3]:
        copy.start()
    assemble(my_ref[0], offsets, parts, panel_ref)
    fill_order(order_ref, at_ref, share)
    fill_picks(at_ref, picks_ref)

    def product(i):
        copies[i].wait()
        if i + 3 < len(copies):
            copies[i + 3].start()
        return jnp.dot(a_ref[starts[i] : starts[i] + block, :], panel_ref[...], preferred_element_type=F32)

    low_lanes = lane_ids((block, LANES)) < PANEL
    later = product(0)
    for i, start in enumerate(starts):
        both = later
        if i + 1 < len(starts):
            later = product(i + 1)
        near = both[:, :LANES]
        near = near * swap_halves(near)
        far = both[:, LANES : 2 * LANES] * both[:, 2 * LANES :]
        largest = jnp.max(jnp.maximum(jnp.abs(near), jnp.abs(far)), axis=1, keepdims=True)
        exponent = jnp.floor(jnp.log2(jnp.maximum(largest, 1e-30))) + 1.0
        scale = jnp.exp2(15.0 - exponent) * MARGIN
        far = nearest(far * scale)
        near = nearest(near * scale)
        far_top = nearest(far * (1 / 256))
        near_top = nearest(near * (1 / 256))
        here = slice(start, start + block)
        terms_ref[here, :LANES] = far_top.astype(BF16)
        terms_ref[here, LANES : 2 * LANES] = (far - far_top * 256.0).astype(BF16)
        terms_ref[here, 2 * LANES : 3 * LANES] = jnp.where(low_lanes, near_top, near - near_top * 256.0).astype(BF16)
        terms_ref[here, 3 * LANES :] = jnp.broadcast_to(exponent, (block, LANES)).astype(BF16)

    def coded(start, size):
        got = jnp.dot(picks_ref[start : start + size, :], terms_ref[...], preferred_element_type=F32)
        far = got[:, :LANES] * 256.0 + got[:, LANES : 2 * LANES]
        pair = got[:, 2 * LANES : 3 * LANES]
        pair = jnp.where(lane_ids(pair.shape) < PANEL, pair * 256.0, pair)
        near = (pair + swap_halves(pair)).astype(jnp.int32) * 65536 + (got[:, 3 * LANES :].astype(jnp.int32) + BIAS)
        return far.astype(jnp.int32), near

    block = half // 2
    for start in range(0, half, block):
        far_low, near_low = coded(start, block)
        far_high, near_high = coded(half + start, block)
        out_ref[start : start + block, :LANES] = far_low * 65536 + (far_high & 65535)
        out_ref[start : start + block, LANES:] = jnp.where(lane_ids(near_low.shape) < PANEL, near_low, near_high)


def rest_products(my_index, order, a_rows, parts, offsets, share):
    rows, depth = a_rows.shape
    return pl.pallas_call(
        functools.partial(rest_product_kernel, offsets, share),
        in_specs=[
            pl.BlockSpec(memory_space=pltpu.SMEM),
            pl.BlockSpec(memory_space=pltpu.VMEM),
            pl.BlockSpec(memory_space=pltpu.HBM),
        ]
        + [pl.BlockSpec(memory_space=pltpu.VMEM)] * len(parts),
        out_specs=pl.BlockSpec(memory_space=pltpu.VMEM),
        out_shape=jax.ShapeDtypeStruct((rows // 2, 2 * LANES), jnp.int32),
        scratch_shapes=[
            pltpu.VMEM((rows, depth), BF16),
            pltpu.VMEM((rows, LANES), jnp.int32),
            pltpu.VMEM((rows, rows), BF16),
            pltpu.VMEM((depth, 3 * LANES), BF16),
            pltpu.VMEM((rows, 4 * LANES), BF16),
            pltpu.SemaphoreType.DMA((rows // DEEP_BLOCK,)),
        ],
        compiler_params=params(32),
        cost_estimate=pl.CostEstimate(
            flops=2 * rows * (3 * depth + 4 * rows) * LANES, bytes_accessed=2 * rows * depth, transcendentals=0
        ),
        name="rest_products",
    )(my_index, order, in_hbm(a_rows), *parts)


def packed_terms(x, terms_ref, start):
    half = x.shape[0]
    first, second, third = (term.astype(F32) for term in split(x, 3))
    near = lane_ids(x.shape) < PANEL
    other = swap_halves(third)
    terms_ref[:half, start : start + LANES] = jnp.where(near, first, swap_halves(second)).astype(BF16)
    terms_ref[half:, start : start + LANES] = jnp.where(near, swap_halves(first), second).astype(BF16)
    terms_ref[:half, start + LANES : start + 2 * LANES] = jnp.where(near, third, other).astype(BF16)
    terms_ref[half:, start + LANES : start + 2 * LANES] = jnp.where(near, other, third).astype(BF16)


def leading_kernel(held, index_ref, arrived_ref, out_ref, terms_ref):
    packed_terms(arrived_ref[...], terms_ref, 0)
    width = -(-held // LANES) * LANES
    picks = one_hot(index_ref[:, :width], terms_ref.shape[0])
    got = whole_sum(jnp.dot(picks, terms_ref[...], preferred_element_type=F32))
    first, second = got[: held // 2], got[held // 2 : held]
    out_ref[0] = jnp.where(lane_ids(first.shape) < PANEL, first, second)


def leading_rows(index, arrived, held):
    rows = index.shape[1]
    return pl.pallas_call(
        functools.partial(leading_kernel, held),
        in_specs=[pl.BlockSpec(memory_space=pltpu.VMEM)] * 2,
        out_specs=pl.BlockSpec(memory_space=pltpu.VMEM),
        out_shape=jax.ShapeDtypeStruct((1, held // 2, LANES), F32),
        scratch_shapes=[pltpu.VMEM((rows, 2 * LANES), BF16)],
        compiler_params=params(),
        cost_estimate=pl.CostEstimate(
            flops=4 * held * rows * LANES, bytes_accessed=2 * rows * LANES, transcendentals=0
        ),
        name="leading_rows",
    )(index, arrived)


def eliminate(block, shift_row):
    rows = lax.broadcasted_iota(jnp.int32, (PANEL, PANEL), 0)
    columns = lax.broadcasted_iota(jnp.int32, (PANEL, PANEL), 1)
    flipped = jnp.transpose(block)
    mirrored = jnp.where(rows >= columns, block, flipped)
    diagonal = shift_row + jnp.sum(jnp.abs(mirrored), axis=0, keepdims=True)
    unit = (rows == columns).astype(F32)
    work = jnp.where(rows == columns, diagonal, mirrored)
    work = jnp.concatenate([work, unit], axis=1)
    height = 8
    groups = [work[start : start + height] for start in range(0, PANEL, height)]
    sublanes = lax.broadcasted_iota(jnp.int32, (height, LANES), 0)
    scaled_rows = []
    for k in range(PANEL):
        home, offset = divmod(k, height)
        row = groups[home][offset : offset + 1, :]
        row = row / row[:, k : k + 1]
        scaled_rows.append(row)
        for g in range(home, PANEL // height):
            column = jnp.broadcast_to(groups[g][:, k : k + 1], (height, LANES))
            if g == home:
                column = jnp.where(sublanes > offset, column, 0.0)
            groups[g] = groups[g] - column * row
    final = jnp.concatenate(groups, axis=0)
    scaled = jnp.concatenate(scaled_rows, axis=0)
    upper = jnp.where(columns >= rows, scaled[:, :PANEL], 0.0)
    pivots = jnp.sum(jnp.where(rows == columns, final[:, :PANEL], 0.0), axis=0, keepdims=True)
    return upper, final[:, PANEL:], pivots


def exact(lhs, rhs, dims):
    return lax.dot_general(lhs, rhs, (dims, ((), ())), precision=lax.Precision.HIGHEST, preferred_element_type=F32)


def update_kernel(offsets, blocks_held, columns, my_ref, index_ref, arrived_ref, shift_ref, resident_hbm, *refs):
    parts = refs[:-12]
    near_hbm, far_hbm, pivots_ref, leading_ref, tail_ref, resident_ref, terms_ref, lead_ref = refs[-12:-4]
    near_ref, far_ref, sem, sems = refs[-4:]
    fetch = pltpu.make_async_copy(resident_hbm, resident_ref, sem)
    fetch.start()
    my_index = my_ref[0]
    size = len(offsets)
    position = 0
    packed = blocks_held * PANEL // 2
    part_rows = PANEL // 2
    for part in parts:
        for number in range(part.shape[0]):
            owner = my_index ^ offsets[position]
            for start in range(0, blocks_held * PANEL, part_rows):
                held, inner = divmod(start, PANEL)
                if start < packed:
                    rows = part[number, start : start + part_rows, :PANEL]
                else:
                    rows = part[number, start - packed : start - packed + part_rows, PANEL:]
                target = pl.multiple_of((held * size + owner) * PANEL + inner, part_rows)
                leading_ref[pl.ds(target, part_rows), :] = rows
            position += 1
    upper, inverse, pivots = eliminate(leading_ref[:PANEL, :], shift_ref[...])
    pivots_ref[...] = pivots
    lower = jnp.transpose(upper)
    needed = tail_ref.shape[1]
    tail = exact(inverse, leading_ref[:needed, :], ((1,), (1,)))
    high, low = split(tail, 2)
    tail_ref[0:PANEL, :] = high
    tail_ref[PANEL : 2 * PANEL, :] = high
    tail_ref[2 * PANEL : 3 * PANEL, :] = low
    tail_ref[3 * PANEL :, :] = low

    block = A_BLOCK
    packed_terms(arrived_ref[...], terms_ref, 0)
    for start in range(0, lead_ref.shape[0], block):
        picks = one_hot(index_ref[:, start : start + block], lead_ref.shape[0])
        got = jnp.dot(picks, terms_ref[...], preferred_element_type=F32)
        lead_ref[start : start + block, :] = whole_sum(got)[:, :PANEL]
    fetch.wait()
    stores = []
    for number, start in enumerate(range(0, lead_ref.shape[0], block)):
        rows_here = slice(start, start + block)
        panel = exact(lead_ref[rows_here, :], inverse, ((1,), (1,))) / pivots
        shown = used = panel
        if start == 0:
            row_ids = lax.broadcasted_iota(jnp.int32, panel.shape, 0)
            top = jnp.logical_and(my_index == 0, row_ids < PANEL)
            used = jnp.where(top, 0.0, panel)
            filled = jnp.concatenate([lower, jnp.zeros((block - PANEL, PANEL), F32)], axis=0)
            shown = jnp.where(top, filled, panel)
        high, low = (term.astype(F32) for term in split(used, 2))
        pair = jnp.concatenate([high, low], axis=1).astype(BF16)
        factors = jnp.concatenate([pair, pair], axis=1)
        update = jnp.dot(factors, tail_ref[...], preferred_element_type=F32)
        shown = jnp.concatenate([shown, jnp.zeros_like(shown)], axis=1)
        near_ref[rows_here, :LANES] = jnp.where(lane_ids(shown.shape) < PANEL, shown, -update[:, :LANES])
        near_ref[rows_here, LANES:] = -update[:, LANES:columns]
        far_ref[rows_here, :] = (resident_ref[rows_here, :].astype(F32) - update[:, columns:]).astype(BF16)
        for which, (source, target) in enumerate(((near_ref, near_hbm), (far_ref, far_hbm))):
            store = pltpu.make_async_copy(
                source.at[pl.ds(start, block), :], target.at[pl.ds(start, block), :], sems.at[which, number]
            )
            store.start()
            stores.append(store)
    for store in stores:
        store.wait()


def updates(my_index, parts, offsets, index, arrived, shift, resident, blocks_held, columns):
    rows, width = resident.shape
    needed = columns + width
    held_rows = len(offsets) * blocks_held * PANEL
    vmem = pl.BlockSpec(memory_space=pltpu.VMEM)
    anywhere = pl.BlockSpec(memory_space=pltpu.HBM)
    return pl.pallas_call(
        functools.partial(update_kernel, offsets, blocks_held, columns),
        in_specs=[pl.BlockSpec(memory_space=pltpu.SMEM), vmem, vmem, vmem, anywhere] + [vmem] * len(parts),
        out_specs=[anywhere, anywhere, vmem],
        out_shape=[
            pltpu.HBM((rows, columns), F32),
            pltpu.HBM((rows, width), BF16),
            jax.ShapeDtypeStruct((1, PANEL), F32),
        ],
        scratch_shapes=[
            pltpu.VMEM((held_rows, PANEL), F32),
            pltpu.VMEM((4 * PANEL, needed), BF16),
            pltpu.VMEM((rows, width), BF16),
            pltpu.VMEM((rows, 2 * LANES), BF16),
            pltpu.VMEM((rows, PANEL), F32),
            pltpu.VMEM((rows, columns), F32),
            pltpu.VMEM((rows, width), BF16),
            pltpu.SemaphoreType.DMA,
            pltpu.SemaphoreType.DMA((2, rows // A_BLOCK)),
        ],
        compiler_params=params(32),
        cost_estimate=pl.CostEstimate(
            flops=2 * rows * needed * 4 * PANEL, bytes_accessed=4 * rows * (columns + width), transcendentals=0
        ),
        name="factor_and_update",
    )(my_index, index, arrived, shift, in_hbm(resident), *parts)


def formed_kernel(index_ref, arrived_ref, near_hbm, out_hbm, near_ref, terms_ref, out_ref, in_sems, out_sems):
    half = arrived_ref.shape[0]
    block = A_BLOCK
    starts = range(0, near_ref.shape[0], block)

    def rows_of(ref, start):
        return ref.at[pl.ds(start, block), :]

    fetches = [
        pltpu.make_async_copy(rows_of(near_hbm, start), rows_of(near_ref, start), in_sems.at[i])
        for i, start in enumerate(starts)
    ]
    for fetch in fetches:
        fetch.start()
    words = arrived_ref[:, LANES:]
    low_lanes = lane_ids(words.shape) < PANEL
    scale = jnp.exp2(((words & 255) - (BIAS + 15)).astype(F32)) * (1 / MARGIN)
    other = swap_halves(scale)
    first, second = (term.astype(F32) for term in split((words >> 16).astype(F32) * scale, 2))
    terms_ref[:half, 2 * LANES :] = jnp.where(low_lanes, first, swap_halves(second)).astype(BF16)
    terms_ref[half:, 2 * LANES :] = jnp.where(low_lanes, swap_halves(first), second).astype(BF16)
    words = arrived_ref[:, :LANES]
    low = (words >> 16).astype(F32) * jnp.where(low_lanes, scale, other)
    high = ((words << 16) >> 16).astype(F32) * jnp.where(low_lanes, other, scale)
    for side, values in enumerate((low, high)):
        first, second = split(values, 2)
        terms_ref[side * half : (side + 1) * half, :LANES] = first
        terms_ref[side * half : (side + 1) * half, LANES : 2 * LANES] = second

    stores = []
    for i, start in enumerate(starts):
        rows_here = slice(start, start + block)
        picks = one_hot(index_ref[:, rows_here], terms_ref.shape[0])
        got = jnp.dot(picks, terms_ref[...], preferred_element_type=F32)
        pair = got[:, 2 * LANES :]
        fetches[i].wait()
        held = near_ref[rows_here, :LANES]
        out_ref[rows_here, :LANES] = jnp.where(
            lane_ids(held.shape) < PANEL, held, (pair + swap_halves(pair)) + held
        )
        out_ref[rows_here, LANES:] = (got[:, :LANES] + got[:, LANES : 2 * LANES]) + near_ref[rows_here, LANES:]
        store = pltpu.make_async_copy(rows_of(out_ref, start), rows_of(out_hbm, start), out_sems.at[i])
        store.start()
        stores.append(store)
    for store in stores:
        store.wait()


def formed_columns(index, arrived, near):
    rows, columns = near.shape
    vmem = pl.BlockSpec(memory_space=pltpu.VMEM)
    anywhere = pl.BlockSpec(memory_space=pltpu.HBM)
    return pl.pallas_call(
        formed_kernel,
        in_specs=[vmem, vmem, anywhere],
        out_specs=anywhere,
        out_shape=pltpu.HBM((rows, columns), F32),
        input_output_aliases={2: 0},
        scratch_shapes=[
            pltpu.VMEM((rows, columns), F32),
            pltpu.VMEM((rows, 3 * LANES), BF16),
            pltpu.VMEM((rows, columns), F32),
            pltpu.SemaphoreType.DMA((rows // A_BLOCK,)),
            pltpu.SemaphoreType.DMA((rows // A_BLOCK,)),
        ],
        compiler_params=params(32),
        cost_estimate=pl.CostEstimate(
            flops=8 * rows * rows * LANES, bytes_accessed=8 * rows * columns, transcendentals=0
        ),
        name="formed_columns",
    )(index, arrived, near)


def swap_rows(x, group):
    rows, width = x.shape
    return lax.all_to_all(
        x.reshape(group, rows // group, width), "wide", split_axis=0, concat_axis=0, tiled=True
    ).reshape(rows, width)


def on_device(a_rows, xa_panel, za_panel, send_order, recv_order, shift, resident):
    rows = a_rows.shape[0]
    columns = xa_panel.shape[1]
    group = lax.axis_size("wide")
    my_index = lax.axis_index("wide").astype(jnp.int32).reshape(1)
    share = rows // group
    half = rows // 2
    few, apart = phases_of(group)

    order, packing = send_order, share
    if share % 16:
        order = send_order.reshape(group, 2, share // 2).transpose(1, 0, 2).reshape(1, rows)
        packing = 0
    source, slot = recv_order // share, recv_order % share
    index = (slot // (share // 2)) * half + source * (share // 2) + slot % (share // 2)

    lead_panel, rest_panel = split_panels(my_index, xa_panel, za_panel)
    send_picks, a_copy = order_picks(order, a_rows, packing)
    lead_parts = join(exchange([lead_panel], few[0], "wide"))
    rest_parts = exchange(tied([rest_panel], *lead_parts), apart[0], "wide")
    for masks in few[1:]:
        lead_parts = exchange(join(lead_parts), masks, "wide")
    rest_parts = tied(rest_parts, *lead_parts)
    for masks in apart[1:-2]:
        rest_parts = exchange(join(rest_parts), masks, "wide")

    lead_out = lead_products(my_index, a_copy, send_picks, lead_parts, offsets_of(few))
    lead_in = swap_rows(tied([lead_out], *rest_parts)[0], group)
    rest_parts = exchange(join(tied(rest_parts, lead_out)), apart[-2], "wide")

    needed = columns + resident.shape[1]
    blocks_held = -(-needed // (PANEL * group))
    leading_parts = [leading_rows(index, lead_in, blocks_held * PANEL)]
    for masks in few:
        leading_parts = exchange(join(leading_parts), masks, "wide")
        if masks is few[0]:
            rest_parts = exchange(tied(rest_parts, *leading_parts), apart[-1], "wide")
    rest_out = rest_products(my_index, order, a_rows, rest_parts, offsets_of(apart), packing)
    rest_in = swap_rows(tied([rest_out], *leading_parts)[0], group)
    near, updated, pivots = updates(
        my_index,
        leading_parts,
        offsets_of(few),
        index,
        tied([lead_in], rest_out)[0],
        shift[None, :],
        resident,
        blocks_held,
        columns,
    )
    factored = formed_columns(index, rest_in, near)
    return (factored, updated, pivots[0])


def solution(mesh):
    placed = (
        P(("parts", "wide"), None),
        P(("parts", "wide"), None),
        P(("parts", "wide"), None),
        P(("parts", "wide"), None),
        P(("parts", "wide"), None),
        P("parts"),
        P(("parts", "wide"), None),
    )
    return jax.shard_map(
        on_device,
        mesh=mesh,
        in_specs=placed,
        out_specs=(P(("parts", "wide"), None), P(("parts", "wide"), None), P("parts")),
        check_vma=False,
    )
```

```python
import functools

import jax
import jax.numpy as jnp
from jax import lax
from jax.experimental import pallas as pl
from jax.experimental.pallas import tpu as pltpu
from jax.sharding import PartitionSpec as P

PANEL = 64
LANES = 128
A_BLOCK = 640
DEEP_BLOCK = 256
F32 = jnp.float32
BF16 = jnp.bfloat16
MIB = 1024 * 1024


def params(mebibytes=12):
    return pltpu.CompilerParams(vmem_limit_bytes=mebibytes * MIB)


def in_hbm(x):
    return pltpu.with_memory_space_constraint(x, pltpu.HBM)


def lane_ids(shape):
    return lax.broadcasted_iota(jnp.int32, shape, len(shape) - 1)


def split(x, count):
    terms = []
    for _ in range(count):
        term = x.astype(BF16)
        terms.append(term)
        x = x - term.astype(F32)
    return terms


def swap_halves(x):
    return pltpu.roll(x, LANES // 2, 1)


def as_column(index_row):
    return jnp.transpose(jnp.broadcast_to(index_row, (LANES, LANES)))


def picks_of(at, width):
    lanes = lane_ids(at.shape)
    return jnp.concatenate(
        [(at == lanes + column).astype(F32).astype(BF16) for column in range(0, width, LANES)], axis=1
    )


def fill_picks(at_ref, picks_ref):
    rows, width = picks_ref.shape
    for start in range(0, rows, LANES):
        picks_ref[start : start + LANES, :] = picks_of(at_ref[start : start + LANES, :], width)


def one_hot(index_row, width):
    chunks = [
        picks_of(as_column(index_row[:, start : start + LANES]), width)
        for start in range(0, index_row.shape[1], LANES)
    ]
    return jnp.concatenate(chunks, axis=0) if len(chunks) > 1 else chunks[0]


def packed_order(share, half, slot):
    part = share // 2
    return (slot % share) // part * half + slot // share * part + slot % part


def fill_order(order_ref, at_ref, share):
    rows = order_ref.shape[1]
    height = 8
    for start in range(0, rows, LANES):
        column = as_column(order_ref[:, start : start + LANES])
        if not share:
            at_ref[start : start + LANES, :] = column
            continue
        for inner in range(0, LANES, height):
            place = packed_order(share, rows // 2, start + inner)
            at_ref[place : place + height, :] = column[inner : inner + height]


def exchange(held, masks, axis):
    size = lax.axis_size(axis)
    combined = [0]
    for mask in masks:
        combined += [other ^ mask for other in combined]
    parts = list(held)
    for mask in combined[1:]:
        parts += [lax.ppermute(part, axis, [(i, i ^ mask) for i in range(size)]) for part in held]
    return parts


def offsets_of(phases):
    offsets = [0]
    for masks in phases:
        combined = [0]
        for mask in masks:
            combined += [other ^ mask for other in combined]
        offsets = [offset ^ mask for mask in combined for offset in offsets]
    return offsets


def join(parts):
    return [jnp.concatenate(parts, axis=0)]


def phases_of(size):
    bits = [1 << bit for bit in reversed(range(size.bit_length() - 1))]
    return [bits[start : start + 2] for start in range(0, len(bits), 2)], [[bit] for bit in bits]


def tied(parts, *earlier):
    return list(lax.optimization_barrier((*parts, *earlier))[: len(parts)])


def picks_kernel(share, order_hbm, a_hbm, picks_ref, copy_ref, order_ref, at_ref, sems):
    fetch = pltpu.make_async_copy(order_hbm, order_ref, sems.at[0])
    copy = pltpu.make_async_copy(a_hbm, copy_ref, sems.at[1])
    fetch.start()
    copy.start()
    fetch.wait()
    fill_order(order_ref, at_ref, share)
    fill_picks(at_ref, picks_ref)
    copy.wait()


def order_picks(order, a_rows, share):
    rows, depth = a_rows.shape
    return pl.pallas_call(
        functools.partial(picks_kernel, share),
        in_specs=[pl.BlockSpec(memory_space=pltpu.HBM)] * 2,
        out_specs=[pl.BlockSpec(memory_space=pltpu.VMEM)] * 2,
        out_shape=[jax.ShapeDtypeStruct((rows, rows), BF16), jax.ShapeDtypeStruct((rows, depth), BF16)],
        scratch_shapes=[
            pltpu.VMEM((1, rows), jnp.int32),
            pltpu.VMEM((rows, LANES), jnp.int32),
            pltpu.SemaphoreType.DMA((2,)),
        ],
        compiler_params=params(),
        cost_estimate=pl.CostEstimate(flops=4 * rows * rows, bytes_accessed=4 * rows * depth, transcendentals=0),
        name="order_picks",
    )(in_hbm(order), in_hbm(a_rows))


def panels_kernel(my_ref, xa_hbm, za_hbm, lead_ref, rest_ref, xa_ref, za_ref, sems):
    copies = [
        pltpu.make_async_copy(xa_hbm, xa_ref, sems.at[0]),
        pltpu.make_async_copy(za_hbm, za_ref, sems.at[1]),
    ]
    for copy in copies:
        copy.start()
    for copy in copies:
        copy.wait()
    lead_ref[0] = jnp.concatenate([xa_ref[:, :PANEL], za_ref[:, :PANEL]], axis=1)
    rest_ref[0, :, :LANES] = jnp.concatenate([xa_ref[:, PANEL:LANES], za_ref[:, PANEL:LANES]], axis=1)
    rest_ref[0, :, LANES : 2 * LANES] = xa_ref[:, LANES:]
    rest_ref[0, :, 2 * LANES :] = za_ref[:, LANES:]


def split_panels(my_index, xa_panel, za_panel):
    depth, columns = xa_panel.shape
    return pl.pallas_call(
        panels_kernel,
        in_specs=[pl.BlockSpec(memory_space=pltpu.SMEM)] + [pl.BlockSpec(memory_space=pltpu.HBM)] * 2,
        out_shape=[
            jax.ShapeDtypeStruct((1, depth, LANES), BF16),
            jax.ShapeDtypeStruct((1, depth, 2 * columns - LANES), BF16),
        ],
        scratch_shapes=[
            pltpu.VMEM((depth, columns), BF16),
            pltpu.VMEM((depth, columns), BF16),
            pltpu.SemaphoreType.DMA((2,)),
        ],
        compiler_params=params(),
        name="split_panels",
    )(my_index, in_hbm(xa_panel), in_hbm(za_panel))


def assemble(my_index, offsets, parts, panel_ref):
    position = 0
    for part in parts:
        for number in range(part.shape[0]):
            depth = part.shape[1]
            start = pl.multiple_of((my_index ^ offsets[position]) * depth, depth)
            panel_ref[pl.ds(start, depth), :] = part[number]
            position += 1


def whole_sum(got):
    pair = got[:, :LANES]
    return (pair + swap_halves(pair)) + got[:, LANES:]


def lead_product_kernel(offsets, my_ref, a_ref, picks_ref, *refs):
    parts, (out_ref, panel_ref, terms_ref) = refs[:-3], refs[-3:]
    assemble(my_ref[0], offsets, parts, panel_ref)
    rows = a_ref.shape[0]
    for start in range(0, rows, DEEP_BLOCK):
        both = jnp.dot(a_ref[start : start + DEEP_BLOCK, :], panel_ref[...], preferred_element_type=F32)
        first, second, third = (term.astype(F32) for term in split(both * swap_halves(both), 3))
        near = lane_ids(both.shape) < PANEL
        terms_ref[start : start + DEEP_BLOCK, :LANES] = jnp.where(near, first, second).astype(BF16)
        terms_ref[start : start + DEEP_BLOCK, LANES:] = third.astype(BF16)
    half = rows // 2
    block = half // 2
    for start in range(0, half, block):
        low = jnp.dot(picks_ref[start : start + block, :], terms_ref[...], preferred_element_type=F32)
        high = jnp.dot(picks_ref[half + start : half + start + block, :], terms_ref[...], preferred_element_type=F32)
        low, high = whole_sum(low), whole_sum(high)
        out_ref[start : start + block, :] = jnp.where(lane_ids(low.shape) < PANEL, low, high)


def lead_products(my_index, a_rows, picks, parts, offsets):
    rows, depth = a_rows.shape
    return pl.pallas_call(
        functools.partial(lead_product_kernel, offsets),
        in_specs=[pl.BlockSpec(memory_space=pltpu.SMEM)] + [pl.BlockSpec(memory_space=pltpu.VMEM)] * (2 + len(parts)),
        out_specs=pl.BlockSpec(memory_space=pltpu.VMEM),
        out_shape=jax.ShapeDtypeStruct((rows // 2, LANES), F32),
        scratch_shapes=[pltpu.VMEM((depth, LANES), BF16), pltpu.VMEM((rows, 2 * LANES), BF16)],
        compiler_params=params(),
        cost_estimate=pl.CostEstimate(
            flops=2 * rows * (depth + 2 * rows) * LANES, bytes_accessed=2 * rows * depth, transcendentals=0
        ),
        name="lead_products",
    )(my_index, a_rows, picks, *parts)


BIAS = 128
MARGIN = 0.9995
ROUNDER = 1.5 * 2.0**23


def nearest(x):
    return (x + ROUNDER) - ROUNDER


def rest_product_kernel(offsets, share, my_ref, order_ref, a_hbm, *refs):
    parts, (out_ref, a_ref, at_ref, picks_ref, panel_ref, terms_ref, sems) = refs[:-7], refs[-7:]
    rows = a_ref.shape[0]
    half = rows // 2
    block = DEEP_BLOCK
    starts = range(0, rows, block)
    copies = [
        pltpu.make_async_copy(a_hbm.at[pl.ds(start, block), :], a_ref.at[pl.ds(start, block), :], sems.at[i])
        for i, start in enumerate(starts)
    ]
    for copy in copies[:3]:
        copy.start()
    assemble(my_ref[0], offsets, parts, panel_ref)
    fill_order(order_ref, at_ref, share)
    fill_picks(at_ref, picks_ref)

    def product(i):
        copies[i].wait()
        if i + 3 < len(copies):
            copies[i + 3].start()
        return jnp.dot(a_ref[starts[i] : starts[i] + block, :], panel_ref[...], preferred_element_type=F32)

    low_lanes = lane_ids((block, LANES)) < PANEL
    later = product(0)
    for i, start in enumerate(starts):
        both = later
        if i + 1 < len(starts):
            later = product(i + 1)
        near = both[:, :LANES]
        near = near * swap_halves(near)
        far = both[:, LANES : 2 * LANES] * both[:, 2 * LANES :]
        largest = jnp.max(jnp.maximum(jnp.abs(near), jnp.abs(far)), axis=1, keepdims=True)
        exponent = jnp.floor(jnp.log2(jnp.maximum(largest, 1e-30))) + 1.0
        scale = jnp.exp2(15.0 - exponent) * MARGIN
        far = nearest(far * scale)
        near = nearest(near * scale)
        far_top = nearest(far * (1 / 256))
        near_top = nearest(near * (1 / 256))
        here = slice(start, start + block)
        terms_ref[here, :LANES] = far_top.astype(BF16)
        terms_ref[here, LANES : 2 * LANES] = (far - far_top * 256.0).astype(BF16)
        terms_ref[here, 2 * LANES : 3 * LANES] = jnp.where(low_lanes, near_top, near - near_top * 256.0).astype(BF16)
        terms_ref[here, 3 * LANES :] = jnp.broadcast_to(exponent, (block, LANES)).astype(BF16)

    def coded(start, size):
        got = jnp.dot(picks_ref[start : start + size, :], terms_ref[...], preferred_element_type=F32)
        far = got[:, :LANES] * 256.0 + got[:, LANES : 2 * LANES]
        pair = got[:, 2 * LANES : 3 * LANES]
        pair = jnp.where(lane_ids(pair.shape) < PANEL, pair * 256.0, pair)
        near = (pair + swap_halves(pair)).astype(jnp.int32) * 65536 + (got[:, 3 * LANES :].astype(jnp.int32) + BIAS)
        return far.astype(jnp.int32), near

    block = half // 2
    for start in range(0, half, block):
        far_low, near_low = coded(start, block)
        far_high, near_high = coded(half + start, block)
        out_ref[start : start + block, :LANES] = far_low * 65536 + (far_high & 65535)
        out_ref[start : start + block, LANES:] = jnp.where(lane_ids(near_low.shape) < PANEL, near_low, near_high)


def rest_products(my_index, order, a_rows, parts, offsets, share):
    rows, depth = a_rows.shape
    return pl.pallas_call(
        functools.partial(rest_product_kernel, offsets, share),
        in_specs=[
            pl.BlockSpec(memory_space=pltpu.SMEM),
            pl.BlockSpec(memory_space=pltpu.VMEM),
            pl.BlockSpec(memory_space=pltpu.HBM),
        ]
        + [pl.BlockSpec(memory_space=pltpu.VMEM)] * len(parts),
        out_specs=pl.BlockSpec(memory_space=pltpu.VMEM),
        out_shape=jax.ShapeDtypeStruct((rows // 2, 2 * LANES), jnp.int32),
        scratch_shapes=[
            pltpu.VMEM((rows, depth), BF16),
            pltpu.VMEM((rows, LANES), jnp.int32),
            pltpu.VMEM((rows, rows), BF16),
            pltpu.VMEM((depth, 3 * LANES), BF16),
            pltpu.VMEM((rows, 4 * LANES), BF16),
            pltpu.SemaphoreType.DMA((rows // DEEP_BLOCK,)),
        ],
        compiler_params=params(32),
        cost_estimate=pl.CostEstimate(
            flops=2 * rows * (3 * depth + 4 * rows) * LANES, bytes_accessed=2 * rows * depth, transcendentals=0
        ),
        name="rest_products",
    )(my_index, order, in_hbm(a_rows), *parts)


def packed_terms(x, terms_ref, start):
    half = x.shape[0]
    first, second, third = (term.astype(F32) for term in split(x, 3))
    near = lane_ids(x.shape) < PANEL
    other = swap_halves(third)
    terms_ref[:half, start : start + LANES] = jnp.where(near, first, swap_halves(second)).astype(BF16)
    terms_ref[half:, start : start + LANES] = jnp.where(near, swap_halves(first), second).astype(BF16)
    terms_ref[:half, start + LANES : start + 2 * LANES] = jnp.where(near, third, other).astype(BF16)
    terms_ref[half:, start + LANES : start + 2 * LANES] = jnp.where(near, other, third).astype(BF16)


def leading_kernel(held, index_ref, arrived_ref, out_ref, terms_ref):
    packed_terms(arrived_ref[...], terms_ref, 0)
    width = -(-held // LANES) * LANES
    picks = one_hot(index_ref[:, :width], terms_ref.shape[0])
    got = whole_sum(jnp.dot(picks, terms_ref[...], preferred_element_type=F32))
    first, second = got[: held // 2], got[held // 2 : held]
    out_ref[0] = jnp.where(lane_ids(first.shape) < PANEL, first, second)


def leading_rows(index, arrived, held):
    rows = index.shape[1]
    return pl.pallas_call(
        functools.partial(leading_kernel, held),
        in_specs=[pl.BlockSpec(memory_space=pltpu.VMEM)] * 2,
        out_specs=pl.BlockSpec(memory_space=pltpu.VMEM),
        out_shape=jax.ShapeDtypeStruct((1, held // 2, LANES), F32),
        scratch_shapes=[pltpu.VMEM((rows, 2 * LANES), BF16)],
        compiler_params=params(),
        cost_estimate=pl.CostEstimate(
            flops=4 * held * rows * LANES, bytes_accessed=2 * rows * LANES, transcendentals=0
        ),
        name="leading_rows",
    )(index, arrived)


def eliminate(block, shift_row):
    rows = lax.broadcasted_iota(jnp.int32, (PANEL, PANEL), 0)
    columns = lax.broadcasted_iota(jnp.int32, (PANEL, PANEL), 1)
    flipped = jnp.transpose(block)
    mirrored = jnp.where(rows >= columns, block, flipped)
    diagonal = shift_row + jnp.sum(jnp.abs(mirrored), axis=0, keepdims=True)
    unit = (rows == columns).astype(F32)
    work = jnp.where(rows == columns, diagonal, mirrored)
    work = jnp.concatenate([work, unit], axis=1)
    height = 8
    groups = [work[start : start + height] for start in range(0, PANEL, height)]
    sublanes = lax.broadcasted_iota(jnp.int32, (height, LANES), 0)
    scaled_rows = []
    for k in range(PANEL):
        home, offset = divmod(k, height)
        row = groups[home][offset : offset + 1, :]
        row = row / row[:, k : k + 1]
        scaled_rows.append(row)
        for g in range(home, PANEL // height):
            column = jnp.broadcast_to(groups[g][:, k : k + 1], (height, LANES))
            if g == home:
                column = jnp.where(sublanes > offset, column, 0.0)
            groups[g] = groups[g] - column * row
    final = jnp.concatenate(groups, axis=0)
    scaled = jnp.concatenate(scaled_rows, axis=0)
    upper = jnp.where(columns >= rows, scaled[:, :PANEL], 0.0)
    pivots = jnp.sum(jnp.where(rows == columns, final[:, :PANEL], 0.0), axis=0, keepdims=True)
    return upper, final[:, PANEL:], pivots


def exact(lhs, rhs, dims):
    return lax.dot_general(lhs, rhs, (dims, ((), ())), precision=lax.Precision.HIGHEST, preferred_element_type=F32)


def update_kernel(offsets, blocks_held, columns, my_ref, index_ref, arrived_ref, shift_ref, resident_hbm, *refs):
    parts = refs[:-12]
    near_hbm, far_hbm, pivots_ref, leading_ref, tail_ref, resident_ref, terms_ref, lead_ref = refs[-12:-4]
    near_ref, far_ref, sem, sems = refs[-4:]
    fetch = pltpu.make_async_copy(resident_hbm, resident_ref, sem)
    fetch.start()
    my_index = my_ref[0]
    size = len(offsets)
    position = 0
    packed = blocks_held * PANEL // 2
    part_rows = PANEL // 2
    for part in parts:
        for number in range(part.shape[0]):
            owner = my_index ^ offsets[position]
            for start in range(0, blocks_held * PANEL, part_rows):
                held, inner = divmod(start, PANEL)
                if start < packed:
                    rows = part[number, start : start + part_rows, :PANEL]
                else:
                    rows = part[number, start - packed : start - packed + part_rows, PANEL:]
                target = pl.multiple_of((held * size + owner) * PANEL + inner, part_rows)
                leading_ref[pl.ds(target, part_rows), :] = rows
            position += 1
    upper, inverse, pivots = eliminate(leading_ref[:PANEL, :], shift_ref[...])
    pivots_ref[...] = pivots
    lower = jnp.transpose(upper)
    needed = tail_ref.shape[1]
    tail = exact(inverse, leading_ref[:needed, :], ((1,), (1,)))
    high, low = split(tail, 2)
    tail_ref[0:PANEL, :] = high
    tail_ref[PANEL : 2 * PANEL, :] = high
    tail_ref[2 * PANEL : 3 * PANEL, :] = low
    tail_ref[3 * PANEL :, :] = low

    block = A_BLOCK
    packed_terms(arrived_ref[...], terms_ref, 0)
    for start in range(0, lead_ref.shape[0], block):
        picks = one_hot(index_ref[:, start : start + block], lead_ref.shape[0])
        got = jnp.dot(picks, terms_ref[...], preferred_element_type=F32)
        lead_ref[start : start + block, :] = whole_sum(got)[:, :PANEL]
    fetch.wait()
    stores = []
    for number, start in enumerate(range(0, lead_ref.shape[0], block)):
        rows_here = slice(start, start + block)
        panel = exact(lead_ref[rows_here, :], inverse, ((1,), (1,))) / pivots
        shown = used = panel
        if start == 0:
            row_ids = lax.broadcasted_iota(jnp.int32, panel.shape, 0)
            top = jnp.logical_and(my_index == 0, row_ids < PANEL)
            used = jnp.where(top, 0.0, panel)
            filled = jnp.concatenate([lower, jnp.zeros((block - PANEL, PANEL), F32)], axis=0)
            shown = jnp.where(top, filled, panel)
        high, low = (term.astype(F32) for term in split(used, 2))
        pair = jnp.concatenate([high, low], axis=1).astype(BF16)
        factors = jnp.concatenate([pair, pair], axis=1)
        update = jnp.dot(factors, tail_ref[...], preferred_element_type=F32)
        shown = jnp.concatenate([shown, jnp.zeros_like(shown)], axis=1)
        near_ref[rows_here, :LANES] = jnp.where(lane_ids(shown.shape) < PANEL, shown, -update[:, :LANES])
        near_ref[rows_here, LANES:] = -update[:, LANES:columns]
        far_ref[rows_here, :] = (resident_ref[rows_here, :].astype(F32) - update[:, columns:]).astype(BF16)
        for which, (source, target) in enumerate(((near_ref, near_hbm), (far_ref, far_hbm))):
            store = pltpu.make_async_copy(
                source.at[pl.ds(start, block), :], target.at[pl.ds(start, block), :], sems.at[which, number]
            )
            store.start()
            stores.append(store)
    for store in stores:
        store.wait()


def updates(my_index, parts, offsets, index, arrived, shift, resident, blocks_held, columns):
    rows, width = resident.shape
    needed = columns + width
    held_rows = len(offsets) * blocks_held * PANEL
    vmem = pl.BlockSpec(memory_space=pltpu.VMEM)
    anywhere = pl.BlockSpec(memory_space=pltpu.HBM)
    return pl.pallas_call(
        functools.partial(update_kernel, offsets, blocks_held, columns),
        in_specs=[pl.BlockSpec(memory_space=pltpu.SMEM), vmem, vmem, vmem, anywhere] + [vmem] * len(parts),
        out_specs=[anywhere, anywhere, vmem],
        out_shape=[
            pltpu.HBM((rows, columns), F32),
            pltpu.HBM((rows, width), BF16),
            jax.ShapeDtypeStruct((1, PANEL), F32),
        ],
        scratch_shapes=[
            pltpu.VMEM((held_rows, PANEL), F32),
            pltpu.VMEM((4 * PANEL, needed), BF16),
            pltpu.VMEM((rows, width), BF16),
            pltpu.VMEM((rows, 2 * LANES), BF16),
            pltpu.VMEM((rows, PANEL), F32),
            pltpu.VMEM((rows, columns), F32),
            pltpu.VMEM((rows, width), BF16),
            pltpu.SemaphoreType.DMA,
            pltpu.SemaphoreType.DMA((2, rows // A_BLOCK)),
        ],
        compiler_params=params(32),
        cost_estimate=pl.CostEstimate(
            flops=2 * rows * needed * 4 * PANEL, bytes_accessed=4 * rows * (columns + width), transcendentals=0
        ),
        name="factor_and_update",
    )(my_index, index, arrived, shift, in_hbm(resident), *parts)


def formed_kernel(index_ref, arrived_ref, near_hbm, out_hbm, near_ref, terms_ref, out_ref, in_sems, out_sems):
    half = arrived_ref.shape[0]
    block = A_BLOCK
    starts = range(0, near_ref.shape[0], block)

    def rows_of(ref, start):
        return ref.at[pl.ds(start, block), :]

    fetches = [
        pltpu.make_async_copy(rows_of(near_hbm, start), rows_of(near_ref, start), in_sems.at[i])
        for i, start in enumerate(starts)
    ]
    for fetch in fetches:
        fetch.start()
    words = arrived_ref[:, LANES:]
    low_lanes = lane_ids(words.shape) < PANEL
    scale = jnp.exp2(((words & 255) - (BIAS + 15)).astype(F32)) * (1 / MARGIN)
    other = swap_halves(scale)
    first, second = (term.astype(F32) for term in split((words >> 16).astype(F32) * scale, 2))
    terms_ref[:half, 2 * LANES :] = jnp.where(low_lanes, first, swap_halves(second)).astype(BF16)
    terms_ref[half:, 2 * LANES :] = jnp.where(low_lanes, swap_halves(first), second).astype(BF16)
    words = arrived_ref[:, :LANES]
    low = (words >> 16).astype(F32) * jnp.where(low_lanes, scale, other)
    high = ((words << 16) >> 16).astype(F32) * jnp.where(low_lanes, other, scale)
    for side, values in enumerate((low, high)):
        first, second = split(values, 2)
        terms_ref[side * half : (side + 1) * half, :LANES] = first
        terms_ref[side * half : (side + 1) * half, LANES : 2 * LANES] = second

    stores = []
    for i, start in enumerate(starts):
        rows_here = slice(start, start + block)
        picks = one_hot(index_ref[:, rows_here], terms_ref.shape[0])
        got = jnp.dot(picks, terms_ref[...], preferred_element_type=F32)
        pair = got[:, 2 * LANES :]
        fetches[i].wait()
        held = near_ref[rows_here, :LANES]
        out_ref[rows_here, :LANES] = jnp.where(
            lane_ids(held.shape) < PANEL, held, (pair + swap_halves(pair)) + held
        )
        out_ref[rows_here, LANES:] = (got[:, :LANES] + got[:, LANES : 2 * LANES]) + near_ref[rows_here, LANES:]
        store = pltpu.make_async_copy(rows_of(out_ref, start), rows_of(out_hbm, start), out_sems.at[i])
        store.start()
        stores.append(store)
    for store in stores:
        store.wait()


def formed_columns(index, arrived, near):
    rows, columns = near.shape
    vmem = pl.BlockSpec(memory_space=pltpu.VMEM)
    anywhere = pl.BlockSpec(memory_space=pltpu.HBM)
    return pl.pallas_call(
        formed_kernel,
        in_specs=[vmem, vmem, anywhere],
        out_specs=anywhere,
        out_shape=pltpu.HBM((rows, columns), F32),
        input_output_aliases={2: 0},
        scratch_shapes=[
            pltpu.VMEM((rows, columns), F32),
            pltpu.VMEM((rows, 3 * LANES), BF16),
            pltpu.VMEM((rows, columns), F32),
            pltpu.SemaphoreType.DMA((rows // A_BLOCK,)),
            pltpu.SemaphoreType.DMA((rows // A_BLOCK,)),
        ],
        compiler_params=params(32),
        cost_estimate=pl.CostEstimate(
            flops=8 * rows * rows * LANES, bytes_accessed=8 * rows * columns, transcendentals=0
        ),
        name="formed_columns",
    )(index, arrived, near)


def swap_rows(x, group):
    rows, width = x.shape
    return lax.all_to_all(
        x.reshape(group, rows // group, width), "wide", split_axis=0, concat_axis=0, tiled=True
    ).reshape(rows, width)


def on_device(a_rows, xa_panel, za_panel, send_order, recv_order, shift, resident):
    rows = a_rows.shape[0]
    columns = xa_panel.shape[1]
    group = lax.axis_size("wide")
    my_index = lax.axis_index("wide").astype(jnp.int32).reshape(1)
    share = rows // group
    half = rows // 2
    few, apart = phases_of(group)

    order, packing = send_order, share
    if share % 16:
        order = send_order.reshape(group, 2, share // 2).transpose(1, 0, 2).reshape(1, rows)
        packing = 0
    source, slot = recv_order // share, recv_order % share
    index = (slot // (share // 2)) * half + source * (share // 2) + slot % (share // 2)

    lead_panel, rest_panel = split_panels(my_index, xa_panel, za_panel)
    send_picks, a_copy = order_picks(order, a_rows, packing)
    lead_parts = [lead_panel]
    for masks in few:
        lead_parts = exchange(join(lead_parts), masks, "wide")
    rest_parts = [rest_panel]
    for number, masks in enumerate(apart[:-2]):
        rest_parts = exchange(join(rest_parts), masks, "wide")
        if number == 0:
            lead_parts = tied(lead_parts, *rest_parts)

    lead_out = lead_products(my_index, a_copy, send_picks, lead_parts, offsets_of(few))
    lead_in = swap_rows(tied([lead_out], *rest_parts)[0], group)
    rest_parts = exchange(join(tied(rest_parts, lead_out)), apart[-2], "wide")
    other_parts = exchange(rest_parts[:1], apart[-1], "wide")[1:]

    needed = columns + resident.shape[1]
    blocks_held = -(-needed // (PANEL * group))
    leading_parts = [leading_rows(index, lead_in, blocks_held * PANEL)]
    for masks in few:
        leading_parts = exchange(join(leading_parts), masks, "wide")
        if masks is few[0]:
            later_parts = exchange(tied(rest_parts[1:], *leading_parts), apart[-1], "wide")
    late = len(later_parts) // 2
    rest_parts = rest_parts + other_parts + later_parts[late:]
    rest_out = rest_products(my_index, order, a_rows, rest_parts, offsets_of(apart), packing)
    rest_in = swap_rows(tied([rest_out], *leading_parts)[0], group)
    near, updated, pivots = updates(
        my_index,
        leading_parts,
        offsets_of(few),
        index,
        tied([lead_in], rest_out)[0],
        shift[None, :],
        resident,
        blocks_held,
        columns,
    )
    factored = formed_columns(index, rest_in, near)
    return (factored, updated, pivots[0])


def solution(mesh):
    placed = (
        P(("parts", "wide"), None),
        P(("parts", "wide"), None),
        P(("parts", "wide"), None),
        P(("parts", "wide"), None),
        P(("parts", "wide"), None),
        P("parts"),
        P(("parts", "wide"), None),
    )
    return jax.shard_map(
        on_device,
        mesh=mesh,
        in_specs=placed,
        out_specs=(P(("parts", "wide"), None), P(("parts", "wide"), None), P("parts")),
        check_vma=False,
    )
```

```python
import functools

import jax
import jax.numpy as jnp
from jax import lax
from jax.experimental import pallas as pl
from jax.experimental.pallas import tpu as pltpu
from jax.sharding import PartitionSpec as P

PANEL = 64
LANES = 128
A_BLOCK = 640
DEEP_BLOCK = 256
F32 = jnp.float32
BF16 = jnp.bfloat16
MIB = 1024 * 1024


def params(mebibytes=12):
    return pltpu.CompilerParams(vmem_limit_bytes=mebibytes * MIB)


def in_hbm(x):
    return pltpu.with_memory_space_constraint(x, pltpu.HBM)


def lane_ids(shape):
    return lax.broadcasted_iota(jnp.int32, shape, len(shape) - 1)


def split(x, count):
    terms = []
    for _ in range(count):
        term = x.astype(BF16)
        terms.append(term)
        x = x - term.astype(F32)
    return terms


def swap_halves(x):
    return pltpu.roll(x, LANES // 2, 1)


def as_column(index_row):
    return jnp.transpose(jnp.broadcast_to(index_row, (LANES, LANES)))


def picks_of(at, width):
    lanes = lane_ids(at.shape)
    return jnp.concatenate(
        [(at == lanes + column).astype(F32).astype(BF16) for column in range(0, width, LANES)], axis=1
    )


def fill_picks(at_ref, picks_ref):
    rows, width = picks_ref.shape
    for start in range(0, rows, LANES):
        picks_ref[start : start + LANES, :] = picks_of(at_ref[start : start + LANES, :], width)


def one_hot(index_row, width):
    chunks = [
        picks_of(as_column(index_row[:, start : start + LANES]), width)
        for start in range(0, index_row.shape[1], LANES)
    ]
    return jnp.concatenate(chunks, axis=0) if len(chunks) > 1 else chunks[0]


def packed_order(share, half, slot):
    part = share // 2
    return (slot % share) // part * half + slot // share * part + slot % part


def fill_order(order_ref, at_ref, share):
    rows = order_ref.shape[1]
    height = 8
    for start in range(0, rows, LANES):
        column = as_column(order_ref[:, start : start + LANES])
        if not share:
            at_ref[start : start + LANES, :] = column
            continue
        for inner in range(0, LANES, height):
            place = packed_order(share, rows // 2, start + inner)
            at_ref[place : place + height, :] = column[inner : inner + height]


def exchange(held, masks, axis):
    size = lax.axis_size(axis)
    combined = [0]
    for mask in masks:
        combined += [other ^ mask for other in combined]
    parts = list(held)
    for mask in combined[1:]:
        parts += [lax.ppermute(part, axis, [(i, i ^ mask) for i in range(size)]) for part in held]
    return parts


def offsets_of(phases):
    offsets = [0]
    for masks in phases:
        combined = [0]
        for mask in masks:
            combined += [other ^ mask for other in combined]
        offsets = [offset ^ mask for mask in combined for offset in offsets]
    return offsets


def join(parts):
    return [jnp.concatenate(parts, axis=0)]


def phases_of(size):
    bits = [1 << bit for bit in reversed(range(size.bit_length() - 1))]
    return [bits[start : start + 2] for start in range(0, len(bits), 2)], [[bit] for bit in bits]


def tied(parts, *earlier):
    return list(lax.optimization_barrier((*parts, *earlier))[: len(parts)])


def picks_kernel(share, order_hbm, a_hbm, picks_ref, copy_ref, order_ref, at_ref, sems):
    fetch = pltpu.make_async_copy(order_hbm, order_ref, sems.at[0])
    copy = pltpu.make_async_copy(a_hbm, copy_ref, sems.at[1])
    fetch.start()
    copy.start()
    fetch.wait()
    fill_order(order_ref, at_ref, share)
    fill_picks(at_ref, picks_ref)
    copy.wait()


def order_picks(order, a_rows, share):
    rows, depth = a_rows.shape
    return pl.pallas_call(
        functools.partial(picks_kernel, share),
        in_specs=[pl.BlockSpec(memory_space=pltpu.HBM)] * 2,
        out_specs=[pl.BlockSpec(memory_space=pltpu.VMEM)] * 2,
        out_shape=[jax.ShapeDtypeStruct((rows, rows), BF16), jax.ShapeDtypeStruct((rows, depth), BF16)],
        scratch_shapes=[
            pltpu.VMEM((1, rows), jnp.int32),
            pltpu.VMEM((rows, LANES), jnp.int32),
            pltpu.SemaphoreType.DMA((2,)),
        ],
        compiler_params=params(),
        cost_estimate=pl.CostEstimate(flops=4 * rows * rows, bytes_accessed=4 * rows * depth, transcendentals=0),
        name="order_picks",
    )(in_hbm(order), in_hbm(a_rows))


def panels_kernel(my_ref, xa_hbm, za_hbm, lead_ref, rest_ref, xa_ref, za_ref, sems):
    copies = [
        pltpu.make_async_copy(xa_hbm, xa_ref, sems.at[0]),
        pltpu.make_async_copy(za_hbm, za_ref, sems.at[1]),
    ]
    for copy in copies:
        copy.start()
    for copy in copies:
        copy.wait()
    lead_ref[0] = jnp.concatenate([xa_ref[:, :PANEL], za_ref[:, :PANEL]], axis=1)
    rest_ref[0, :, :LANES] = jnp.concatenate([xa_ref[:, PANEL:LANES], za_ref[:, PANEL:LANES]], axis=1)
    rest_ref[0, :, LANES : 2 * LANES] = xa_ref[:, LANES:]
    rest_ref[0, :, 2 * LANES :] = za_ref[:, LANES:]


def split_panels(my_index, xa_panel, za_panel):
    depth, columns = xa_panel.shape
    return pl.pallas_call(
        panels_kernel,
        in_specs=[pl.BlockSpec(memory_space=pltpu.SMEM)] + [pl.BlockSpec(memory_space=pltpu.HBM)] * 2,
        out_shape=[
            jax.ShapeDtypeStruct((1, depth, LANES), BF16),
            jax.ShapeDtypeStruct((1, depth, 2 * columns - LANES), BF16),
        ],
        scratch_shapes=[
            pltpu.VMEM((depth, columns), BF16),
            pltpu.VMEM((depth, columns), BF16),
            pltpu.SemaphoreType.DMA((2,)),
        ],
        compiler_params=params(),
        name="split_panels",
    )(my_index, in_hbm(xa_panel), in_hbm(za_panel))


def assemble(my_index, offsets, parts, panel_ref):
    position = 0
    for part in parts:
        for number in range(part.shape[0]):
            depth = part.shape[1]
            start = pl.multiple_of((my_index ^ offsets[position]) * depth, depth)
            panel_ref[pl.ds(start, depth), :] = part[number]
            position += 1


def whole_sum(got):
    pair = got[:, :LANES]
    return (pair + swap_halves(pair)) + got[:, LANES:]


def lead_product_kernel(offsets, my_ref, a_ref, picks_ref, *refs):
    parts, (out_ref, panel_ref, terms_ref) = refs[:-3], refs[-3:]
    assemble(my_ref[0], offsets, parts, panel_ref)
    rows = a_ref.shape[0]
    for start in range(0, rows, DEEP_BLOCK):
        both = jnp.dot(a_ref[start : start + DEEP_BLOCK, :], panel_ref[...], preferred_element_type=F32)
        first, second, third = (term.astype(F32) for term in split(both * swap_halves(both), 3))
        near = lane_ids(both.shape) < PANEL
        terms_ref[start : start + DEEP_BLOCK, :LANES] = jnp.where(near, first, second).astype(BF16)
        terms_ref[start : start + DEEP_BLOCK, LANES:] = third.astype(BF16)
    half = rows // 2
    block = half // 2
    for start in range(0, half, block):
        low = jnp.dot(picks_ref[start : start + block, :], terms_ref[...], preferred_element_type=F32)
        high = jnp.dot(picks_ref[half + start : half + start + block, :], terms_ref[...], preferred_element_type=F32)
        low, high = whole_sum(low), whole_sum(high)
        out_ref[start : start + block, :] = jnp.where(lane_ids(low.shape) < PANEL, low, high)


def lead_products(my_index, a_rows, picks, parts, offsets):
    rows, depth = a_rows.shape
    return pl.pallas_call(
        functools.partial(lead_product_kernel, offsets),
        in_specs=[pl.BlockSpec(memory_space=pltpu.SMEM)] + [pl.BlockSpec(memory_space=pltpu.VMEM)] * (2 + len(parts)),
        out_specs=pl.BlockSpec(memory_space=pltpu.VMEM),
        out_shape=jax.ShapeDtypeStruct((rows // 2, LANES), F32),
        scratch_shapes=[pltpu.VMEM((depth, LANES), BF16), pltpu.VMEM((rows, 2 * LANES), BF16)],
        compiler_params=params(24),
        cost_estimate=pl.CostEstimate(
            flops=2 * rows * (depth + 2 * rows) * LANES, bytes_accessed=2 * rows * depth, transcendentals=0
        ),
        name="lead_products",
    )(my_index, a_rows, picks, *parts)


BIAS = 128
MARGIN = 0.9995
ROUNDER = 1.5 * 2.0**23


def tight_split(part):
    first = -(-part // 16) * 8
    return first if part % 8 == 0 and part <= PANEL and 2 * first - part >= 8 else 0


def words_shape(half, part):
    first = tight_split(part)
    return (half // part * (part + first), LANES) if first else (half, 2 * LANES)


def nearest(x):
    return (x + ROUNDER) - ROUNDER


def rest_product_kernel(offsets, share, part_rows, my_ref, order_ref, a_hbm, *refs):
    parts, (out_ref, a_ref, at_ref, picks_ref, panel_ref, terms_ref, sems) = refs[:-7], refs[-7:]
    rows = a_ref.shape[0]
    half = rows // 2
    block = DEEP_BLOCK
    starts = range(0, rows, block)
    copies = [
        pltpu.make_async_copy(a_hbm.at[pl.ds(start, block), :], a_ref.at[pl.ds(start, block), :], sems.at[i])
        for i, start in enumerate(starts)
    ]
    for copy in copies[:3]:
        copy.start()
    assemble(my_ref[0], offsets, parts, panel_ref)
    fill_order(order_ref, at_ref, share)
    fill_picks(at_ref, picks_ref)

    def product(i):
        copies[i].wait()
        if i + 3 < len(copies):
            copies[i + 3].start()
        return jnp.dot(a_ref[starts[i] : starts[i] + block, :], panel_ref[...], preferred_element_type=F32)

    low_lanes = lane_ids((block, LANES)) < PANEL
    later = product(0)
    for i, start in enumerate(starts):
        both = later
        if i + 1 < len(starts):
            later = product(i + 1)
        near = both[:, :LANES]
        near = near * swap_halves(near)
        far = both[:, LANES : 2 * LANES] * both[:, 2 * LANES :]
        largest = jnp.max(jnp.maximum(jnp.abs(near), jnp.abs(far)), axis=1, keepdims=True)
        exponent = jnp.floor(jnp.log2(jnp.maximum(largest, 1e-30))) + 1.0
        scale = jnp.exp2(15.0 - exponent) * MARGIN
        far = nearest(far * scale)
        near = nearest(near * scale)
        far_top = nearest(far * (1 / 256))
        near_top = nearest(near * (1 / 256))
        here = slice(start, start + block)
        terms_ref[here, :LANES] = far_top.astype(BF16)
        terms_ref[here, LANES : 2 * LANES] = (far - far_top * 256.0).astype(BF16)
        terms_ref[here, 2 * LANES : 3 * LANES] = jnp.where(low_lanes, near_top, near - near_top * 256.0).astype(BF16)
        terms_ref[here, 3 * LANES :] = jnp.broadcast_to(exponent, (block, LANES)).astype(BF16)

    def coded(start, size):
        got = jnp.dot(picks_ref[start : start + size, :], terms_ref[...], preferred_element_type=F32)
        far = got[:, :LANES] * 256.0 + got[:, LANES : 2 * LANES]
        pair = got[:, 2 * LANES : 3 * LANES]
        pair = jnp.where(lane_ids(pair.shape) < PANEL, pair * 256.0, pair)
        near = (pair + swap_halves(pair)).astype(jnp.int32)
        return far.astype(jnp.int32), near, got[:, 3 * LANES :]

    block = half // 2
    first = tight_split(part_rows)
    low_lanes = lane_ids((8, LANES)) < PANEL
    eights = lax.broadcasted_iota(jnp.int32, (8, LANES), 0)
    places = lax.broadcasted_iota(jnp.int32, (part_rows, LANES), 0) + PANEL
    for start in range(0, half, block):
        far_low, near_low, exponent_low = coded(start, block)
        far_high, near_high, exponent_high = coded(half + start, block)
        far = far_low * 65536 + (far_high & 65535)
        if not first:
            near = jnp.where(
                lane_ids(near_low.shape) < PANEL,
                near_low * 65536 + (exponent_low.astype(jnp.int32) + BIAS),
                near_high * 65536 + (exponent_high.astype(jnp.int32) + BIAS),
            )
            out_ref[start : start + block, :LANES] = far
            out_ref[start : start + block, LANES:] = near
            continue
        near = near_low * 65536 + (near_high & 65535)
        second = part_rows - first
        mine = lane_ids((part_rows, LANES)) == places
        for inner in range(0, block, part_rows):
            base = (start + inner) // part_rows * (part_rows + first)
            words = near[inner : inner + part_rows]
            rows = [
                jnp.sum(jnp.where(mine, exponent[inner : inner + part_rows], 0.0), axis=0, keepdims=True)
                for exponent in (exponent_low, exponent_high)
            ]
            rows = jnp.where(eights == 0, rows[0], jnp.where(eights == 1, rows[1], 0.0)).astype(jnp.int32)
            out_ref[base : base + part_rows, :] = far[inner : inner + part_rows]
            base += part_rows
            spare = [words[: first - second - 8]] if first > second + 8 else []
            both = jnp.concatenate([words[first:], rows, *spare], axis=0)
            out_ref[base : base + first, :] = jnp.where(lane_ids(both.shape) < PANEL, words[:first], both)


def rest_products(my_index, order, a_rows, parts, offsets, share, part_rows):
    rows, depth = a_rows.shape
    return pl.pallas_call(
        functools.partial(rest_product_kernel, offsets, share, part_rows),
        in_specs=[
            pl.BlockSpec(memory_space=pltpu.SMEM),
            pl.BlockSpec(memory_space=pltpu.VMEM),
            pl.BlockSpec(memory_space=pltpu.HBM),
        ]
        + [pl.BlockSpec(memory_space=pltpu.VMEM)] * len(parts),
        out_specs=pl.BlockSpec(memory_space=pltpu.VMEM),
        out_shape=jax.ShapeDtypeStruct(words_shape(rows // 2, part_rows), jnp.int32),
        scratch_shapes=[
            pltpu.VMEM((rows, depth), BF16),
            pltpu.VMEM((rows, LANES), jnp.int32),
            pltpu.VMEM((rows, rows), BF16),
            pltpu.VMEM((depth, 3 * LANES), BF16),
            pltpu.VMEM((rows, 4 * LANES), BF16),
            pltpu.SemaphoreType.DMA((rows // DEEP_BLOCK,)),
        ],
        compiler_params=params(32),
        cost_estimate=pl.CostEstimate(
            flops=2 * rows * (3 * depth + 4 * rows) * LANES, bytes_accessed=2 * rows * depth, transcendentals=0
        ),
        name="rest_products",
    )(my_index, order, in_hbm(a_rows), *parts)


def packed_terms(x, terms_ref, start):
    half = x.shape[0]
    first, second, third = (term.astype(F32) for term in split(x, 3))
    near = lane_ids(x.shape) < PANEL
    other = swap_halves(third)
    terms_ref[:half, start : start + LANES] = jnp.where(near, first, swap_halves(second)).astype(BF16)
    terms_ref[half:, start : start + LANES] = jnp.where(near, swap_halves(first), second).astype(BF16)
    terms_ref[:half, start + LANES : start + 2 * LANES] = jnp.where(near, third, other).astype(BF16)
    terms_ref[half:, start + LANES : start + 2 * LANES] = jnp.where(near, other, third).astype(BF16)


def leading_kernel(held, index_ref, arrived_ref, out_ref, terms_ref):
    packed_terms(arrived_ref[...], terms_ref, 0)
    width = -(-held // LANES) * LANES
    picks = one_hot(index_ref[:, :width], terms_ref.shape[0])
    got = whole_sum(jnp.dot(picks, terms_ref[...], preferred_element_type=F32))
    first, second = got[: held // 2], got[held // 2 : held]
    out_ref[0] = jnp.where(lane_ids(first.shape) < PANEL, first, second)


def leading_rows(index, arrived, held):
    rows = index.shape[1]
    return pl.pallas_call(
        functools.partial(leading_kernel, held),
        in_specs=[pl.BlockSpec(memory_space=pltpu.VMEM)] * 2,
        out_specs=pl.BlockSpec(memory_space=pltpu.VMEM),
        out_shape=jax.ShapeDtypeStruct((1, held // 2, LANES), F32),
        scratch_shapes=[pltpu.VMEM((rows, 2 * LANES), BF16)],
        compiler_params=params(),
        cost_estimate=pl.CostEstimate(
            flops=4 * held * rows * LANES, bytes_accessed=2 * rows * LANES, transcendentals=0
        ),
        name="leading_rows",
    )(index, arrived)


def eliminate(block, shift_row):
    rows = lax.broadcasted_iota(jnp.int32, (PANEL, PANEL), 0)
    columns = lax.broadcasted_iota(jnp.int32, (PANEL, PANEL), 1)
    flipped = jnp.transpose(block)
    mirrored = jnp.where(rows >= columns, block, flipped)
    diagonal = shift_row + jnp.sum(jnp.abs(mirrored), axis=0, keepdims=True)
    unit = (rows == columns).astype(F32)
    work = jnp.where(rows == columns, diagonal, mirrored)
    work = jnp.concatenate([work, unit], axis=1)
    height = 8
    groups = [work[start : start + height] for start in range(0, PANEL, height)]
    sublanes = lax.broadcasted_iota(jnp.int32, (height, LANES), 0)
    scaled_rows = []
    for k in range(PANEL):
        home, offset = divmod(k, height)
        row = groups[home][offset : offset + 1, :]
        row = row / row[:, k : k + 1]
        scaled_rows.append(row)
        for g in range(home, PANEL // height):
            column = jnp.broadcast_to(groups[g][:, k : k + 1], (height, LANES))
            if g == home:
                column = jnp.where(sublanes > offset, column, 0.0)
            groups[g] = groups[g] - column * row
    final = jnp.concatenate(groups, axis=0)
    scaled = jnp.concatenate(scaled_rows, axis=0)
    upper = jnp.where(columns >= rows, scaled[:, :PANEL], 0.0)
    pivots = jnp.sum(jnp.where(rows == columns, final[:, :PANEL], 0.0), axis=0, keepdims=True)
    return upper, final[:, PANEL:], pivots


def exact(lhs, rhs, dims):
    return lax.dot_general(lhs, rhs, (dims, ((), ())), precision=lax.Precision.HIGHEST, preferred_element_type=F32)


def update_kernel(offsets, blocks_held, columns, my_ref, index_ref, arrived_ref, shift_ref, resident_hbm, *refs):
    parts = refs[:-12]
    near_hbm, far_hbm, pivots_ref, leading_ref, tail_ref, resident_ref, terms_ref, lead_ref = refs[-12:-4]
    near_ref, far_ref, sem, sems = refs[-4:]
    fetch = pltpu.make_async_copy(resident_hbm, resident_ref, sem)
    fetch.start()
    my_index = my_ref[0]
    size = len(offsets)
    position = 0
    packed = blocks_held * PANEL // 2
    part_rows = PANEL // 2
    for part in parts:
        for number in range(part.shape[0]):
            owner = my_index ^ offsets[position]
            for start in range(0, blocks_held * PANEL, part_rows):
                held, inner = divmod(start, PANEL)
                if start < packed:
                    rows = part[number, start : start + part_rows, :PANEL]
                else:
                    rows = part[number, start - packed : start - packed + part_rows, PANEL:]
                target = pl.multiple_of((held * size + owner) * PANEL + inner, part_rows)
                leading_ref[pl.ds(target, part_rows), :] = rows
            position += 1
    upper, inverse, pivots = eliminate(leading_ref[:PANEL, :], shift_ref[...])
    pivots_ref[...] = pivots
    lower = jnp.transpose(upper)
    needed = tail_ref.shape[1]
    tail = exact(inverse, leading_ref[:needed, :], ((1,), (1,)))
    high, low = split(tail, 2)
    tail_ref[0:PANEL, :] = high
    tail_ref[PANEL : 2 * PANEL, :] = high
    tail_ref[2 * PANEL : 3 * PANEL, :] = low
    tail_ref[3 * PANEL :, :] = low

    block = A_BLOCK
    packed_terms(arrived_ref[...], terms_ref, 0)
    for start in range(0, lead_ref.shape[0], block):
        picks = one_hot(index_ref[:, start : start + block], lead_ref.shape[0])
        got = jnp.dot(picks, terms_ref[...], preferred_element_type=F32)
        lead_ref[start : start + block, :] = whole_sum(got)[:, :PANEL]
    fetch.wait()
    stores = []
    for number, start in enumerate(range(0, lead_ref.shape[0], block)):
        rows_here = slice(start, start + block)
        panel = exact(lead_ref[rows_here, :], inverse, ((1,), (1,))) / pivots
        shown = used = panel
        if start == 0:
            row_ids = lax.broadcasted_iota(jnp.int32, panel.shape, 0)
            top = jnp.logical_and(my_index == 0, row_ids < PANEL)
            used = jnp.where(top, 0.0, panel)
            filled = jnp.concatenate([lower, jnp.zeros((block - PANEL, PANEL), F32)], axis=0)
            shown = jnp.where(top, filled, panel)
        high, low = (term.astype(F32) for term in split(used, 2))
        pair = jnp.concatenate([high, low], axis=1).astype(BF16)
        factors = jnp.concatenate([pair, pair], axis=1)
        update = jnp.dot(factors, tail_ref[...], preferred_element_type=F32)
        shown = jnp.concatenate([shown, jnp.zeros_like(shown)], axis=1)
        near_ref[rows_here, :LANES] = jnp.where(lane_ids(shown.shape) < PANEL, shown, -update[:, :LANES])
        near_ref[rows_here, LANES:] = -update[:, LANES:columns]
        far_ref[rows_here, :] = (resident_ref[rows_here, :].astype(F32) - update[:, columns:]).astype(BF16)
        for which, (source, target) in enumerate(((near_ref, near_hbm), (far_ref, far_hbm))):
            store = pltpu.make_async_copy(
                source.at[pl.ds(start, block), :], target.at[pl.ds(start, block), :], sems.at[which, number]
            )
            store.start()
            stores.append(store)
    for store in stores:
        store.wait()


def updates(my_index, parts, offsets, index, arrived, shift, resident, blocks_held, columns):
    rows, width = resident.shape
    needed = columns + width
    held_rows = len(offsets) * blocks_held * PANEL
    vmem = pl.BlockSpec(memory_space=pltpu.VMEM)
    anywhere = pl.BlockSpec(memory_space=pltpu.HBM)
    return pl.pallas_call(
        functools.partial(update_kernel, offsets, blocks_held, columns),
        in_specs=[pl.BlockSpec(memory_space=pltpu.SMEM), vmem, vmem, vmem, anywhere] + [vmem] * len(parts),
        out_specs=[anywhere, anywhere, vmem],
        out_shape=[
            pltpu.HBM((rows, columns), F32),
            pltpu.HBM((rows, width), BF16),
            jax.ShapeDtypeStruct((1, PANEL), F32),
        ],
        scratch_shapes=[
            pltpu.VMEM((held_rows, PANEL), F32),
            pltpu.VMEM((4 * PANEL, needed), BF16),
            pltpu.VMEM((rows, width), BF16),
            pltpu.VMEM((rows, 2 * LANES), BF16),
            pltpu.VMEM((rows, PANEL), F32),
            pltpu.VMEM((rows, columns), F32),
            pltpu.VMEM((rows, width), BF16),
            pltpu.SemaphoreType.DMA,
            pltpu.SemaphoreType.DMA((2, rows // A_BLOCK)),
        ],
        compiler_params=params(32),
        cost_estimate=pl.CostEstimate(
            flops=2 * rows * needed * 4 * PANEL, bytes_accessed=4 * rows * (columns + width), transcendentals=0
        ),
        name="factor_and_update",
    )(my_index, index, arrived, shift, in_hbm(resident), *parts)


def upper_half(words):
    return (words >> 16).astype(F32)


def lower_half(words):
    return ((words << 16) >> 16).astype(F32)


def loose_values(arrived_ref):
    words = arrived_ref[:, LANES:]
    low_lanes = lane_ids(words.shape) < PANEL
    scale = jnp.exp2(((words & 255) - (BIAS + 15)).astype(F32)) * (1 / MARGIN)
    other = swap_halves(scale)
    near = upper_half(words) * scale
    words = arrived_ref[:, :LANES]
    low = upper_half(words) * jnp.where(low_lanes, scale, other)
    return low, lower_half(words) * jnp.where(low_lanes, other, scale), near


def tight_values(arrived_ref, part_rows, values_ref):
    first = tight_split(part_rows)
    second = part_rows - first
    step = part_rows + first
    sources = arrived_ref.shape[0] // step
    pairs = [arrived_ref[i * step + part_rows + second : i * step + part_rows + second + 2, :] for i in range(sources)]
    spare = jnp.zeros((LANES - 2 * sources, LANES), jnp.int32)
    exponents = jnp.concatenate([*pairs, spare], axis=0)
    scales = jnp.exp2(jnp.transpose(exponents.astype(F32)) - 15.0) * (1 / MARGIN)
    scales = scales[PANEL : PANEL + part_rows]
    low_lanes = lane_ids((part_rows, LANES)) < PANEL
    for i in range(sources):
        base = i * step
        here = slice(i * part_rows, (i + 1) * part_rows)
        low_scale = jnp.broadcast_to(scales[:, 2 * i : 2 * i + 1], (part_rows, LANES))
        high_scale = jnp.broadcast_to(scales[:, 2 * i + 1 : 2 * i + 2], (part_rows, LANES))
        words = arrived_ref[base : base + part_rows, :]
        values_ref[0, here, :] = upper_half(words) * low_scale
        values_ref[1, here, :] = lower_half(words) * high_scale
        words = arrived_ref[base + part_rows : base + step, :]
        words = jnp.concatenate([words, swap_halves(words[:second])], axis=0)
        words = jnp.where(low_lanes, words, swap_halves(words))
        values_ref[2, here, :] = jnp.where(low_lanes, upper_half(words) * low_scale, lower_half(words) * high_scale)
    return values_ref[0], values_ref[1], values_ref[2]


def formed_kernel(
    part_rows, index_ref, arrived_ref, near_hbm, out_hbm, near_ref, terms_ref, out_ref, values_ref, in_sems, out_sems
):
    half = terms_ref.shape[0] // 2
    first = tight_split(part_rows)
    block = A_BLOCK
    starts = range(0, near_ref.shape[0], block)

    def rows_of(ref, start):
        return ref.at[pl.ds(start, block), :]

    fetches = [
        pltpu.make_async_copy(rows_of(near_hbm, start), rows_of(near_ref, start), in_sems.at[i])
        for i, start in enumerate(starts)
    ]
    for fetch in fetches:
        fetch.start()
    low, high, near = loose_values(arrived_ref) if not first else tight_values(arrived_ref, part_rows, values_ref)
    for side, values in enumerate((low, high)):
        one, two = split(values, 2)
        terms_ref[side * half : (side + 1) * half, :LANES] = one
        terms_ref[side * half : (side + 1) * half, LANES : 2 * LANES] = two
    low_lanes = lane_ids(near.shape) < PANEL
    one, two = (term.astype(F32) for term in split(near, 2))
    terms_ref[:half, 2 * LANES :] = jnp.where(low_lanes, one, swap_halves(two)).astype(BF16)
    terms_ref[half:, 2 * LANES :] = jnp.where(low_lanes, swap_halves(one), two).astype(BF16)

    stores = []
    for i, start in enumerate(starts):
        rows_here = slice(start, start + block)
        picks = one_hot(index_ref[:, rows_here], terms_ref.shape[0])
        got = jnp.dot(picks, terms_ref[...], preferred_element_type=F32)
        pair = got[:, 2 * LANES :]
        fetches[i].wait()
        held = near_ref[rows_here, :LANES]
        out_ref[rows_here, :LANES] = jnp.where(
            lane_ids(held.shape) < PANEL, held, (pair + swap_halves(pair)) + held
        )
        out_ref[rows_here, LANES:] = (got[:, :LANES] + got[:, LANES : 2 * LANES]) + near_ref[rows_here, LANES:]
        store = pltpu.make_async_copy(rows_of(out_ref, start), rows_of(out_hbm, start), out_sems.at[i])
        store.start()
        stores.append(store)
    for store in stores:
        store.wait()


def formed_columns(index, arrived, near, part_rows):
    rows, columns = near.shape
    vmem = pl.BlockSpec(memory_space=pltpu.VMEM)
    anywhere = pl.BlockSpec(memory_space=pltpu.HBM)
    return pl.pallas_call(
        functools.partial(formed_kernel, part_rows),
        in_specs=[vmem, vmem, anywhere],
        out_specs=anywhere,
        out_shape=pltpu.HBM((rows, columns), F32),
        input_output_aliases={2: 0},
        scratch_shapes=[
            pltpu.VMEM((rows, columns), F32),
            pltpu.VMEM((rows, 3 * LANES), BF16),
            pltpu.VMEM((rows, columns), F32),
            pltpu.VMEM((3, rows // 2, LANES), F32),
            pltpu.SemaphoreType.DMA((rows // A_BLOCK,)),
            pltpu.SemaphoreType.DMA((rows // A_BLOCK,)),
        ],
        compiler_params=params(32),
        cost_estimate=pl.CostEstimate(
            flops=8 * rows * rows * LANES, bytes_accessed=8 * rows * columns, transcendentals=0
        ),
        name="formed_columns",
    )(index, arrived, near)


def swap_rows(x, group):
    rows, width = x.shape
    return lax.all_to_all(
        x.reshape(group, rows // group, width), "wide", split_axis=0, concat_axis=0, tiled=True
    ).reshape(rows, width)


def on_device(a_rows, xa_panel, za_panel, send_order, recv_order, shift, resident):
    rows = a_rows.shape[0]
    columns = xa_panel.shape[1]
    group = lax.axis_size("wide")
    my_index = lax.axis_index("wide").astype(jnp.int32).reshape(1)
    share = rows // group
    half = rows // 2
    few, apart = phases_of(group)

    order, packing = send_order, share
    if share % 16:
        order = send_order.reshape(group, 2, share // 2).transpose(1, 0, 2).reshape(1, rows)
        packing = 0
    source, slot = recv_order // share, recv_order % share
    index = (slot // (share // 2)) * half + source * (share // 2) + slot % (share // 2)

    lead_panel, rest_panel = split_panels(my_index, xa_panel, za_panel)
    send_picks, a_copy = order_picks(order, a_rows, packing)
    lead_parts = [lead_panel]
    for masks in few:
        lead_parts = exchange(join(lead_parts), masks, "wide")
    rest_parts = [rest_panel]
    for number, masks in enumerate(apart[:-2]):
        rest_parts = exchange(join(rest_parts), masks, "wide")
        if number == 0:
            lead_parts = tied(lead_parts, *rest_parts)

    lead_out = lead_products(my_index, a_copy, send_picks, lead_parts, offsets_of(few))
    lead_in = swap_rows(tied([lead_out], *rest_parts)[0], group)
    rest_parts = exchange(join(tied(rest_parts, lead_out)), apart[-2], "wide")
    other_parts = exchange(rest_parts[:1], apart[-1], "wide")[1:]

    needed = columns + resident.shape[1]
    blocks_held = -(-needed // (PANEL * group))
    leading_parts = [leading_rows(index, lead_in, blocks_held * PANEL)]
    for masks in few:
        leading_parts = exchange(join(leading_parts), masks, "wide")
        if masks is few[0]:
            later_parts = exchange(tied(rest_parts[1:], *leading_parts), apart[-1], "wide")
    late = len(later_parts) // 2
    rest_parts = rest_parts + other_parts + later_parts[late:]
    rest_out = rest_products(
        my_index, order, a_rows, rest_parts, offsets_of(apart), packing, share // 2
    )
    rest_in = swap_rows(tied([rest_out], *leading_parts)[0], group)
    near, updated, pivots = updates(
        my_index,
        leading_parts,
        offsets_of(few),
        index,
        tied([lead_in], rest_out)[0],
        shift[None, :],
        resident,
        blocks_held,
        columns,
    )
    factored = formed_columns(index, rest_in, near, share // 2)
    return (factored, updated, pivots[0])


def solution(mesh):
    placed = (
        P(("parts", "wide"), None),
        P(("parts", "wide"), None),
        P(("parts", "wide"), None),
        P(("parts", "wide"), None),
        P(("parts", "wide"), None),
        P("parts"),
        P(("parts", "wide"), None),
    )
    return jax.shard_map(
        on_device,
        mesh=mesh,
        in_specs=placed,
        out_specs=(P(("parts", "wide"), None), P(("parts", "wide"), None), P("parts")),
        check_vma=False,
    )
```

```python
import functools

import jax
import jax.numpy as jnp
from jax import lax
from jax.experimental import pallas as pl
from jax.experimental.pallas import tpu as pltpu
from jax.sharding import PartitionSpec as P

PANEL = 64
LANES = 128
A_BLOCK = 640
DEEP_BLOCK = 256
F32 = jnp.float32
BF16 = jnp.bfloat16
MIB = 1024 * 1024


def params(mebibytes=12):
    return pltpu.CompilerParams(vmem_limit_bytes=mebibytes * MIB)


def in_hbm(x):
    return pltpu.with_memory_space_constraint(x, pltpu.HBM)


def lane_ids(shape):
    return lax.broadcasted_iota(jnp.int32, shape, len(shape) - 1)


def split(x, count):
    terms = []
    for _ in range(count):
        term = x.astype(BF16)
        terms.append(term)
        x = x - term.astype(F32)
    return terms


def swap_halves(x):
    return pltpu.roll(x, LANES // 2, 1)


def as_column(index_row):
    return jnp.transpose(jnp.broadcast_to(index_row, (LANES, LANES)))


def picks_of(at, width):
    lanes = lane_ids(at.shape)
    return jnp.concatenate(
        [(at == lanes + column).astype(F32).astype(BF16) for column in range(0, width, LANES)], axis=1
    )


def fill_picks(at_ref, picks_ref):
    rows, width = picks_ref.shape
    for start in range(0, rows, LANES):
        picks_ref[start : start + LANES, :] = picks_of(at_ref[start : start + LANES, :], width)


def one_hot(index_row, width):
    chunks = [
        picks_of(as_column(index_row[:, start : start + LANES]), width)
        for start in range(0, index_row.shape[1], LANES)
    ]
    return jnp.concatenate(chunks, axis=0) if len(chunks) > 1 else chunks[0]


def packed_order(share, half, slot):
    part = share // 2
    return (slot % share) // part * half + slot // share * part + slot % part


def fill_order(order_ref, at_ref, share):
    rows = order_ref.shape[1]
    height = 8
    for start in range(0, rows, LANES):
        column = as_column(order_ref[:, start : start + LANES])
        if not share:
            at_ref[start : start + LANES, :] = column
            continue
        for inner in range(0, LANES, height):
            place = packed_order(share, rows // 2, start + inner)
            at_ref[place : place + height, :] = column[inner : inner + height]


def exchange(held, masks, axis):
    size = lax.axis_size(axis)
    combined = [0]
    for mask in masks:
        combined += [other ^ mask for other in combined]
    parts = list(held)
    for mask in combined[1:]:
        parts += [lax.ppermute(part, axis, [(i, i ^ mask) for i in range(size)]) for part in held]
    return parts


def offsets_of(phases):
    offsets = [0]
    for masks in phases:
        combined = [0]
        for mask in masks:
            combined += [other ^ mask for other in combined]
        offsets = [offset ^ mask for mask in combined for offset in offsets]
    return offsets


def join(parts):
    return [jnp.concatenate(parts, axis=0)]


def phases_of(size):
    bits = [1 << bit for bit in reversed(range(size.bit_length() - 1))]
    return [bits[start : start + 2] for start in range(0, len(bits), 2)], [[bit] for bit in bits]


def tied(parts, *earlier):
    return list(lax.optimization_barrier((*parts, *earlier))[: len(parts)])


def picks_kernel(share, order_hbm, a_hbm, picks_ref, copy_ref, order_ref, at_ref, sems):
    fetch = pltpu.make_async_copy(order_hbm, order_ref, sems.at[0])
    copy = pltpu.make_async_copy(a_hbm, copy_ref, sems.at[1])
    fetch.start()
    copy.start()
    fetch.wait()
    fill_order(order_ref, at_ref, share)
    fill_picks(at_ref, picks_ref)
    copy.wait()


def order_picks(order, a_rows, share):
    rows, depth = a_rows.shape
    return pl.pallas_call(
        functools.partial(picks_kernel, share),
        in_specs=[pl.BlockSpec(memory_space=pltpu.HBM)] * 2,
        out_specs=[pl.BlockSpec(memory_space=pltpu.VMEM)] * 2,
        out_shape=[jax.ShapeDtypeStruct((rows, rows), BF16), jax.ShapeDtypeStruct((rows, depth), BF16)],
        scratch_shapes=[
            pltpu.VMEM((1, rows), jnp.int32),
            pltpu.VMEM((rows, LANES), jnp.int32),
            pltpu.SemaphoreType.DMA((2,)),
        ],
        compiler_params=params(),
        cost_estimate=pl.CostEstimate(flops=4 * rows * rows, bytes_accessed=4 * rows * depth, transcendentals=0),
        name="order_picks",
    )(in_hbm(order), in_hbm(a_rows))


def panels_kernel(my_ref, xa_hbm, za_hbm, lead_ref, rest_ref, xa_ref, za_ref, sems):
    copies = [
        pltpu.make_async_copy(xa_hbm, xa_ref, sems.at[0]),
        pltpu.make_async_copy(za_hbm, za_ref, sems.at[1]),
    ]
    for copy in copies:
        copy.start()
    for copy in copies:
        copy.wait()
    lead_ref[0] = jnp.concatenate([xa_ref[:, :PANEL], za_ref[:, :PANEL]], axis=1)
    rest_ref[0, :, :LANES] = jnp.concatenate([xa_ref[:, PANEL:LANES], za_ref[:, PANEL:LANES]], axis=1)
    rest_ref[0, :, LANES : 2 * LANES] = xa_ref[:, LANES:]
    rest_ref[0, :, 2 * LANES :] = za_ref[:, LANES:]


def split_panels(my_index, xa_panel, za_panel):
    depth, columns = xa_panel.shape
    return pl.pallas_call(
        panels_kernel,
        in_specs=[pl.BlockSpec(memory_space=pltpu.SMEM)] + [pl.BlockSpec(memory_space=pltpu.HBM)] * 2,
        out_shape=[
            jax.ShapeDtypeStruct((1, depth, LANES), BF16),
            jax.ShapeDtypeStruct((1, depth, 2 * columns - LANES), BF16),
        ],
        scratch_shapes=[
            pltpu.VMEM((depth, columns), BF16),
            pltpu.VMEM((depth, columns), BF16),
            pltpu.SemaphoreType.DMA((2,)),
        ],
        compiler_params=params(),
        name="split_panels",
    )(my_index, in_hbm(xa_panel), in_hbm(za_panel))


def assemble(my_index, offsets, parts, panel_ref):
    position = 0
    for part in parts:
        for number in range(part.shape[0]):
            depth = part.shape[1]
            start = pl.multiple_of((my_index ^ offsets[position]) * depth, depth)
            panel_ref[pl.ds(start, depth), :] = part[number]
            position += 1


def whole_sum(got):
    pair = got[:, :LANES]
    return (pair + swap_halves(pair)) + got[:, LANES:]


def lead_product_kernel(offsets, my_ref, a_ref, picks_ref, *refs):
    parts, (out_hbm, panel_ref, terms_ref, out_ref, sems) = refs[:-5], refs[-5:]
    assemble(my_ref[0], offsets, parts, panel_ref)
    rows = a_ref.shape[0]
    for start in range(0, rows, DEEP_BLOCK):
        both = jnp.dot(a_ref[start : start + DEEP_BLOCK, :], panel_ref[...], preferred_element_type=F32)
        first, second, third = (term.astype(F32) for term in split(both * swap_halves(both), 3))
        near = lane_ids(both.shape) < PANEL
        terms_ref[start : start + DEEP_BLOCK, :LANES] = jnp.where(near, first, second).astype(BF16)
        terms_ref[start : start + DEEP_BLOCK, LANES:] = third.astype(BF16)
    half = rows // 2
    block = half // 2
    stores = []
    for number, start in enumerate(range(0, half, block)):
        low = jnp.dot(picks_ref[start : start + block, :], terms_ref[...], preferred_element_type=F32)
        high = jnp.dot(picks_ref[half + start : half + start + block, :], terms_ref[...], preferred_element_type=F32)
        low, high = whole_sum(low), whole_sum(high)
        out_ref[start : start + block, :] = jnp.where(lane_ids(low.shape) < PANEL, low, high)
        stores.append(store_rows(out_ref, out_hbm, start, block, sems.at[number]))
    for store in stores:
        store.wait()


def lead_products(my_index, a_rows, picks, parts, offsets):
    rows, depth = a_rows.shape
    return pl.pallas_call(
        functools.partial(lead_product_kernel, offsets),
        in_specs=[pl.BlockSpec(memory_space=pltpu.SMEM)] + [pl.BlockSpec(memory_space=pltpu.VMEM)] * (2 + len(parts)),
        out_specs=pl.BlockSpec(memory_space=pltpu.HBM),
        out_shape=pltpu.HBM((rows // 2, LANES), F32),
        scratch_shapes=[
            pltpu.VMEM((depth, LANES), BF16),
            pltpu.VMEM((rows, 2 * LANES), BF16),
            pltpu.VMEM((rows // 2, LANES), F32),
            pltpu.SemaphoreType.DMA((2,)),
        ],
        compiler_params=params(24),
        cost_estimate=pl.CostEstimate(
            flops=2 * rows * (depth + 2 * rows) * LANES, bytes_accessed=2 * rows * depth, transcendentals=0
        ),
        name="lead_products",
    )(my_index, a_rows, picks, *parts)


BIAS = 128
MARGIN = 0.9995
ROUNDER = 1.5 * 2.0**23


def tight_split(part):
    first = -(-part // 16) * 8
    return first if part % 8 == 0 and part <= PANEL and 2 * first - part >= 8 else 0


def words_shape(half, part):
    first = tight_split(part)
    return (half // part * (part + first), LANES) if first else (half, 2 * LANES)


def store_rows(source, target, start, size, sem):
    rows = pl.ds(start, size)
    copy = pltpu.make_async_copy(source.at[rows, :], target.at[rows, :], sem)
    copy.start()
    return copy


def nearest(x):
    return (x + ROUNDER) - ROUNDER


def rest_product_kernel(offsets, part_rows, my_ref, picks_hbm, a_hbm, *refs):
    parts, (out_hbm, a_ref, picks_ref, panel_ref, terms_ref, out_ref, sems, pick_sem, out_sems) = refs[:-9], refs[-9:]
    rows = a_ref.shape[0]
    half = rows // 2
    block = DEEP_BLOCK
    starts = range(0, rows, block)
    copies = [
        pltpu.make_async_copy(a_hbm.at[pl.ds(start, block), :], a_ref.at[pl.ds(start, block), :], sems.at[i])
        for i, start in enumerate(starts)
    ]
    for copy in copies[:3]:
        copy.start()
    fetch = pltpu.make_async_copy(picks_hbm, picks_ref, pick_sem)
    assemble(my_ref[0], offsets, parts, panel_ref)

    def product(i):
        copies[i].wait()
        if i + 3 < len(copies):
            copies[i + 3].start()
        if i + 3 == len(copies):
            fetch.start()
        return jnp.dot(a_ref[starts[i] : starts[i] + block, :], panel_ref[...], preferred_element_type=F32)

    low_lanes = lane_ids((block, LANES)) < PANEL
    later = product(0)
    for i, start in enumerate(starts):
        both = later
        if i + 1 < len(starts):
            later = product(i + 1)
        near = both[:, :LANES]
        near = near * swap_halves(near)
        far = both[:, LANES : 2 * LANES] * both[:, 2 * LANES :]
        largest = jnp.max(jnp.maximum(jnp.abs(near), jnp.abs(far)), axis=1, keepdims=True)
        exponent = jnp.floor(jnp.log2(jnp.maximum(largest, 1e-30))) + 1.0
        scale = jnp.exp2(15.0 - exponent) * MARGIN
        far = nearest(far * scale)
        near = nearest(near * scale)
        far_top = nearest(far * (1 / 256))
        near_top = nearest(near * (1 / 256))
        here = slice(start, start + block)
        terms_ref[here, :LANES] = far_top.astype(BF16)
        terms_ref[here, LANES : 2 * LANES] = (far - far_top * 256.0).astype(BF16)
        terms_ref[here, 2 * LANES : 3 * LANES] = jnp.where(low_lanes, near_top, near - near_top * 256.0).astype(BF16)
        terms_ref[here, 3 * LANES :] = jnp.broadcast_to(exponent, (block, LANES)).astype(BF16)

    def coded(start, size):
        got = jnp.dot(picks_ref[start : start + size, :], terms_ref[...], preferred_element_type=F32)
        far = got[:, :LANES] * 256.0 + got[:, LANES : 2 * LANES]
        pair = got[:, 2 * LANES : 3 * LANES]
        pair = jnp.where(lane_ids(pair.shape) < PANEL, pair * 256.0, pair)
        near = (pair + swap_halves(pair)).astype(jnp.int32)
        return far.astype(jnp.int32), near, got[:, 3 * LANES :]

    block = half // 2
    first = tight_split(part_rows)
    low_lanes = lane_ids((8, LANES)) < PANEL
    eights = lax.broadcasted_iota(jnp.int32, (8, LANES), 0)
    places = lax.broadcasted_iota(jnp.int32, (part_rows, LANES), 0) + PANEL
    fetch.wait()
    stores = []
    for number, start in enumerate(range(0, half, block)):
        far_low, near_low, exponent_low = coded(start, block)
        far_high, near_high, exponent_high = coded(half + start, block)
        far = far_low * 65536 + (far_high & 65535)
        if not first:
            near = jnp.where(
                lane_ids(near_low.shape) < PANEL,
                near_low * 65536 + (exponent_low.astype(jnp.int32) + BIAS),
                near_high * 65536 + (exponent_high.astype(jnp.int32) + BIAS),
            )
            out_ref[start : start + block, :LANES] = far
            out_ref[start : start + block, LANES:] = near
            stores.append(store_rows(out_ref, out_hbm, start, block, out_sems.at[number]))
            continue
        near = near_low * 65536 + (near_high & 65535)
        second = part_rows - first
        mine = lane_ids((part_rows, LANES)) == places
        for inner in range(0, block, part_rows):
            base = (start + inner) // part_rows * (part_rows + first)
            words = near[inner : inner + part_rows]
            rows = [
                jnp.sum(jnp.where(mine, exponent[inner : inner + part_rows], 0.0), axis=0, keepdims=True)
                for exponent in (exponent_low, exponent_high)
            ]
            rows = jnp.where(eights == 0, rows[0], jnp.where(eights == 1, rows[1], 0.0)).astype(jnp.int32)
            out_ref[base : base + part_rows, :] = far[inner : inner + part_rows]
            base += part_rows
            spare = [words[: first - second - 8]] if first > second + 8 else []
            both = jnp.concatenate([words[first:], rows, *spare], axis=0)
            out_ref[base : base + first, :] = jnp.where(lane_ids(both.shape) < PANEL, words[:first], both)
        size = block // part_rows * (part_rows + first)
        stores.append(store_rows(out_ref, out_hbm, number * size, size, out_sems.at[number]))
    for store in stores:
        store.wait()


def rest_products(my_index, picks, a_rows, parts, offsets, part_rows):
    rows, depth = a_rows.shape
    shape = words_shape(rows // 2, part_rows)
    return pl.pallas_call(
        functools.partial(rest_product_kernel, offsets, part_rows),
        in_specs=[
            pl.BlockSpec(memory_space=pltpu.SMEM),
            pl.BlockSpec(memory_space=pltpu.HBM),
            pl.BlockSpec(memory_space=pltpu.HBM),
        ]
        + [pl.BlockSpec(memory_space=pltpu.VMEM)] * len(parts),
        out_specs=pl.BlockSpec(memory_space=pltpu.HBM),
        out_shape=pltpu.HBM(shape, jnp.int32),
        scratch_shapes=[
            pltpu.VMEM((rows, depth), BF16),
            pltpu.VMEM((rows, rows), BF16),
            pltpu.VMEM((depth, 3 * LANES), BF16),
            pltpu.VMEM((rows, 4 * LANES), BF16),
            pltpu.VMEM(shape, jnp.int32),
            pltpu.SemaphoreType.DMA((rows // DEEP_BLOCK,)),
            pltpu.SemaphoreType.DMA,
            pltpu.SemaphoreType.DMA((2,)),
        ],
        compiler_params=params(32),
        cost_estimate=pl.CostEstimate(
            flops=2 * rows * (3 * depth + 4 * rows) * LANES, bytes_accessed=2 * rows * depth, transcendentals=0
        ),
        name="rest_products",
    )(my_index, in_hbm(picks), in_hbm(a_rows), *parts)


def packed_terms(x, terms_ref, start):
    half = x.shape[0]
    first, second, third = (term.astype(F32) for term in split(x, 3))
    near = lane_ids(x.shape) < PANEL
    other = swap_halves(third)
    terms_ref[:half, start : start + LANES] = jnp.where(near, first, swap_halves(second)).astype(BF16)
    terms_ref[half:, start : start + LANES] = jnp.where(near, swap_halves(first), second).astype(BF16)
    terms_ref[:half, start + LANES : start + 2 * LANES] = jnp.where(near, third, other).astype(BF16)
    terms_ref[half:, start + LANES : start + 2 * LANES] = jnp.where(near, other, third).astype(BF16)


def leading_kernel(held, index_ref, arrived_ref, out_ref, terms_ref):
    packed_terms(arrived_ref[...], terms_ref, 0)
    width = -(-held // LANES) * LANES
    picks = one_hot(index_ref[:, :width], terms_ref.shape[0])
    got = whole_sum(jnp.dot(picks, terms_ref[...], preferred_element_type=F32))
    first, second = got[: held // 2], got[held // 2 : held]
    out_ref[0] = jnp.where(lane_ids(first.shape) < PANEL, first, second)


def leading_rows(index, arrived, held):
    rows = index.shape[1]
    return pl.pallas_call(
        functools.partial(leading_kernel, held),
        in_specs=[pl.BlockSpec(memory_space=pltpu.VMEM)] * 2,
        out_specs=pl.BlockSpec(memory_space=pltpu.VMEM),
        out_shape=jax.ShapeDtypeStruct((1, held // 2, LANES), F32),
        scratch_shapes=[pltpu.VMEM((rows, 2 * LANES), BF16)],
        compiler_params=params(),
        cost_estimate=pl.CostEstimate(
            flops=4 * held * rows * LANES, bytes_accessed=2 * rows * LANES, transcendentals=0
        ),
        name="leading_rows",
    )(index, arrived)


def eliminate(block, shift_row):
    rows = lax.broadcasted_iota(jnp.int32, (PANEL, PANEL), 0)
    columns = lax.broadcasted_iota(jnp.int32, (PANEL, PANEL), 1)
    flipped = jnp.transpose(block)
    mirrored = jnp.where(rows >= columns, block, flipped)
    diagonal = shift_row + jnp.sum(jnp.abs(mirrored), axis=0, keepdims=True)
    unit = (rows == columns).astype(F32)
    work = jnp.where(rows == columns, diagonal, mirrored)
    work = jnp.concatenate([work, unit], axis=1)
    height = 8
    groups = [work[start : start + height] for start in range(0, PANEL, height)]
    sublanes = lax.broadcasted_iota(jnp.int32, (height, LANES), 0)
    scaled_rows = []
    for k in range(PANEL):
        home, offset = divmod(k, height)
        row = groups[home][offset : offset + 1, :]
        row = row / row[:, k : k + 1]
        scaled_rows.append(row)
        for g in range(home, PANEL // height):
            column = jnp.broadcast_to(groups[g][:, k : k + 1], (height, LANES))
            if g == home:
                column = jnp.where(sublanes > offset, column, 0.0)
            groups[g] = groups[g] - column * row
    final = jnp.concatenate(groups, axis=0)
    scaled = jnp.concatenate(scaled_rows, axis=0)
    upper = jnp.where(columns >= rows, scaled[:, :PANEL], 0.0)
    pivots = jnp.sum(jnp.where(rows == columns, final[:, :PANEL], 0.0), axis=0, keepdims=True)
    return upper, final[:, PANEL:], pivots


def exact(lhs, rhs, dims):
    return lax.dot_general(lhs, rhs, (dims, ((), ())), precision=lax.Precision.HIGHEST, preferred_element_type=F32)


def update_kernel(offsets, blocks_held, columns, my_ref, index_ref, arrived_ref, shift_ref, resident_hbm, *refs):
    parts = refs[:-12]
    near_hbm, far_hbm, pivots_ref, leading_ref, tail_ref, resident_ref, terms_ref, lead_ref = refs[-12:-4]
    near_ref, far_ref, sem, sems = refs[-4:]
    fetch = pltpu.make_async_copy(resident_hbm, resident_ref, sem)
    fetch.start()
    my_index = my_ref[0]
    size = len(offsets)
    position = 0
    packed = blocks_held * PANEL // 2
    part_rows = PANEL // 2
    for part in parts:
        for number in range(part.shape[0]):
            owner = my_index ^ offsets[position]
            for start in range(0, blocks_held * PANEL, part_rows):
                held, inner = divmod(start, PANEL)
                if start < packed:
                    rows = part[number, start : start + part_rows, :PANEL]
                else:
                    rows = part[number, start - packed : start - packed + part_rows, PANEL:]
                target = pl.multiple_of((held * size + owner) * PANEL + inner, part_rows)
                leading_ref[pl.ds(target, part_rows), :] = rows
            position += 1
    upper, inverse, pivots = eliminate(leading_ref[:PANEL, :], shift_ref[...])
    pivots_ref[...] = pivots
    lower = jnp.transpose(upper)
    needed = tail_ref.shape[1]
    tail = exact(inverse, leading_ref[:needed, :], ((1,), (1,)))
    high, low = split(tail, 2)
    tail_ref[0:PANEL, :] = high
    tail_ref[PANEL : 2 * PANEL, :] = high
    tail_ref[2 * PANEL : 3 * PANEL, :] = low
    tail_ref[3 * PANEL :, :] = low

    block = A_BLOCK
    packed_terms(arrived_ref[...], terms_ref, 0)
    for start in range(0, lead_ref.shape[0], block):
        picks = one_hot(index_ref[:, start : start + block], lead_ref.shape[0])
        got = jnp.dot(picks, terms_ref[...], preferred_element_type=F32)
        lead_ref[start : start + block, :] = whole_sum(got)[:, :PANEL]
    fetch.wait()
    stores = []
    for number, start in enumerate(range(0, lead_ref.shape[0], block)):
        rows_here = slice(start, start + block)
        panel = exact(lead_ref[rows_here, :], inverse, ((1,), (1,))) / pivots
        shown = used = panel
        if start == 0:
            row_ids = lax.broadcasted_iota(jnp.int32, panel.shape, 0)
            top = jnp.logical_and(my_index == 0, row_ids < PANEL)
            used = jnp.where(top, 0.0, panel)
            filled = jnp.concatenate([lower, jnp.zeros((block - PANEL, PANEL), F32)], axis=0)
            shown = jnp.where(top, filled, panel)
        high, low = (term.astype(F32) for term in split(used, 2))
        pair = jnp.concatenate([high, low], axis=1).astype(BF16)
        factors = jnp.concatenate([pair, pair], axis=1)
        update = jnp.dot(factors, tail_ref[...], preferred_element_type=F32)
        shown = jnp.concatenate([shown, jnp.zeros_like(shown)], axis=1)
        near_ref[rows_here, :LANES] = jnp.where(lane_ids(shown.shape) < PANEL, shown, -update[:, :LANES])
        near_ref[rows_here, LANES:] = -update[:, LANES:columns]
        far_ref[rows_here, :] = (resident_ref[rows_here, :].astype(F32) - update[:, columns:]).astype(BF16)
        for which, (source, target) in enumerate(((near_ref, near_hbm), (far_ref, far_hbm))):
            store = pltpu.make_async_copy(
                source.at[pl.ds(start, block), :], target.at[pl.ds(start, block), :], sems.at[which, number]
            )
            store.start()
            stores.append(store)
    for store in stores:
        store.wait()


def updates(my_index, parts, offsets, index, arrived, shift, resident, blocks_held, columns):
    rows, width = resident.shape
    needed = columns + width
    held_rows = len(offsets) * blocks_held * PANEL
    vmem = pl.BlockSpec(memory_space=pltpu.VMEM)
    anywhere = pl.BlockSpec(memory_space=pltpu.HBM)
    return pl.pallas_call(
        functools.partial(update_kernel, offsets, blocks_held, columns),
        in_specs=[pl.BlockSpec(memory_space=pltpu.SMEM), vmem, vmem, vmem, anywhere] + [vmem] * len(parts),
        out_specs=[anywhere, anywhere, vmem],
        out_shape=[
            pltpu.HBM((rows, columns), F32),
            pltpu.HBM((rows, width), BF16),
            jax.ShapeDtypeStruct((1, PANEL), F32),
        ],
        scratch_shapes=[
            pltpu.VMEM((held_rows, PANEL), F32),
            pltpu.VMEM((4 * PANEL, needed), BF16),
            pltpu.VMEM((rows, width), BF16),
            pltpu.VMEM((rows, 2 * LANES), BF16),
            pltpu.VMEM((rows, PANEL), F32),
            pltpu.VMEM((rows, columns), F32),
            pltpu.VMEM((rows, width), BF16),
            pltpu.SemaphoreType.DMA,
            pltpu.SemaphoreType.DMA((2, rows // A_BLOCK)),
        ],
        compiler_params=params(32),
        cost_estimate=pl.CostEstimate(
            flops=2 * rows * needed * 4 * PANEL, bytes_accessed=4 * rows * (columns + width), transcendentals=0
        ),
        name="factor_and_update",
    )(my_index, index, arrived, shift, in_hbm(resident), *parts)


def upper_half(words):
    return (words >> 16).astype(F32)


def lower_half(words):
    return ((words << 16) >> 16).astype(F32)


def loose_values(arrived_ref):
    words = arrived_ref[:, LANES:]
    low_lanes = lane_ids(words.shape) < PANEL
    scale = jnp.exp2(((words & 255) - (BIAS + 15)).astype(F32)) * (1 / MARGIN)
    other = swap_halves(scale)
    near = upper_half(words) * scale
    words = arrived_ref[:, :LANES]
    low = upper_half(words) * jnp.where(low_lanes, scale, other)
    return low, lower_half(words) * jnp.where(low_lanes, other, scale), near


def tight_values(arrived_ref, part_rows, values_ref):
    first = tight_split(part_rows)
    second = part_rows - first
    step = part_rows + first
    sources = arrived_ref.shape[0] // step
    pairs = [arrived_ref[i * step + part_rows + second : i * step + part_rows + second + 2, :] for i in range(sources)]
    spare = jnp.zeros((LANES - 2 * sources, LANES), jnp.int32)
    exponents = jnp.concatenate([*pairs, spare], axis=0)
    scales = jnp.exp2(jnp.transpose(exponents.astype(F32)) - 15.0) * (1 / MARGIN)
    scales = scales[PANEL : PANEL + part_rows]
    low_lanes = lane_ids((part_rows, LANES)) < PANEL
    for i in range(sources):
        base = i * step
        here = slice(i * part_rows, (i + 1) * part_rows)
        low_scale = jnp.broadcast_to(scales[:, 2 * i : 2 * i + 1], (part_rows, LANES))
        high_scale = jnp.broadcast_to(scales[:, 2 * i + 1 : 2 * i + 2], (part_rows, LANES))
        words = arrived_ref[base : base + part_rows, :]
        values_ref[0, here, :] = upper_half(words) * low_scale
        values_ref[1, here, :] = lower_half(words) * high_scale
        words = arrived_ref[base + part_rows : base + step, :]
        words = jnp.concatenate([words, swap_halves(words[:second])], axis=0)
        words = jnp.where(low_lanes, words, swap_halves(words))
        values_ref[2, here, :] = jnp.where(low_lanes, upper_half(words) * low_scale, lower_half(words) * high_scale)
    return values_ref[0], values_ref[1], values_ref[2]


def store_blocks(rows):
    size = 4 * LANES
    return [(start, min(size, rows - start)) for start in range(0, rows, size)]


def formed_kernel(
    part_rows, index_ref, arrived_ref, near_hbm, out_hbm, near_ref, terms_ref, out_ref, values_ref, in_sems, out_sems
):
    half = terms_ref.shape[0] // 2
    first = tight_split(part_rows)
    blocks = store_blocks(near_ref.shape[0])
    fetches = [store_rows(near_hbm, near_ref, start, size, in_sems.at[i]) for i, (start, size) in enumerate(blocks)]
    low, high, near = loose_values(arrived_ref) if not first else tight_values(arrived_ref, part_rows, values_ref)
    for side, values in enumerate((low, high)):
        one, two = split(values, 2)
        terms_ref[side * half : (side + 1) * half, :LANES] = one
        terms_ref[side * half : (side + 1) * half, LANES : 2 * LANES] = two
    low_lanes = lane_ids(near.shape) < PANEL
    one, two = (term.astype(F32) for term in split(near, 2))
    terms_ref[:half, 2 * LANES :] = jnp.where(low_lanes, one, swap_halves(two)).astype(BF16)
    terms_ref[half:, 2 * LANES :] = jnp.where(low_lanes, swap_halves(one), two).astype(BF16)

    stores = []
    for i, (start, size) in enumerate(blocks):
        rows_here = slice(start, start + size)
        picks = one_hot(index_ref[:, rows_here], terms_ref.shape[0])
        got = jnp.dot(picks, terms_ref[...], preferred_element_type=F32)
        pair = got[:, 2 * LANES :]
        fetches[i].wait()
        held = near_ref[rows_here, :LANES]
        out_ref[rows_here, :LANES] = jnp.where(
            lane_ids(held.shape) < PANEL, held, (pair + swap_halves(pair)) + held
        )
        out_ref[rows_here, LANES:] = (got[:, :LANES] + got[:, LANES : 2 * LANES]) + near_ref[rows_here, LANES:]
        stores.append(store_rows(out_ref, out_hbm, start, size, out_sems.at[i]))
    for store in stores:
        store.wait()


def formed_columns(index, arrived, near, part_rows):
    rows, columns = near.shape
    vmem = pl.BlockSpec(memory_space=pltpu.VMEM)
    anywhere = pl.BlockSpec(memory_space=pltpu.HBM)
    return pl.pallas_call(
        functools.partial(formed_kernel, part_rows),
        in_specs=[vmem, vmem, anywhere],
        out_specs=anywhere,
        out_shape=pltpu.HBM((rows, columns), F32),
        input_output_aliases={2: 0},
        scratch_shapes=[
            pltpu.VMEM((rows, columns), F32),
            pltpu.VMEM((rows, 3 * LANES), BF16),
            pltpu.VMEM((rows, columns), F32),
            pltpu.VMEM((3, rows // 2, LANES), F32),
            pltpu.SemaphoreType.DMA((len(store_blocks(rows)),)),
            pltpu.SemaphoreType.DMA((len(store_blocks(rows)),)),
        ],
        compiler_params=params(32),
        cost_estimate=pl.CostEstimate(
            flops=8 * rows * rows * LANES, bytes_accessed=8 * rows * columns, transcendentals=0
        ),
        name="formed_columns",
    )(index, arrived, near)


def swap_rows(x, group):
    rows, width = x.shape
    return lax.all_to_all(
        x.reshape(group, rows // group, width), "wide", split_axis=0, concat_axis=0, tiled=True
    ).reshape(rows, width)


def on_device(a_rows, xa_panel, za_panel, send_order, recv_order, shift, resident):
    rows = a_rows.shape[0]
    columns = xa_panel.shape[1]
    group = lax.axis_size("wide")
    my_index = lax.axis_index("wide").astype(jnp.int32).reshape(1)
    share = rows // group
    half = rows // 2
    few, apart = phases_of(group)

    order, packing = send_order, share
    if share % 16:
        order = send_order.reshape(group, 2, share // 2).transpose(1, 0, 2).reshape(1, rows)
        packing = 0
    source, slot = recv_order // share, recv_order % share
    index = (slot // (share // 2)) * half + source * (share // 2) + slot % (share // 2)

    lead_panel, rest_panel = split_panels(my_index, xa_panel, za_panel)
    send_picks, a_copy = order_picks(order, a_rows, packing)
    lead_parts = [lead_panel]
    for masks in few:
        lead_parts = exchange(join(lead_parts), masks, "wide")
    rest_parts = [rest_panel]
    for number, masks in enumerate(apart[:-2]):
        rest_parts = exchange(join(rest_parts), masks, "wide")
        if number == 0:
            lead_parts = tied(lead_parts, *rest_parts)

    lead_out = lead_products(my_index, a_copy, send_picks, lead_parts, offsets_of(few))
    lead_in = swap_rows(tied([lead_out], *rest_parts)[0], group)
    rest_parts = exchange(join(tied(rest_parts, lead_out)), apart[-2], "wide")
    other_parts = exchange(rest_parts[:1], apart[-1], "wide")[1:]

    needed = columns + resident.shape[1]
    blocks_held = -(-needed // (PANEL * group))
    leading_parts = [leading_rows(index, lead_in, blocks_held * PANEL)]
    for masks in few:
        leading_parts = exchange(join(leading_parts), masks, "wide")
        if masks is few[0]:
            later_parts = exchange(tied(rest_parts[1:], *leading_parts), apart[-1], "wide")
    late = len(later_parts) // 2
    rest_parts = rest_parts + other_parts + later_parts[late:]
    rest_out = rest_products(my_index, send_picks, a_rows, rest_parts, offsets_of(apart), share // 2)
    rest_in = swap_rows(tied([rest_out], *leading_parts)[0], group)
    near, updated, pivots = updates(
        my_index,
        leading_parts,
        offsets_of(few),
        index,
        tied([lead_in], rest_out)[0],
        shift[None, :],
        resident,
        blocks_held,
        columns,
    )
    factored = formed_columns(index, rest_in, near, share // 2)
    return (factored, updated, pivots[0])


def solution(mesh):
    placed = (
        P(("parts", "wide"), None),
        P(("parts", "wide"), None),
        P(("parts", "wide"), None),
        P(("parts", "wide"), None),
        P(("parts", "wide"), None),
        P("parts"),
        P(("parts", "wide"), None),
    )
    return jax.shard_map(
        on_device,
        mesh=mesh,
        in_specs=placed,
        out_specs=(P(("parts", "wide"), None), P(("parts", "wide"), None), P("parts")),
        check_vma=False,
    )
```

```python
import functools

import jax
import jax.numpy as jnp
from jax import lax
from jax.experimental import pallas as pl
from jax.experimental.pallas import tpu as pltpu
from jax.sharding import PartitionSpec as P

PANEL = 64
LANES = 128
A_BLOCK = 640
DEEP_BLOCK = 256
F32 = jnp.float32
BF16 = jnp.bfloat16
MIB = 1024 * 1024


def params(mebibytes=12):
    return pltpu.CompilerParams(vmem_limit_bytes=mebibytes * MIB)


def in_hbm(x):
    return pltpu.with_memory_space_constraint(x, pltpu.HBM)


def lane_ids(shape):
    return lax.broadcasted_iota(jnp.int32, shape, len(shape) - 1)


def split(x, count):
    terms = []
    for _ in range(count):
        term = x.astype(BF16)
        terms.append(term)
        x = x - term.astype(F32)
    return terms


def swap_halves(x):
    return pltpu.roll(x, LANES // 2, 1)


def as_column(index_row):
    return jnp.transpose(jnp.broadcast_to(index_row, (LANES, LANES)))


def picks_of(at, width):
    lanes = lane_ids(at.shape)
    return jnp.concatenate(
        [(at == lanes + column).astype(F32).astype(BF16) for column in range(0, width, LANES)], axis=1
    )


def fill_picks(at_ref, picks_ref):
    rows, width = picks_ref.shape
    for start in range(0, rows, LANES):
        picks_ref[start : start + LANES, :] = picks_of(at_ref[start : start + LANES, :], width)


def one_hot(index_row, width):
    chunks = [
        picks_of(as_column(index_row[:, start : start + LANES]), width)
        for start in range(0, index_row.shape[1], LANES)
    ]
    return jnp.concatenate(chunks, axis=0) if len(chunks) > 1 else chunks[0]


def packed_order(share, half, slot):
    part = share // 2
    return (slot % share) // part * half + slot // share * part + slot % part


def fill_order(order_ref, at_ref, share):
    rows = order_ref.shape[1]
    height = 8
    for start in range(0, rows, LANES):
        column = as_column(order_ref[:, start : start + LANES])
        if not share:
            at_ref[start : start + LANES, :] = column
            continue
        for inner in range(0, LANES, height):
            place = packed_order(share, rows // 2, start + inner)
            at_ref[place : place + height, :] = column[inner : inner + height]


def exchange(held, masks, axis):
    size = lax.axis_size(axis)
    combined = [0]
    for mask in masks:
        combined += [other ^ mask for other in combined]
    parts = list(held)
    for mask in combined[1:]:
        parts += [lax.ppermute(part, axis, [(i, i ^ mask) for i in range(size)]) for part in held]
    return parts


def offsets_of(phases):
    offsets = [0]
    for masks in phases:
        combined = [0]
        for mask in masks:
            combined += [other ^ mask for other in combined]
        offsets = [offset ^ mask for mask in combined for offset in offsets]
    return offsets


def join(parts):
    return [jnp.concatenate(parts, axis=0)]


def phases_of(size):
    bits = [1 << bit for bit in reversed(range(size.bit_length() - 1))]
    return [bits[start : start + 2] for start in range(0, len(bits), 2)], [[bit] for bit in bits]


def tied(parts, *earlier):
    return list(lax.optimization_barrier((*parts, *earlier))[: len(parts)])


def picks_kernel(share, order_hbm, a_hbm, picks_ref, copy_ref, order_ref, at_ref, sems):
    fetch = pltpu.make_async_copy(order_hbm, order_ref, sems.at[0])
    copy = pltpu.make_async_copy(a_hbm, copy_ref, sems.at[1])
    fetch.start()
    copy.start()
    fetch.wait()
    fill_order(order_ref, at_ref, share)
    fill_picks(at_ref, picks_ref)
    copy.wait()


def order_picks(order, a_rows, share):
    rows, depth = a_rows.shape
    return pl.pallas_call(
        functools.partial(picks_kernel, share),
        in_specs=[pl.BlockSpec(memory_space=pltpu.HBM)] * 2,
        out_specs=[pl.BlockSpec(memory_space=pltpu.VMEM)] * 2,
        out_shape=[jax.ShapeDtypeStruct((rows, rows), BF16), jax.ShapeDtypeStruct((rows, depth), BF16)],
        scratch_shapes=[
            pltpu.VMEM((1, rows), jnp.int32),
            pltpu.VMEM((rows, LANES), jnp.int32),
            pltpu.SemaphoreType.DMA((2,)),
        ],
        compiler_params=params(),
        cost_estimate=pl.CostEstimate(flops=4 * rows * rows, bytes_accessed=4 * rows * depth, transcendentals=0),
        name="order_picks",
    )(in_hbm(order), in_hbm(a_rows))


def panels_kernel(my_ref, xa_hbm, za_hbm, lead_ref, rest_ref, xa_ref, za_ref, sems):
    copies = [
        pltpu.make_async_copy(xa_hbm, xa_ref, sems.at[0]),
        pltpu.make_async_copy(za_hbm, za_ref, sems.at[1]),
    ]
    for copy in copies:
        copy.start()
    for copy in copies:
        copy.wait()
    lead_ref[0] = jnp.concatenate([xa_ref[:, :PANEL], za_ref[:, :PANEL]], axis=1)
    rest_ref[0, :, :LANES] = jnp.concatenate([xa_ref[:, PANEL:LANES], za_ref[:, PANEL:LANES]], axis=1)
    rest_ref[0, :, LANES : 2 * LANES] = xa_ref[:, LANES:]
    rest_ref[0, :, 2 * LANES :] = za_ref[:, LANES:]


def split_panels(my_index, xa_panel, za_panel):
    depth, columns = xa_panel.shape
    return pl.pallas_call(
        panels_kernel,
        in_specs=[pl.BlockSpec(memory_space=pltpu.SMEM)] + [pl.BlockSpec(memory_space=pltpu.HBM)] * 2,
        out_shape=[
            jax.ShapeDtypeStruct((1, depth, LANES), BF16),
            jax.ShapeDtypeStruct((1, depth, 2 * columns - LANES), BF16),
        ],
        scratch_shapes=[
            pltpu.VMEM((depth, columns), BF16),
            pltpu.VMEM((depth, columns), BF16),
            pltpu.SemaphoreType.DMA((2,)),
        ],
        compiler_params=params(),
        name="split_panels",
    )(my_index, in_hbm(xa_panel), in_hbm(za_panel))


def assemble(my_index, offsets, parts, panel_ref):
    position = 0
    for part in parts:
        for number in range(part.shape[0]):
            depth = part.shape[1]
            start = pl.multiple_of((my_index ^ offsets[position]) * depth, depth)
            panel_ref[pl.ds(start, depth), :] = part[number]
            position += 1


def whole_sum(got):
    pair = got[:, :LANES]
    return (pair + swap_halves(pair)) + got[:, LANES:]


def lead_product_kernel(offsets, my_ref, a_ref, picks_ref, *refs):
    parts, (out_hbm, panel_ref, terms_ref, out_ref, sems) = refs[:-5], refs[-5:]
    assemble(my_ref[0], offsets, parts, panel_ref)
    rows = a_ref.shape[0]
    for start in range(0, rows, DEEP_BLOCK):
        both = jnp.dot(a_ref[start : start + DEEP_BLOCK, :], panel_ref[...], preferred_element_type=F32)
        first, second, third = (term.astype(F32) for term in split(both * swap_halves(both), 3))
        near = lane_ids(both.shape) < PANEL
        terms_ref[start : start + DEEP_BLOCK, :LANES] = jnp.where(near, first, second).astype(BF16)
        terms_ref[start : start + DEEP_BLOCK, LANES:] = third.astype(BF16)
    half = rows // 2
    block = half // 2
    stores = []
    for number, start in enumerate(range(0, half, block)):
        low = jnp.dot(picks_ref[start : start + block, :], terms_ref[...], preferred_element_type=F32)
        high = jnp.dot(picks_ref[half + start : half + start + block, :], terms_ref[...], preferred_element_type=F32)
        low, high = whole_sum(low), whole_sum(high)
        out_ref[start : start + block, :] = jnp.where(lane_ids(low.shape) < PANEL, low, high)
        stores.append(store_rows(out_ref, out_hbm, start, block, sems.at[number]))
    for store in stores:
        store.wait()


def lead_products(my_index, a_rows, picks, parts, offsets):
    rows, depth = a_rows.shape
    return pl.pallas_call(
        functools.partial(lead_product_kernel, offsets),
        in_specs=[pl.BlockSpec(memory_space=pltpu.SMEM)] + [pl.BlockSpec(memory_space=pltpu.VMEM)] * (2 + len(parts)),
        out_specs=pl.BlockSpec(memory_space=pltpu.HBM),
        out_shape=pltpu.HBM((rows // 2, LANES), F32),
        scratch_shapes=[
            pltpu.VMEM((depth, LANES), BF16),
            pltpu.VMEM((rows, 2 * LANES), BF16),
            pltpu.VMEM((rows // 2, LANES), F32),
            pltpu.SemaphoreType.DMA((2,)),
        ],
        compiler_params=params(24),
        cost_estimate=pl.CostEstimate(
            flops=2 * rows * (depth + 2 * rows) * LANES, bytes_accessed=2 * rows * depth, transcendentals=0
        ),
        name="lead_products",
    )(my_index, a_rows, picks, *parts)


BIAS = 128
MARGIN = 0.9995
ROUNDER = 1.5 * 2.0**23


def tight_split(part):
    first = -(-part // 16) * 8
    return first if part % 8 == 0 and part <= PANEL and 2 * first - part >= 8 else 0


def words_shape(half, part):
    first = tight_split(part)
    return (half // part * (part + first), LANES) if first else (half, 2 * LANES)


def store_rows(source, target, start, size, sem):
    rows = pl.ds(start, size)
    copy = pltpu.make_async_copy(source.at[rows, :], target.at[rows, :], sem)
    copy.start()
    return copy


def nearest(x):
    return (x + ROUNDER) - ROUNDER


def rest_product_kernel(offsets, my_ref, a_hbm, *refs):
    parts, (terms_ref, a_ref, panel_ref, sems) = refs[:-4], refs[-4:]
    rows = a_ref.shape[0]
    block = DEEP_BLOCK
    starts = range(0, rows, block)
    copies = [
        pltpu.make_async_copy(a_hbm.at[pl.ds(start, block), :], a_ref.at[pl.ds(start, block), :], sems.at[i])
        for i, start in enumerate(starts)
    ]
    for copy in copies[:3]:
        copy.start()
    assemble(my_ref[0], offsets, parts, panel_ref)

    def product(i):
        copies[i].wait()
        if i + 3 < len(copies):
            copies[i + 3].start()
        return jnp.dot(a_ref[starts[i] : starts[i] + block, :], panel_ref[...], preferred_element_type=F32)

    low_lanes = lane_ids((block, LANES)) < PANEL
    later = product(0)
    for i, start in enumerate(starts):
        both = later
        if i + 1 < len(starts):
            later = product(i + 1)
        near = both[:, :LANES]
        near = near * swap_halves(near)
        far = both[:, LANES : 2 * LANES] * both[:, 2 * LANES :]
        largest = jnp.max(jnp.maximum(jnp.abs(near), jnp.abs(far)), axis=1, keepdims=True)
        exponent = jnp.floor(jnp.log2(jnp.maximum(largest, 1e-30))) + 1.0
        scale = jnp.exp2(15.0 - exponent) * MARGIN
        far = nearest(far * scale)
        near = nearest(near * scale)
        far_top = nearest(far * (1 / 256))
        near_top = nearest(near * (1 / 256))
        here = slice(start, start + block)
        terms_ref[here, :LANES] = far_top.astype(BF16)
        terms_ref[here, LANES : 2 * LANES] = (far - far_top * 256.0).astype(BF16)
        terms_ref[here, 2 * LANES : 3 * LANES] = jnp.where(low_lanes, near_top, near - near_top * 256.0).astype(BF16)
        terms_ref[here, 3 * LANES :] = jnp.broadcast_to(exponent, (block, LANES)).astype(BF16)


def rest_order_kernel(part_rows, picks_hbm, terms_ref, out_hbm, picks_ref, out_ref, sems, out_sems):
    half = terms_ref.shape[0] // 2
    quarter = half // 2
    fetches = [
        store_rows(picks_hbm, picks_ref, start, quarter, sems.at[i])
        for i, start in enumerate((0, half, quarter, half + quarter))
    ]

    def coded(start, size):
        got = jnp.dot(picks_ref[start : start + size, :], terms_ref[...], preferred_element_type=F32)
        far = got[:, :LANES] * 256.0 + got[:, LANES : 2 * LANES]
        pair = got[:, 2 * LANES : 3 * LANES]
        pair = jnp.where(lane_ids(pair.shape) < PANEL, pair * 256.0, pair)
        near = (pair + swap_halves(pair)).astype(jnp.int32)
        return far.astype(jnp.int32), near, got[:, 3 * LANES :]

    block = half // 2
    first = tight_split(part_rows)
    low_lanes = lane_ids((8, LANES)) < PANEL
    eights = lax.broadcasted_iota(jnp.int32, (8, LANES), 0)
    places = lax.broadcasted_iota(jnp.int32, (part_rows, LANES), 0) + PANEL
    stores = []
    for number, start in enumerate(range(0, half, block)):
        fetches[2 * number].wait()
        fetches[2 * number + 1].wait()
        far_low, near_low, exponent_low = coded(start, block)
        far_high, near_high, exponent_high = coded(half + start, block)
        far = far_low * 65536 + (far_high & 65535)
        if not first:
            near = jnp.where(
                lane_ids(near_low.shape) < PANEL,
                near_low * 65536 + (exponent_low.astype(jnp.int32) + BIAS),
                near_high * 65536 + (exponent_high.astype(jnp.int32) + BIAS),
            )
            out_ref[start : start + block, :LANES] = far
            out_ref[start : start + block, LANES:] = near
            stores.append(store_rows(out_ref, out_hbm, start, block, out_sems.at[number]))
            continue
        near = near_low * 65536 + (near_high & 65535)
        second = part_rows - first
        mine = lane_ids((part_rows, LANES)) == places
        for inner in range(0, block, part_rows):
            base = (start + inner) // part_rows * (part_rows + first)
            words = near[inner : inner + part_rows]
            rows = [
                jnp.sum(jnp.where(mine, exponent[inner : inner + part_rows], 0.0), axis=0, keepdims=True)
                for exponent in (exponent_low, exponent_high)
            ]
            rows = jnp.where(eights == 0, rows[0], jnp.where(eights == 1, rows[1], 0.0)).astype(jnp.int32)
            out_ref[base : base + part_rows, :] = far[inner : inner + part_rows]
            base += part_rows
            spare = [words[: first - second - 8]] if first > second + 8 else []
            both = jnp.concatenate([words[first:], rows, *spare], axis=0)
            out_ref[base : base + first, :] = jnp.where(lane_ids(both.shape) < PANEL, words[:first], both)
        size = block // part_rows * (part_rows + first)
        stores.append(store_rows(out_ref, out_hbm, number * size, size, out_sems.at[number]))
    for store in stores:
        store.wait()


def rest_products(my_index, a_rows, parts, offsets):
    rows, depth = a_rows.shape
    vmem = pl.BlockSpec(memory_space=pltpu.VMEM)
    return pl.pallas_call(
        functools.partial(rest_product_kernel, offsets),
        in_specs=[pl.BlockSpec(memory_space=pltpu.SMEM), pl.BlockSpec(memory_space=pltpu.HBM)] + [vmem] * len(parts),
        out_specs=vmem,
        out_shape=jax.ShapeDtypeStruct((rows, 4 * LANES), BF16),
        scratch_shapes=[
            pltpu.VMEM((rows, depth), BF16),
            pltpu.VMEM((depth, 3 * LANES), BF16),
            pltpu.SemaphoreType.DMA((rows // DEEP_BLOCK,)),
        ],
        compiler_params=params(32),
        cost_estimate=pl.CostEstimate(
            flops=6 * rows * depth * LANES, bytes_accessed=2 * rows * depth, transcendentals=0
        ),
        name="rest_products",
    )(my_index, in_hbm(a_rows), *parts)


def rest_order(picks, terms, part_rows):
    rows = picks.shape[0]
    shape = words_shape(rows // 2, part_rows)
    hbm = pl.BlockSpec(memory_space=pltpu.HBM)
    return pl.pallas_call(
        functools.partial(rest_order_kernel, part_rows),
        in_specs=[hbm, pl.BlockSpec(memory_space=pltpu.VMEM)],
        out_specs=hbm,
        out_shape=pltpu.HBM(shape, jnp.int32),
        scratch_shapes=[
            pltpu.VMEM((rows, rows), BF16),
            pltpu.VMEM(shape, jnp.int32),
            pltpu.SemaphoreType.DMA((4,)),
            pltpu.SemaphoreType.DMA((2,)),
        ],
        compiler_params=params(24),
        cost_estimate=pl.CostEstimate(
            flops=8 * rows * rows * LANES, bytes_accessed=2 * rows * rows, transcendentals=0
        ),
        name="rest_order",
    )(in_hbm(picks), terms)


def packed_terms(x, terms_ref, start):
    half = x.shape[0]
    first, second, third = (term.astype(F32) for term in split(x, 3))
    near = lane_ids(x.shape) < PANEL
    other = swap_halves(third)
    terms_ref[:half, start : start + LANES] = jnp.where(near, first, swap_halves(second)).astype(BF16)
    terms_ref[half:, start : start + LANES] = jnp.where(near, swap_halves(first), second).astype(BF16)
    terms_ref[:half, start + LANES : start + 2 * LANES] = jnp.where(near, third, other).astype(BF16)
    terms_ref[half:, start + LANES : start + 2 * LANES] = jnp.where(near, other, third).astype(BF16)


def leading_kernel(held, index_ref, arrived_ref, out_ref, terms_ref):
    packed_terms(arrived_ref[...], terms_ref, 0)
    width = -(-held // LANES) * LANES
    picks = one_hot(index_ref[:, :width], terms_ref.shape[0])
    got = whole_sum(jnp.dot(picks, terms_ref[...], preferred_element_type=F32))
    first, second = got[: held // 2], got[held // 2 : held]
    out_ref[0] = jnp.where(lane_ids(first.shape) < PANEL, first, second)


def leading_rows(index, arrived, held):
    rows = index.shape[1]
    return pl.pallas_call(
        functools.partial(leading_kernel, held),
        in_specs=[pl.BlockSpec(memory_space=pltpu.VMEM)] * 2,
        out_specs=pl.BlockSpec(memory_space=pltpu.VMEM),
        out_shape=jax.ShapeDtypeStruct((1, held // 2, LANES), F32),
        scratch_shapes=[pltpu.VMEM((rows, 2 * LANES), BF16)],
        compiler_params=params(),
        cost_estimate=pl.CostEstimate(
            flops=4 * held * rows * LANES, bytes_accessed=2 * rows * LANES, transcendentals=0
        ),
        name="leading_rows",
    )(index, arrived)


def eliminate(block, shift_row):
    rows = lax.broadcasted_iota(jnp.int32, (PANEL, PANEL), 0)
    columns = lax.broadcasted_iota(jnp.int32, (PANEL, PANEL), 1)
    flipped = jnp.transpose(block)
    mirrored = jnp.where(rows >= columns, block, flipped)
    diagonal = shift_row + jnp.sum(jnp.abs(mirrored), axis=0, keepdims=True)
    unit = (rows == columns).astype(F32)
    work = jnp.where(rows == columns, diagonal, mirrored)
    work = jnp.concatenate([work, unit], axis=1)
    height = 8
    groups = [work[start : start + height] for start in range(0, PANEL, height)]
    sublanes = lax.broadcasted_iota(jnp.int32, (height, LANES), 0)
    scaled_rows = []
    for k in range(PANEL):
        home, offset = divmod(k, height)
        row = groups[home][offset : offset + 1, :]
        row = row / row[:, k : k + 1]
        scaled_rows.append(row)
        for g in range(home, PANEL // height):
            column = jnp.broadcast_to(groups[g][:, k : k + 1], (height, LANES))
            if g == home:
                column = jnp.where(sublanes > offset, column, 0.0)
            groups[g] = groups[g] - column * row
    final = jnp.concatenate(groups, axis=0)
    scaled = jnp.concatenate(scaled_rows, axis=0)
    upper = jnp.where(columns >= rows, scaled[:, :PANEL], 0.0)
    pivots = jnp.sum(jnp.where(rows == columns, final[:, :PANEL], 0.0), axis=0, keepdims=True)
    return upper, final[:, PANEL:], pivots


def exact(lhs, rhs, dims):
    return lax.dot_general(lhs, rhs, (dims, ((), ())), precision=lax.Precision.HIGHEST, preferred_element_type=F32)


def update_kernel(offsets, blocks_held, columns, my_ref, index_ref, arrived_ref, shift_ref, resident_hbm, *refs):
    parts = refs[:-12]
    near_hbm, far_hbm, pivots_ref, leading_ref, tail_ref, resident_ref, terms_ref, lead_ref = refs[-12:-4]
    near_ref, far_ref, sem, sems = refs[-4:]
    fetch = pltpu.make_async_copy(resident_hbm, resident_ref, sem)
    fetch.start()
    my_index = my_ref[0]
    size = len(offsets)
    position = 0
    packed = blocks_held * PANEL // 2
    part_rows = PANEL // 2
    for part in parts:
        for number in range(part.shape[0]):
            owner = my_index ^ offsets[position]
            for start in range(0, blocks_held * PANEL, part_rows):
                held, inner = divmod(start, PANEL)
                if start < packed:
                    rows = part[number, start : start + part_rows, :PANEL]
                else:
                    rows = part[number, start - packed : start - packed + part_rows, PANEL:]
                target = pl.multiple_of((held * size + owner) * PANEL + inner, part_rows)
                leading_ref[pl.ds(target, part_rows), :] = rows
            position += 1
    upper, inverse, pivots = eliminate(leading_ref[:PANEL, :], shift_ref[...])
    pivots_ref[...] = pivots
    lower = jnp.transpose(upper)
    needed = tail_ref.shape[1]
    tail = exact(inverse, leading_ref[:needed, :], ((1,), (1,)))
    high, low = split(tail, 2)
    tail_ref[0:PANEL, :] = high
    tail_ref[PANEL : 2 * PANEL, :] = high
    tail_ref[2 * PANEL : 3 * PANEL, :] = low
    tail_ref[3 * PANEL :, :] = low

    block = A_BLOCK
    packed_terms(arrived_ref[...], terms_ref, 0)
    for start in range(0, lead_ref.shape[0], block):
        picks = one_hot(index_ref[:, start : start + block], lead_ref.shape[0])
        got = jnp.dot(picks, terms_ref[...], preferred_element_type=F32)
        lead_ref[start : start + block, :] = whole_sum(got)[:, :PANEL]
    fetch.wait()
    stores = []
    for number, start in enumerate(range(0, lead_ref.shape[0], block)):
        rows_here = slice(start, start + block)
        panel = exact(lead_ref[rows_here, :], inverse, ((1,), (1,))) / pivots
        shown = used = panel
        if start == 0:
            row_ids = lax.broadcasted_iota(jnp.int32, panel.shape, 0)
            top = jnp.logical_and(my_index == 0, row_ids < PANEL)
            used = jnp.where(top, 0.0, panel)
            filled = jnp.concatenate([lower, jnp.zeros((block - PANEL, PANEL), F32)], axis=0)
            shown = jnp.where(top, filled, panel)
        high, low = (term.astype(F32) for term in split(used, 2))
        pair = jnp.concatenate([high, low], axis=1).astype(BF16)
        factors = jnp.concatenate([pair, pair], axis=1)
        update = jnp.dot(factors, tail_ref[...], preferred_element_type=F32)
        shown = jnp.concatenate([shown, jnp.zeros_like(shown)], axis=1)
        near_ref[rows_here, :LANES] = jnp.where(lane_ids(shown.shape) < PANEL, shown, -update[:, :LANES])
        near_ref[rows_here, LANES:] = -update[:, LANES:columns]
        far_ref[rows_here, :] = (resident_ref[rows_here, :].astype(F32) - update[:, columns:]).astype(BF16)
        for which, (source, target) in enumerate(((near_ref, near_hbm), (far_ref, far_hbm))):
            store = pltpu.make_async_copy(
                source.at[pl.ds(start, block), :], target.at[pl.ds(start, block), :], sems.at[which, number]
            )
            store.start()
            stores.append(store)
    for store in stores:
        store.wait()


def updates(my_index, parts, offsets, index, arrived, shift, resident, blocks_held, columns):
    rows, width = resident.shape
    needed = columns + width
    held_rows = len(offsets) * blocks_held * PANEL
    vmem = pl.BlockSpec(memory_space=pltpu.VMEM)
    anywhere = pl.BlockSpec(memory_space=pltpu.HBM)
    return pl.pallas_call(
        functools.partial(update_kernel, offsets, blocks_held, columns),
        in_specs=[pl.BlockSpec(memory_space=pltpu.SMEM), vmem, vmem, vmem, anywhere] + [vmem] * len(parts),
        out_specs=[anywhere, anywhere, vmem],
        out_shape=[
            pltpu.HBM((rows, columns), F32),
            pltpu.HBM((rows, width), BF16),
            jax.ShapeDtypeStruct((1, PANEL), F32),
        ],
        scratch_shapes=[
            pltpu.VMEM((held_rows, PANEL), F32),
            pltpu.VMEM((4 * PANEL, needed), BF16),
            pltpu.VMEM((rows, width), BF16),
            pltpu.VMEM((rows, 2 * LANES), BF16),
            pltpu.VMEM((rows, PANEL), F32),
            pltpu.VMEM((rows, columns), F32),
            pltpu.VMEM((rows, width), BF16),
            pltpu.SemaphoreType.DMA,
            pltpu.SemaphoreType.DMA((2, rows // A_BLOCK)),
        ],
        compiler_params=params(32),
        cost_estimate=pl.CostEstimate(
            flops=2 * rows * needed * 4 * PANEL, bytes_accessed=4 * rows * (columns + width), transcendentals=0
        ),
        name="factor_and_update",
    )(my_index, index, arrived, shift, in_hbm(resident), *parts)


def upper_half(words):
    return (words >> 16).astype(F32)


def lower_half(words):
    return ((words << 16) >> 16).astype(F32)


def loose_values(arrived_ref):
    words = arrived_ref[:, LANES:]
    low_lanes = lane_ids(words.shape) < PANEL
    scale = jnp.exp2(((words & 255) - (BIAS + 15)).astype(F32)) * (1 / MARGIN)
    other = swap_halves(scale)
    near = upper_half(words) * scale
    words = arrived_ref[:, :LANES]
    low = upper_half(words) * jnp.where(low_lanes, scale, other)
    return low, lower_half(words) * jnp.where(low_lanes, other, scale), near


def tight_values(arrived_ref, part_rows, values_ref):
    first = tight_split(part_rows)
    second = part_rows - first
    step = part_rows + first
    sources = arrived_ref.shape[0] // step
    pairs = [arrived_ref[i * step + part_rows + second : i * step + part_rows + second + 2, :] for i in range(sources)]
    spare = jnp.zeros((LANES - 2 * sources, LANES), jnp.int32)
    exponents = jnp.concatenate([*pairs, spare], axis=0)
    scales = jnp.exp2(jnp.transpose(exponents.astype(F32)) - 15.0) * (1 / MARGIN)
    scales = scales[PANEL : PANEL + part_rows]
    low_lanes = lane_ids((part_rows, LANES)) < PANEL
    for i in range(sources):
        base = i * step
        here = slice(i * part_rows, (i + 1) * part_rows)
        low_scale = jnp.broadcast_to(scales[:, 2 * i : 2 * i + 1], (part_rows, LANES))
        high_scale = jnp.broadcast_to(scales[:, 2 * i + 1 : 2 * i + 2], (part_rows, LANES))
        words = arrived_ref[base : base + part_rows, :]
        values_ref[0, here, :] = upper_half(words) * low_scale
        values_ref[1, here, :] = lower_half(words) * high_scale
        words = arrived_ref[base + part_rows : base + step, :]
        words = jnp.concatenate([words, swap_halves(words[:second])], axis=0)
        words = jnp.where(low_lanes, words, swap_halves(words))
        values_ref[2, here, :] = jnp.where(low_lanes, upper_half(words) * low_scale, lower_half(words) * high_scale)
    return values_ref[0], values_ref[1], values_ref[2]


def store_blocks(rows):
    size = 4 * LANES
    return [(start, min(size, rows - start)) for start in range(0, rows, size)]


def formed_kernel(
    part_rows, index_ref, arrived_ref, near_hbm, out_hbm, near_ref, terms_ref, out_ref, values_ref, in_sems, out_sems
):
    half = terms_ref.shape[0] // 2
    first = tight_split(part_rows)
    blocks = store_blocks(near_ref.shape[0])
    fetches = [store_rows(near_hbm, near_ref, start, size, in_sems.at[i]) for i, (start, size) in enumerate(blocks)]
    low, high, near = loose_values(arrived_ref) if not first else tight_values(arrived_ref, part_rows, values_ref)
    for side, values in enumerate((low, high)):
        one, two = split(values, 2)
        terms_ref[side * half : (side + 1) * half, :LANES] = one
        terms_ref[side * half : (side + 1) * half, LANES : 2 * LANES] = two
    low_lanes = lane_ids(near.shape) < PANEL
    one, two = (term.astype(F32) for term in split(near, 2))
    terms_ref[:half, 2 * LANES :] = jnp.where(low_lanes, one, swap_halves(two)).astype(BF16)
    terms_ref[half:, 2 * LANES :] = jnp.where(low_lanes, swap_halves(one), two).astype(BF16)

    stores = []
    for i, (start, size) in enumerate(blocks):
        rows_here = slice(start, start + size)
        picks = one_hot(index_ref[:, rows_here], terms_ref.shape[0])
        got = jnp.dot(picks, terms_ref[...], preferred_element_type=F32)
        pair = got[:, 2 * LANES :]
        fetches[i].wait()
        held = near_ref[rows_here, :LANES]
        out_ref[rows_here, :LANES] = jnp.where(
            lane_ids(held.shape) < PANEL, held, (pair + swap_halves(pair)) + held
        )
        out_ref[rows_here, LANES:] = (got[:, :LANES] + got[:, LANES : 2 * LANES]) + near_ref[rows_here, LANES:]
        stores.append(store_rows(out_ref, out_hbm, start, size, out_sems.at[i]))
    for store in stores:
        store.wait()


def formed_columns(index, arrived, near, part_rows):
    rows, columns = near.shape
    vmem = pl.BlockSpec(memory_space=pltpu.VMEM)
    anywhere = pl.BlockSpec(memory_space=pltpu.HBM)
    return pl.pallas_call(
        functools.partial(formed_kernel, part_rows),
        in_specs=[vmem, vmem, anywhere],
        out_specs=anywhere,
        out_shape=pltpu.HBM((rows, columns), F32),
        input_output_aliases={2: 0},
        scratch_shapes=[
            pltpu.VMEM((rows, columns), F32),
            pltpu.VMEM((rows, 3 * LANES), BF16),
            pltpu.VMEM((rows, columns), F32),
            pltpu.VMEM((3, rows // 2, LANES), F32),
            pltpu.SemaphoreType.DMA((len(store_blocks(rows)),)),
            pltpu.SemaphoreType.DMA((len(store_blocks(rows)),)),
        ],
        compiler_params=params(32),
        cost_estimate=pl.CostEstimate(
            flops=8 * rows * rows * LANES, bytes_accessed=8 * rows * columns, transcendentals=0
        ),
        name="formed_columns",
    )(index, arrived, near)


def swap_rows(x, group):
    rows, width = x.shape
    return lax.all_to_all(
        x.reshape(group, rows // group, width), "wide", split_axis=0, concat_axis=0, tiled=True
    ).reshape(rows, width)


def on_device(a_rows, xa_panel, za_panel, send_order, recv_order, shift, resident):
    rows = a_rows.shape[0]
    columns = xa_panel.shape[1]
    group = lax.axis_size("wide")
    my_index = lax.axis_index("wide").astype(jnp.int32).reshape(1)
    share = rows // group
    half = rows // 2
    few, apart = phases_of(group)

    order, packing = send_order, share
    if share % 16:
        order = send_order.reshape(group, 2, share // 2).transpose(1, 0, 2).reshape(1, rows)
        packing = 0
    source, slot = recv_order // share, recv_order % share
    index = (slot // (share // 2)) * half + source * (share // 2) + slot % (share // 2)

    lead_panel, rest_panel = split_panels(my_index, xa_panel, za_panel)
    send_picks, a_copy = order_picks(order, a_rows, packing)
    lead_parts = [lead_panel]
    for masks in few:
        lead_parts = exchange(join(lead_parts), masks, "wide")
    rest_parts = [rest_panel]
    for number, masks in enumerate(apart[:-2]):
        rest_parts = exchange(rest_parts, masks, "wide")
        if number == 0:
            rest_parts = tied(rest_parts, send_picks)
        rest_parts = join(rest_parts)

    lead_out = lead_products(my_index, a_copy, send_picks, tied(lead_parts, *rest_parts), offsets_of(few))
    rest_parts = exchange(rest_parts, apart[-2], "wide")
    lead_in = swap_rows(lead_out, group)
    rest_parts = exchange(tied(rest_parts, lead_out), apart[-1], "wide")
    rest_terms = rest_products(my_index, a_rows, rest_parts, offsets_of(apart))

    needed = columns + resident.shape[1]
    blocks_held = -(-needed // (PANEL * group))
    packed = leading_rows(index, tied([lead_in], rest_terms)[0], blocks_held * PANEL)
    leading_parts = join(exchange([packed], few[0], "wide"))
    rest_out = rest_order(send_picks, tied([rest_terms], *leading_parts)[0], share // 2)
    for masks in few[1:]:
        leading_parts = exchange(join(leading_parts), masks, "wide")
    rest_in = swap_rows(rest_out, group)
    near, updated, pivots = updates(
        my_index,
        leading_parts,
        offsets_of(few),
        index,
        tied([lead_in], rest_out)[0],
        shift[None, :],
        resident,
        blocks_held,
        columns,
    )
    factored = formed_columns(index, rest_in, near, share // 2)
    return (factored, updated, pivots[0])


def solution(mesh):
    placed = (
        P(("parts", "wide"), None),
        P(("parts", "wide"), None),
        P(("parts", "wide"), None),
        P(("parts", "wide"), None),
        P(("parts", "wide"), None),
        P("parts"),
        P(("parts", "wide"), None),
    )
    return jax.shard_map(
        on_device,
        mesh=mesh,
        in_specs=placed,
        out_specs=(P(("parts", "wide"), None), P(("parts", "wide"), None), P("parts")),
        check_vma=False,
    )
```

```python
import functools

import jax
import jax.numpy as jnp
from jax import lax
from jax.experimental import pallas as pl
from jax.experimental.pallas import tpu as pltpu
from jax.sharding import PartitionSpec as P

PANEL = 64
LANES = 128
A_BLOCK = 640
DEEP_BLOCK = 256
F32 = jnp.float32
BF16 = jnp.bfloat16
MIB = 1024 * 1024


def params(mebibytes=12):
    return pltpu.CompilerParams(vmem_limit_bytes=mebibytes * MIB)


def in_hbm(x):
    return pltpu.with_memory_space_constraint(x, pltpu.HBM)


def lane_ids(shape):
    return lax.broadcasted_iota(jnp.int32, shape, len(shape) - 1)


def split(x, count):
    terms = []
    for _ in range(count):
        term = x.astype(BF16)
        terms.append(term)
        x = x - term.astype(F32)
    return terms


def swap_halves(x):
    return pltpu.roll(x, LANES // 2, 1)


def as_column(index_row):
    return jnp.transpose(jnp.broadcast_to(index_row, (LANES, LANES)))


def picks_of(at, width):
    lanes = lane_ids(at.shape)
    return jnp.concatenate(
        [(at == lanes + column).astype(F32).astype(BF16) for column in range(0, width, LANES)], axis=1
    )


def fill_picks(at_ref, picks_ref):
    rows, width = picks_ref.shape
    for start in range(0, rows, LANES):
        picks_ref[start : start + LANES, :] = picks_of(at_ref[start : start + LANES, :], width)


def one_hot(index_row, width):
    chunks = [
        picks_of(as_column(index_row[:, start : start + LANES]), width)
        for start in range(0, index_row.shape[1], LANES)
    ]
    return jnp.concatenate(chunks, axis=0) if len(chunks) > 1 else chunks[0]


def packed_order(share, half, slot):
    part = share // 2
    return (slot % share) // part * half + slot // share * part + slot % part


def fill_order(order_ref, at_ref, share):
    rows = order_ref.shape[1]
    height = 8
    for start in range(0, rows, LANES):
        column = as_column(order_ref[:, start : start + LANES])
        if not share:
            at_ref[start : start + LANES, :] = column
            continue
        for inner in range(0, LANES, height):
            place = packed_order(share, rows // 2, start + inner)
            at_ref[place : place + height, :] = column[inner : inner + height]


def exchange(held, masks, axis):
    size = lax.axis_size(axis)
    combined = [0]
    for mask in masks:
        combined += [other ^ mask for other in combined]
    parts = list(held)
    for mask in combined[1:]:
        parts += [lax.ppermute(part, axis, [(i, i ^ mask) for i in range(size)]) for part in held]
    return parts


def offsets_of(phases):
    offsets = [0]
    for masks in phases:
        combined = [0]
        for mask in masks:
            combined += [other ^ mask for other in combined]
        offsets = [offset ^ mask for mask in combined for offset in offsets]
    return offsets


def join(parts):
    return [jnp.concatenate(parts, axis=0)]


def phases_of(size):
    bits = [1 << bit for bit in reversed(range(size.bit_length() - 1))]
    return [bits[start : start + 2] for start in range(0, len(bits), 2)], [[bit] for bit in bits]


def tied(parts, *earlier):
    return list(lax.optimization_barrier((*parts, *earlier))[: len(parts)])


def picks_kernel(share, order_hbm, a_hbm, picks_ref, copy_ref, order_ref, at_ref, sems):
    fetch = pltpu.make_async_copy(order_hbm, order_ref, sems.at[0])
    copy = pltpu.make_async_copy(a_hbm, copy_ref, sems.at[1])
    fetch.start()
    copy.start()
    fetch.wait()
    fill_order(order_ref, at_ref, share)
    fill_picks(at_ref, picks_ref)
    copy.wait()


def order_picks(order, a_rows, share):
    rows, depth = a_rows.shape
    return pl.pallas_call(
        functools.partial(picks_kernel, share),
        in_specs=[pl.BlockSpec(memory_space=pltpu.HBM)] * 2,
        out_specs=[pl.BlockSpec(memory_space=pltpu.VMEM)] * 2,
        out_shape=[jax.ShapeDtypeStruct((rows, rows), BF16), jax.ShapeDtypeStruct((rows, depth), BF16)],
        scratch_shapes=[
            pltpu.VMEM((1, rows), jnp.int32),
            pltpu.VMEM((rows, LANES), jnp.int32),
            pltpu.SemaphoreType.DMA((2,)),
        ],
        compiler_params=params(),
        cost_estimate=pl.CostEstimate(flops=4 * rows * rows, bytes_accessed=4 * rows * depth, transcendentals=0),
        name="order_picks",
    )(in_hbm(order), in_hbm(a_rows))


def panels_kernel(my_ref, xa_hbm, za_hbm, lead_ref, rest_ref, xa_ref, za_ref, sems):
    copies = [
        pltpu.make_async_copy(xa_hbm, xa_ref, sems.at[0]),
        pltpu.make_async_copy(za_hbm, za_ref, sems.at[1]),
    ]
    for copy in copies:
        copy.start()
    for copy in copies:
        copy.wait()
    lead_ref[0] = jnp.concatenate([xa_ref[:, :PANEL], za_ref[:, :PANEL]], axis=1)
    rest_ref[0, :, :LANES] = jnp.concatenate([xa_ref[:, PANEL:LANES], za_ref[:, PANEL:LANES]], axis=1)
    rest_ref[0, :, LANES : 2 * LANES] = xa_ref[:, LANES:]
    rest_ref[0, :, 2 * LANES :] = za_ref[:, LANES:]


def split_panels(my_index, xa_panel, za_panel):
    depth, columns = xa_panel.shape
    return pl.pallas_call(
        panels_kernel,
        in_specs=[pl.BlockSpec(memory_space=pltpu.SMEM)] + [pl.BlockSpec(memory_space=pltpu.HBM)] * 2,
        out_shape=[
            jax.ShapeDtypeStruct((1, depth, LANES), BF16),
            jax.ShapeDtypeStruct((1, depth, 2 * columns - LANES), BF16),
        ],
        scratch_shapes=[
            pltpu.VMEM((depth, columns), BF16),
            pltpu.VMEM((depth, columns), BF16),
            pltpu.SemaphoreType.DMA((2,)),
        ],
        compiler_params=params(),
        name="split_panels",
    )(my_index, in_hbm(xa_panel), in_hbm(za_panel))


def assemble(my_index, offsets, parts, panel_ref):
    position = 0
    for part in parts:
        for number in range(part.shape[0]):
            depth = part.shape[1]
            start = pl.multiple_of((my_index ^ offsets[position]) * depth, depth)
            panel_ref[pl.ds(start, depth), :] = part[number]
            position += 1


def whole_sum(got):
    pair = got[:, :LANES]
    return (pair + swap_halves(pair)) + got[:, LANES:]


def store_rows(source, target, start, size, sem):
    rows = pl.ds(start, size)
    copy = pltpu.make_async_copy(source.at[rows, :], target.at[rows, :], sem)
    copy.start()
    return copy


def lead_product_kernel(offsets, my_ref, a_ref, picks_ref, *refs):
    parts, (out_hbm, panel_ref, terms_ref, out_ref, sems) = refs[:-5], refs[-5:]
    assemble(my_ref[0], offsets, parts, panel_ref)
    rows = a_ref.shape[0]
    for start in range(0, rows, DEEP_BLOCK):
        both = jnp.dot(a_ref[start : start + DEEP_BLOCK, :], panel_ref[...], preferred_element_type=F32)
        first, second, third = (term.astype(F32) for term in split(both * swap_halves(both), 3))
        near = lane_ids(both.shape) < PANEL
        terms_ref[start : start + DEEP_BLOCK, :LANES] = jnp.where(near, first, second).astype(BF16)
        terms_ref[start : start + DEEP_BLOCK, LANES:] = third.astype(BF16)
    half = rows // 2
    block = half // 2
    stores = []
    for number, start in enumerate(range(0, half, block)):
        low = jnp.dot(picks_ref[start : start + block, :], terms_ref[...], preferred_element_type=F32)
        high = jnp.dot(picks_ref[half + start : half + start + block, :], terms_ref[...], preferred_element_type=F32)
        low, high = whole_sum(low), whole_sum(high)
        out_ref[start : start + block, :] = jnp.where(lane_ids(low.shape) < PANEL, low, high)
        stores.append(store_rows(out_ref, out_hbm, start, block, sems.at[number]))
    for store in stores:
        store.wait()


def lead_products(my_index, a_rows, picks, parts, offsets):
    rows, depth = a_rows.shape
    return pl.pallas_call(
        functools.partial(lead_product_kernel, offsets),
        in_specs=[pl.BlockSpec(memory_space=pltpu.SMEM)] + [pl.BlockSpec(memory_space=pltpu.VMEM)] * (2 + len(parts)),
        out_specs=pl.BlockSpec(memory_space=pltpu.HBM),
        out_shape=pltpu.HBM((rows // 2, LANES), F32),
        scratch_shapes=[
            pltpu.VMEM((depth, LANES), BF16),
            pltpu.VMEM((rows, 2 * LANES), BF16),
            pltpu.VMEM((rows // 2, LANES), F32),
            pltpu.SemaphoreType.DMA((2,)),
        ],
        compiler_params=params(24),
        cost_estimate=pl.CostEstimate(
            flops=2 * rows * (depth + 2 * rows) * LANES, bytes_accessed=2 * rows * depth, transcendentals=0
        ),
        name="lead_products",
    )(my_index, a_rows, picks, *parts)


BIAS = 128
MARGIN = 0.9995
ROUNDER = 1.5 * 2.0**23


def tight_split(part):
    first = -(-part // 16) * 8
    return first if part % 8 == 0 and part <= PANEL and 2 * first - part >= 8 else 0


def words_shape(half, part):
    first = tight_split(part)
    return (half // part * (part + first), LANES) if first else (half, 2 * LANES)


def nearest(x):
    return (x + ROUNDER) - ROUNDER


def rest_product_kernel(offsets, share, part_rows, my_ref, order_ref, a_hbm, *refs):
    parts, (out_ref, a_ref, at_ref, picks_ref, panel_ref, terms_ref, sems) = refs[:-7], refs[-7:]
    rows = a_ref.shape[0]
    half = rows // 2
    block = DEEP_BLOCK
    starts = range(0, rows, block)
    copies = [
        pltpu.make_async_copy(a_hbm.at[pl.ds(start, block), :], a_ref.at[pl.ds(start, block), :], sems.at[i])
        for i, start in enumerate(starts)
    ]
    for copy in copies[:3]:
        copy.start()
    assemble(my_ref[0], offsets, parts, panel_ref)
    fill_order(order_ref, at_ref, share)
    fill_picks(at_ref, picks_ref)

    def product(i):
        copies[i].wait()
        if i + 3 < len(copies):
            copies[i + 3].start()
        return jnp.dot(a_ref[starts[i] : starts[i] + block, :], panel_ref[...], preferred_element_type=F32)

    low_lanes = lane_ids((block, LANES)) < PANEL
    later = product(0)
    for i, start in enumerate(starts):
        both = later
        if i + 1 < len(starts):
            later = product(i + 1)
        near = both[:, :LANES]
        near = near * swap_halves(near)
        far = both[:, LANES : 2 * LANES] * both[:, 2 * LANES :]
        largest = jnp.max(jnp.maximum(jnp.abs(near), jnp.abs(far)), axis=1, keepdims=True)
        exponent = jnp.floor(jnp.log2(jnp.maximum(largest, 1e-30))) + 1.0
        scale = jnp.exp2(15.0 - exponent) * MARGIN
        far = nearest(far * scale)
        near = nearest(near * scale)
        far_top = nearest(far * (1 / 256))
        near_top = nearest(near * (1 / 256))
        here = slice(start, start + block)
        terms_ref[here, :LANES] = far_top.astype(BF16)
        terms_ref[here, LANES : 2 * LANES] = (far - far_top * 256.0).astype(BF16)
        terms_ref[here, 2 * LANES : 3 * LANES] = jnp.where(low_lanes, near_top, near - near_top * 256.0).astype(BF16)
        terms_ref[here, 3 * LANES :] = jnp.broadcast_to(exponent, (block, LANES)).astype(BF16)

    def coded(start, size):
        got = jnp.dot(picks_ref[start : start + size, :], terms_ref[...], preferred_element_type=F32)
        far = got[:, :LANES] * 256.0 + got[:, LANES : 2 * LANES]
        pair = got[:, 2 * LANES : 3 * LANES]
        pair = jnp.where(lane_ids(pair.shape) < PANEL, pair * 256.0, pair)
        near = (pair + swap_halves(pair)).astype(jnp.int32)
        return far.astype(jnp.int32), near, got[:, 3 * LANES :]

    block = half // 2
    first = tight_split(part_rows)
    low_lanes = lane_ids((8, LANES)) < PANEL
    eights = lax.broadcasted_iota(jnp.int32, (8, LANES), 0)
    places = lax.broadcasted_iota(jnp.int32, (part_rows, LANES), 0) + PANEL
    for start in range(0, half, block):
        far_low, near_low, exponent_low = coded(start, block)
        far_high, near_high, exponent_high = coded(half + start, block)
        far = far_low * 65536 + (far_high & 65535)
        if not first:
            near = jnp.where(
                lane_ids(near_low.shape) < PANEL,
                near_low * 65536 + (exponent_low.astype(jnp.int32) + BIAS),
                near_high * 65536 + (exponent_high.astype(jnp.int32) + BIAS),
            )
            out_ref[start : start + block, :LANES] = far
            out_ref[start : start + block, LANES:] = near
            continue
        near = near_low * 65536 + (near_high & 65535)
        second = part_rows - first
        mine = lane_ids((part_rows, LANES)) == places
        for inner in range(0, block, part_rows):
            base = (start + inner) // part_rows * (part_rows + first)
            words = near[inner : inner + part_rows]
            rows = [
                jnp.sum(jnp.where(mine, exponent[inner : inner + part_rows], 0.0), axis=0, keepdims=True)
                for exponent in (exponent_low, exponent_high)
            ]
            rows = jnp.where(eights == 0, rows[0], jnp.where(eights == 1, rows[1], 0.0)).astype(jnp.int32)
            out_ref[base : base + part_rows, :] = far[inner : inner + part_rows]
            base += part_rows
            spare = [words[: first - second - 8]] if first > second + 8 else []
            both = jnp.concatenate([words[first:], rows, *spare], axis=0)
            out_ref[base : base + first, :] = jnp.where(lane_ids(both.shape) < PANEL, words[:first], both)


def rest_products(my_index, order, a_rows, parts, offsets, share, part_rows):
    rows, depth = a_rows.shape
    return pl.pallas_call(
        functools.partial(rest_product_kernel, offsets, share, part_rows),
        in_specs=[
            pl.BlockSpec(memory_space=pltpu.SMEM),
            pl.BlockSpec(memory_space=pltpu.VMEM),
            pl.BlockSpec(memory_space=pltpu.HBM),
        ]
        + [pl.BlockSpec(memory_space=pltpu.VMEM)] * len(parts),
        out_specs=pl.BlockSpec(memory_space=pltpu.VMEM),
        out_shape=jax.ShapeDtypeStruct(words_shape(rows // 2, part_rows), jnp.int32),
        scratch_shapes=[
            pltpu.VMEM((rows, depth), BF16),
            pltpu.VMEM((rows, LANES), jnp.int32),
            pltpu.VMEM((rows, rows), BF16),
            pltpu.VMEM((depth, 3 * LANES), BF16),
            pltpu.VMEM((rows, 4 * LANES), BF16),
            pltpu.SemaphoreType.DMA((rows // DEEP_BLOCK,)),
        ],
        compiler_params=params(32),
        cost_estimate=pl.CostEstimate(
            flops=2 * rows * (3 * depth + 4 * rows) * LANES, bytes_accessed=2 * rows * depth, transcendentals=0
        ),
        name="rest_products",
    )(my_index, order, in_hbm(a_rows), *parts)


def packed_terms(x, terms_ref, start):
    half = x.shape[0]
    first, second, third = (term.astype(F32) for term in split(x, 3))
    near = lane_ids(x.shape) < PANEL
    other = swap_halves(third)
    terms_ref[:half, start : start + LANES] = jnp.where(near, first, swap_halves(second)).astype(BF16)
    terms_ref[half:, start : start + LANES] = jnp.where(near, swap_halves(first), second).astype(BF16)
    terms_ref[:half, start + LANES : start + 2 * LANES] = jnp.where(near, third, other).astype(BF16)
    terms_ref[half:, start + LANES : start + 2 * LANES] = jnp.where(near, other, third).astype(BF16)


def leading_kernel(held, index_ref, arrived_ref, out_ref, terms_ref):
    packed_terms(arrived_ref[...], terms_ref, 0)
    width = -(-held // LANES) * LANES
    picks = one_hot(index_ref[:, :width], terms_ref.shape[0])
    got = whole_sum(jnp.dot(picks, terms_ref[...], preferred_element_type=F32))
    first, second = got[: held // 2], got[held // 2 : held]
    out_ref[0] = jnp.where(lane_ids(first.shape) < PANEL, first, second)


def leading_rows(index, arrived, held):
    rows = index.shape[1]
    return pl.pallas_call(
        functools.partial(leading_kernel, held),
        in_specs=[pl.BlockSpec(memory_space=pltpu.VMEM)] * 2,
        out_specs=pl.BlockSpec(memory_space=pltpu.VMEM),
        out_shape=jax.ShapeDtypeStruct((1, held // 2, LANES), F32),
        scratch_shapes=[pltpu.VMEM((rows, 2 * LANES), BF16)],
        compiler_params=params(),
        cost_estimate=pl.CostEstimate(
            flops=4 * held * rows * LANES, bytes_accessed=2 * rows * LANES, transcendentals=0
        ),
        name="leading_rows",
    )(index, arrived)


def eliminate(block, shift_row):
    rows = lax.broadcasted_iota(jnp.int32, (PANEL, PANEL), 0)
    columns = lax.broadcasted_iota(jnp.int32, (PANEL, PANEL), 1)
    flipped = jnp.transpose(block)
    mirrored = jnp.where(rows >= columns, block, flipped)
    diagonal = shift_row + jnp.sum(jnp.abs(mirrored), axis=0, keepdims=True)
    unit = (rows == columns).astype(F32)
    work = jnp.where(rows == columns, diagonal, mirrored)
    work = jnp.concatenate([work, unit], axis=1)
    height = 8
    groups = [work[start : start + height] for start in range(0, PANEL, height)]
    sublanes = lax.broadcasted_iota(jnp.int32, (height, LANES), 0)
    scaled_rows = []
    for k in range(PANEL):
        home, offset = divmod(k, height)
        row = groups[home][offset : offset + 1, :]
        row = row / row[:, k : k + 1]
        scaled_rows.append(row)
        for g in range(home, PANEL // height):
            column = jnp.broadcast_to(groups[g][:, k : k + 1], (height, LANES))
            if g == home:
                column = jnp.where(sublanes > offset, column, 0.0)
            groups[g] = groups[g] - column * row
    final = jnp.concatenate(groups, axis=0)
    scaled = jnp.concatenate(scaled_rows, axis=0)
    upper = jnp.where(columns >= rows, scaled[:, :PANEL], 0.0)
    pivots = jnp.sum(jnp.where(rows == columns, final[:, :PANEL], 0.0), axis=0, keepdims=True)
    return upper, final[:, PANEL:], pivots


def exact(lhs, rhs, dims):
    return lax.dot_general(lhs, rhs, (dims, ((), ())), precision=lax.Precision.HIGHEST, preferred_element_type=F32)


def update_kernel(offsets, blocks_held, columns, my_ref, index_ref, arrived_ref, shift_ref, resident_hbm, *refs):
    parts = refs[:-12]
    near_hbm, far_hbm, pivots_ref, leading_ref, tail_ref, resident_ref, terms_ref, lead_ref = refs[-12:-4]
    near_ref, far_ref, sem, sems = refs[-4:]
    fetch = pltpu.make_async_copy(resident_hbm, resident_ref, sem)
    fetch.start()
    my_index = my_ref[0]
    size = len(offsets)
    position = 0
    packed = blocks_held * PANEL // 2
    part_rows = PANEL // 2
    for part in parts:
        for number in range(part.shape[0]):
            owner = my_index ^ offsets[position]
            for start in range(0, blocks_held * PANEL, part_rows):
                held, inner = divmod(start, PANEL)
                if start < packed:
                    rows = part[number, start : start + part_rows, :PANEL]
                else:
                    rows = part[number, start - packed : start - packed + part_rows, PANEL:]
                target = pl.multiple_of((held * size + owner) * PANEL + inner, part_rows)
                leading_ref[pl.ds(target, part_rows), :] = rows
            position += 1
    upper, inverse, pivots = eliminate(leading_ref[:PANEL, :], shift_ref[...])
    pivots_ref[...] = pivots
    lower = jnp.transpose(upper)
    needed = tail_ref.shape[1]
    tail = exact(inverse, leading_ref[:needed, :], ((1,), (1,)))
    high, low = split(tail, 2)
    tail_ref[0:PANEL, :] = high
    tail_ref[PANEL : 2 * PANEL, :] = high
    tail_ref[2 * PANEL : 3 * PANEL, :] = low
    tail_ref[3 * PANEL :, :] = low

    block = A_BLOCK
    packed_terms(arrived_ref[...], terms_ref, 0)
    for start in range(0, lead_ref.shape[0], block):
        picks = one_hot(index_ref[:, start : start + block], lead_ref.shape[0])
        got = jnp.dot(picks, terms_ref[...], preferred_element_type=F32)
        lead_ref[start : start + block, :] = whole_sum(got)[:, :PANEL]
    fetch.wait()
    stores = []
    for number, start in enumerate(range(0, lead_ref.shape[0], block)):
        rows_here = slice(start, start + block)
        panel = exact(lead_ref[rows_here, :], inverse, ((1,), (1,))) / pivots
        shown = used = panel
        if start == 0:
            row_ids = lax.broadcasted_iota(jnp.int32, panel.shape, 0)
            top = jnp.logical_and(my_index == 0, row_ids < PANEL)
            used = jnp.where(top, 0.0, panel)
            filled = jnp.concatenate([lower, jnp.zeros((block - PANEL, PANEL), F32)], axis=0)
            shown = jnp.where(top, filled, panel)
        high, low = (term.astype(F32) for term in split(used, 2))
        pair = jnp.concatenate([high, low], axis=1).astype(BF16)
        factors = jnp.concatenate([pair, pair], axis=1)
        update = jnp.dot(factors, tail_ref[...], preferred_element_type=F32)
        shown = jnp.concatenate([shown, jnp.zeros_like(shown)], axis=1)
        near_ref[rows_here, :LANES] = jnp.where(lane_ids(shown.shape) < PANEL, shown, -update[:, :LANES])
        near_ref[rows_here, LANES:] = -update[:, LANES:columns]
        far_ref[rows_here, :] = (resident_ref[rows_here, :].astype(F32) - update[:, columns:]).astype(BF16)
        for which, (source, target) in enumerate(((near_ref, near_hbm), (far_ref, far_hbm))):
            store = pltpu.make_async_copy(
                source.at[pl.ds(start, block), :], target.at[pl.ds(start, block), :], sems.at[which, number]
            )
            store.start()
            stores.append(store)
    for store in stores:
        store.wait()


def updates(my_index, parts, offsets, index, arrived, shift, resident, blocks_held, columns):
    rows, width = resident.shape
    needed = columns + width
    held_rows = len(offsets) * blocks_held * PANEL
    vmem = pl.BlockSpec(memory_space=pltpu.VMEM)
    anywhere = pl.BlockSpec(memory_space=pltpu.HBM)
    return pl.pallas_call(
        functools.partial(update_kernel, offsets, blocks_held, columns),
        in_specs=[pl.BlockSpec(memory_space=pltpu.SMEM), vmem, vmem, vmem, anywhere] + [vmem] * len(parts),
        out_specs=[anywhere, anywhere, vmem],
        out_shape=[
            pltpu.HBM((rows, columns), F32),
            pltpu.HBM((rows, width), BF16),
            jax.ShapeDtypeStruct((1, PANEL), F32),
        ],
        scratch_shapes=[
            pltpu.VMEM((held_rows, PANEL), F32),
            pltpu.VMEM((4 * PANEL, needed), BF16),
            pltpu.VMEM((rows, width), BF16),
            pltpu.VMEM((rows, 2 * LANES), BF16),
            pltpu.VMEM((rows, PANEL), F32),
            pltpu.VMEM((rows, columns), F32),
            pltpu.VMEM((rows, width), BF16),
            pltpu.SemaphoreType.DMA,
            pltpu.SemaphoreType.DMA((2, rows // A_BLOCK)),
        ],
        compiler_params=params(32),
        cost_estimate=pl.CostEstimate(
            flops=2 * rows * needed * 4 * PANEL, bytes_accessed=4 * rows * (columns + width), transcendentals=0
        ),
        name="factor_and_update",
    )(my_index, index, arrived, shift, in_hbm(resident), *parts)


def upper_half(words):
    return (words >> 16).astype(F32)


def lower_half(words):
    return ((words << 16) >> 16).astype(F32)


def loose_values(arrived_ref):
    words = arrived_ref[:, LANES:]
    low_lanes = lane_ids(words.shape) < PANEL
    scale = jnp.exp2(((words & 255) - (BIAS + 15)).astype(F32)) * (1 / MARGIN)
    other = swap_halves(scale)
    near = upper_half(words) * scale
    words = arrived_ref[:, :LANES]
    low = upper_half(words) * jnp.where(low_lanes, scale, other)
    return low, lower_half(words) * jnp.where(low_lanes, other, scale), near


def tight_values(arrived_ref, part_rows, values_ref):
    first = tight_split(part_rows)
    second = part_rows - first
    step = part_rows + first
    sources = arrived_ref.shape[0] // step
    pairs = [arrived_ref[i * step + part_rows + second : i * step + part_rows + second + 2, :] for i in range(sources)]
    spare = jnp.zeros((LANES - 2 * sources, LANES), jnp.int32)
    exponents = jnp.concatenate([*pairs, spare], axis=0)
    scales = jnp.exp2(jnp.transpose(exponents.astype(F32)) - 15.0) * (1 / MARGIN)
    scales = scales[PANEL : PANEL + part_rows]
    low_lanes = lane_ids((part_rows, LANES)) < PANEL
    for i in range(sources):
        base = i * step
        here = slice(i * part_rows, (i + 1) * part_rows)
        low_scale = jnp.broadcast_to(scales[:, 2 * i : 2 * i + 1], (part_rows, LANES))
        high_scale = jnp.broadcast_to(scales[:, 2 * i + 1 : 2 * i + 2], (part_rows, LANES))
        words = arrived_ref[base : base + part_rows, :]
        values_ref[0, here, :] = upper_half(words) * low_scale
        values_ref[1, here, :] = lower_half(words) * high_scale
        words = arrived_ref[base + part_rows : base + step, :]
        words = jnp.concatenate([words, swap_halves(words[:second])], axis=0)
        words = jnp.where(low_lanes, words, swap_halves(words))
        values_ref[2, here, :] = jnp.where(low_lanes, upper_half(words) * low_scale, lower_half(words) * high_scale)
    return values_ref[0], values_ref[1], values_ref[2]


def formed_kernel(
    part_rows, index_ref, arrived_ref, near_hbm, out_hbm, near_ref, terms_ref, out_ref, values_ref, in_sems, out_sems
):
    half = terms_ref.shape[0] // 2
    first = tight_split(part_rows)
    block = A_BLOCK
    starts = range(0, near_ref.shape[0], block)

    def rows_of(ref, start):
        return ref.at[pl.ds(start, block), :]

    fetches = [
        pltpu.make_async_copy(rows_of(near_hbm, start), rows_of(near_ref, start), in_sems.at[i])
        for i, start in enumerate(starts)
    ]
    for fetch in fetches:
        fetch.start()
    low, high, near = loose_values(arrived_ref) if not first else tight_values(arrived_ref, part_rows, values_ref)
    for side, values in enumerate((low, high)):
        one, two = split(values, 2)
        terms_ref[side * half : (side + 1) * half, :LANES] = one
        terms_ref[side * half : (side + 1) * half, LANES : 2 * LANES] = two
    low_lanes = lane_ids(near.shape) < PANEL
    one, two = (term.astype(F32) for term in split(near, 2))
    terms_ref[:half, 2 * LANES :] = jnp.where(low_lanes, one, swap_halves(two)).astype(BF16)
    terms_ref[half:, 2 * LANES :] = jnp.where(low_lanes, swap_halves(one), two).astype(BF16)

    stores = []
    for i, start in enumerate(starts):
        rows_here = slice(start, start + block)
        picks = one_hot(index_ref[:, rows_here], terms_ref.shape[0])
        got = jnp.dot(picks, terms_ref[...], preferred_element_type=F32)
        pair = got[:, 2 * LANES :]
        fetches[i].wait()
        held = near_ref[rows_here, :LANES]
        out_ref[rows_here, :LANES] = jnp.where(
            lane_ids(held.shape) < PANEL, held, (pair + swap_halves(pair)) + held
        )
        out_ref[rows_here, LANES:] = (got[:, :LANES] + got[:, LANES : 2 * LANES]) + near_ref[rows_here, LANES:]
        store = pltpu.make_async_copy(rows_of(out_ref, start), rows_of(out_hbm, start), out_sems.at[i])
        store.start()
        stores.append(store)
    for store in stores:
        store.wait()


def formed_columns(index, arrived, near, part_rows):
    rows, columns = near.shape
    vmem = pl.BlockSpec(memory_space=pltpu.VMEM)
    anywhere = pl.BlockSpec(memory_space=pltpu.HBM)
    return pl.pallas_call(
        functools.partial(formed_kernel, part_rows),
        in_specs=[vmem, vmem, anywhere],
        out_specs=anywhere,
        out_shape=pltpu.HBM((rows, columns), F32),
        input_output_aliases={2: 0},
        scratch_shapes=[
            pltpu.VMEM((rows, columns), F32),
            pltpu.VMEM((rows, 3 * LANES), BF16),
            pltpu.VMEM((rows, columns), F32),
            pltpu.VMEM((3, rows // 2, LANES), F32),
            pltpu.SemaphoreType.DMA((rows // A_BLOCK,)),
            pltpu.SemaphoreType.DMA((rows // A_BLOCK,)),
        ],
        compiler_params=params(32),
        cost_estimate=pl.CostEstimate(
            flops=8 * rows * rows * LANES, bytes_accessed=8 * rows * columns, transcendentals=0
        ),
        name="formed_columns",
    )(index, arrived, near)


def swap_rows(x, group):
    rows, width = x.shape
    return lax.all_to_all(
        x.reshape(group, rows // group, width), "wide", split_axis=0, concat_axis=0, tiled=True
    ).reshape(rows, width)


def on_device(a_rows, xa_panel, za_panel, send_order, recv_order, shift, resident):
    rows = a_rows.shape[0]
    columns = xa_panel.shape[1]
    group = lax.axis_size("wide")
    my_index = lax.axis_index("wide").astype(jnp.int32).reshape(1)
    share = rows // group
    half = rows // 2
    few, apart = phases_of(group)

    order, packing = send_order, share
    if share % 16:
        order = send_order.reshape(group, 2, share // 2).transpose(1, 0, 2).reshape(1, rows)
        packing = 0
    source, slot = recv_order // share, recv_order % share
    index = (slot // (share // 2)) * half + source * (share // 2) + slot % (share // 2)

    lead_panel, rest_panel = split_panels(my_index, xa_panel, za_panel)
    send_picks, a_copy = order_picks(order, a_rows, packing)
    lead_parts = [lead_panel]
    for masks in few:
        lead_parts = exchange(join(lead_parts), masks, "wide")
    rest_parts = tied([rest_panel], send_picks)
    for number, masks in enumerate(apart[:-2]):
        rest_parts = exchange(join(rest_parts), masks, "wide")
        if number == 0:
            lead_parts = tied(lead_parts, *rest_parts)

    lead_out = lead_products(my_index, a_copy, send_picks, lead_parts, offsets_of(few))
    lead_in = swap_rows(tied([lead_out], *rest_parts)[0], group)
    rest_parts = exchange(join(tied(rest_parts, lead_out)), apart[-2], "wide")
    other_parts = exchange(rest_parts[:1], apart[-1], "wide")[1:]

    needed = columns + resident.shape[1]
    blocks_held = -(-needed // (PANEL * group))
    leading_parts = [leading_rows(index, lead_in, blocks_held * PANEL)]
    for masks in few:
        leading_parts = exchange(join(leading_parts), masks, "wide")
        if masks is few[0]:
            later_parts = exchange(tied(rest_parts[1:], *leading_parts), apart[-1], "wide")
    late = len(later_parts) // 2
    rest_parts = rest_parts + other_parts + later_parts[late:]
    rest_out = rest_products(
        my_index, order, a_rows, rest_parts, offsets_of(apart), packing, share // 2
    )
    rest_in = swap_rows(tied([rest_out], *leading_parts)[0], group)
    near, updated, pivots = updates(
        my_index,
        leading_parts,
        offsets_of(few),
        index,
        tied([lead_in], rest_out)[0],
        shift[None, :],
        resident,
        blocks_held,
        columns,
    )
    factored = formed_columns(index, rest_in, near, share // 2)
    return (factored, updated, pivots[0])


def solution(mesh):
    placed = (
        P(("parts", "wide"), None),
        P(("parts", "wide"), None),
        P(("parts", "wide"), None),
        P(("parts", "wide"), None),
        P(("parts", "wide"), None),
        P("parts"),
        P(("parts", "wide"), None),
    )
    return jax.shard_map(
        on_device,
        mesh=mesh,
        in_specs=placed,
        out_specs=(P(("parts", "wide"), None), P(("parts", "wide"), None), P("parts")),
        check_vma=False,
    )
```

```python
import functools

import jax
import jax.numpy as jnp
from jax import lax
from jax.experimental import pallas as pl
from jax.experimental.pallas import tpu as pltpu
from jax.sharding import PartitionSpec as P

PANEL = 64
LANES = 128
A_BLOCK = 640
DEEP_BLOCK = 256
F32 = jnp.float32
BF16 = jnp.bfloat16
MIB = 1024 * 1024


def params(mebibytes=12):
    return pltpu.CompilerParams(vmem_limit_bytes=mebibytes * MIB)


def in_hbm(x):
    return pltpu.with_memory_space_constraint(x, pltpu.HBM)


def lane_ids(shape):
    return lax.broadcasted_iota(jnp.int32, shape, len(shape) - 1)


def split(x, count):
    terms = []
    for _ in range(count):
        term = x.astype(BF16)
        terms.append(term)
        x = x - term.astype(F32)
    return terms


def swap_halves(x):
    return pltpu.roll(x, LANES // 2, 1)


def as_column(index_row):
    return jnp.transpose(jnp.broadcast_to(index_row, (LANES, LANES)))


def picks_of(at, width):
    lanes = lane_ids(at.shape)
    return jnp.concatenate(
        [(at == lanes + column).astype(F32).astype(BF16) for column in range(0, width, LANES)], axis=1
    )


def fill_picks(at_ref, picks_ref):
    rows, width = picks_ref.shape
    for start in range(0, rows, LANES):
        picks_ref[start : start + LANES, :] = picks_of(at_ref[start : start + LANES, :], width)


def one_hot(index_row, width):
    chunks = [
        picks_of(as_column(index_row[:, start : start + LANES]), width)
        for start in range(0, index_row.shape[1], LANES)
    ]
    return jnp.concatenate(chunks, axis=0) if len(chunks) > 1 else chunks[0]


def packed_order(share, half, slot):
    part = share // 2
    return (slot % share) // part * half + slot // share * part + slot % part


def fill_order(order_ref, at_ref, share):
    rows = order_ref.shape[1]
    height = 8
    for start in range(0, rows, LANES):
        column = as_column(order_ref[:, start : start + LANES])
        if not share:
            at_ref[start : start + LANES, :] = column
            continue
        for inner in range(0, LANES, height):
            place = packed_order(share, rows // 2, start + inner)
            at_ref[place : place + height, :] = column[inner : inner + height]


def exchange(held, masks, axis):
    size = lax.axis_size(axis)
    combined = [0]
    for mask in masks:
        combined += [other ^ mask for other in combined]
    parts = list(held)
    for mask in combined[1:]:
        parts += [lax.ppermute(part, axis, [(i, i ^ mask) for i in range(size)]) for part in held]
    return parts


def offsets_of(phases):
    offsets = [0]
    for masks in phases:
        combined = [0]
        for mask in masks:
            combined += [other ^ mask for other in combined]
        offsets = [offset ^ mask for mask in combined for offset in offsets]
    return offsets


def join(parts):
    return [jnp.concatenate(parts, axis=0)]


def phases_of(size):
    bits = [1 << bit for bit in reversed(range(size.bit_length() - 1))]
    return [bits[start : start + 2] for start in range(0, len(bits), 2)], [[bit] for bit in bits]


def tied(parts, *earlier):
    return list(lax.optimization_barrier((*parts, *earlier))[: len(parts)])


def picks_kernel(share, order_hbm, a_hbm, picks_ref, copy_ref, order_ref, at_ref, sems):
    fetch = pltpu.make_async_copy(order_hbm, order_ref, sems.at[0])
    copy = pltpu.make_async_copy(a_hbm, copy_ref, sems.at[1])
    fetch.start()
    copy.start()
    fetch.wait()
    fill_order(order_ref, at_ref, share)
    fill_picks(at_ref, picks_ref)
    copy.wait()


def order_picks(order, a_rows, share):
    rows, depth = a_rows.shape
    return pl.pallas_call(
        functools.partial(picks_kernel, share),
        in_specs=[pl.BlockSpec(memory_space=pltpu.HBM)] * 2,
        out_specs=[pl.BlockSpec(memory_space=pltpu.VMEM)] * 2,
        out_shape=[jax.ShapeDtypeStruct((rows, rows), BF16), jax.ShapeDtypeStruct((rows, depth), BF16)],
        scratch_shapes=[
            pltpu.VMEM((1, rows), jnp.int32),
            pltpu.VMEM((rows, LANES), jnp.int32),
            pltpu.SemaphoreType.DMA((2,)),
        ],
        compiler_params=params(),
        cost_estimate=pl.CostEstimate(flops=4 * rows * rows, bytes_accessed=4 * rows * depth, transcendentals=0),
        name="order_picks",
    )(in_hbm(order), in_hbm(a_rows))


def panels_kernel(my_ref, xa_hbm, za_hbm, lead_ref, rest_ref, xa_ref, za_ref, sems):
    copies = [
        pltpu.make_async_copy(xa_hbm, xa_ref, sems.at[0]),
        pltpu.make_async_copy(za_hbm, za_ref, sems.at[1]),
    ]
    for copy in copies:
        copy.start()
    for copy in copies:
        copy.wait()
    lead_ref[0] = jnp.concatenate([xa_ref[:, :PANEL], za_ref[:, :PANEL]], axis=1)
    rest_ref[0, :, :LANES] = jnp.concatenate([xa_ref[:, PANEL:LANES], za_ref[:, PANEL:LANES]], axis=1)
    rest_ref[0, :, LANES : 2 * LANES] = xa_ref[:, LANES:]
    rest_ref[0, :, 2 * LANES :] = za_ref[:, LANES:]


def split_panels(my_index, xa_panel, za_panel):
    depth, columns = xa_panel.shape
    return pl.pallas_call(
        panels_kernel,
        in_specs=[pl.BlockSpec(memory_space=pltpu.SMEM)] + [pl.BlockSpec(memory_space=pltpu.HBM)] * 2,
        out_shape=[
            jax.ShapeDtypeStruct((1, depth, LANES), BF16),
            jax.ShapeDtypeStruct((1, depth, 2 * columns - LANES), BF16),
        ],
        scratch_shapes=[
            pltpu.VMEM((depth, columns), BF16),
            pltpu.VMEM((depth, columns), BF16),
            pltpu.SemaphoreType.DMA((2,)),
        ],
        compiler_params=params(),
        name="split_panels",
    )(my_index, in_hbm(xa_panel), in_hbm(za_panel))


def assemble(my_index, offsets, parts, panel_ref):
    position = 0
    for part in parts:
        for number in range(part.shape[0]):
            depth = part.shape[1]
            start = pl.multiple_of((my_index ^ offsets[position]) * depth, depth)
            panel_ref[pl.ds(start, depth), :] = part[number]
            position += 1


def whole_sum(got):
    pair = got[:, :LANES]
    return (pair + swap_halves(pair)) + got[:, LANES:]


def store_rows(source, target, start, size, sem):
    rows = pl.ds(start, size)
    copy = pltpu.make_async_copy(source.at[rows, :], target.at[rows, :], sem)
    copy.start()
    return copy


def lead_product_kernel(offsets, my_ref, a_ref, picks_ref, *refs):
    parts, (out_hbm, panel_ref, terms_ref, out_ref, sems) = refs[:-5], refs[-5:]
    assemble(my_ref[0], offsets, parts, panel_ref)
    rows = a_ref.shape[0]
    for start in range(0, rows, DEEP_BLOCK):
        both = jnp.dot(a_ref[start : start + DEEP_BLOCK, :], panel_ref[...], preferred_element_type=F32)
        first, second, third = (term.astype(F32) for term in split(both * swap_halves(both), 3))
        near = lane_ids(both.shape) < PANEL
        terms_ref[start : start + DEEP_BLOCK, :LANES] = jnp.where(near, first, second).astype(BF16)
        terms_ref[start : start + DEEP_BLOCK, LANES:] = third.astype(BF16)
    half = rows // 2
    block = half // 2
    stores = []
    for number, start in enumerate(range(0, half, block)):
        low = jnp.dot(picks_ref[start : start + block, :], terms_ref[...], preferred_element_type=F32)
        high = jnp.dot(picks_ref[half + start : half + start + block, :], terms_ref[...], preferred_element_type=F32)
        low, high = whole_sum(low), whole_sum(high)
        out_ref[start : start + block, :] = jnp.where(lane_ids(low.shape) < PANEL, low, high)
        stores.append(store_rows(out_ref, out_hbm, start, block, sems.at[number]))
    for store in stores:
        store.wait()


def lead_products(my_index, a_rows, picks, parts, offsets):
    rows, depth = a_rows.shape
    return pl.pallas_call(
        functools.partial(lead_product_kernel, offsets),
        in_specs=[pl.BlockSpec(memory_space=pltpu.SMEM)] + [pl.BlockSpec(memory_space=pltpu.VMEM)] * (2 + len(parts)),
        out_specs=pl.BlockSpec(memory_space=pltpu.HBM),
        out_shape=pltpu.HBM((rows // 2, LANES), F32),
        scratch_shapes=[
            pltpu.VMEM((depth, LANES), BF16),
            pltpu.VMEM((rows, 2 * LANES), BF16),
            pltpu.VMEM((rows // 2, LANES), F32),
            pltpu.SemaphoreType.DMA((2,)),
        ],
        compiler_params=params(24),
        cost_estimate=pl.CostEstimate(
            flops=2 * rows * (depth + 2 * rows) * LANES, bytes_accessed=2 * rows * depth, transcendentals=0
        ),
        name="lead_products",
    )(my_index, a_rows, picks, *parts)


BIAS = 128
MARGIN = 0.9995
ROUNDER = 1.5 * 2.0**23


def tight_split(part):
    first = -(-part // 16) * 8
    return first if part % 8 == 0 and part <= PANEL and 2 * first - part >= 8 else 0


def words_shape(half, part):
    first = tight_split(part)
    return (half // part * (part + first), LANES) if first else (half, 2 * LANES)


def nearest(x):
    return (x + ROUNDER) - ROUNDER


def rest_product_kernel(offsets, share, part_rows, my_ref, order_ref, a_hbm, *refs):
    parts, (out_ref, a_ref, at_ref, picks_ref, panel_ref, terms_ref, sems) = refs[:-7], refs[-7:]
    rows = a_ref.shape[0]
    half = rows // 2
    block = DEEP_BLOCK
    starts = range(0, rows, block)
    copies = [
        pltpu.make_async_copy(a_hbm.at[pl.ds(start, block), :], a_ref.at[pl.ds(start, block), :], sems.at[i])
        for i, start in enumerate(starts)
    ]
    for copy in copies[:3]:
        copy.start()
    assemble(my_ref[0], offsets, parts, panel_ref)
    fill_order(order_ref, at_ref, share)
    fill_picks(at_ref, picks_ref)

    def product(i):
        copies[i].wait()
        if i + 3 < len(copies):
            copies[i + 3].start()
        return jnp.dot(a_ref[starts[i] : starts[i] + block, :], panel_ref[...], preferred_element_type=F32)

    low_lanes = lane_ids((block, LANES)) < PANEL
    later = product(0)
    for i, start in enumerate(starts):
        both = later
        if i + 1 < len(starts):
            later = product(i + 1)
        near = both[:, :LANES]
        near = near * swap_halves(near)
        far = both[:, LANES : 2 * LANES] * both[:, 2 * LANES :]
        largest = jnp.max(jnp.maximum(jnp.abs(near), jnp.abs(far)), axis=1, keepdims=True)
        exponent = jnp.floor(jnp.log2(jnp.maximum(largest, 1e-30))) + 1.0
        scale = jnp.exp2(15.0 - exponent) * MARGIN
        far = nearest(far * scale)
        near = nearest(near * scale)
        far_top = nearest(far * (1 / 256))
        near_top = nearest(near * (1 / 256))
        here = slice(start, start + block)
        terms_ref[here, :LANES] = far_top.astype(BF16)
        terms_ref[here, LANES : 2 * LANES] = (far - far_top * 256.0).astype(BF16)
        terms_ref[here, 2 * LANES : 3 * LANES] = jnp.where(low_lanes, near_top, near - near_top * 256.0).astype(BF16)
        terms_ref[here, 3 * LANES :] = jnp.broadcast_to(exponent, (block, LANES)).astype(BF16)

    def coded(start, size):
        got = jnp.dot(picks_ref[start : start + size, :], terms_ref[...], preferred_element_type=F32)
        far = got[:, :LANES] * 256.0 + got[:, LANES : 2 * LANES]
        pair = got[:, 2 * LANES : 3 * LANES]
        pair = jnp.where(lane_ids(pair.shape) < PANEL, pair * 256.0, pair)
        near = (pair + swap_halves(pair)).astype(jnp.int32)
        return far.astype(jnp.int32), near, got[:, 3 * LANES :]

    block = half // 2
    first = tight_split(part_rows)
    low_lanes = lane_ids((8, LANES)) < PANEL
    eights = lax.broadcasted_iota(jnp.int32, (8, LANES), 0)
    places = lax.broadcasted_iota(jnp.int32, (part_rows, LANES), 0) + PANEL
    for start in range(0, half, block):
        far_low, near_low, exponent_low = coded(start, block)
        far_high, near_high, exponent_high = coded(half + start, block)
        far = far_low * 65536 + (far_high & 65535)
        if not first:
            near = jnp.where(
                lane_ids(near_low.shape) < PANEL,
                near_low * 65536 + (exponent_low.astype(jnp.int32) + BIAS),
                near_high * 65536 + (exponent_high.astype(jnp.int32) + BIAS),
            )
            out_ref[start : start + block, :LANES] = far
            out_ref[start : start + block, LANES:] = near
            continue
        near = near_low * 65536 + (near_high & 65535)
        second = part_rows - first
        mine = lane_ids((part_rows, LANES)) == places
        for inner in range(0, block, part_rows):
            base = (start + inner) // part_rows * (part_rows + first)
            words = near[inner : inner + part_rows]
            rows = [
                jnp.sum(jnp.where(mine, exponent[inner : inner + part_rows], 0.0), axis=0, keepdims=True)
                for exponent in (exponent_low, exponent_high)
            ]
            rows = jnp.where(eights == 0, rows[0], jnp.where(eights == 1, rows[1], 0.0)).astype(jnp.int32)
            out_ref[base : base + part_rows, :] = far[inner : inner + part_rows]
            base += part_rows
            spare = [words[: first - second - 8]] if first > second + 8 else []
            both = jnp.concatenate([words[first:], rows, *spare], axis=0)
            out_ref[base : base + first, :] = jnp.where(lane_ids(both.shape) < PANEL, words[:first], both)


def rest_products(my_index, order, a_rows, parts, offsets, share, part_rows):
    rows, depth = a_rows.shape
    return pl.pallas_call(
        functools.partial(rest_product_kernel, offsets, share, part_rows),
        in_specs=[
            pl.BlockSpec(memory_space=pltpu.SMEM),
            pl.BlockSpec(memory_space=pltpu.VMEM),
            pl.BlockSpec(memory_space=pltpu.HBM),
        ]
        + [pl.BlockSpec(memory_space=pltpu.VMEM)] * len(parts),
        out_specs=pl.BlockSpec(memory_space=pltpu.VMEM),
        out_shape=jax.ShapeDtypeStruct(words_shape(rows // 2, part_rows), jnp.int32),
        scratch_shapes=[
            pltpu.VMEM((rows, depth), BF16),
            pltpu.VMEM((rows, LANES), jnp.int32),
            pltpu.VMEM((rows, rows), BF16),
            pltpu.VMEM((depth, 3 * LANES), BF16),
            pltpu.VMEM((rows, 4 * LANES), BF16),
            pltpu.SemaphoreType.DMA((rows // DEEP_BLOCK,)),
        ],
        compiler_params=params(32),
        cost_estimate=pl.CostEstimate(
            flops=2 * rows * (3 * depth + 4 * rows) * LANES, bytes_accessed=2 * rows * depth, transcendentals=0
        ),
        name="rest_products",
    )(my_index, order, in_hbm(a_rows), *parts)


def packed_terms(x, terms_ref, start):
    half = x.shape[0]
    first, second, third = (term.astype(F32) for term in split(x, 3))
    near = lane_ids(x.shape) < PANEL
    other = swap_halves(third)
    terms_ref[:half, start : start + LANES] = jnp.where(near, first, swap_halves(second)).astype(BF16)
    terms_ref[half:, start : start + LANES] = jnp.where(near, swap_halves(first), second).astype(BF16)
    terms_ref[:half, start + LANES : start + 2 * LANES] = jnp.where(near, third, other).astype(BF16)
    terms_ref[half:, start + LANES : start + 2 * LANES] = jnp.where(near, other, third).astype(BF16)


def leading_kernel(held, index_ref, arrived_ref, out_ref, terms_ref):
    packed_terms(arrived_ref[...], terms_ref, 0)
    width = -(-held // LANES) * LANES
    picks = one_hot(index_ref[:, :width], terms_ref.shape[0])
    got = whole_sum(jnp.dot(picks, terms_ref[...], preferred_element_type=F32))
    first, second = got[: held // 2], got[held // 2 : held]
    out_ref[0] = jnp.where(lane_ids(first.shape) < PANEL, first, second)


def leading_rows(index, arrived, held):
    rows = index.shape[1]
    return pl.pallas_call(
        functools.partial(leading_kernel, held),
        in_specs=[pl.BlockSpec(memory_space=pltpu.VMEM)] * 2,
        out_specs=pl.BlockSpec(memory_space=pltpu.VMEM),
        out_shape=jax.ShapeDtypeStruct((1, held // 2, LANES), F32),
        scratch_shapes=[pltpu.VMEM((rows, 2 * LANES), BF16)],
        compiler_params=params(),
        cost_estimate=pl.CostEstimate(
            flops=4 * held * rows * LANES, bytes_accessed=2 * rows * LANES, transcendentals=0
        ),
        name="leading_rows",
    )(index, arrived)


def eliminate(block, shift_row):
    rows = lax.broadcasted_iota(jnp.int32, (PANEL, PANEL), 0)
    columns = lax.broadcasted_iota(jnp.int32, (PANEL, PANEL), 1)
    flipped = jnp.transpose(block)
    mirrored = jnp.where(rows >= columns, block, flipped)
    diagonal = shift_row + jnp.sum(jnp.abs(mirrored), axis=0, keepdims=True)
    unit = (rows == columns).astype(F32)
    work = jnp.where(rows == columns, diagonal, mirrored)
    work = jnp.concatenate([work, unit], axis=1)
    height = 8
    groups = [work[start : start + height] for start in range(0, PANEL, height)]
    sublanes = lax.broadcasted_iota(jnp.int32, (height, LANES), 0)
    scaled_rows = []
    for k in range(PANEL):
        home, offset = divmod(k, height)
        row = groups[home][offset : offset + 1, :]
        row = row / row[:, k : k + 1]
        scaled_rows.append(row)
        for g in range(home, PANEL // height):
            column = jnp.broadcast_to(groups[g][:, k : k + 1], (height, LANES))
            if g == home:
                column = jnp.where(sublanes > offset, column, 0.0)
            groups[g] = groups[g] - column * row
    final = jnp.concatenate(groups, axis=0)
    scaled = jnp.concatenate(scaled_rows, axis=0)
    upper = jnp.where(columns >= rows, scaled[:, :PANEL], 0.0)
    pivots = jnp.sum(jnp.where(rows == columns, final[:, :PANEL], 0.0), axis=0, keepdims=True)
    return upper, final[:, PANEL:], pivots


def exact(lhs, rhs, dims):
    return lax.dot_general(lhs, rhs, (dims, ((), ())), precision=lax.Precision.HIGHEST, preferred_element_type=F32)


def update_kernel(offsets, blocks_held, columns, my_ref, index_ref, arrived_ref, shift_ref, resident_hbm, *refs):
    parts = refs[:-12]
    near_hbm, far_hbm, pivots_ref, leading_ref, tail_ref, resident_ref, terms_ref, lead_ref = refs[-12:-4]
    near_ref, far_ref, sem, sems = refs[-4:]
    fetch = pltpu.make_async_copy(resident_hbm, resident_ref, sem)
    fetch.start()
    my_index = my_ref[0]
    size = len(offsets)
    position = 0
    packed = blocks_held * PANEL // 2
    part_rows = PANEL // 2
    for part in parts:
        for number in range(part.shape[0]):
            owner = my_index ^ offsets[position]
            for start in range(0, blocks_held * PANEL, part_rows):
                held, inner = divmod(start, PANEL)
                if start < packed:
                    rows = part[number, start : start + part_rows, :PANEL]
                else:
                    rows = part[number, start - packed : start - packed + part_rows, PANEL:]
                target = pl.multiple_of((held * size + owner) * PANEL + inner, part_rows)
                leading_ref[pl.ds(target, part_rows), :] = rows
            position += 1
    upper, inverse, pivots = eliminate(leading_ref[:PANEL, :], shift_ref[...])
    pivots_ref[...] = pivots
    lower = jnp.transpose(upper)
    needed = tail_ref.shape[1]
    tail = exact(inverse, leading_ref[:needed, :], ((1,), (1,)))
    high, low = split(tail, 2)
    tail_ref[0:PANEL, :] = high
    tail_ref[PANEL : 2 * PANEL, :] = high
    tail_ref[2 * PANEL : 3 * PANEL, :] = low
    tail_ref[3 * PANEL :, :] = low

    block = A_BLOCK
    packed_terms(arrived_ref[...], terms_ref, 0)
    for start in range(0, lead_ref.shape[0], block):
        picks = one_hot(index_ref[:, start : start + block], lead_ref.shape[0])
        got = jnp.dot(picks, terms_ref[...], preferred_element_type=F32)
        lead_ref[start : start + block, :] = whole_sum(got)[:, :PANEL]
    fetch.wait()
    stores = []
    for number, start in enumerate(range(0, lead_ref.shape[0], block)):
        rows_here = slice(start, start + block)
        panel = exact(lead_ref[rows_here, :], inverse, ((1,), (1,))) / pivots
        shown = used = panel
        if start == 0:
            row_ids = lax.broadcasted_iota(jnp.int32, panel.shape, 0)
            top = jnp.logical_and(my_index == 0, row_ids < PANEL)
            used = jnp.where(top, 0.0, panel)
            filled = jnp.concatenate([lower, jnp.zeros((block - PANEL, PANEL), F32)], axis=0)
            shown = jnp.where(top, filled, panel)
        high, low = (term.astype(F32) for term in split(used, 2))
        pair = jnp.concatenate([high, low], axis=1).astype(BF16)
        factors = jnp.concatenate([pair, pair], axis=1)
        update = jnp.dot(factors, tail_ref[...], preferred_element_type=F32)
        shown = jnp.concatenate([shown, jnp.zeros_like(shown)], axis=1)
        near_ref[rows_here, :LANES] = jnp.where(lane_ids(shown.shape) < PANEL, shown, -update[:, :LANES])
        near_ref[rows_here, LANES:] = -update[:, LANES:columns]
        far_ref[rows_here, :] = (resident_ref[rows_here, :].astype(F32) - update[:, columns:]).astype(BF16)
        for which, (source, target) in enumerate(((near_ref, near_hbm), (far_ref, far_hbm))):
            store = pltpu.make_async_copy(
                source.at[pl.ds(start, block), :], target.at[pl.ds(start, block), :], sems.at[which, number]
            )
            store.start()
            stores.append(store)
    for store in stores:
        store.wait()


def updates(my_index, parts, offsets, index, arrived, shift, resident, blocks_held, columns):
    rows, width = resident.shape
    needed = columns + width
    held_rows = len(offsets) * blocks_held * PANEL
    vmem = pl.BlockSpec(memory_space=pltpu.VMEM)
    anywhere = pl.BlockSpec(memory_space=pltpu.HBM)
    return pl.pallas_call(
        functools.partial(update_kernel, offsets, blocks_held, columns),
        in_specs=[pl.BlockSpec(memory_space=pltpu.SMEM), vmem, vmem, vmem, anywhere] + [vmem] * len(parts),
        out_specs=[anywhere, anywhere, vmem],
        out_shape=[
            pltpu.HBM((rows, columns), F32),
            pltpu.HBM((rows, width), BF16),
            jax.ShapeDtypeStruct((1, PANEL), F32),
        ],
        scratch_shapes=[
            pltpu.VMEM((held_rows, PANEL), F32),
            pltpu.VMEM((4 * PANEL, needed), BF16),
            pltpu.VMEM((rows, width), BF16),
            pltpu.VMEM((rows, 2 * LANES), BF16),
            pltpu.VMEM((rows, PANEL), F32),
            pltpu.VMEM((rows, columns), F32),
            pltpu.VMEM((rows, width), BF16),
            pltpu.SemaphoreType.DMA,
            pltpu.SemaphoreType.DMA((2, rows // A_BLOCK)),
        ],
        compiler_params=params(32),
        cost_estimate=pl.CostEstimate(
            flops=2 * rows * needed * 4 * PANEL, bytes_accessed=4 * rows * (columns + width), transcendentals=0
        ),
        name="factor_and_update",
    )(my_index, index, arrived, shift, in_hbm(resident), *parts)


def upper_half(words):
    return (words >> 16).astype(F32)


def lower_half(words):
    return ((words << 16) >> 16).astype(F32)


def loose_values(arrived_ref):
    words = arrived_ref[:, LANES:]
    low_lanes = lane_ids(words.shape) < PANEL
    scale = jnp.exp2(((words & 255) - (BIAS + 15)).astype(F32)) * (1 / MARGIN)
    other = swap_halves(scale)
    near = upper_half(words) * scale
    words = arrived_ref[:, :LANES]
    low = upper_half(words) * jnp.where(low_lanes, scale, other)
    return low, lower_half(words) * jnp.where(low_lanes, other, scale), near


def tight_values(arrived_ref, part_rows, values_ref):
    first = tight_split(part_rows)
    second = part_rows - first
    step = part_rows + first
    sources = arrived_ref.shape[0] // step
    pairs = [arrived_ref[i * step + part_rows + second : i * step + part_rows + second + 2, :] for i in range(sources)]
    spare = jnp.zeros((LANES - 2 * sources, LANES), jnp.int32)
    exponents = jnp.concatenate([*pairs, spare], axis=0)
    scales = jnp.exp2(jnp.transpose(exponents.astype(F32)) - 15.0) * (1 / MARGIN)
    scales = scales[PANEL : PANEL + part_rows]
    low_lanes = lane_ids((part_rows, LANES)) < PANEL
    for i in range(sources):
        base = i * step
        here = slice(i * part_rows, (i + 1) * part_rows)
        low_scale = jnp.broadcast_to(scales[:, 2 * i : 2 * i + 1], (part_rows, LANES))
        high_scale = jnp.broadcast_to(scales[:, 2 * i + 1 : 2 * i + 2], (part_rows, LANES))
        words = arrived_ref[base : base + part_rows, :]
        values_ref[0, here, :] = upper_half(words) * low_scale
        values_ref[1, here, :] = lower_half(words) * high_scale
        words = arrived_ref[base + part_rows : base + step, :]
        words = jnp.concatenate([words, swap_halves(words[:second])], axis=0)
        words = jnp.where(low_lanes, words, swap_halves(words))
        values_ref[2, here, :] = jnp.where(low_lanes, upper_half(words) * low_scale, lower_half(words) * high_scale)
    return values_ref[0], values_ref[1], values_ref[2]


def formed_kernel(
    part_rows, index_ref, arrived_ref, near_hbm, out_hbm, near_ref, terms_ref, out_ref, values_ref, in_sems, out_sems
):
    half = terms_ref.shape[0] // 2
    first = tight_split(part_rows)
    block = A_BLOCK
    starts = range(0, near_ref.shape[0], block)

    def rows_of(ref, start):
        return ref.at[pl.ds(start, block), :]

    fetches = [
        pltpu.make_async_copy(rows_of(near_hbm, start), rows_of(near_ref, start), in_sems.at[i])
        for i, start in enumerate(starts)
    ]
    for fetch in fetches:
        fetch.start()
    low, high, near = loose_values(arrived_ref) if not first else tight_values(arrived_ref, part_rows, values_ref)
    for side, values in enumerate((low, high)):
        one, two = split(values, 2)
        terms_ref[side * half : (side + 1) * half, :LANES] = one
        terms_ref[side * half : (side + 1) * half, LANES : 2 * LANES] = two
    low_lanes = lane_ids(near.shape) < PANEL
    one, two = (term.astype(F32) for term in split(near, 2))
    terms_ref[:half, 2 * LANES :] = jnp.where(low_lanes, one, swap_halves(two)).astype(BF16)
    terms_ref[half:, 2 * LANES :] = jnp.where(low_lanes, swap_halves(one), two).astype(BF16)

    stores = []
    for i, start in enumerate(starts):
        rows_here = slice(start, start + block)
        picks = one_hot(index_ref[:, rows_here], terms_ref.shape[0])
        got = jnp.dot(picks, terms_ref[...], preferred_element_type=F32)
        pair = got[:, 2 * LANES :]
        fetches[i].wait()
        held = near_ref[rows_here, :LANES]
        out_ref[rows_here, :LANES] = jnp.where(
            lane_ids(held.shape) < PANEL, held, (pair + swap_halves(pair)) + held
        )
        out_ref[rows_here, LANES:] = (got[:, :LANES] + got[:, LANES : 2 * LANES]) + near_ref[rows_here, LANES:]
        store = pltpu.make_async_copy(rows_of(out_ref, start), rows_of(out_hbm, start), out_sems.at[i])
        store.start()
        stores.append(store)
    for store in stores:
        store.wait()


def formed_columns(index, arrived, near, part_rows):
    rows, columns = near.shape
    vmem = pl.BlockSpec(memory_space=pltpu.VMEM)
    anywhere = pl.BlockSpec(memory_space=pltpu.HBM)
    return pl.pallas_call(
        functools.partial(formed_kernel, part_rows),
        in_specs=[vmem, vmem, anywhere],
        out_specs=anywhere,
        out_shape=pltpu.HBM((rows, columns), F32),
        input_output_aliases={2: 0},
        scratch_shapes=[
            pltpu.VMEM((rows, columns), F32),
            pltpu.VMEM((rows, 3 * LANES), BF16),
            pltpu.VMEM((rows, columns), F32),
            pltpu.VMEM((3, rows // 2, LANES), F32),
            pltpu.SemaphoreType.DMA((rows // A_BLOCK,)),
            pltpu.SemaphoreType.DMA((rows // A_BLOCK,)),
        ],
        compiler_params=params(32),
        cost_estimate=pl.CostEstimate(
            flops=8 * rows * rows * LANES, bytes_accessed=8 * rows * columns, transcendentals=0
        ),
        name="formed_columns",
    )(index, arrived, near)


def swap_rows(x, group):
    rows, width = x.shape
    return lax.all_to_all(
        x.reshape(group, rows // group, width), "wide", split_axis=0, concat_axis=0, tiled=True
    ).reshape(rows, width)


def on_device(a_rows, xa_panel, za_panel, send_order, recv_order, shift, resident):
    rows = a_rows.shape[0]
    columns = xa_panel.shape[1]
    group = lax.axis_size("wide")
    my_index = lax.axis_index("wide").astype(jnp.int32).reshape(1)
    share = rows // group
    half = rows // 2
    few, apart = phases_of(group)

    order, packing = send_order, share
    if share % 16:
        order = send_order.reshape(group, 2, share // 2).transpose(1, 0, 2).reshape(1, rows)
        packing = 0
    source, slot = recv_order // share, recv_order % share
    index = (slot // (share // 2)) * half + source * (share // 2) + slot % (share // 2)

    lead_panel, rest_panel = split_panels(my_index, xa_panel, za_panel)
    send_picks, a_copy = order_picks(order, a_rows, packing)
    steps = few[:-1] + [[mask] for mask in few[-1]]
    lead_parts = [lead_panel]
    for masks in steps:
        lead_parts = exchange(join(lead_parts), masks, "wide")
    rest_parts = tied([rest_panel], send_picks)
    for number, masks in enumerate(apart[:-2]):
        rest_parts = exchange(join(rest_parts), masks, "wide")
        if number == 0:
            lead_parts = tied(lead_parts, *rest_parts)

    lead_out = lead_products(my_index, a_copy, send_picks, lead_parts, offsets_of(steps))
    lead_in = swap_rows(tied([lead_out], *rest_parts)[0], group)
    rest_parts = exchange(join(tied(rest_parts, lead_out)), apart[-2], "wide")
    other_parts = exchange(rest_parts[:1], apart[-1], "wide")[1:]

    needed = columns + resident.shape[1]
    blocks_held = -(-needed // (PANEL * group))
    leading_parts = [leading_rows(index, lead_in, blocks_held * PANEL)]
    for masks in few:
        leading_parts = exchange(join(leading_parts), masks, "wide")
        if masks is few[0]:
            later_parts = exchange(tied(rest_parts[1:], *leading_parts), apart[-1], "wide")
    late = len(later_parts) // 2
    rest_parts = rest_parts + other_parts + later_parts[late:]
    rest_out = rest_products(
        my_index, order, a_rows, rest_parts, offsets_of(apart), packing, share // 2
    )
    rest_in = swap_rows(tied([rest_out], *leading_parts)[0], group)
    near, updated, pivots = updates(
        my_index,
        leading_parts,
        offsets_of(few),
        index,
        tied([lead_in], rest_out)[0],
        shift[None, :],
        resident,
        blocks_held,
        columns,
    )
    factored = formed_columns(index, rest_in, near, share // 2)
    return (factored, updated, pivots[0])


def solution(mesh):
    placed = (
        P(("parts", "wide"), None),
        P(("parts", "wide"), None),
        P(("parts", "wide"), None),
        P(("parts", "wide"), None),
        P(("parts", "wide"), None),
        P("parts"),
        P(("parts", "wide"), None),
    )
    return jax.shard_map(
        on_device,
        mesh=mesh,
        in_specs=placed,
        out_specs=(P(("parts", "wide"), None), P(("parts", "wide"), None), P("parts")),
        check_vma=False,
    )
```

```python
import functools

import jax
import jax.numpy as jnp
from jax import lax
from jax.experimental import pallas as pl
from jax.experimental.pallas import tpu as pltpu
from jax.sharding import PartitionSpec as P

PANEL = 64
LANES = 128
A_BLOCK = 640
DEEP_BLOCK = 256
F32 = jnp.float32
BF16 = jnp.bfloat16
MIB = 1024 * 1024


def params(mebibytes=12):
    return pltpu.CompilerParams(vmem_limit_bytes=mebibytes * MIB)


def in_hbm(x):
    return pltpu.with_memory_space_constraint(x, pltpu.HBM)


def lane_ids(shape):
    return lax.broadcasted_iota(jnp.int32, shape, len(shape) - 1)


def split(x, count):
    terms = []
    for _ in range(count):
        term = x.astype(BF16)
        terms.append(term)
        x = x - term.astype(F32)
    return terms


def swap_halves(x):
    return pltpu.roll(x, LANES // 2, 1)


def as_column(index_row):
    return jnp.transpose(jnp.broadcast_to(index_row, (LANES, LANES)))


def picks_of(at, width):
    lanes = lane_ids(at.shape)
    return jnp.concatenate(
        [(at == lanes + column).astype(F32).astype(BF16) for column in range(0, width, LANES)], axis=1
    )


def fill_picks(at_ref, picks_ref):
    rows, width = picks_ref.shape
    for start in range(0, rows, LANES):
        picks_ref[start : start + LANES, :] = picks_of(at_ref[start : start + LANES, :], width)


def one_hot(index_row, width):
    chunks = [
        picks_of(as_column(index_row[:, start : start + LANES]), width)
        for start in range(0, index_row.shape[1], LANES)
    ]
    return jnp.concatenate(chunks, axis=0) if len(chunks) > 1 else chunks[0]


def packed_order(share, half, slot):
    part = share // 2
    return (slot % share) // part * half + slot // share * part + slot % part


def fill_order(order_ref, at_ref, share):
    rows = order_ref.shape[1]
    height = 8
    for start in range(0, rows, LANES):
        column = as_column(order_ref[:, start : start + LANES])
        if not share:
            at_ref[start : start + LANES, :] = column
            continue
        for inner in range(0, LANES, height):
            place = packed_order(share, rows // 2, start + inner)
            at_ref[place : place + height, :] = column[inner : inner + height]


def exchange(held, masks, axis):
    size = lax.axis_size(axis)
    combined = [0]
    for mask in masks:
        combined += [other ^ mask for other in combined]
    parts = list(held)
    for mask in combined[1:]:
        parts += [lax.ppermute(part, axis, [(i, i ^ mask) for i in range(size)]) for part in held]
    return parts


def offsets_of(phases):
    offsets = [0]
    for masks in phases:
        combined = [0]
        for mask in masks:
            combined += [other ^ mask for other in combined]
        offsets = [offset ^ mask for mask in combined for offset in offsets]
    return offsets


def join(parts):
    return [jnp.concatenate(parts, axis=0)]


def phases_of(size):
    bits = [1 << bit for bit in reversed(range(size.bit_length() - 1))]
    return [bits[start : start + 2] for start in range(0, len(bits), 2)], [[bit] for bit in bits]


def tied(parts, *earlier):
    return list(lax.optimization_barrier((*parts, *earlier))[: len(parts)])


def picks_kernel(share, order_hbm, a_hbm, picks_ref, copy_ref, order_ref, at_ref, sems):
    fetch = pltpu.make_async_copy(order_hbm, order_ref, sems.at[0])
    copy = pltpu.make_async_copy(a_hbm, copy_ref, sems.at[1])
    fetch.start()
    copy.start()
    fetch.wait()
    fill_order(order_ref, at_ref, share)
    fill_picks(at_ref, picks_ref)
    copy.wait()


def order_picks(order, a_rows, share):
    rows, depth = a_rows.shape
    return pl.pallas_call(
        functools.partial(picks_kernel, share),
        in_specs=[pl.BlockSpec(memory_space=pltpu.HBM)] * 2,
        out_specs=[pl.BlockSpec(memory_space=pltpu.VMEM)] * 2,
        out_shape=[jax.ShapeDtypeStruct((rows, rows), BF16), jax.ShapeDtypeStruct((rows, depth), BF16)],
        scratch_shapes=[
            pltpu.VMEM((1, rows), jnp.int32),
            pltpu.VMEM((rows, LANES), jnp.int32),
            pltpu.SemaphoreType.DMA((2,)),
        ],
        compiler_params=params(),
        cost_estimate=pl.CostEstimate(flops=4 * rows * rows, bytes_accessed=4 * rows * depth, transcendentals=0),
        name="order_picks",
    )(in_hbm(order), in_hbm(a_rows))


def panels_kernel(my_ref, xa_hbm, za_hbm, lead_ref, rest_ref, xa_ref, za_ref, sems):
    copies = [
        pltpu.make_async_copy(xa_hbm, xa_ref, sems.at[0]),
        pltpu.make_async_copy(za_hbm, za_ref, sems.at[1]),
    ]
    for copy in copies:
        copy.start()
    for copy in copies:
        copy.wait()
    lead_ref[0] = jnp.concatenate([xa_ref[:, :PANEL], za_ref[:, :PANEL]], axis=1)
    rest_ref[0, :, :LANES] = jnp.concatenate([xa_ref[:, PANEL:LANES], za_ref[:, PANEL:LANES]], axis=1)
    rest_ref[0, :, LANES : 2 * LANES] = xa_ref[:, LANES:]
    rest_ref[0, :, 2 * LANES :] = za_ref[:, LANES:]


def split_panels(my_index, xa_panel, za_panel):
    depth, columns = xa_panel.shape
    return pl.pallas_call(
        panels_kernel,
        in_specs=[pl.BlockSpec(memory_space=pltpu.SMEM)] + [pl.BlockSpec(memory_space=pltpu.HBM)] * 2,
        out_shape=[
            jax.ShapeDtypeStruct((1, depth, LANES), BF16),
            jax.ShapeDtypeStruct((1, depth, 2 * columns - LANES), BF16),
        ],
        scratch_shapes=[
            pltpu.VMEM((depth, columns), BF16),
            pltpu.VMEM((depth, columns), BF16),
            pltpu.SemaphoreType.DMA((2,)),
        ],
        compiler_params=params(),
        name="split_panels",
    )(my_index, in_hbm(xa_panel), in_hbm(za_panel))


def assemble(my_index, offsets, parts, panel_ref):
    position = 0
    for part in parts:
        for number in range(part.shape[0]):
            depth = part.shape[1]
            start = pl.multiple_of((my_index ^ offsets[position]) * depth, depth)
            panel_ref[pl.ds(start, depth), :] = part[number]
            position += 1


def whole_sum(got):
    pair = got[:, :LANES]
    return (pair + swap_halves(pair)) + got[:, LANES:]


def store_rows(source, target, start, size, sem):
    rows = pl.ds(start, size)
    copy = pltpu.make_async_copy(source.at[rows, :], target.at[rows, :], sem)
    copy.start()
    return copy


def lead_product_kernel(offsets, my_ref, a_ref, picks_ref, *refs):
    parts, (out_hbm, panel_ref, terms_ref, out_ref, sems) = refs[:-5], refs[-5:]
    assemble(my_ref[0], offsets, parts, panel_ref)
    rows = a_ref.shape[0]
    for start in range(0, rows, DEEP_BLOCK):
        both = jnp.dot(a_ref[start : start + DEEP_BLOCK, :], panel_ref[...], preferred_element_type=F32)
        first, second, third = (term.astype(F32) for term in split(both * swap_halves(both), 3))
        near = lane_ids(both.shape) < PANEL
        terms_ref[start : start + DEEP_BLOCK, :LANES] = jnp.where(near, first, second).astype(BF16)
        terms_ref[start : start + DEEP_BLOCK, LANES:] = third.astype(BF16)
    half = rows // 2
    block = half // 2
    stores = []
    for number, start in enumerate(range(0, half, block)):
        low = jnp.dot(picks_ref[start : start + block, :], terms_ref[...], preferred_element_type=F32)
        high = jnp.dot(picks_ref[half + start : half + start + block, :], terms_ref[...], preferred_element_type=F32)
        low, high = whole_sum(low), whole_sum(high)
        out_ref[start : start + block, :] = jnp.where(lane_ids(low.shape) < PANEL, low, high)
        stores.append(store_rows(out_ref, out_hbm, start, block, sems.at[number]))
    for store in stores:
        store.wait()


def lead_products(my_index, a_rows, picks, parts, offsets):
    rows, depth = a_rows.shape
    return pl.pallas_call(
        functools.partial(lead_product_kernel, offsets),
        in_specs=[pl.BlockSpec(memory_space=pltpu.SMEM)] + [pl.BlockSpec(memory_space=pltpu.VMEM)] * (2 + len(parts)),
        out_specs=pl.BlockSpec(memory_space=pltpu.HBM),
        out_shape=pltpu.HBM((rows // 2, LANES), F32),
        scratch_shapes=[
            pltpu.VMEM((depth, LANES), BF16),
            pltpu.VMEM((rows, 2 * LANES), BF16),
            pltpu.VMEM((rows // 2, LANES), F32),
            pltpu.SemaphoreType.DMA((2,)),
        ],
        compiler_params=params(24),
        cost_estimate=pl.CostEstimate(
            flops=2 * rows * (depth + 2 * rows) * LANES, bytes_accessed=2 * rows * depth, transcendentals=0
        ),
        name="lead_products",
    )(my_index, a_rows, picks, *parts)


BIAS = 128
MARGIN = 0.9995
ROUNDER = 1.5 * 2.0**23


def tight_split(part):
    first = -(-part // 16) * 8
    return first if part % 8 == 0 and part <= PANEL and 2 * first - part >= 8 else 0


def words_shape(half, part):
    first = tight_split(part)
    return (half // part * (part + first), LANES) if first else (half, 2 * LANES)


def nearest(x):
    return (x + ROUNDER) - ROUNDER


def rest_product_kernel(offsets, share, part_rows, my_ref, order_ref, a_hbm, *refs):
    parts, (out_hbm, a_ref, at_ref, picks_ref, panel_ref, terms_ref, out_ref, sems, out_sems) = refs[:-9], refs[-9:]
    rows = a_ref.shape[0]
    half = rows // 2
    block = DEEP_BLOCK
    starts = range(0, rows, block)
    copies = [
        pltpu.make_async_copy(a_hbm.at[pl.ds(start, block), :], a_ref.at[pl.ds(start, block), :], sems.at[i])
        for i, start in enumerate(starts)
    ]
    copies[0].start()
    assemble(my_ref[0], offsets, parts, panel_ref)
    for copy in copies[1:3]:
        copy.start()
    fill_order(order_ref, at_ref, share)

    def product(i):
        copies[i].wait()
        if i + 3 < len(copies):
            copies[i + 3].start()
        return jnp.dot(a_ref[starts[i] : starts[i] + block, :], panel_ref[...], preferred_element_type=F32)

    low_lanes = lane_ids((block, LANES)) < PANEL
    later = product(0)
    for i, start in enumerate(starts):
        both = later
        if i + 1 < len(starts):
            later = product(i + 1)
        picks_ref[start : start + block, :] = picks_of(at_ref[start : start + block, :], rows)
        near = both[:, :LANES]
        near = near * swap_halves(near)
        far = both[:, LANES : 2 * LANES] * both[:, 2 * LANES :]
        largest = jnp.max(jnp.maximum(jnp.abs(near), jnp.abs(far)), axis=1, keepdims=True)
        exponent = jnp.floor(jnp.log2(jnp.maximum(largest, 1e-30))) + 1.0
        scale = jnp.exp2(15.0 - exponent) * MARGIN
        far = nearest(far * scale)
        near = nearest(near * scale)
        far_top = nearest(far * (1 / 256))
        near_top = nearest(near * (1 / 256))
        here = slice(start, start + block)
        terms_ref[here, :LANES] = far_top.astype(BF16)
        terms_ref[here, LANES : 2 * LANES] = (far - far_top * 256.0).astype(BF16)
        terms_ref[here, 2 * LANES : 3 * LANES] = jnp.where(low_lanes, near_top, near - near_top * 256.0).astype(BF16)
        terms_ref[here, 3 * LANES :] = jnp.broadcast_to(exponent, (block, LANES)).astype(BF16)

    def coded(start, size):
        got = jnp.dot(picks_ref[start : start + size, :], terms_ref[...], preferred_element_type=F32)
        far = got[:, :LANES] * 256.0 + got[:, LANES : 2 * LANES]
        pair = got[:, 2 * LANES : 3 * LANES]
        pair = jnp.where(lane_ids(pair.shape) < PANEL, pair * 256.0, pair)
        near = (pair + swap_halves(pair)).astype(jnp.int32)
        return far.astype(jnp.int32), near, got[:, 3 * LANES :]

    block = half // 2
    first = tight_split(part_rows)
    low_lanes = lane_ids((8, LANES)) < PANEL
    eights = lax.broadcasted_iota(jnp.int32, (8, LANES), 0)
    places = lax.broadcasted_iota(jnp.int32, (part_rows, LANES), 0) + PANEL
    stores = []
    for number, start in enumerate(range(0, half, block)):
        far_low, near_low, exponent_low = coded(start, block)
        far_high, near_high, exponent_high = coded(half + start, block)
        far = far_low * 65536 + (far_high & 65535)
        if not first:
            near = jnp.where(
                lane_ids(near_low.shape) < PANEL,
                near_low * 65536 + (exponent_low.astype(jnp.int32) + BIAS),
                near_high * 65536 + (exponent_high.astype(jnp.int32) + BIAS),
            )
            out_ref[start : start + block, :LANES] = far
            out_ref[start : start + block, LANES:] = near
            stores.append(store_rows(out_ref, out_hbm, start, block, out_sems.at[number]))
            continue
        near = near_low * 65536 + (near_high & 65535)
        second = part_rows - first
        mine = lane_ids((part_rows, LANES)) == places
        for inner in range(0, block, part_rows):
            base = (start + inner) // part_rows * (part_rows + first)
            words = near[inner : inner + part_rows]
            rows = [
                jnp.sum(jnp.where(mine, exponent[inner : inner + part_rows], 0.0), axis=0, keepdims=True)
                for exponent in (exponent_low, exponent_high)
            ]
            rows = jnp.where(eights == 0, rows[0], jnp.where(eights == 1, rows[1], 0.0)).astype(jnp.int32)
            out_ref[base : base + part_rows, :] = far[inner : inner + part_rows]
            base += part_rows
            spare = [words[: first - second - 8]] if first > second + 8 else []
            both = jnp.concatenate([words[first:], rows, *spare], axis=0)
            out_ref[base : base + first, :] = jnp.where(lane_ids(both.shape) < PANEL, words[:first], both)
        size = block // part_rows * (part_rows + first)
        stores.append(store_rows(out_ref, out_hbm, number * size, size, out_sems.at[number]))
    for store in stores:
        store.wait()


def rest_products(my_index, order, a_rows, parts, offsets, share, part_rows):
    rows, depth = a_rows.shape
    shape = words_shape(rows // 2, part_rows)
    return pl.pallas_call(
        functools.partial(rest_product_kernel, offsets, share, part_rows),
        in_specs=[
            pl.BlockSpec(memory_space=pltpu.SMEM),
            pl.BlockSpec(memory_space=pltpu.VMEM),
            pl.BlockSpec(memory_space=pltpu.HBM),
        ]
        + [pl.BlockSpec(memory_space=pltpu.VMEM)] * len(parts),
        out_specs=pl.BlockSpec(memory_space=pltpu.HBM),
        out_shape=pltpu.HBM(shape, jnp.int32),
        scratch_shapes=[
            pltpu.VMEM((rows, depth), BF16),
            pltpu.VMEM((rows, LANES), jnp.int32),
            pltpu.VMEM((rows, rows), BF16),
            pltpu.VMEM((depth, 3 * LANES), BF16),
            pltpu.VMEM((rows, 4 * LANES), BF16),
            pltpu.VMEM(shape, jnp.int32),
            pltpu.SemaphoreType.DMA((rows // DEEP_BLOCK,)),
            pltpu.SemaphoreType.DMA((2,)),
        ],
        compiler_params=params(32),
        cost_estimate=pl.CostEstimate(
            flops=2 * rows * (3 * depth + 4 * rows) * LANES, bytes_accessed=2 * rows * depth, transcendentals=0
        ),
        name="rest_products",
    )(my_index, order, in_hbm(a_rows), *parts)


def packed_terms(x, terms_ref, start):
    half = x.shape[0]
    first, second, third = (term.astype(F32) for term in split(x, 3))
    near = lane_ids(x.shape) < PANEL
    other = swap_halves(third)
    terms_ref[:half, start : start + LANES] = jnp.where(near, first, swap_halves(second)).astype(BF16)
    terms_ref[half:, start : start + LANES] = jnp.where(near, swap_halves(first), second).astype(BF16)
    terms_ref[:half, start + LANES : start + 2 * LANES] = jnp.where(near, third, other).astype(BF16)
    terms_ref[half:, start + LANES : start + 2 * LANES] = jnp.where(near, other, third).astype(BF16)


def leading_kernel(held, index_ref, arrived_ref, out_ref, terms_ref):
    packed_terms(arrived_ref[...], terms_ref, 0)
    width = -(-held // LANES) * LANES
    picks = one_hot(index_ref[:, :width], terms_ref.shape[0])
    got = whole_sum(jnp.dot(picks, terms_ref[...], preferred_element_type=F32))
    first, second = got[: held // 2], got[held // 2 : held]
    out_ref[0] = jnp.where(lane_ids(first.shape) < PANEL, first, second)


def leading_rows(index, arrived, held):
    rows = index.shape[1]
    return pl.pallas_call(
        functools.partial(leading_kernel, held),
        in_specs=[pl.BlockSpec(memory_space=pltpu.VMEM)] * 2,
        out_specs=pl.BlockSpec(memory_space=pltpu.VMEM),
        out_shape=jax.ShapeDtypeStruct((1, held // 2, LANES), F32),
        scratch_shapes=[pltpu.VMEM((rows, 2 * LANES), BF16)],
        compiler_params=params(),
        cost_estimate=pl.CostEstimate(
            flops=4 * held * rows * LANES, bytes_accessed=2 * rows * LANES, transcendentals=0
        ),
        name="leading_rows",
    )(index, arrived)


def eliminate(block, shift_row):
    rows = lax.broadcasted_iota(jnp.int32, (PANEL, PANEL), 0)
    columns = lax.broadcasted_iota(jnp.int32, (PANEL, PANEL), 1)
    flipped = jnp.transpose(block)
    mirrored = jnp.where(rows >= columns, block, flipped)
    diagonal = shift_row + jnp.sum(jnp.abs(mirrored), axis=0, keepdims=True)
    unit = (rows == columns).astype(F32)
    work = jnp.where(rows == columns, diagonal, mirrored)
    work = jnp.concatenate([work, unit], axis=1)
    height = 8
    groups = [work[start : start + height] for start in range(0, PANEL, height)]
    sublanes = lax.broadcasted_iota(jnp.int32, (height, LANES), 0)
    scaled_rows = []
    for k in range(PANEL):
        home, offset = divmod(k, height)
        row = groups[home][offset : offset + 1, :]
        row = row / row[:, k : k + 1]
        scaled_rows.append(row)
        for g in range(home, PANEL // height):
            column = jnp.broadcast_to(groups[g][:, k : k + 1], (height, LANES))
            if g == home:
                column = jnp.where(sublanes > offset, column, 0.0)
            groups[g] = groups[g] - column * row
    final = jnp.concatenate(groups, axis=0)
    scaled = jnp.concatenate(scaled_rows, axis=0)
    upper = jnp.where(columns >= rows, scaled[:, :PANEL], 0.0)
    pivots = jnp.sum(jnp.where(rows == columns, final[:, :PANEL], 0.0), axis=0, keepdims=True)
    return upper, final[:, PANEL:], pivots


def exact(lhs, rhs, dims):
    return lax.dot_general(lhs, rhs, (dims, ((), ())), precision=lax.Precision.HIGHEST, preferred_element_type=F32)


def update_kernel(offsets, blocks_held, columns, my_ref, index_ref, arrived_ref, shift_ref, resident_hbm, *refs):
    parts = refs[:-12]
    near_hbm, far_hbm, pivots_ref, leading_ref, tail_ref, resident_ref, terms_ref, lead_ref = refs[-12:-4]
    near_ref, far_ref, sem, sems = refs[-4:]
    fetch = pltpu.make_async_copy(resident_hbm, resident_ref, sem)
    fetch.start()
    my_index = my_ref[0]
    size = len(offsets)
    position = 0
    packed = blocks_held * PANEL // 2
    part_rows = PANEL // 2
    for part in parts:
        for number in range(part.shape[0]):
            owner = my_index ^ offsets[position]
            for start in range(0, blocks_held * PANEL, part_rows):
                held, inner = divmod(start, PANEL)
                if start < packed:
                    rows = part[number, start : start + part_rows, :PANEL]
                else:
                    rows = part[number, start - packed : start - packed + part_rows, PANEL:]
                target = pl.multiple_of((held * size + owner) * PANEL + inner, part_rows)
                leading_ref[pl.ds(target, part_rows), :] = rows
            position += 1
    upper, inverse, pivots = eliminate(leading_ref[:PANEL, :], shift_ref[...])
    pivots_ref[...] = pivots
    lower = jnp.transpose(upper)
    needed = tail_ref.shape[1]
    tail = exact(inverse, leading_ref[:needed, :], ((1,), (1,)))
    high, low = split(tail, 2)
    tail_ref[0:PANEL, :] = high
    tail_ref[PANEL : 2 * PANEL, :] = high
    tail_ref[2 * PANEL : 3 * PANEL, :] = low
    tail_ref[3 * PANEL :, :] = low

    block = A_BLOCK
    packed_terms(arrived_ref[...], terms_ref, 0)
    for start in range(0, lead_ref.shape[0], block):
        picks = one_hot(index_ref[:, start : start + block], lead_ref.shape[0])
        got = jnp.dot(picks, terms_ref[...], preferred_element_type=F32)
        lead_ref[start : start + block, :] = whole_sum(got)[:, :PANEL]
    fetch.wait()
    stores = []
    for number, start in enumerate(range(0, lead_ref.shape[0], block)):
        rows_here = slice(start, start + block)
        panel = exact(lead_ref[rows_here, :], inverse, ((1,), (1,))) / pivots
        shown = used = panel
        if start == 0:
            row_ids = lax.broadcasted_iota(jnp.int32, panel.shape, 0)
            top = jnp.logical_and(my_index == 0, row_ids < PANEL)
            used = jnp.where(top, 0.0, panel)
            filled = jnp.concatenate([lower, jnp.zeros((block - PANEL, PANEL), F32)], axis=0)
            shown = jnp.where(top, filled, panel)
        high, low = (term.astype(F32) for term in split(used, 2))
        pair = jnp.concatenate([high, low], axis=1).astype(BF16)
        factors = jnp.concatenate([pair, pair], axis=1)
        update = jnp.dot(factors, tail_ref[...], preferred_element_type=F32)
        shown = jnp.concatenate([shown, jnp.zeros_like(shown)], axis=1)
        near_ref[rows_here, :LANES] = jnp.where(lane_ids(shown.shape) < PANEL, shown, -update[:, :LANES])
        near_ref[rows_here, LANES:] = -update[:, LANES:columns]
        far_ref[rows_here, :] = (resident_ref[rows_here, :].astype(F32) - update[:, columns:]).astype(BF16)
        for which, (source, target) in enumerate(((near_ref, near_hbm), (far_ref, far_hbm))):
            store = pltpu.make_async_copy(
                source.at[pl.ds(start, block), :], target.at[pl.ds(start, block), :], sems.at[which, number]
            )
            store.start()
            stores.append(store)
    for store in stores:
        store.wait()


def updates(my_index, parts, offsets, index, arrived, shift, resident, blocks_held, columns):
    rows, width = resident.shape
    needed = columns + width
    held_rows = len(offsets) * blocks_held * PANEL
    vmem = pl.BlockSpec(memory_space=pltpu.VMEM)
    anywhere = pl.BlockSpec(memory_space=pltpu.HBM)
    return pl.pallas_call(
        functools.partial(update_kernel, offsets, blocks_held, columns),
        in_specs=[pl.BlockSpec(memory_space=pltpu.SMEM), vmem, vmem, vmem, anywhere] + [vmem] * len(parts),
        out_specs=[anywhere, anywhere, vmem],
        out_shape=[
            pltpu.HBM((rows, columns), F32),
            pltpu.HBM((rows, width), BF16),
            jax.ShapeDtypeStruct((1, PANEL), F32),
        ],
        scratch_shapes=[
            pltpu.VMEM((held_rows, PANEL), F32),
            pltpu.VMEM((4 * PANEL, needed), BF16),
            pltpu.VMEM((rows, width), BF16),
            pltpu.VMEM((rows, 2 * LANES), BF16),
            pltpu.VMEM((rows, PANEL), F32),
            pltpu.VMEM((rows, columns), F32),
            pltpu.VMEM((rows, width), BF16),
            pltpu.SemaphoreType.DMA,
            pltpu.SemaphoreType.DMA((2, rows // A_BLOCK)),
        ],
        compiler_params=params(32),
        cost_estimate=pl.CostEstimate(
            flops=2 * rows * needed * 4 * PANEL, bytes_accessed=4 * rows * (columns + width), transcendentals=0
        ),
        name="factor_and_update",
    )(my_index, index, arrived, shift, in_hbm(resident), *parts)


def upper_half(words):
    return (words >> 16).astype(F32)


def lower_half(words):
    return ((words << 16) >> 16).astype(F32)


def loose_values(arrived_ref):
    words = arrived_ref[:, LANES:]
    low_lanes = lane_ids(words.shape) < PANEL
    scale = jnp.exp2(((words & 255) - (BIAS + 15)).astype(F32)) * (1 / MARGIN)
    other = swap_halves(scale)
    near = upper_half(words) * scale
    words = arrived_ref[:, :LANES]
    low = upper_half(words) * jnp.where(low_lanes, scale, other)
    return low, lower_half(words) * jnp.where(low_lanes, other, scale), near


def tight_values(arrived_ref, part_rows, values_ref):
    first = tight_split(part_rows)
    second = part_rows - first
    step = part_rows + first
    sources = arrived_ref.shape[0] // step
    pairs = [arrived_ref[i * step + part_rows + second : i * step + part_rows + second + 2, :] for i in range(sources)]
    spare = jnp.zeros((LANES - 2 * sources, LANES), jnp.int32)
    exponents = jnp.concatenate([*pairs, spare], axis=0)
    scales = jnp.exp2(jnp.transpose(exponents.astype(F32)) - 15.0) * (1 / MARGIN)
    scales = scales[PANEL : PANEL + part_rows]
    low_lanes = lane_ids((part_rows, LANES)) < PANEL
    for i in range(sources):
        base = i * step
        here = slice(i * part_rows, (i + 1) * part_rows)
        low_scale = jnp.broadcast_to(scales[:, 2 * i : 2 * i + 1], (part_rows, LANES))
        high_scale = jnp.broadcast_to(scales[:, 2 * i + 1 : 2 * i + 2], (part_rows, LANES))
        words = arrived_ref[base : base + part_rows, :]
        values_ref[0, here, :] = upper_half(words) * low_scale
        values_ref[1, here, :] = lower_half(words) * high_scale
        words = arrived_ref[base + part_rows : base + step, :]
        words = jnp.concatenate([words, swap_halves(words[:second])], axis=0)
        words = jnp.where(low_lanes, words, swap_halves(words))
        values_ref[2, here, :] = jnp.where(low_lanes, upper_half(words) * low_scale, lower_half(words) * high_scale)
    return values_ref[0], values_ref[1], values_ref[2]


def formed_kernel(
    part_rows, index_ref, arrived_ref, near_hbm, out_hbm, near_ref, terms_ref, out_ref, values_ref, in_sems, out_sems
):
    half = terms_ref.shape[0] // 2
    first = tight_split(part_rows)
    block = A_BLOCK
    starts = range(0, near_ref.shape[0], block)

    def rows_of(ref, start):
        return ref.at[pl.ds(start, block), :]

    fetches = [
        pltpu.make_async_copy(rows_of(near_hbm, start), rows_of(near_ref, start), in_sems.at[i])
        for i, start in enumerate(starts)
    ]
    for fetch in fetches:
        fetch.start()
    low, high, near = loose_values(arrived_ref) if not first else tight_values(arrived_ref, part_rows, values_ref)
    for side, values in enumerate((low, high)):
        one, two = split(values, 2)
        terms_ref[side * half : (side + 1) * half, :LANES] = one
        terms_ref[side * half : (side + 1) * half, LANES : 2 * LANES] = two
    low_lanes = lane_ids(near.shape) < PANEL
    one, two = (term.astype(F32) for term in split(near, 2))
    terms_ref[:half, 2 * LANES :] = jnp.where(low_lanes, one, swap_halves(two)).astype(BF16)
    terms_ref[half:, 2 * LANES :] = jnp.where(low_lanes, swap_halves(one), two).astype(BF16)

    stores = []
    for i, start in enumerate(starts):
        rows_here = slice(start, start + block)
        picks = one_hot(index_ref[:, rows_here], terms_ref.shape[0])
        got = jnp.dot(picks, terms_ref[...], preferred_element_type=F32)
        pair = got[:, 2 * LANES :]
        fetches[i].wait()
        held = near_ref[rows_here, :LANES]
        out_ref[rows_here, :LANES] = jnp.where(
            lane_ids(held.shape) < PANEL, held, (pair + swap_halves(pair)) + held
        )
        out_ref[rows_here, LANES:] = (got[:, :LANES] + got[:, LANES : 2 * LANES]) + near_ref[rows_here, LANES:]
        store = pltpu.make_async_copy(rows_of(out_ref, start), rows_of(out_hbm, start), out_sems.at[i])
        store.start()
        stores.append(store)
    for store in stores:
        store.wait()


def formed_columns(index, arrived, near, part_rows):
    rows, columns = near.shape
    vmem = pl.BlockSpec(memory_space=pltpu.VMEM)
    anywhere = pl.BlockSpec(memory_space=pltpu.HBM)
    return pl.pallas_call(
        functools.partial(formed_kernel, part_rows),
        in_specs=[vmem, vmem, anywhere],
        out_specs=anywhere,
        out_shape=pltpu.HBM((rows, columns), F32),
        input_output_aliases={2: 0},
        scratch_shapes=[
            pltpu.VMEM((rows, columns), F32),
            pltpu.VMEM((rows, 3 * LANES), BF16),
            pltpu.VMEM((rows, columns), F32),
            pltpu.VMEM((3, rows // 2, LANES), F32),
            pltpu.SemaphoreType.DMA((rows // A_BLOCK,)),
            pltpu.SemaphoreType.DMA((rows // A_BLOCK,)),
        ],
        compiler_params=params(32),
        cost_estimate=pl.CostEstimate(
            flops=8 * rows * rows * LANES, bytes_accessed=8 * rows * columns, transcendentals=0
        ),
        name="formed_columns",
    )(index, arrived, near)


def swap_rows(x, group):
    rows, width = x.shape
    return lax.all_to_all(
        x.reshape(group, rows // group, width), "wide", split_axis=0, concat_axis=0, tiled=True
    ).reshape(rows, width)


def on_device(a_rows, xa_panel, za_panel, send_order, recv_order, shift, resident):
    rows = a_rows.shape[0]
    columns = xa_panel.shape[1]
    group = lax.axis_size("wide")
    my_index = lax.axis_index("wide").astype(jnp.int32).reshape(1)
    share = rows // group
    half = rows // 2
    few, apart = phases_of(group)

    order, packing = send_order, share
    if share % 16:
        order = send_order.reshape(group, 2, share // 2).transpose(1, 0, 2).reshape(1, rows)
        packing = 0
    source, slot = recv_order // share, recv_order % share
    index = (slot // (share // 2)) * half + source * (share // 2) + slot % (share // 2)

    lead_panel, rest_panel = split_panels(my_index, xa_panel, za_panel)
    send_picks, a_copy = order_picks(order, a_rows, packing)
    steps = few[:-1] + [[mask] for mask in few[-1]]
    lead_parts = [lead_panel]
    for masks in steps:
        lead_parts = exchange(join(lead_parts), masks, "wide")
    rest_parts = tied([rest_panel], send_picks)
    for number, masks in enumerate(apart[:-2]):
        rest_parts = exchange(join(rest_parts), masks, "wide")
        if number == 0:
            lead_parts = tied(lead_parts, *rest_parts)

    lead_out = lead_products(my_index, a_copy, send_picks, lead_parts, offsets_of(steps))
    lead_in = swap_rows(lead_out, group)
    rest_parts = exchange(join(tied(rest_parts, lead_out)), apart[-2], "wide")
    other_parts = exchange(rest_parts[:1], apart[-1], "wide")[1:]

    needed = columns + resident.shape[1]
    blocks_held = -(-needed // (PANEL * group))
    leading_parts = [leading_rows(index, lead_in, blocks_held * PANEL)]
    for masks in few:
        leading_parts = exchange(join(leading_parts), masks, "wide")
        if masks is few[0]:
            later_parts = exchange(tied(rest_parts[1:], *leading_parts), apart[-1], "wide")
    late = len(later_parts) // 2
    rest_parts = rest_parts + other_parts + later_parts[late:]
    rest_out = rest_products(
        my_index, order, a_rows, rest_parts, offsets_of(apart), packing, share // 2
    )
    rest_in = swap_rows(tied([rest_out], *leading_parts)[0], group)
    near, updated, pivots = updates(
        my_index,
        leading_parts,
        offsets_of(few),
        index,
        tied([lead_in], rest_out)[0],
        shift[None, :],
        resident,
        blocks_held,
        columns,
    )
    factored = formed_columns(index, rest_in, near, share // 2)
    return (factored, updated, pivots[0])


def solution(mesh):
    placed = (
        P(("parts", "wide"), None),
        P(("parts", "wide"), None),
        P(("parts", "wide"), None),
        P(("parts", "wide"), None),
        P(("parts", "wide"), None),
        P("parts"),
        P(("parts", "wide"), None),
    )
    return jax.shard_map(
        on_device,
        mesh=mesh,
        in_specs=placed,
        out_specs=(P(("parts", "wide"), None), P(("parts", "wide"), None), P("parts")),
        check_vma=False,
    )
```

```python
import functools

import jax
import jax.numpy as jnp
from jax import lax
from jax.experimental import pallas as pl
from jax.experimental.pallas import tpu as pltpu
from jax.sharding import PartitionSpec as P

PANEL = 64
LANES = 128
A_BLOCK = 640
DEEP_BLOCK = 256
F32 = jnp.float32
BF16 = jnp.bfloat16
MIB = 1024 * 1024


def params(mebibytes=12):
    return pltpu.CompilerParams(vmem_limit_bytes=mebibytes * MIB)


def in_hbm(x):
    return pltpu.with_memory_space_constraint(x, pltpu.HBM)


def lane_ids(shape):
    return lax.broadcasted_iota(jnp.int32, shape, len(shape) - 1)


def split(x, count):
    terms = []
    for _ in range(count):
        term = x.astype(BF16)
        terms.append(term)
        x = x - term.astype(F32)
    return terms


def swap_halves(x):
    return pltpu.roll(x, LANES // 2, 1)


def as_column(index_row):
    return jnp.transpose(jnp.broadcast_to(index_row, (LANES, LANES)))


def picks_of(at, width):
    lanes = lane_ids(at.shape)
    return jnp.concatenate(
        [(at == lanes + column).astype(F32).astype(BF16) for column in range(0, width, LANES)], axis=1
    )


def fill_picks(at_ref, picks_ref):
    rows, width = picks_ref.shape
    for start in range(0, rows, LANES):
        picks_ref[start : start + LANES, :] = picks_of(at_ref[start : start + LANES, :], width)


def one_hot(index_row, width):
    chunks = [
        picks_of(as_column(index_row[:, start : start + LANES]), width)
        for start in range(0, index_row.shape[1], LANES)
    ]
    return jnp.concatenate(chunks, axis=0) if len(chunks) > 1 else chunks[0]


def packed_order(share, half, slot):
    part = share // 2
    return (slot % share) // part * half + slot // share * part + slot % part


def fill_order(order_ref, at_ref, share):
    rows = order_ref.shape[1]
    height = 8
    for start in range(0, rows, LANES):
        column = as_column(order_ref[:, start : start + LANES])
        if not share:
            at_ref[start : start + LANES, :] = column
            continue
        for inner in range(0, LANES, height):
            place = packed_order(share, rows // 2, start + inner)
            at_ref[place : place + height, :] = column[inner : inner + height]


def exchange(held, masks, axis):
    size = lax.axis_size(axis)
    combined = [0]
    for mask in masks:
        combined += [other ^ mask for other in combined]
    parts = list(held)
    for mask in combined[1:]:
        parts += [lax.ppermute(part, axis, [(i, i ^ mask) for i in range(size)]) for part in held]
    return parts


def offsets_of(phases):
    offsets = [0]
    for masks in phases:
        combined = [0]
        for mask in masks:
            combined += [other ^ mask for other in combined]
        offsets = [offset ^ mask for mask in combined for offset in offsets]
    return offsets


def join(parts):
    return [jnp.concatenate(parts, axis=0)]


def phases_of(size):
    bits = [1 << bit for bit in reversed(range(size.bit_length() - 1))]
    return [bits[start : start + 2] for start in range(0, len(bits), 2)], [[bit] for bit in bits]


def tied(parts, *earlier):
    return list(lax.optimization_barrier((*parts, *earlier))[: len(parts)])


def picks_kernel(share, order_hbm, a_hbm, picks_ref, copy_ref, order_ref, at_ref, sems):
    fetch = pltpu.make_async_copy(order_hbm, order_ref, sems.at[0])
    copy = pltpu.make_async_copy(a_hbm, copy_ref, sems.at[1])
    fetch.start()
    copy.start()
    fetch.wait()
    fill_order(order_ref, at_ref, share)
    fill_picks(at_ref, picks_ref)
    copy.wait()


def order_picks(order, a_rows, share):
    rows, depth = a_rows.shape
    return pl.pallas_call(
        functools.partial(picks_kernel, share),
        in_specs=[pl.BlockSpec(memory_space=pltpu.HBM)] * 2,
        out_specs=[pl.BlockSpec(memory_space=pltpu.VMEM)] * 2,
        out_shape=[jax.ShapeDtypeStruct((rows, rows), BF16), jax.ShapeDtypeStruct((rows, depth), BF16)],
        scratch_shapes=[
            pltpu.VMEM((1, rows), jnp.int32),
            pltpu.VMEM((rows, LANES), jnp.int32),
            pltpu.SemaphoreType.DMA((2,)),
        ],
        compiler_params=params(),
        cost_estimate=pl.CostEstimate(flops=4 * rows * rows, bytes_accessed=4 * rows * depth, transcendentals=0),
        name="order_picks",
    )(in_hbm(order), in_hbm(a_rows))


def panels_kernel(my_ref, xa_hbm, za_hbm, lead_ref, rest_ref, xa_ref, za_ref, sems):
    copies = [
        pltpu.make_async_copy(xa_hbm, xa_ref, sems.at[0]),
        pltpu.make_async_copy(za_hbm, za_ref, sems.at[1]),
    ]
    for copy in copies:
        copy.start()
    for copy in copies:
        copy.wait()
    lead_ref[0] = jnp.concatenate([xa_ref[:, :PANEL], za_ref[:, :PANEL]], axis=1)
    rest_ref[0, :, :LANES] = jnp.concatenate([xa_ref[:, PANEL:LANES], za_ref[:, PANEL:LANES]], axis=1)
    rest_ref[0, :, LANES : 2 * LANES] = xa_ref[:, LANES:]
    rest_ref[0, :, 2 * LANES :] = za_ref[:, LANES:]


def split_panels(my_index, xa_panel, za_panel):
    depth, columns = xa_panel.shape
    return pl.pallas_call(
        panels_kernel,
        in_specs=[pl.BlockSpec(memory_space=pltpu.SMEM)] + [pl.BlockSpec(memory_space=pltpu.HBM)] * 2,
        out_shape=[
            jax.ShapeDtypeStruct((1, depth, LANES), BF16),
            jax.ShapeDtypeStruct((1, depth, 2 * columns - LANES), BF16),
        ],
        scratch_shapes=[
            pltpu.VMEM((depth, columns), BF16),
            pltpu.VMEM((depth, columns), BF16),
            pltpu.SemaphoreType.DMA((2,)),
        ],
        compiler_params=params(),
        name="split_panels",
    )(my_index, in_hbm(xa_panel), in_hbm(za_panel))


def assemble(my_index, offsets, parts, panel_ref):
    position = 0
    for part in parts:
        for number in range(part.shape[0]):
            depth = part.shape[1]
            start = pl.multiple_of((my_index ^ offsets[position]) * depth, depth)
            panel_ref[pl.ds(start, depth), :] = part[number]
            position += 1


def whole_sum(got):
    pair = got[:, :LANES]
    return (pair + swap_halves(pair)) + got[:, LANES:]


def store_rows(source, target, start, size, sem):
    rows = pl.ds(start, size)
    copy = pltpu.make_async_copy(source.at[rows, :], target.at[rows, :], sem)
    copy.start()
    return copy


def lead_product_kernel(offsets, my_ref, a_ref, picks_ref, *refs):
    parts, (out_hbm, panel_ref, terms_ref, out_ref, sems) = refs[:-5], refs[-5:]
    assemble(my_ref[0], offsets, parts, panel_ref)
    rows = a_ref.shape[0]
    for start in range(0, rows, DEEP_BLOCK):
        both = jnp.dot(a_ref[start : start + DEEP_BLOCK, :], panel_ref[...], preferred_element_type=F32)
        first, second, third = (term.astype(F32) for term in split(both * swap_halves(both), 3))
        near = lane_ids(both.shape) < PANEL
        terms_ref[start : start + DEEP_BLOCK, :LANES] = jnp.where(near, first, second).astype(BF16)
        terms_ref[start : start + DEEP_BLOCK, LANES:] = third.astype(BF16)
    half = rows // 2
    block = half // 2
    stores = []
    for number, start in enumerate(range(0, half, block)):
        low = jnp.dot(picks_ref[start : start + block, :], terms_ref[...], preferred_element_type=F32)
        high = jnp.dot(picks_ref[half + start : half + start + block, :], terms_ref[...], preferred_element_type=F32)
        low, high = whole_sum(low), whole_sum(high)
        out_ref[start : start + block, :] = jnp.where(lane_ids(low.shape) < PANEL, low, high)
        stores.append(store_rows(out_ref, out_hbm, start, block, sems.at[number]))
    for store in stores:
        store.wait()


def lead_products(my_index, a_rows, picks, parts, offsets):
    rows, depth = a_rows.shape
    return pl.pallas_call(
        functools.partial(lead_product_kernel, offsets),
        in_specs=[pl.BlockSpec(memory_space=pltpu.SMEM)] + [pl.BlockSpec(memory_space=pltpu.VMEM)] * (2 + len(parts)),
        out_specs=pl.BlockSpec(memory_space=pltpu.HBM),
        out_shape=pltpu.HBM((rows // 2, LANES), F32),
        scratch_shapes=[
            pltpu.VMEM((depth, LANES), BF16),
            pltpu.VMEM((rows, 2 * LANES), BF16),
            pltpu.VMEM((rows // 2, LANES), F32),
            pltpu.SemaphoreType.DMA((2,)),
        ],
        compiler_params=params(24),
        cost_estimate=pl.CostEstimate(
            flops=2 * rows * (depth + 2 * rows) * LANES, bytes_accessed=2 * rows * depth, transcendentals=0
        ),
        name="lead_products",
    )(my_index, a_rows, picks, *parts)


BIAS = 128
MARGIN = 0.9995
ROUNDER = 1.5 * 2.0**23


def tight_split(part):
    first = -(-part // 16) * 8
    return first if part % 8 == 0 and part <= PANEL and 2 * first - part >= 8 else 0


def words_shape(half, part):
    first = tight_split(part)
    return (half // part * (part + first), LANES) if first else (half, 2 * LANES)


def nearest(x):
    return (x + ROUNDER) - ROUNDER


def rest_product_kernel(offsets, share, part_rows, my_ref, order_ref, a_hbm, *refs):
    parts, (out_ref, a_ref, at_ref, picks_ref, panel_ref, terms_ref, sems) = refs[:-7], refs[-7:]
    rows = a_ref.shape[0]
    half = rows // 2
    block = DEEP_BLOCK
    starts = range(0, rows, block)
    copies = [
        pltpu.make_async_copy(a_hbm.at[pl.ds(start, block), :], a_ref.at[pl.ds(start, block), :], sems.at[i])
        for i, start in enumerate(starts)
    ]
    for copy in copies[:3]:
        copy.start()
    assemble(my_ref[0], offsets, parts, panel_ref)
    fill_order(order_ref, at_ref, share)
    fill_picks(at_ref, picks_ref)

    def product(i):
        copies[i].wait()
        if i + 3 < len(copies):
            copies[i + 3].start()
        return jnp.dot(a_ref[starts[i] : starts[i] + block, :], panel_ref[...], preferred_element_type=F32)

    low_lanes = lane_ids((block, LANES)) < PANEL
    later = product(0)
    for i, start in enumerate(starts):
        both = later
        if i + 1 < len(starts):
            later = product(i + 1)
        near = both[:, :LANES]
        near = near * swap_halves(near)
        far = both[:, LANES : 2 * LANES] * both[:, 2 * LANES :]
        largest = jnp.max(jnp.maximum(jnp.abs(near), jnp.abs(far)), axis=1, keepdims=True)
        exponent = jnp.floor(jnp.log2(jnp.maximum(largest, 1e-30))) + 1.0
        scale = jnp.exp2(15.0 - exponent) * MARGIN
        far = nearest(far * scale)
        near = nearest(near * scale)
        far_top = nearest(far * (1 / 256))
        near_top = nearest(near * (1 / 256))
        here = slice(start, start + block)
        terms_ref[here, :LANES] = far_top.astype(BF16)
        terms_ref[here, LANES : 2 * LANES] = (far - far_top * 256.0).astype(BF16)
        terms_ref[here, 2 * LANES : 3 * LANES] = jnp.where(low_lanes, near_top, near - near_top * 256.0).astype(BF16)
        terms_ref[here, 3 * LANES :] = jnp.broadcast_to(exponent, (block, LANES)).astype(BF16)

    def coded(start, size):
        got = jnp.dot(picks_ref[start : start + size, :], terms_ref[...], preferred_element_type=F32)
        far = got[:, :LANES] * 256.0 + got[:, LANES : 2 * LANES]
        pair = got[:, 2 * LANES : 3 * LANES]
        pair = jnp.where(lane_ids(pair.shape) < PANEL, pair * 256.0, pair)
        near = (pair + swap_halves(pair)).astype(jnp.int32)
        return far.astype(jnp.int32), near, got[:, 3 * LANES :]

    block = half // 2
    first = tight_split(part_rows)
    low_lanes = lane_ids((8, LANES)) < PANEL
    eights = lax.broadcasted_iota(jnp.int32, (8, LANES), 0)
    places = lax.broadcasted_iota(jnp.int32, (part_rows, LANES), 0) + PANEL
    for start in range(0, half, block):
        far_low, near_low, exponent_low = coded(start, block)
        far_high, near_high, exponent_high = coded(half + start, block)
        far = far_low * 65536 + (far_high & 65535)
        if not first:
            near = jnp.where(
                lane_ids(near_low.shape) < PANEL,
                near_low * 65536 + (exponent_low.astype(jnp.int32) + BIAS),
                near_high * 65536 + (exponent_high.astype(jnp.int32) + BIAS),
            )
            out_ref[start : start + block, :LANES] = far
            out_ref[start : start + block, LANES:] = near
            continue
        near = near_low * 65536 + (near_high & 65535)
        second = part_rows - first
        mine = lane_ids((part_rows, LANES)) == places
        for inner in range(0, block, part_rows):
            base = (start + inner) // part_rows * (part_rows + first)
            words = near[inner : inner + part_rows]
            rows = [
                jnp.sum(jnp.where(mine, exponent[inner : inner + part_rows], 0.0), axis=0, keepdims=True)
                for exponent in (exponent_low, exponent_high)
            ]
            rows = jnp.where(eights == 0, rows[0], jnp.where(eights == 1, rows[1], 0.0)).astype(jnp.int32)
            out_ref[base : base + part_rows, :] = far[inner : inner + part_rows]
            base += part_rows
            spare = [words[: first - second - 8]] if first > second + 8 else []
            both = jnp.concatenate([words[first:], rows, *spare], axis=0)
            out_ref[base : base + first, :] = jnp.where(lane_ids(both.shape) < PANEL, words[:first], both)


def rest_products(my_index, order, a_rows, parts, offsets, share, part_rows):
    rows, depth = a_rows.shape
    return pl.pallas_call(
        functools.partial(rest_product_kernel, offsets, share, part_rows),
        in_specs=[
            pl.BlockSpec(memory_space=pltpu.SMEM),
            pl.BlockSpec(memory_space=pltpu.VMEM),
            pl.BlockSpec(memory_space=pltpu.HBM),
        ]
        + [pl.BlockSpec(memory_space=pltpu.VMEM)] * len(parts),
        out_specs=pl.BlockSpec(memory_space=pltpu.VMEM),
        out_shape=jax.ShapeDtypeStruct(words_shape(rows // 2, part_rows), jnp.int32),
        scratch_shapes=[
            pltpu.VMEM((rows, depth), BF16),
            pltpu.VMEM((rows, LANES), jnp.int32),
            pltpu.VMEM((rows, rows), BF16),
            pltpu.VMEM((depth, 3 * LANES), BF16),
            pltpu.VMEM((rows, 4 * LANES), BF16),
            pltpu.SemaphoreType.DMA((rows // DEEP_BLOCK,)),
        ],
        compiler_params=params(32),
        cost_estimate=pl.CostEstimate(
            flops=2 * rows * (3 * depth + 4 * rows) * LANES, bytes_accessed=2 * rows * depth, transcendentals=0
        ),
        name="rest_products",
    )(my_index, order, in_hbm(a_rows), *parts)


def packed_terms(x, terms_ref, start):
    half = x.shape[0]
    first, second, third = (term.astype(F32) for term in split(x, 3))
    near = lane_ids(x.shape) < PANEL
    other = swap_halves(third)
    terms_ref[:half, start : start + LANES] = jnp.where(near, first, swap_halves(second)).astype(BF16)
    terms_ref[half:, start : start + LANES] = jnp.where(near, swap_halves(first), second).astype(BF16)
    terms_ref[:half, start + LANES : start + 2 * LANES] = jnp.where(near, third, other).astype(BF16)
    terms_ref[half:, start + LANES : start + 2 * LANES] = jnp.where(near, other, third).astype(BF16)


def leading_kernel(held, index_ref, arrived_ref, out_ref, terms_ref):
    packed_terms(arrived_ref[...], terms_ref, 0)
    width = -(-held // LANES) * LANES
    picks = one_hot(index_ref[:, :width], terms_ref.shape[0])
    got = whole_sum(jnp.dot(picks, terms_ref[...], preferred_element_type=F32))
    first, second = got[: held // 2], got[held // 2 : held]
    out_ref[0] = jnp.where(lane_ids(first.shape) < PANEL, first, second)


def leading_rows(index, arrived, held):
    rows = index.shape[1]
    return pl.pallas_call(
        functools.partial(leading_kernel, held),
        in_specs=[pl.BlockSpec(memory_space=pltpu.VMEM)] * 2,
        out_specs=pl.BlockSpec(memory_space=pltpu.VMEM),
        out_shape=jax.ShapeDtypeStruct((1, held // 2, LANES), F32),
        scratch_shapes=[pltpu.VMEM((rows, 2 * LANES), BF16)],
        compiler_params=params(),
        cost_estimate=pl.CostEstimate(
            flops=4 * held * rows * LANES, bytes_accessed=2 * rows * LANES, transcendentals=0
        ),
        name="leading_rows",
    )(index, arrived)


def eliminate(block, shift_row):
    rows = lax.broadcasted_iota(jnp.int32, (PANEL, PANEL), 0)
    columns = lax.broadcasted_iota(jnp.int32, (PANEL, PANEL), 1)
    flipped = jnp.transpose(block)
    mirrored = jnp.where(rows >= columns, block, flipped)
    diagonal = shift_row + jnp.sum(jnp.abs(mirrored), axis=0, keepdims=True)
    unit = (rows == columns).astype(F32)
    work = jnp.where(rows == columns, diagonal, mirrored)
    work = jnp.concatenate([work, unit], axis=1)
    height = 8
    groups = [work[start : start + height] for start in range(0, PANEL, height)]
    sublanes = lax.broadcasted_iota(jnp.int32, (height, LANES), 0)
    scaled_rows = []
    for k in range(PANEL):
        home, offset = divmod(k, height)
        row = groups[home][offset : offset + 1, :]
        row = row / row[:, k : k + 1]
        scaled_rows.append(row)
        for g in range(home, PANEL // height):
            column = jnp.broadcast_to(groups[g][:, k : k + 1], (height, LANES))
            if g == home:
                column = jnp.where(sublanes > offset, column, 0.0)
            groups[g] = groups[g] - column * row
    final = jnp.concatenate(groups, axis=0)
    scaled = jnp.concatenate(scaled_rows, axis=0)
    upper = jnp.where(columns >= rows, scaled[:, :PANEL], 0.0)
    pivots = jnp.sum(jnp.where(rows == columns, final[:, :PANEL], 0.0), axis=0, keepdims=True)
    return upper, final[:, PANEL:], pivots


def exact(lhs, rhs, dims):
    return lax.dot_general(lhs, rhs, (dims, ((), ())), precision=lax.Precision.HIGHEST, preferred_element_type=F32)


def update_kernel(offsets, blocks_held, columns, my_ref, index_ref, arrived_ref, shift_ref, resident_hbm, *refs):
    parts = refs[:-12]
    near_hbm, far_hbm, pivots_ref, leading_ref, tail_ref, resident_ref, terms_ref, lead_ref = refs[-12:-4]
    near_ref, far_ref, sem, sems = refs[-4:]
    fetch = pltpu.make_async_copy(resident_hbm, resident_ref, sem)
    fetch.start()
    my_index = my_ref[0]
    size = len(offsets)
    position = 0
    packed = blocks_held * PANEL // 2
    part_rows = PANEL // 2
    for part in parts:
        for number in range(part.shape[0]):
            owner = my_index ^ offsets[position]
            for start in range(0, blocks_held * PANEL, part_rows):
                held, inner = divmod(start, PANEL)
                if start < packed:
                    rows = part[number, start : start + part_rows, :PANEL]
                else:
                    rows = part[number, start - packed : start - packed + part_rows, PANEL:]
                target = pl.multiple_of((held * size + owner) * PANEL + inner, part_rows)
                leading_ref[pl.ds(target, part_rows), :] = rows
            position += 1
    upper, inverse, pivots = eliminate(leading_ref[:PANEL, :], shift_ref[...])
    pivots_ref[...] = pivots
    lower = jnp.transpose(upper)
    needed = tail_ref.shape[1]
    tail = exact(inverse, leading_ref[:needed, :], ((1,), (1,)))
    high, low = split(tail, 2)
    tail_ref[0:PANEL, :] = high
    tail_ref[PANEL : 2 * PANEL, :] = high
    tail_ref[2 * PANEL : 3 * PANEL, :] = low
    tail_ref[3 * PANEL :, :] = low

    block = A_BLOCK
    packed_terms(arrived_ref[...], terms_ref, 0)
    for start in range(0, lead_ref.shape[0], block):
        picks = one_hot(index_ref[:, start : start + block], lead_ref.shape[0])
        got = jnp.dot(picks, terms_ref[...], preferred_element_type=F32)
        lead_ref[start : start + block, :] = whole_sum(got)[:, :PANEL]
    fetch.wait()
    stores = []
    for number, start in enumerate(range(0, lead_ref.shape[0], block)):
        rows_here = slice(start, start + block)
        panel = exact(lead_ref[rows_here, :], inverse, ((1,), (1,))) / pivots
        shown = used = panel
        if start == 0:
            row_ids = lax.broadcasted_iota(jnp.int32, panel.shape, 0)
            top = jnp.logical_and(my_index == 0, row_ids < PANEL)
            used = jnp.where(top, 0.0, panel)
            filled = jnp.concatenate([lower, jnp.zeros((block - PANEL, PANEL), F32)], axis=0)
            shown = jnp.where(top, filled, panel)
        high, low = (term.astype(F32) for term in split(used, 2))
        pair = jnp.concatenate([high, low], axis=1).astype(BF16)
        factors = jnp.concatenate([pair, pair], axis=1)
        update = jnp.dot(factors, tail_ref[...], preferred_element_type=F32)
        shown = jnp.concatenate([shown, jnp.zeros_like(shown)], axis=1)
        near_ref[rows_here, :LANES] = jnp.where(lane_ids(shown.shape) < PANEL, shown, -update[:, :LANES])
        near_ref[rows_here, LANES:] = -update[:, LANES:columns]
        far_ref[rows_here, :] = (resident_ref[rows_here, :].astype(F32) - update[:, columns:]).astype(BF16)
        for which, (source, target) in enumerate(((near_ref, near_hbm), (far_ref, far_hbm))):
            store = pltpu.make_async_copy(
                source.at[pl.ds(start, block), :], target.at[pl.ds(start, block), :], sems.at[which, number]
            )
            store.start()
            stores.append(store)
    for store in stores:
        store.wait()


def updates(my_index, parts, offsets, index, arrived, shift, resident, blocks_held, columns):
    rows, width = resident.shape
    needed = columns + width
    held_rows = len(offsets) * blocks_held * PANEL
    vmem = pl.BlockSpec(memory_space=pltpu.VMEM)
    anywhere = pl.BlockSpec(memory_space=pltpu.HBM)
    return pl.pallas_call(
        functools.partial(update_kernel, offsets, blocks_held, columns),
        in_specs=[pl.BlockSpec(memory_space=pltpu.SMEM), vmem, vmem, vmem, anywhere] + [vmem] * len(parts),
        out_specs=[anywhere, anywhere, vmem],
        out_shape=[
            pltpu.HBM((rows, columns), F32),
            pltpu.HBM((rows, width), BF16),
            jax.ShapeDtypeStruct((1, PANEL), F32),
        ],
        scratch_shapes=[
            pltpu.VMEM((held_rows, PANEL), F32),
            pltpu.VMEM((4 * PANEL, needed), BF16),
            pltpu.VMEM((rows, width), BF16),
            pltpu.VMEM((rows, 2 * LANES), BF16),
            pltpu.VMEM((rows, PANEL), F32),
            pltpu.VMEM((rows, columns), F32),
            pltpu.VMEM((rows, width), BF16),
            pltpu.SemaphoreType.DMA,
            pltpu.SemaphoreType.DMA((2, rows // A_BLOCK)),
        ],
        compiler_params=params(32),
        cost_estimate=pl.CostEstimate(
            flops=2 * rows * needed * 4 * PANEL, bytes_accessed=4 * rows * (columns + width), transcendentals=0
        ),
        name="factor_and_update",
    )(my_index, index, arrived, shift, in_hbm(resident), *parts)


def upper_half(words):
    return (words >> 16).astype(F32)


def lower_half(words):
    return ((words << 16) >> 16).astype(F32)


def loose_values(arrived_ref):
    words = arrived_ref[:, LANES:]
    low_lanes = lane_ids(words.shape) < PANEL
    scale = jnp.exp2(((words & 255) - (BIAS + 15)).astype(F32)) * (1 / MARGIN)
    other = swap_halves(scale)
    near = upper_half(words) * scale
    words = arrived_ref[:, :LANES]
    low = upper_half(words) * jnp.where(low_lanes, scale, other)
    return low, lower_half(words) * jnp.where(low_lanes, other, scale), near


def tight_values(arrived_ref, part_rows, values_ref):
    first = tight_split(part_rows)
    second = part_rows - first
    step = part_rows + first
    sources = arrived_ref.shape[0] // step
    pairs = [arrived_ref[i * step + part_rows + second : i * step + part_rows + second + 2, :] for i in range(sources)]
    spare = jnp.zeros((LANES - 2 * sources, LANES), jnp.int32)
    exponents = jnp.concatenate([*pairs, spare], axis=0)
    scales = jnp.exp2(jnp.transpose(exponents.astype(F32)) - 15.0) * (1 / MARGIN)
    scales = scales[PANEL : PANEL + part_rows]
    low_lanes = lane_ids((part_rows, LANES)) < PANEL
    for i in range(sources):
        base = i * step
        here = slice(i * part_rows, (i + 1) * part_rows)
        low_scale = jnp.broadcast_to(scales[:, 2 * i : 2 * i + 1], (part_rows, LANES))
        high_scale = jnp.broadcast_to(scales[:, 2 * i + 1 : 2 * i + 2], (part_rows, LANES))
        words = arrived_ref[base : base + part_rows, :]
        values_ref[0, here, :] = upper_half(words) * low_scale
        values_ref[1, here, :] = lower_half(words) * high_scale
        words = arrived_ref[base + part_rows : base + step, :]
        words = jnp.concatenate([words, swap_halves(words[:second])], axis=0)
        words = jnp.where(low_lanes, words, swap_halves(words))
        values_ref[2, here, :] = jnp.where(low_lanes, upper_half(words) * low_scale, lower_half(words) * high_scale)
    return values_ref[0], values_ref[1], values_ref[2]


def formed_kernel(
    part_rows, index_ref, arrived_ref, near_hbm, out_hbm, near_ref, terms_ref, out_ref, values_ref, in_sems, out_sems
):
    half = terms_ref.shape[0] // 2
    first = tight_split(part_rows)
    block = A_BLOCK
    starts = range(0, near_ref.shape[0], block)

    def rows_of(ref, start):
        return ref.at[pl.ds(start, block), :]

    fetches = [
        pltpu.make_async_copy(rows_of(near_hbm, start), rows_of(near_ref, start), in_sems.at[i])
        for i, start in enumerate(starts)
    ]
    for fetch in fetches:
        fetch.start()
    low, high, near = loose_values(arrived_ref) if not first else tight_values(arrived_ref, part_rows, values_ref)
    for side, values in enumerate((low, high)):
        one, two = split(values, 2)
        terms_ref[side * half : (side + 1) * half, :LANES] = one
        terms_ref[side * half : (side + 1) * half, LANES : 2 * LANES] = two
    low_lanes = lane_ids(near.shape) < PANEL
    one, two = (term.astype(F32) for term in split(near, 2))
    terms_ref[:half, 2 * LANES :] = jnp.where(low_lanes, one, swap_halves(two)).astype(BF16)
    terms_ref[half:, 2 * LANES :] = jnp.where(low_lanes, swap_halves(one), two).astype(BF16)

    stores = []
    for i, start in enumerate(starts):
        rows_here = slice(start, start + block)
        picks = one_hot(index_ref[:, rows_here], terms_ref.shape[0])
        got = jnp.dot(picks, terms_ref[...], preferred_element_type=F32)
        pair = got[:, 2 * LANES :]
        fetches[i].wait()
        held = near_ref[rows_here, :LANES]
        out_ref[rows_here, :LANES] = jnp.where(
            lane_ids(held.shape) < PANEL, held, (pair + swap_halves(pair)) + held
        )
        out_ref[rows_here, LANES:] = (got[:, :LANES] + got[:, LANES : 2 * LANES]) + near_ref[rows_here, LANES:]
        store = pltpu.make_async_copy(rows_of(out_ref, start), rows_of(out_hbm, start), out_sems.at[i])
        store.start()
        stores.append(store)
    for store in stores:
        store.wait()


def formed_columns(index, arrived, near, part_rows):
    rows, columns = near.shape
    vmem = pl.BlockSpec(memory_space=pltpu.VMEM)
    anywhere = pl.BlockSpec(memory_space=pltpu.HBM)
    return pl.pallas_call(
        functools.partial(formed_kernel, part_rows),
        in_specs=[vmem, vmem, anywhere],
        out_specs=anywhere,
        out_shape=pltpu.HBM((rows, columns), F32),
        input_output_aliases={2: 0},
        scratch_shapes=[
            pltpu.VMEM((rows, columns), F32),
            pltpu.VMEM((rows, 3 * LANES), BF16),
            pltpu.VMEM((rows, columns), F32),
            pltpu.VMEM((3, rows // 2, LANES), F32),
            pltpu.SemaphoreType.DMA((rows // A_BLOCK,)),
            pltpu.SemaphoreType.DMA((rows // A_BLOCK,)),
        ],
        compiler_params=params(32),
        cost_estimate=pl.CostEstimate(
            flops=8 * rows * rows * LANES, bytes_accessed=8 * rows * columns, transcendentals=0
        ),
        name="formed_columns",
    )(index, arrived, near)


def swap_rows(x, group):
    rows, width = x.shape
    return lax.all_to_all(
        x.reshape(group, rows // group, width), "wide", split_axis=0, concat_axis=0, tiled=True
    ).reshape(rows, width)


def on_device(a_rows, xa_panel, za_panel, send_order, recv_order, shift, resident):
    rows = a_rows.shape[0]
    columns = xa_panel.shape[1]
    group = lax.axis_size("wide")
    my_index = lax.axis_index("wide").astype(jnp.int32).reshape(1)
    share = rows // group
    half = rows // 2
    few, apart = phases_of(group)

    order, packing = send_order, share
    if share % 16:
        order = send_order.reshape(group, 2, share // 2).transpose(1, 0, 2).reshape(1, rows)
        packing = 0
    source, slot = recv_order // share, recv_order % share
    index = (slot // (share // 2)) * half + source * (share // 2) + slot % (share // 2)

    lead_panel, rest_panel = split_panels(my_index, xa_panel, za_panel)
    send_picks, a_copy = order_picks(order, a_rows, packing)
    steps = few[:-1] + [[mask] for mask in few[-1]]
    lead_parts = [lead_panel]
    for masks in steps[:-1]:
        lead_parts = exchange(join(lead_parts), masks, "wide")
    rest_parts = tied([rest_panel], send_picks)
    for number, masks in enumerate(apart[:-2]):
        rest_parts = exchange(join(rest_parts), masks, "wide")
        if number == 0:
            lead_parts = exchange(join(tied(lead_parts, *rest_parts)), steps[-1], "wide")

    lead_out = lead_products(my_index, a_copy, send_picks, lead_parts, offsets_of(steps))
    lead_in = swap_rows(tied([lead_out], *rest_parts)[0], group)
    rest_parts = exchange(join(tied(rest_parts, lead_out)), apart[-2], "wide")
    other_parts = exchange(rest_parts[:1], apart[-1], "wide")[1:]

    needed = columns + resident.shape[1]
    blocks_held = -(-needed // (PANEL * group))
    leading_parts = [leading_rows(index, lead_in, blocks_held * PANEL)]
    for masks in few:
        leading_parts = exchange(join(leading_parts), masks, "wide")
        if masks is few[0]:
            later_parts = exchange(tied(rest_parts[1:], *leading_parts), apart[-1], "wide")
    late = len(later_parts) // 2
    rest_parts = rest_parts + other_parts + later_parts[late:]
    rest_out = rest_products(
        my_index, order, a_rows, rest_parts, offsets_of(apart), packing, share // 2
    )
    rest_in = swap_rows(tied([rest_out], *leading_parts)[0], group)
    near, updated, pivots = updates(
        my_index,
        leading_parts,
        offsets_of(few),
        index,
        tied([lead_in], rest_out)[0],
        shift[None, :],
        resident,
        blocks_held,
        columns,
    )
    factored = formed_columns(index, rest_in, near, share // 2)
    return (factored, updated, pivots[0])


def solution(mesh):
    placed = (
        P(("parts", "wide"), None),
        P(("parts", "wide"), None),
        P(("parts", "wide"), None),
        P(("parts", "wide"), None),
        P(("parts", "wide"), None),
        P("parts"),
        P(("parts", "wide"), None),
    )
    return jax.shard_map(
        on_device,
        mesh=mesh,
        in_specs=placed,
        out_specs=(P(("parts", "wide"), None), P(("parts", "wide"), None), P("parts")),
        check_vma=False,
    )
```

```python
import functools

import jax
import jax.numpy as jnp
from jax import lax
from jax.experimental import pallas as pl
from jax.experimental.pallas import tpu as pltpu
from jax.sharding import PartitionSpec as P

PANEL = 64
LANES = 128
A_BLOCK = 640
DEEP_BLOCK = 256
F32 = jnp.float32
BF16 = jnp.bfloat16
MIB = 1024 * 1024


def params(mebibytes=12):
    return pltpu.CompilerParams(vmem_limit_bytes=mebibytes * MIB)


def in_hbm(x):
    return pltpu.with_memory_space_constraint(x, pltpu.HBM)


def lane_ids(shape):
    return lax.broadcasted_iota(jnp.int32, shape, len(shape) - 1)


def split(x, count):
    terms = []
    for _ in range(count):
        term = x.astype(BF16)
        terms.append(term)
        x = x - term.astype(F32)
    return terms


def swap_halves(x):
    return pltpu.roll(x, LANES // 2, 1)


def as_column(index_row):
    return jnp.transpose(jnp.broadcast_to(index_row, (LANES, LANES)))


def picks_of(at, width):
    lanes = lane_ids(at.shape)
    return jnp.concatenate(
        [(at == lanes + column).astype(F32).astype(BF16) for column in range(0, width, LANES)], axis=1
    )


def fill_picks(at_ref, picks_ref):
    rows, width = picks_ref.shape
    for start in range(0, rows, LANES):
        picks_ref[start : start + LANES, :] = picks_of(at_ref[start : start + LANES, :], width)


def one_hot(index_row, width):
    chunks = [
        picks_of(as_column(index_row[:, start : start + LANES]), width)
        for start in range(0, index_row.shape[1], LANES)
    ]
    return jnp.concatenate(chunks, axis=0) if len(chunks) > 1 else chunks[0]


def packed_order(share, half, slot):
    part = share // 2
    return (slot % share) // part * half + slot // share * part + slot % part


def fill_order(order_ref, at_ref, share):
    rows = order_ref.shape[1]
    height = 8
    for start in range(0, rows, LANES):
        column = as_column(order_ref[:, start : start + LANES])
        if not share:
            at_ref[start : start + LANES, :] = column
            continue
        for inner in range(0, LANES, height):
            place = packed_order(share, rows // 2, start + inner)
            at_ref[place : place + height, :] = column[inner : inner + height]


def exchange(held, masks, axis):
    size = lax.axis_size(axis)
    combined = [0]
    for mask in masks:
        combined += [other ^ mask for other in combined]
    parts = list(held)
    for mask in combined[1:]:
        parts += [lax.ppermute(part, axis, [(i, i ^ mask) for i in range(size)]) for part in held]
    return parts


def offsets_of(phases):
    offsets = [0]
    for masks in phases:
        combined = [0]
        for mask in masks:
            combined += [other ^ mask for other in combined]
        offsets = [offset ^ mask for mask in combined for offset in offsets]
    return offsets


def join(parts):
    return [jnp.concatenate(parts, axis=0)]


def phases_of(size):
    bits = [1 << bit for bit in reversed(range(size.bit_length() - 1))]
    return [bits[start : start + 2] for start in range(0, len(bits), 2)], [[bit] for bit in bits]


def tied(parts, *earlier):
    return list(lax.optimization_barrier((*parts, *earlier))[: len(parts)])


def picks_kernel(share, order_hbm, a_hbm, picks_ref, copy_ref, order_ref, at_ref, sems):
    fetch = pltpu.make_async_copy(order_hbm, order_ref, sems.at[0])
    copy = pltpu.make_async_copy(a_hbm, copy_ref, sems.at[1])
    fetch.start()
    copy.start()
    fetch.wait()
    fill_order(order_ref, at_ref, share)
    fill_picks(at_ref, picks_ref)
    copy.wait()


def order_picks(order, a_rows, share):
    rows, depth = a_rows.shape
    return pl.pallas_call(
        functools.partial(picks_kernel, share),
        in_specs=[pl.BlockSpec(memory_space=pltpu.HBM)] * 2,
        out_specs=[pl.BlockSpec(memory_space=pltpu.VMEM)] * 2,
        out_shape=[jax.ShapeDtypeStruct((rows, rows), BF16), jax.ShapeDtypeStruct((rows, depth), BF16)],
        scratch_shapes=[
            pltpu.VMEM((1, rows), jnp.int32),
            pltpu.VMEM((rows, LANES), jnp.int32),
            pltpu.SemaphoreType.DMA((2,)),
        ],
        compiler_params=params(),
        cost_estimate=pl.CostEstimate(flops=4 * rows * rows, bytes_accessed=4 * rows * depth, transcendentals=0),
        name="order_picks",
    )(in_hbm(order), in_hbm(a_rows))


def panels_kernel(my_ref, xa_hbm, za_hbm, lead_ref, rest_ref, xa_ref, za_ref, sems):
    copies = [
        pltpu.make_async_copy(xa_hbm, xa_ref, sems.at[0]),
        pltpu.make_async_copy(za_hbm, za_ref, sems.at[1]),
    ]
    for copy in copies:
        copy.start()
    for copy in copies:
        copy.wait()
    lead_ref[0] = jnp.concatenate([xa_ref[:, :PANEL], za_ref[:, :PANEL]], axis=1)
    rest_ref[0, :, :LANES] = jnp.concatenate([xa_ref[:, PANEL:LANES], za_ref[:, PANEL:LANES]], axis=1)
    rest_ref[0, :, LANES : 2 * LANES] = xa_ref[:, LANES:]
    rest_ref[0, :, 2 * LANES :] = za_ref[:, LANES:]


def split_panels(my_index, xa_panel, za_panel):
    depth, columns = xa_panel.shape
    return pl.pallas_call(
        panels_kernel,
        in_specs=[pl.BlockSpec(memory_space=pltpu.SMEM)] + [pl.BlockSpec(memory_space=pltpu.HBM)] * 2,
        out_shape=[
            jax.ShapeDtypeStruct((1, depth, LANES), BF16),
            jax.ShapeDtypeStruct((1, depth, 2 * columns - LANES), BF16),
        ],
        scratch_shapes=[
            pltpu.VMEM((depth, columns), BF16),
            pltpu.VMEM((depth, columns), BF16),
            pltpu.SemaphoreType.DMA((2,)),
        ],
        compiler_params=params(),
        name="split_panels",
    )(my_index, in_hbm(xa_panel), in_hbm(za_panel))


def assemble(my_index, offsets, parts, panel_ref):
    position = 0
    for part in parts:
        for number in range(part.shape[0]):
            depth = part.shape[1]
            start = pl.multiple_of((my_index ^ offsets[position]) * depth, depth)
            panel_ref[pl.ds(start, depth), :] = part[number]
            position += 1


def whole_sum(got):
    pair = got[:, :LANES]
    return (pair + swap_halves(pair)) + got[:, LANES:]


def store_rows(source, target, start, size, sem):
    rows = pl.ds(start, size)
    copy = pltpu.make_async_copy(source.at[rows, :], target.at[rows, :], sem)
    copy.start()
    return copy


def lead_product_kernel(offsets, my_ref, a_ref, picks_ref, *refs):
    parts, (out_hbm, panel_ref, terms_ref, out_ref, sems) = refs[:-5], refs[-5:]
    assemble(my_ref[0], offsets, parts, panel_ref)
    rows = a_ref.shape[0]
    for start in range(0, rows, DEEP_BLOCK):
        both = jnp.dot(a_ref[start : start + DEEP_BLOCK, :], panel_ref[...], preferred_element_type=F32)
        first, second, third = (term.astype(F32) for term in split(both * swap_halves(both), 3))
        near = lane_ids(both.shape) < PANEL
        terms_ref[start : start + DEEP_BLOCK, :LANES] = jnp.where(near, first, second).astype(BF16)
        terms_ref[start : start + DEEP_BLOCK, LANES:] = third.astype(BF16)
    half = rows // 2
    block = half // 2
    stores = []
    for number, start in enumerate(range(0, half, block)):
        low = jnp.dot(picks_ref[start : start + block, :], terms_ref[...], preferred_element_type=F32)
        high = jnp.dot(picks_ref[half + start : half + start + block, :], terms_ref[...], preferred_element_type=F32)
        low, high = whole_sum(low), whole_sum(high)
        out_ref[start : start + block, :] = jnp.where(lane_ids(low.shape) < PANEL, low, high)
        stores.append(store_rows(out_ref, out_hbm, start, block, sems.at[number]))
    for store in stores:
        store.wait()


def lead_products(my_index, a_rows, picks, parts, offsets):
    rows, depth = a_rows.shape
    return pl.pallas_call(
        functools.partial(lead_product_kernel, offsets),
        in_specs=[pl.BlockSpec(memory_space=pltpu.SMEM)] + [pl.BlockSpec(memory_space=pltpu.VMEM)] * (2 + len(parts)),
        out_specs=pl.BlockSpec(memory_space=pltpu.HBM),
        out_shape=pltpu.HBM((rows // 2, LANES), F32),
        scratch_shapes=[
            pltpu.VMEM((depth, LANES), BF16),
            pltpu.VMEM((rows, 2 * LANES), BF16),
            pltpu.VMEM((rows // 2, LANES), F32),
            pltpu.SemaphoreType.DMA((2,)),
        ],
        compiler_params=params(24),
        cost_estimate=pl.CostEstimate(
            flops=2 * rows * (depth + 2 * rows) * LANES, bytes_accessed=2 * rows * depth, transcendentals=0
        ),
        name="lead_products",
    )(my_index, a_rows, picks, *parts)


BIAS = 128
MARGIN = 0.9995
ROUNDER = 1.5 * 2.0**23


def tight_split(part):
    first = -(-part // 16) * 8
    return first if part % 8 == 0 and part <= PANEL and 2 * first - part >= 8 else 0


def words_shape(half, part):
    first = tight_split(part)
    return (half // part * (part + first), LANES) if first else (half, 2 * LANES)


def nearest(x):
    return (x + ROUNDER) - ROUNDER


def rest_product_kernel(offsets, share, part_rows, my_ref, order_ref, a_hbm, *refs):
    parts, (out_ref, a_ref, at_ref, picks_ref, panel_ref, terms_ref, sems) = refs[:-7], refs[-7:]
    rows = a_ref.shape[0]
    half = rows // 2
    block = DEEP_BLOCK
    starts = range(0, rows, block)
    copies = [
        pltpu.make_async_copy(a_hbm.at[pl.ds(start, block), :], a_ref.at[pl.ds(start, block), :], sems.at[i])
        for i, start in enumerate(starts)
    ]
    for copy in copies[:3]:
        copy.start()
    assemble(my_ref[0], offsets, parts, panel_ref)
    fill_order(order_ref, at_ref, share)
    fill_picks(at_ref, picks_ref)

    def product(i):
        copies[i].wait()
        if i + 3 < len(copies):
            copies[i + 3].start()
        return jnp.dot(a_ref[starts[i] : starts[i] + block, :], panel_ref[...], preferred_element_type=F32)

    low_lanes = lane_ids((block, LANES)) < PANEL
    later = product(0)
    for i, start in enumerate(starts):
        both = later
        if i + 1 < len(starts):
            later = product(i + 1)
        near = both[:, :LANES]
        near = near * swap_halves(near)
        far = both[:, LANES : 2 * LANES] * both[:, 2 * LANES :]
        largest = jnp.max(jnp.maximum(jnp.abs(near), jnp.abs(far)), axis=1, keepdims=True)
        exponent = jnp.floor(jnp.log2(jnp.maximum(largest, 1e-30))) + 1.0
        scale = jnp.exp2(15.0 - exponent) * MARGIN
        far = nearest(far * scale)
        near = nearest(near * scale)
        far_top = nearest(far * (1 / 256))
        near_top = nearest(near * (1 / 256))
        here = slice(start, start + block)
        terms_ref[here, :LANES] = far_top.astype(BF16)
        terms_ref[here, LANES : 2 * LANES] = (far - far_top * 256.0).astype(BF16)
        terms_ref[here, 2 * LANES : 3 * LANES] = jnp.where(low_lanes, near_top, near - near_top * 256.0).astype(BF16)
        terms_ref[here, 3 * LANES :] = jnp.broadcast_to(exponent, (block, LANES)).astype(BF16)

    def coded(start, size):
        got = jnp.dot(picks_ref[start : start + size, :], terms_ref[...], preferred_element_type=F32)
        far = got[:, :LANES] * 256.0 + got[:, LANES : 2 * LANES]
        pair = got[:, 2 * LANES : 3 * LANES]
        pair = jnp.where(lane_ids(pair.shape) < PANEL, pair * 256.0, pair)
        near = (pair + swap_halves(pair)).astype(jnp.int32)
        return far.astype(jnp.int32), near, got[:, 3 * LANES :]

    block = half // 2
    first = tight_split(part_rows)
    low_lanes = lane_ids((8, LANES)) < PANEL
    eights = lax.broadcasted_iota(jnp.int32, (8, LANES), 0)
    places = lax.broadcasted_iota(jnp.int32, (part_rows, LANES), 0) + PANEL
    for start in range(0, half, block):
        far_low, near_low, exponent_low = coded(start, block)
        far_high, near_high, exponent_high = coded(half + start, block)
        far = far_low * 65536 + (far_high & 65535)
        if not first:
            near = jnp.where(
                lane_ids(near_low.shape) < PANEL,
                near_low * 65536 + (exponent_low.astype(jnp.int32) + BIAS),
                near_high * 65536 + (exponent_high.astype(jnp.int32) + BIAS),
            )
            out_ref[start : start + block, :LANES] = far
            out_ref[start : start + block, LANES:] = near
            continue
        near = near_low * 65536 + (near_high & 65535)
        second = part_rows - first
        mine = lane_ids((part_rows, LANES)) == places
        for inner in range(0, block, part_rows):
            base = (start + inner) // part_rows * (part_rows + first)
            words = near[inner : inner + part_rows]
            rows = [
                jnp.sum(jnp.where(mine, exponent[inner : inner + part_rows], 0.0), axis=0, keepdims=True)
                for exponent in (exponent_low, exponent_high)
            ]
            rows = jnp.where(eights == 0, rows[0], jnp.where(eights == 1, rows[1], 0.0)).astype(jnp.int32)
            out_ref[base : base + part_rows, :] = far[inner : inner + part_rows]
            base += part_rows
            spare = [words[: first - second - 8]] if first > second + 8 else []
            both = jnp.concatenate([words[first:], rows, *spare], axis=0)
            out_ref[base : base + first, :] = jnp.where(lane_ids(both.shape) < PANEL, words[:first], both)


def rest_products(my_index, order, a_rows, parts, offsets, share, part_rows):
    rows, depth = a_rows.shape
    return pl.pallas_call(
        functools.partial(rest_product_kernel, offsets, share, part_rows),
        in_specs=[
            pl.BlockSpec(memory_space=pltpu.SMEM),
            pl.BlockSpec(memory_space=pltpu.VMEM),
            pl.BlockSpec(memory_space=pltpu.HBM),
        ]
        + [pl.BlockSpec(memory_space=pltpu.VMEM)] * len(parts),
        out_specs=pl.BlockSpec(memory_space=pltpu.VMEM),
        out_shape=jax.ShapeDtypeStruct(words_shape(rows // 2, part_rows), jnp.int32),
        scratch_shapes=[
            pltpu.VMEM((rows, depth), BF16),
            pltpu.VMEM((rows, LANES), jnp.int32),
            pltpu.VMEM((rows, rows), BF16),
            pltpu.VMEM((depth, 3 * LANES), BF16),
            pltpu.VMEM((rows, 4 * LANES), BF16),
            pltpu.SemaphoreType.DMA((rows // DEEP_BLOCK,)),
        ],
        compiler_params=params(32),
        cost_estimate=pl.CostEstimate(
            flops=2 * rows * (3 * depth + 4 * rows) * LANES, bytes_accessed=2 * rows * depth, transcendentals=0
        ),
        name="rest_products",
    )(my_index, order, in_hbm(a_rows), *parts)


def packed_terms(x, terms_ref, start):
    half = x.shape[0]
    first, second, third = (term.astype(F32) for term in split(x, 3))
    near = lane_ids(x.shape) < PANEL
    other = swap_halves(third)
    terms_ref[:half, start : start + LANES] = jnp.where(near, first, swap_halves(second)).astype(BF16)
    terms_ref[half:, start : start + LANES] = jnp.where(near, swap_halves(first), second).astype(BF16)
    terms_ref[:half, start + LANES : start + 2 * LANES] = jnp.where(near, third, other).astype(BF16)
    terms_ref[half:, start + LANES : start + 2 * LANES] = jnp.where(near, other, third).astype(BF16)


def leading_kernel(held, index_ref, arrived_ref, out_ref, terms_ref):
    packed_terms(arrived_ref[...], terms_ref, 0)
    width = -(-held // LANES) * LANES
    picks = one_hot(index_ref[:, :width], terms_ref.shape[0])
    got = whole_sum(jnp.dot(picks, terms_ref[...], preferred_element_type=F32))
    first, second = got[: held // 2], got[held // 2 : held]
    out_ref[0] = jnp.where(lane_ids(first.shape) < PANEL, first, second)


def leading_rows(index, arrived, held):
    rows = index.shape[1]
    return pl.pallas_call(
        functools.partial(leading_kernel, held),
        in_specs=[pl.BlockSpec(memory_space=pltpu.VMEM)] * 2,
        out_specs=pl.BlockSpec(memory_space=pltpu.VMEM),
        out_shape=jax.ShapeDtypeStruct((1, held // 2, LANES), F32),
        scratch_shapes=[pltpu.VMEM((rows, 2 * LANES), BF16)],
        compiler_params=params(),
        cost_estimate=pl.CostEstimate(
            flops=4 * held * rows * LANES, bytes_accessed=2 * rows * LANES, transcendentals=0
        ),
        name="leading_rows",
    )(index, arrived)


def eliminate(block, shift_row):
    rows = lax.broadcasted_iota(jnp.int32, (PANEL, PANEL), 0)
    columns = lax.broadcasted_iota(jnp.int32, (PANEL, PANEL), 1)
    flipped = jnp.transpose(block)
    mirrored = jnp.where(rows >= columns, block, flipped)
    diagonal = shift_row + jnp.sum(jnp.abs(mirrored), axis=0, keepdims=True)
    unit = (rows == columns).astype(F32)
    work = jnp.where(rows == columns, diagonal, mirrored)
    work = jnp.concatenate([work, unit], axis=1)
    height = 8
    groups = [work[start : start + height] for start in range(0, PANEL, height)]
    sublanes = lax.broadcasted_iota(jnp.int32, (height, LANES), 0)
    scaled_rows = []
    for k in range(PANEL):
        home, offset = divmod(k, height)
        row = groups[home][offset : offset + 1, :]
        row = row / row[:, k : k + 1]
        scaled_rows.append(row)
        for g in range(home, PANEL // height):
            column = jnp.broadcast_to(groups[g][:, k : k + 1], (height, LANES))
            if g == home:
                column = jnp.where(sublanes > offset, column, 0.0)
            groups[g] = groups[g] - column * row
    final = jnp.concatenate(groups, axis=0)
    scaled = jnp.concatenate(scaled_rows, axis=0)
    upper = jnp.where(columns >= rows, scaled[:, :PANEL], 0.0)
    pivots = jnp.sum(jnp.where(rows == columns, final[:, :PANEL], 0.0), axis=0, keepdims=True)
    return upper, final[:, PANEL:], pivots


def exact(lhs, rhs, dims):
    return lax.dot_general(lhs, rhs, (dims, ((), ())), precision=lax.Precision.HIGHEST, preferred_element_type=F32)


def update_kernel(offsets, blocks_held, columns, my_ref, index_ref, arrived_ref, shift_ref, resident_hbm, *refs):
    parts = refs[:-12]
    near_hbm, far_hbm, pivots_ref, leading_ref, tail_ref, resident_ref, terms_ref, lead_ref = refs[-12:-4]
    near_ref, far_ref, sem, sems = refs[-4:]
    fetch = pltpu.make_async_copy(resident_hbm, resident_ref, sem)
    fetch.start()
    my_index = my_ref[0]
    size = len(offsets)
    position = 0
    packed = blocks_held * PANEL // 2
    part_rows = PANEL // 2
    for part in parts:
        for number in range(part.shape[0]):
            owner = my_index ^ offsets[position]
            for start in range(0, blocks_held * PANEL, part_rows):
                held, inner = divmod(start, PANEL)
                if start < packed:
                    rows = part[number, start : start + part_rows, :PANEL]
                else:
                    rows = part[number, start - packed : start - packed + part_rows, PANEL:]
                target = pl.multiple_of((held * size + owner) * PANEL + inner, part_rows)
                leading_ref[pl.ds(target, part_rows), :] = rows
            position += 1
    upper, inverse, pivots = eliminate(leading_ref[:PANEL, :], shift_ref[...])
    pivots_ref[...] = pivots
    lower = jnp.transpose(upper)
    needed = tail_ref.shape[1]
    tail = exact(inverse, leading_ref[:needed, :], ((1,), (1,)))
    high, low = split(tail, 2)
    tail_ref[0:PANEL, :] = high
    tail_ref[PANEL : 2 * PANEL, :] = high
    tail_ref[2 * PANEL : 3 * PANEL, :] = low
    tail_ref[3 * PANEL :, :] = low

    block = A_BLOCK
    packed_terms(arrived_ref[...], terms_ref, 0)
    for start in range(0, lead_ref.shape[0], block):
        picks = one_hot(index_ref[:, start : start + block], lead_ref.shape[0])
        got = jnp.dot(picks, terms_ref[...], preferred_element_type=F32)
        lead_ref[start : start + block, :] = whole_sum(got)[:, :PANEL]
    fetch.wait()
    stores = []
    for number, start in enumerate(range(0, lead_ref.shape[0], block)):
        rows_here = slice(start, start + block)
        panel = exact(lead_ref[rows_here, :], inverse, ((1,), (1,))) / pivots
        shown = used = panel
        if start == 0:
            row_ids = lax.broadcasted_iota(jnp.int32, panel.shape, 0)
            top = jnp.logical_and(my_index == 0, row_ids < PANEL)
            used = jnp.where(top, 0.0, panel)
            filled = jnp.concatenate([lower, jnp.zeros((block - PANEL, PANEL), F32)], axis=0)
            shown = jnp.where(top, filled, panel)
        high, low = (term.astype(F32) for term in split(used, 2))
        pair = jnp.concatenate([high, low], axis=1).astype(BF16)
        factors = jnp.concatenate([pair, pair], axis=1)
        update = jnp.dot(factors, tail_ref[...], preferred_element_type=F32)
        shown = jnp.concatenate([shown, jnp.zeros_like(shown)], axis=1)
        near_ref[rows_here, :LANES] = jnp.where(lane_ids(shown.shape) < PANEL, shown, -update[:, :LANES])
        near_ref[rows_here, LANES:] = -update[:, LANES:columns]
        far_ref[rows_here, :] = (resident_ref[rows_here, :].astype(F32) - update[:, columns:]).astype(BF16)
        for which, (source, target) in enumerate(((near_ref, near_hbm), (far_ref, far_hbm))):
            store = pltpu.make_async_copy(
                source.at[pl.ds(start, block), :], target.at[pl.ds(start, block), :], sems.at[which, number]
            )
            store.start()
            stores.append(store)
    for store in stores:
        store.wait()


def updates(my_index, parts, offsets, index, arrived, shift, resident, blocks_held, columns):
    rows, width = resident.shape
    needed = columns + width
    held_rows = len(offsets) * blocks_held * PANEL
    vmem = pl.BlockSpec(memory_space=pltpu.VMEM)
    anywhere = pl.BlockSpec(memory_space=pltpu.HBM)
    return pl.pallas_call(
        functools.partial(update_kernel, offsets, blocks_held, columns),
        in_specs=[pl.BlockSpec(memory_space=pltpu.SMEM), vmem, vmem, vmem, anywhere] + [vmem] * len(parts),
        out_specs=[anywhere, anywhere, vmem],
        out_shape=[
            pltpu.HBM((rows, columns), F32),
            pltpu.HBM((rows, width), BF16),
            jax.ShapeDtypeStruct((1, PANEL), F32),
        ],
        scratch_shapes=[
            pltpu.VMEM((held_rows, PANEL), F32),
            pltpu.VMEM((4 * PANEL, needed), BF16),
            pltpu.VMEM((rows, width), BF16),
            pltpu.VMEM((rows, 2 * LANES), BF16),
            pltpu.VMEM((rows, PANEL), F32),
            pltpu.VMEM((rows, columns), F32),
            pltpu.VMEM((rows, width), BF16),
            pltpu.SemaphoreType.DMA,
            pltpu.SemaphoreType.DMA((2, rows // A_BLOCK)),
        ],
        compiler_params=params(32),
        cost_estimate=pl.CostEstimate(
            flops=2 * rows * needed * 4 * PANEL, bytes_accessed=4 * rows * (columns + width), transcendentals=0
        ),
        name="factor_and_update",
    )(my_index, index, arrived, shift, in_hbm(resident), *parts)


def upper_half(words):
    return (words >> 16).astype(F32)


def lower_half(words):
    return ((words << 16) >> 16).astype(F32)


def loose_values(arrived_ref):
    words = arrived_ref[:, LANES:]
    low_lanes = lane_ids(words.shape) < PANEL
    scale = jnp.exp2(((words & 255) - (BIAS + 15)).astype(F32)) * (1 / MARGIN)
    other = swap_halves(scale)
    near = upper_half(words) * scale
    words = arrived_ref[:, :LANES]
    low = upper_half(words) * jnp.where(low_lanes, scale, other)
    return low, lower_half(words) * jnp.where(low_lanes, other, scale), near


def tight_values(arrived_ref, part_rows, values_ref):
    first = tight_split(part_rows)
    second = part_rows - first
    step = part_rows + first
    sources = arrived_ref.shape[0] // step
    pairs = [arrived_ref[i * step + part_rows + second : i * step + part_rows + second + 2, :] for i in range(sources)]
    spare = jnp.zeros((LANES - 2 * sources, LANES), jnp.int32)
    exponents = jnp.concatenate([*pairs, spare], axis=0)
    scales = jnp.exp2(jnp.transpose(exponents.astype(F32)) - 15.0) * (1 / MARGIN)
    scales = scales[PANEL : PANEL + part_rows]
    low_lanes = lane_ids((part_rows, LANES)) < PANEL
    for i in range(sources):
        base = i * step
        here = slice(i * part_rows, (i + 1) * part_rows)
        low_scale = jnp.broadcast_to(scales[:, 2 * i : 2 * i + 1], (part_rows, LANES))
        high_scale = jnp.broadcast_to(scales[:, 2 * i + 1 : 2 * i + 2], (part_rows, LANES))
        words = arrived_ref[base : base + part_rows, :]
        values_ref[0, here, :] = upper_half(words) * low_scale
        values_ref[1, here, :] = lower_half(words) * high_scale
        words = arrived_ref[base + part_rows : base + step, :]
        words = jnp.concatenate([words, swap_halves(words[:second])], axis=0)
        words = jnp.where(low_lanes, words, swap_halves(words))
        values_ref[2, here, :] = jnp.where(low_lanes, upper_half(words) * low_scale, lower_half(words) * high_scale)
    return values_ref[0], values_ref[1], values_ref[2]


def formed_kernel(
    part_rows, index_ref, arrived_ref, near_hbm, out_hbm, near_ref, terms_ref, out_ref, values_ref, in_sems, out_sems
):
    half = terms_ref.shape[0] // 2
    first = tight_split(part_rows)
    block = A_BLOCK
    starts = range(0, near_ref.shape[0], block)

    def rows_of(ref, start):
        return ref.at[pl.ds(start, block), :]

    fetches = [
        pltpu.make_async_copy(rows_of(near_hbm, start), rows_of(near_ref, start), in_sems.at[i])
        for i, start in enumerate(starts)
    ]
    for fetch in fetches:
        fetch.start()
    low, high, near = loose_values(arrived_ref) if not first else tight_values(arrived_ref, part_rows, values_ref)
    for side, values in enumerate((low, high)):
        one, two = split(values, 2)
        terms_ref[side * half : (side + 1) * half, :LANES] = one
        terms_ref[side * half : (side + 1) * half, LANES : 2 * LANES] = two
    low_lanes = lane_ids(near.shape) < PANEL
    one, two = (term.astype(F32) for term in split(near, 2))
    terms_ref[:half, 2 * LANES :] = jnp.where(low_lanes, one, swap_halves(two)).astype(BF16)
    terms_ref[half:, 2 * LANES :] = jnp.where(low_lanes, swap_halves(one), two).astype(BF16)

    stores = []
    for i, start in enumerate(starts):
        rows_here = slice(start, start + block)
        picks = one_hot(index_ref[:, rows_here], terms_ref.shape[0])
        got = jnp.dot(picks, terms_ref[...], preferred_element_type=F32)
        pair = got[:, 2 * LANES :]
        fetches[i].wait()
        held = near_ref[rows_here, :LANES]
        out_ref[rows_here, :LANES] = jnp.where(
            lane_ids(held.shape) < PANEL, held, (pair + swap_halves(pair)) + held
        )
        out_ref[rows_here, LANES:] = (got[:, :LANES] + got[:, LANES : 2 * LANES]) + near_ref[rows_here, LANES:]
        store = pltpu.make_async_copy(rows_of(out_ref, start), rows_of(out_hbm, start), out_sems.at[i])
        store.start()
        stores.append(store)
    for store in stores:
        store.wait()


def formed_columns(index, arrived, near, part_rows):
    rows, columns = near.shape
    vmem = pl.BlockSpec(memory_space=pltpu.VMEM)
    anywhere = pl.BlockSpec(memory_space=pltpu.HBM)
    return pl.pallas_call(
        functools.partial(formed_kernel, part_rows),
        in_specs=[vmem, vmem, anywhere],
        out_specs=anywhere,
        out_shape=pltpu.HBM((rows, columns), F32),
        input_output_aliases={2: 0},
        scratch_shapes=[
            pltpu.VMEM((rows, columns), F32),
            pltpu.VMEM((rows, 3 * LANES), BF16),
            pltpu.VMEM((rows, columns), F32),
            pltpu.VMEM((3, rows // 2, LANES), F32),
            pltpu.SemaphoreType.DMA((rows // A_BLOCK,)),
            pltpu.SemaphoreType.DMA((rows // A_BLOCK,)),
        ],
        compiler_params=params(32),
        cost_estimate=pl.CostEstimate(
            flops=8 * rows * rows * LANES, bytes_accessed=8 * rows * columns, transcendentals=0
        ),
        name="formed_columns",
    )(index, arrived, near)


def swap_rows(x, group):
    rows, width = x.shape
    return lax.all_to_all(
        x.reshape(group, rows // group, width), "wide", split_axis=0, concat_axis=0, tiled=True
    ).reshape(rows, width)


def on_device(a_rows, xa_panel, za_panel, send_order, recv_order, shift, resident):
    rows = a_rows.shape[0]
    columns = xa_panel.shape[1]
    group = lax.axis_size("wide")
    my_index = lax.axis_index("wide").astype(jnp.int32).reshape(1)
    share = rows // group
    half = rows // 2
    few, apart = phases_of(group)

    order, packing = send_order, share
    if share % 16:
        order = send_order.reshape(group, 2, share // 2).transpose(1, 0, 2).reshape(1, rows)
        packing = 0
    source, slot = recv_order // share, recv_order % share
    index = (slot // (share // 2)) * half + source * (share // 2) + slot % (share // 2)

    lead_panel, rest_panel = split_panels(my_index, xa_panel, za_panel)
    send_picks, a_copy = order_picks(order, a_rows, packing)
    steps = few[:-1] + [[mask] for mask in few[-1]]
    lead_parts = join(exchange([lead_panel], steps[0], "wide"))
    rest_parts = exchange(tied([rest_panel], *lead_parts), apart[0], "wide")
    for masks in steps[1:-1]:
        lead_parts = exchange(join(lead_parts), masks, "wide")
    lead_parts = exchange(tied(join(lead_parts), send_picks), steps[-1], "wide")
    lead_parts = tied(lead_parts, *rest_parts)

    lead_out = lead_products(my_index, a_copy, send_picks, lead_parts, offsets_of(steps))
    lead_in = swap_rows(lead_out, group)
    rest_parts = tied(rest_parts, lead_out)
    for masks in apart[1:-1]:
        rest_parts = exchange(join(rest_parts), masks, "wide")
    other_parts = exchange(rest_parts[:1], apart[-1], "wide")[1:]

    needed = columns + resident.shape[1]
    blocks_held = -(-needed // (PANEL * group))
    leading_parts = [leading_rows(index, lead_in, blocks_held * PANEL)]
    for masks in few:
        leading_parts = exchange(join(leading_parts), masks, "wide")
        if masks is few[0]:
            later_parts = exchange(tied(rest_parts[1:], *leading_parts), apart[-1], "wide")
    late = len(later_parts) // 2
    rest_parts = rest_parts + other_parts + later_parts[late:]
    rest_out = rest_products(
        my_index, order, a_rows, rest_parts, offsets_of(apart), packing, share // 2
    )
    rest_in = swap_rows(tied([rest_out], *leading_parts)[0], group)
    near, updated, pivots = updates(
        my_index,
        leading_parts,
        offsets_of(few),
        index,
        tied([lead_in], rest_out)[0],
        shift[None, :],
        resident,
        blocks_held,
        columns,
    )
    factored = formed_columns(index, rest_in, near, share // 2)
    return (factored, updated, pivots[0])


def solution(mesh):
    placed = (
        P(("parts", "wide"), None),
        P(("parts", "wide"), None),
        P(("parts", "wide"), None),
        P(("parts", "wide"), None),
        P(("parts", "wide"), None),
        P("parts"),
        P(("parts", "wide"), None),
    )
    return jax.shard_map(
        on_device,
        mesh=mesh,
        in_specs=placed,
        out_specs=(P(("parts", "wide"), None), P(("parts", "wide"), None), P("parts")),
        check_vma=False,
    )
```

```python
import functools

import jax
import jax.numpy as jnp
from jax import lax
from jax.experimental import pallas as pl
from jax.experimental.pallas import tpu as pltpu
from jax.sharding import PartitionSpec as P

PANEL = 64
LANES = 128
A_BLOCK = 640
DEEP_BLOCK = 256
F32 = jnp.float32
BF16 = jnp.bfloat16
MIB = 1024 * 1024


def params(mebibytes=12):
    return pltpu.CompilerParams(vmem_limit_bytes=mebibytes * MIB)


def in_hbm(x):
    return pltpu.with_memory_space_constraint(x, pltpu.HBM)


def lane_ids(shape):
    return lax.broadcasted_iota(jnp.int32, shape, len(shape) - 1)


def split(x, count):
    terms = []
    for _ in range(count):
        term = x.astype(BF16)
        terms.append(term)
        x = x - term.astype(F32)
    return terms


def swap_halves(x):
    return pltpu.roll(x, LANES // 2, 1)


def as_column(index_row):
    return jnp.transpose(jnp.broadcast_to(index_row, (LANES, LANES)))


def picks_of(at, width):
    lanes = lane_ids(at.shape)
    return jnp.concatenate(
        [(at == lanes + column).astype(F32).astype(BF16) for column in range(0, width, LANES)], axis=1
    )


def fill_picks(at_ref, picks_ref):
    rows, width = picks_ref.shape
    for start in range(0, rows, LANES):
        picks_ref[start : start + LANES, :] = picks_of(at_ref[start : start + LANES, :], width)


def one_hot(index_row, width):
    chunks = [
        picks_of(as_column(index_row[:, start : start + LANES]), width)
        for start in range(0, index_row.shape[1], LANES)
    ]
    return jnp.concatenate(chunks, axis=0) if len(chunks) > 1 else chunks[0]


def packed_order(share, half, slot):
    part = share // 2
    return (slot % share) // part * half + slot // share * part + slot % part


def fill_order(order_ref, at_ref, share):
    rows = order_ref.shape[1]
    height = 8
    for start in range(0, rows, LANES):
        column = as_column(order_ref[:, start : start + LANES])
        if not share:
            at_ref[start : start + LANES, :] = column
            continue
        for inner in range(0, LANES, height):
            place = packed_order(share, rows // 2, start + inner)
            at_ref[place : place + height, :] = column[inner : inner + height]


def exchange(held, masks, axis):
    size = lax.axis_size(axis)
    combined = [0]
    for mask in masks:
        combined += [other ^ mask for other in combined]
    parts = list(held)
    for mask in combined[1:]:
        parts += [lax.ppermute(part, axis, [(i, i ^ mask) for i in range(size)]) for part in held]
    return parts


def offsets_of(phases):
    offsets = [0]
    for masks in phases:
        combined = [0]
        for mask in masks:
            combined += [other ^ mask for other in combined]
        offsets = [offset ^ mask for mask in combined for offset in offsets]
    return offsets


def join(parts):
    return [jnp.concatenate(parts, axis=0)]


def phases_of(size):
    bits = [1 << bit for bit in reversed(range(size.bit_length() - 1))]
    return [bits[start : start + 2] for start in range(0, len(bits), 2)], [[bit] for bit in bits]


def tied(parts, *earlier):
    return list(lax.optimization_barrier((*parts, *earlier))[: len(parts)])


def picks_kernel(share, order_hbm, a_hbm, picks_ref, copy_ref, order_ref, at_ref, sems):
    fetch = pltpu.make_async_copy(order_hbm, order_ref, sems.at[0])
    copy = pltpu.make_async_copy(a_hbm, copy_ref, sems.at[1])
    fetch.start()
    copy.start()
    fetch.wait()
    fill_order(order_ref, at_ref, share)
    fill_picks(at_ref, picks_ref)
    copy.wait()


def order_picks(order, a_rows, share):
    rows, depth = a_rows.shape
    return pl.pallas_call(
        functools.partial(picks_kernel, share),
        in_specs=[pl.BlockSpec(memory_space=pltpu.HBM)] * 2,
        out_specs=[pl.BlockSpec(memory_space=pltpu.VMEM)] * 2,
        out_shape=[jax.ShapeDtypeStruct((rows, rows), BF16), jax.ShapeDtypeStruct((rows, depth), BF16)],
        scratch_shapes=[
            pltpu.VMEM((1, rows), jnp.int32),
            pltpu.VMEM((rows, LANES), jnp.int32),
            pltpu.SemaphoreType.DMA((2,)),
        ],
        compiler_params=params(),
        cost_estimate=pl.CostEstimate(flops=4 * rows * rows, bytes_accessed=4 * rows * depth, transcendentals=0),
        name="order_picks",
    )(in_hbm(order), in_hbm(a_rows))


def panels_kernel(my_ref, xa_hbm, za_hbm, lead_ref, rest_ref, xa_ref, za_ref, sems):
    copies = [
        pltpu.make_async_copy(xa_hbm, xa_ref, sems.at[0]),
        pltpu.make_async_copy(za_hbm, za_ref, sems.at[1]),
    ]
    for copy in copies:
        copy.start()
    for copy in copies:
        copy.wait()
    lead_ref[0] = jnp.concatenate([xa_ref[:, :PANEL], za_ref[:, :PANEL]], axis=1)
    rest_ref[0, :, :LANES] = jnp.concatenate([xa_ref[:, PANEL:LANES], za_ref[:, PANEL:LANES]], axis=1)
    rest_ref[0, :, LANES : 2 * LANES] = xa_ref[:, LANES:]
    rest_ref[0, :, 2 * LANES :] = za_ref[:, LANES:]


def split_panels(my_index, xa_panel, za_panel):
    depth, columns = xa_panel.shape
    return pl.pallas_call(
        panels_kernel,
        in_specs=[pl.BlockSpec(memory_space=pltpu.SMEM)] + [pl.BlockSpec(memory_space=pltpu.HBM)] * 2,
        out_shape=[
            jax.ShapeDtypeStruct((1, depth, LANES), BF16),
            jax.ShapeDtypeStruct((1, depth, 2 * columns - LANES), BF16),
        ],
        scratch_shapes=[
            pltpu.VMEM((depth, columns), BF16),
            pltpu.VMEM((depth, columns), BF16),
            pltpu.SemaphoreType.DMA((2,)),
        ],
        compiler_params=params(),
        name="split_panels",
    )(my_index, in_hbm(xa_panel), in_hbm(za_panel))


def assemble(my_index, offsets, parts, panel_ref):
    position = 0
    for part in parts:
        for number in range(part.shape[0]):
            depth = part.shape[1]
            start = pl.multiple_of((my_index ^ offsets[position]) * depth, depth)
            panel_ref[pl.ds(start, depth), :] = part[number]
            position += 1


def whole_sum(got):
    pair = got[:, :LANES]
    return (pair + swap_halves(pair)) + got[:, LANES:]


def store_rows(source, target, start, size, sem):
    rows = pl.ds(start, size)
    copy = pltpu.make_async_copy(source.at[rows, :], target.at[rows, :], sem)
    copy.start()
    return copy


def lead_product_kernel(offsets, my_ref, a_ref, picks_ref, *refs):
    parts, (out_hbm, panel_ref, terms_ref, out_ref, sems) = refs[:-5], refs[-5:]
    assemble(my_ref[0], offsets, parts, panel_ref)
    rows = a_ref.shape[0]
    for start in range(0, rows, DEEP_BLOCK):
        both = jnp.dot(a_ref[start : start + DEEP_BLOCK, :], panel_ref[...], preferred_element_type=F32)
        first, second, third = (term.astype(F32) for term in split(both * swap_halves(both), 3))
        near = lane_ids(both.shape) < PANEL
        terms_ref[start : start + DEEP_BLOCK, :LANES] = jnp.where(near, first, second).astype(BF16)
        terms_ref[start : start + DEEP_BLOCK, LANES:] = third.astype(BF16)
    half = rows // 2
    block = half // 2
    stores = []
    for number, start in enumerate(range(0, half, block)):
        low = jnp.dot(picks_ref[start : start + block, :], terms_ref[...], preferred_element_type=F32)
        high = jnp.dot(picks_ref[half + start : half + start + block, :], terms_ref[...], preferred_element_type=F32)
        low, high = whole_sum(low), whole_sum(high)
        out_ref[start : start + block, :] = jnp.where(lane_ids(low.shape) < PANEL, low, high)
        stores.append(store_rows(out_ref, out_hbm, start, block, sems.at[number]))
    for store in stores:
        store.wait()


def lead_products(my_index, a_rows, picks, parts, offsets):
    rows, depth = a_rows.shape
    return pl.pallas_call(
        functools.partial(lead_product_kernel, offsets),
        in_specs=[pl.BlockSpec(memory_space=pltpu.SMEM)] + [pl.BlockSpec(memory_space=pltpu.VMEM)] * (2 + len(parts)),
        out_specs=pl.BlockSpec(memory_space=pltpu.HBM),
        out_shape=pltpu.HBM((rows // 2, LANES), F32),
        scratch_shapes=[
            pltpu.VMEM((depth, LANES), BF16),
            pltpu.VMEM((rows, 2 * LANES), BF16),
            pltpu.VMEM((rows // 2, LANES), F32),
            pltpu.SemaphoreType.DMA((2,)),
        ],
        compiler_params=params(24),
        cost_estimate=pl.CostEstimate(
            flops=2 * rows * (depth + 2 * rows) * LANES, bytes_accessed=2 * rows * depth, transcendentals=0
        ),
        name="lead_products",
    )(my_index, a_rows, picks, *parts)


BIAS = 128
MARGIN = 0.9995
ROUNDER = 1.5 * 2.0**23


def tight_split(part):
    first = -(-part // 16) * 8
    return first if part % 8 == 0 and part <= PANEL and 2 * first - part >= 8 else 0


def words_shape(half, part):
    first = tight_split(part)
    return (half // part * (part + first), LANES) if first else (half, 2 * LANES)


def nearest(x):
    return (x + ROUNDER) - ROUNDER


def rest_product_kernel(offsets, share, part_rows, my_ref, order_ref, a_hbm, *refs):
    parts, (out_ref, a_ref, at_ref, picks_ref, panel_ref, terms_ref, sems) = refs[:-7], refs[-7:]
    rows = a_ref.shape[0]
    half = rows // 2
    block = DEEP_BLOCK
    starts = range(0, rows, block)
    copies = [
        pltpu.make_async_copy(a_hbm.at[pl.ds(start, block), :], a_ref.at[pl.ds(start, block), :], sems.at[i])
        for i, start in enumerate(starts)
    ]
    for copy in copies[:3]:
        copy.start()
    assemble(my_ref[0], offsets, parts, panel_ref)
    fill_order(order_ref, at_ref, share)
    fill_picks(at_ref, picks_ref)

    def product(i):
        copies[i].wait()
        if i + 3 < len(copies):
            copies[i + 3].start()
        return jnp.dot(a_ref[starts[i] : starts[i] + block, :], panel_ref[...], preferred_element_type=F32)

    low_lanes = lane_ids((block, LANES)) < PANEL
    later = product(0)
    for i, start in enumerate(starts):
        both = later
        if i + 1 < len(starts):
            later = product(i + 1)
        near = both[:, :LANES]
        near = near * swap_halves(near)
        far = both[:, LANES : 2 * LANES] * both[:, 2 * LANES :]
        largest = jnp.max(jnp.maximum(jnp.abs(near), jnp.abs(far)), axis=1, keepdims=True)
        exponent = jnp.floor(jnp.log2(jnp.maximum(largest, 1e-30))) + 1.0
        scale = jnp.exp2(15.0 - exponent) * MARGIN
        far = nearest(far * scale)
        near = nearest(near * scale)
        far_top = nearest(far * (1 / 256))
        near_top = nearest(near * (1 / 256))
        here = slice(start, start + block)
        terms_ref[here, :LANES] = far_top.astype(BF16)
        terms_ref[here, LANES : 2 * LANES] = (far - far_top * 256.0).astype(BF16)
        terms_ref[here, 2 * LANES : 3 * LANES] = jnp.where(low_lanes, near_top, near - near_top * 256.0).astype(BF16)
        terms_ref[here, 3 * LANES :] = jnp.broadcast_to(exponent, (block, LANES)).astype(BF16)

    def coded(start, size):
        got = jnp.dot(picks_ref[start : start + size, :], terms_ref[...], preferred_element_type=F32)
        far = got[:, :LANES] * 256.0 + got[:, LANES : 2 * LANES]
        pair = got[:, 2 * LANES : 3 * LANES]
        pair = jnp.where(lane_ids(pair.shape) < PANEL, pair * 256.0, pair)
        near = (pair + swap_halves(pair)).astype(jnp.int32)
        return far.astype(jnp.int32), near, got[:, 3 * LANES :]

    block = half // 2
    first = tight_split(part_rows)
    low_lanes = lane_ids((8, LANES)) < PANEL
    eights = lax.broadcasted_iota(jnp.int32, (8, LANES), 0)
    places = lax.broadcasted_iota(jnp.int32, (part_rows, LANES), 0) + PANEL
    for start in range(0, half, block):
        far_low, near_low, exponent_low = coded(start, block)
        far_high, near_high, exponent_high = coded(half + start, block)
        far = far_low * 65536 + (far_high & 65535)
        if not first:
            near = jnp.where(
                lane_ids(near_low.shape) < PANEL,
                near_low * 65536 + (exponent_low.astype(jnp.int32) + BIAS),
                near_high * 65536 + (exponent_high.astype(jnp.int32) + BIAS),
            )
            out_ref[start : start + block, :LANES] = far
            out_ref[start : start + block, LANES:] = near
            continue
        near = near_low * 65536 + (near_high & 65535)
        second = part_rows - first
        mine = lane_ids((part_rows, LANES)) == places
        for inner in range(0, block, part_rows):
            base = (start + inner) // part_rows * (part_rows + first)
            words = near[inner : inner + part_rows]
            rows = [
                jnp.sum(jnp.where(mine, exponent[inner : inner + part_rows], 0.0), axis=0, keepdims=True)
                for exponent in (exponent_low, exponent_high)
            ]
            rows = jnp.where(eights == 0, rows[0], jnp.where(eights == 1, rows[1], 0.0)).astype(jnp.int32)
            out_ref[base : base + part_rows, :] = far[inner : inner + part_rows]
            base += part_rows
            spare = [words[: first - second - 8]] if first > second + 8 else []
            both = jnp.concatenate([words[first:], rows, *spare], axis=0)
            out_ref[base : base + first, :] = jnp.where(lane_ids(both.shape) < PANEL, words[:first], both)


def rest_products(my_index, order, a_rows, parts, offsets, share, part_rows):
    rows, depth = a_rows.shape
    return pl.pallas_call(
        functools.partial(rest_product_kernel, offsets, share, part_rows),
        in_specs=[
            pl.BlockSpec(memory_space=pltpu.SMEM),
            pl.BlockSpec(memory_space=pltpu.VMEM),
            pl.BlockSpec(memory_space=pltpu.HBM),
        ]
        + [pl.BlockSpec(memory_space=pltpu.VMEM)] * len(parts),
        out_specs=pl.BlockSpec(memory_space=pltpu.VMEM),
        out_shape=jax.ShapeDtypeStruct(words_shape(rows // 2, part_rows), jnp.int32),
        scratch_shapes=[
            pltpu.VMEM((rows, depth), BF16),
            pltpu.VMEM((rows, LANES), jnp.int32),
            pltpu.VMEM((rows, rows), BF16),
            pltpu.VMEM((depth, 3 * LANES), BF16),
            pltpu.VMEM((rows, 4 * LANES), BF16),
            pltpu.SemaphoreType.DMA((rows // DEEP_BLOCK,)),
        ],
        compiler_params=params(32),
        cost_estimate=pl.CostEstimate(
            flops=2 * rows * (3 * depth + 4 * rows) * LANES, bytes_accessed=2 * rows * depth, transcendentals=0
        ),
        name="rest_products",
    )(my_index, order, in_hbm(a_rows), *parts)


def packed_terms(x, terms_ref, start):
    half = x.shape[0]
    first, second, third = (term.astype(F32) for term in split(x, 3))
    near = lane_ids(x.shape) < PANEL
    other = swap_halves(third)
    terms_ref[:half, start : start + LANES] = jnp.where(near, first, swap_halves(second)).astype(BF16)
    terms_ref[half:, start : start + LANES] = jnp.where(near, swap_halves(first), second).astype(BF16)
    terms_ref[:half, start + LANES : start + 2 * LANES] = jnp.where(near, third, other).astype(BF16)
    terms_ref[half:, start + LANES : start + 2 * LANES] = jnp.where(near, other, third).astype(BF16)


def leading_kernel(held, index_ref, arrived_ref, out_ref, terms_ref):
    packed_terms(arrived_ref[...], terms_ref, 0)
    width = -(-held // LANES) * LANES
    picks = one_hot(index_ref[:, :width], terms_ref.shape[0])
    got = whole_sum(jnp.dot(picks, terms_ref[...], preferred_element_type=F32))
    first, second = got[: held // 2], got[held // 2 : held]
    out_ref[0] = jnp.where(lane_ids(first.shape) < PANEL, first, second)


def leading_rows(index, arrived, held):
    rows = index.shape[1]
    return pl.pallas_call(
        functools.partial(leading_kernel, held),
        in_specs=[pl.BlockSpec(memory_space=pltpu.VMEM)] * 2,
        out_specs=pl.BlockSpec(memory_space=pltpu.VMEM),
        out_shape=jax.ShapeDtypeStruct((1, held // 2, LANES), F32),
        scratch_shapes=[pltpu.VMEM((rows, 2 * LANES), BF16)],
        compiler_params=params(),
        cost_estimate=pl.CostEstimate(
            flops=4 * held * rows * LANES, bytes_accessed=2 * rows * LANES, transcendentals=0
        ),
        name="leading_rows",
    )(index, arrived)


def eliminate(block, shift_row):
    rows = lax.broadcasted_iota(jnp.int32, (PANEL, PANEL), 0)
    columns = lax.broadcasted_iota(jnp.int32, (PANEL, PANEL), 1)
    flipped = jnp.transpose(block)
    mirrored = jnp.where(rows >= columns, block, flipped)
    diagonal = shift_row + jnp.sum(jnp.abs(mirrored), axis=0, keepdims=True)
    unit = (rows == columns).astype(F32)
    work = jnp.where(rows == columns, diagonal, mirrored)
    work = jnp.concatenate([work, unit], axis=1)
    height = 8
    groups = [work[start : start + height] for start in range(0, PANEL, height)]
    sublanes = lax.broadcasted_iota(jnp.int32, (height, LANES), 0)
    scaled_rows = []
    for k in range(PANEL):
        home, offset = divmod(k, height)
        row = groups[home][offset : offset + 1, :]
        row = row / row[:, k : k + 1]
        scaled_rows.append(row)
        for g in range(home, PANEL // height):
            column = jnp.broadcast_to(groups[g][:, k : k + 1], (height, LANES))
            if g == home:
                column = jnp.where(sublanes > offset, column, 0.0)
            groups[g] = groups[g] - column * row
    final = jnp.concatenate(groups, axis=0)
    scaled = jnp.concatenate(scaled_rows, axis=0)
    upper = jnp.where(columns >= rows, scaled[:, :PANEL], 0.0)
    pivots = jnp.sum(jnp.where(rows == columns, final[:, :PANEL], 0.0), axis=0, keepdims=True)
    return upper, final[:, PANEL:], pivots


def exact(lhs, rhs, dims):
    return lax.dot_general(lhs, rhs, (dims, ((), ())), precision=lax.Precision.HIGHEST, preferred_element_type=F32)


def update_kernel(offsets, blocks_held, columns, my_ref, index_ref, arrived_ref, shift_ref, resident_hbm, *refs):
    parts = refs[:-12]
    near_hbm, far_hbm, pivots_ref, leading_ref, tail_ref, resident_ref, terms_ref, lead_ref = refs[-12:-4]
    near_ref, far_ref, sem, sems = refs[-4:]
    fetch = pltpu.make_async_copy(resident_hbm, resident_ref, sem)
    fetch.start()
    my_index = my_ref[0]
    size = len(offsets)
    position = 0
    packed = blocks_held * PANEL // 2
    part_rows = PANEL // 2
    for part in parts:
        for number in range(part.shape[0]):
            owner = my_index ^ offsets[position]
            for start in range(0, blocks_held * PANEL, part_rows):
                held, inner = divmod(start, PANEL)
                if start < packed:
                    rows = part[number, start : start + part_rows, :PANEL]
                else:
                    rows = part[number, start - packed : start - packed + part_rows, PANEL:]
                target = pl.multiple_of((held * size + owner) * PANEL + inner, part_rows)
                leading_ref[pl.ds(target, part_rows), :] = rows
            position += 1
    upper, inverse, pivots = eliminate(leading_ref[:PANEL, :], shift_ref[...])
    pivots_ref[...] = pivots
    lower = jnp.transpose(upper)
    needed = tail_ref.shape[1]
    tail = exact(inverse, leading_ref[:needed, :], ((1,), (1,)))
    high, low = split(tail, 2)
    tail_ref[0:PANEL, :] = high
    tail_ref[PANEL : 2 * PANEL, :] = high
    tail_ref[2 * PANEL : 3 * PANEL, :] = low
    tail_ref[3 * PANEL :, :] = low

    block = A_BLOCK
    packed_terms(arrived_ref[...], terms_ref, 0)
    for start in range(0, lead_ref.shape[0], block):
        picks = one_hot(index_ref[:, start : start + block], lead_ref.shape[0])
        got = jnp.dot(picks, terms_ref[...], preferred_element_type=F32)
        lead_ref[start : start + block, :] = whole_sum(got)[:, :PANEL]
    fetch.wait()
    stores = []
    for number, start in enumerate(range(0, lead_ref.shape[0], block)):
        rows_here = slice(start, start + block)
        panel = exact(lead_ref[rows_here, :], inverse, ((1,), (1,))) / pivots
        shown = used = panel
        if start == 0:
            row_ids = lax.broadcasted_iota(jnp.int32, panel.shape, 0)
            top = jnp.logical_and(my_index == 0, row_ids < PANEL)
            used = jnp.where(top, 0.0, panel)
            filled = jnp.concatenate([lower, jnp.zeros((block - PANEL, PANEL), F32)], axis=0)
            shown = jnp.where(top, filled, panel)
        high, low = (term.astype(F32) for term in split(used, 2))
        pair = jnp.concatenate([high, low], axis=1).astype(BF16)
        factors = jnp.concatenate([pair, pair], axis=1)
        update = jnp.dot(factors, tail_ref[...], preferred_element_type=F32)
        shown = jnp.concatenate([shown, jnp.zeros_like(shown)], axis=1)
        near_ref[rows_here, :LANES] = jnp.where(lane_ids(shown.shape) < PANEL, shown, -update[:, :LANES])
        near_ref[rows_here, LANES:] = -update[:, LANES:columns]
        far_ref[rows_here, :] = (resident_ref[rows_here, :].astype(F32) - update[:, columns:]).astype(BF16)
        for which, (source, target) in enumerate(((near_ref, near_hbm), (far_ref, far_hbm))):
            store = pltpu.make_async_copy(
                source.at[pl.ds(start, block), :], target.at[pl.ds(start, block), :], sems.at[which, number]
            )
            store.start()
            stores.append(store)
    for store in stores:
        store.wait()


def updates(my_index, parts, offsets, index, arrived, shift, resident, blocks_held, columns):
    rows, width = resident.shape
    needed = columns + width
    held_rows = len(offsets) * blocks_held * PANEL
    vmem = pl.BlockSpec(memory_space=pltpu.VMEM)
    anywhere = pl.BlockSpec(memory_space=pltpu.HBM)
    return pl.pallas_call(
        functools.partial(update_kernel, offsets, blocks_held, columns),
        in_specs=[pl.BlockSpec(memory_space=pltpu.SMEM), vmem, vmem, vmem, anywhere] + [vmem] * len(parts),
        out_specs=[anywhere, anywhere, vmem],
        out_shape=[
            pltpu.HBM((rows, columns), F32),
            pltpu.HBM((rows, width), BF16),
            jax.ShapeDtypeStruct((1, PANEL), F32),
        ],
        scratch_shapes=[
            pltpu.VMEM((held_rows, PANEL), F32),
            pltpu.VMEM((4 * PANEL, needed), BF16),
            pltpu.VMEM((rows, width), BF16),
            pltpu.VMEM((rows, 2 * LANES), BF16),
            pltpu.VMEM((rows, PANEL), F32),
            pltpu.VMEM((rows, columns), F32),
            pltpu.VMEM((rows, width), BF16),
            pltpu.SemaphoreType.DMA,
            pltpu.SemaphoreType.DMA((2, rows // A_BLOCK)),
        ],
        compiler_params=params(32),
        cost_estimate=pl.CostEstimate(
            flops=2 * rows * needed * 4 * PANEL, bytes_accessed=4 * rows * (columns + width), transcendentals=0
        ),
        name="factor_and_update",
    )(my_index, index, arrived, shift, in_hbm(resident), *parts)


def upper_half(words):
    return (words >> 16).astype(F32)


def lower_half(words):
    return ((words << 16) >> 16).astype(F32)


def loose_values(arrived_ref):
    words = arrived_ref[:, LANES:]
    low_lanes = lane_ids(words.shape) < PANEL
    scale = jnp.exp2(((words & 255) - (BIAS + 15)).astype(F32)) * (1 / MARGIN)
    other = swap_halves(scale)
    near = upper_half(words) * scale
    words = arrived_ref[:, :LANES]
    low = upper_half(words) * jnp.where(low_lanes, scale, other)
    return low, lower_half(words) * jnp.where(low_lanes, other, scale), near


def tight_values(arrived_ref, part_rows, values_ref):
    first = tight_split(part_rows)
    second = part_rows - first
    step = part_rows + first
    sources = arrived_ref.shape[0] // step
    pairs = [arrived_ref[i * step + part_rows + second : i * step + part_rows + second + 2, :] for i in range(sources)]
    spare = jnp.zeros((LANES - 2 * sources, LANES), jnp.int32)
    exponents = jnp.concatenate([*pairs, spare], axis=0)
    scales = jnp.exp2(jnp.transpose(exponents.astype(F32)) - 15.0) * (1 / MARGIN)
    scales = scales[PANEL : PANEL + part_rows]
    low_lanes = lane_ids((part_rows, LANES)) < PANEL
    for i in range(sources):
        base = i * step
        here = slice(i * part_rows, (i + 1) * part_rows)
        low_scale = jnp.broadcast_to(scales[:, 2 * i : 2 * i + 1], (part_rows, LANES))
        high_scale = jnp.broadcast_to(scales[:, 2 * i + 1 : 2 * i + 2], (part_rows, LANES))
        words = arrived_ref[base : base + part_rows, :]
        values_ref[0, here, :] = upper_half(words) * low_scale
        values_ref[1, here, :] = lower_half(words) * high_scale
        words = arrived_ref[base + part_rows : base + step, :]
        words = jnp.concatenate([words, swap_halves(words[:second])], axis=0)
        words = jnp.where(low_lanes, words, swap_halves(words))
        values_ref[2, here, :] = jnp.where(low_lanes, upper_half(words) * low_scale, lower_half(words) * high_scale)
    return values_ref[0], values_ref[1], values_ref[2]


def formed_kernel(
    part_rows, index_ref, arrived_ref, near_hbm, out_hbm, near_ref, terms_ref, out_ref, values_ref, in_sems, out_sems
):
    half = terms_ref.shape[0] // 2
    first = tight_split(part_rows)
    block = A_BLOCK
    starts = range(0, near_ref.shape[0], block)

    def rows_of(ref, start):
        return ref.at[pl.ds(start, block), :]

    fetches = [
        pltpu.make_async_copy(rows_of(near_hbm, start), rows_of(near_ref, start), in_sems.at[i])
        for i, start in enumerate(starts)
    ]
    for fetch in fetches:
        fetch.start()
    low, high, near = loose_values(arrived_ref) if not first else tight_values(arrived_ref, part_rows, values_ref)
    for side, values in enumerate((low, high)):
        one, two = split(values, 2)
        terms_ref[side * half : (side + 1) * half, :LANES] = one
        terms_ref[side * half : (side + 1) * half, LANES : 2 * LANES] = two
    low_lanes = lane_ids(near.shape) < PANEL
    one, two = (term.astype(F32) for term in split(near, 2))
    terms_ref[:half, 2 * LANES :] = jnp.where(low_lanes, one, swap_halves(two)).astype(BF16)
    terms_ref[half:, 2 * LANES :] = jnp.where(low_lanes, swap_halves(one), two).astype(BF16)

    stores = []
    for i, start in enumerate(starts):
        rows_here = slice(start, start + block)
        picks = one_hot(index_ref[:, rows_here], terms_ref.shape[0])
        got = jnp.dot(picks, terms_ref[...], preferred_element_type=F32)
        pair = got[:, 2 * LANES :]
        fetches[i].wait()
        held = near_ref[rows_here, :LANES]
        out_ref[rows_here, :LANES] = jnp.where(
            lane_ids(held.shape) < PANEL, held, (pair + swap_halves(pair)) + held
        )
        out_ref[rows_here, LANES:] = (got[:, :LANES] + got[:, LANES : 2 * LANES]) + near_ref[rows_here, LANES:]
        store = pltpu.make_async_copy(rows_of(out_ref, start), rows_of(out_hbm, start), out_sems.at[i])
        store.start()
        stores.append(store)
    for store in stores:
        store.wait()


def formed_columns(index, arrived, near, part_rows):
    rows, columns = near.shape
    vmem = pl.BlockSpec(memory_space=pltpu.VMEM)
    anywhere = pl.BlockSpec(memory_space=pltpu.HBM)
    return pl.pallas_call(
        functools.partial(formed_kernel, part_rows),
        in_specs=[vmem, vmem, anywhere],
        out_specs=anywhere,
        out_shape=pltpu.HBM((rows, columns), F32),
        input_output_aliases={2: 0},
        scratch_shapes=[
            pltpu.VMEM((rows, columns), F32),
            pltpu.VMEM((rows, 3 * LANES), BF16),
            pltpu.VMEM((rows, columns), F32),
            pltpu.VMEM((3, rows // 2, LANES), F32),
            pltpu.SemaphoreType.DMA((rows // A_BLOCK,)),
            pltpu.SemaphoreType.DMA((rows // A_BLOCK,)),
        ],
        compiler_params=params(32),
        cost_estimate=pl.CostEstimate(
            flops=8 * rows * rows * LANES, bytes_accessed=8 * rows * columns, transcendentals=0
        ),
        name="formed_columns",
    )(index, arrived, near)


def swap_rows(x, group):
    rows, width = x.shape
    return lax.all_to_all(
        x.reshape(group, rows // group, width), "wide", split_axis=0, concat_axis=0, tiled=True
    ).reshape(rows, width)


def on_device(a_rows, xa_panel, za_panel, send_order, recv_order, shift, resident):
    rows = a_rows.shape[0]
    columns = xa_panel.shape[1]
    group = lax.axis_size("wide")
    my_index = lax.axis_index("wide").astype(jnp.int32).reshape(1)
    share = rows // group
    half = rows // 2
    few, apart = phases_of(group)

    order, packing = send_order, share
    if share % 16:
        order = send_order.reshape(group, 2, share // 2).transpose(1, 0, 2).reshape(1, rows)
        packing = 0
    source, slot = recv_order // share, recv_order % share
    index = (slot // (share // 2)) * half + source * (share // 2) + slot % (share // 2)

    lead_panel, rest_panel = split_panels(my_index, xa_panel, za_panel)
    send_picks, a_copy = order_picks(order, a_rows, packing)
    steps = few[:-1] + [[mask] for mask in few[-1]]
    lead_parts = join(exchange([lead_panel], steps[0], "wide"))
    rest_parts = exchange(tied([rest_panel], *lead_parts), apart[0], "wide")
    for masks in steps[1:-1]:
        lead_parts = exchange(join(lead_parts), masks, "wide")
    lead_parts = exchange(tied(join(lead_parts), send_picks), steps[-1], "wide")

    lead_out = lead_products(my_index, a_copy, send_picks, lead_parts, offsets_of(steps))
    lead_in = swap_rows(lead_out, group)
    rest_parts = tied(rest_parts, lead_out)
    for masks in apart[1:-1]:
        rest_parts = exchange(join(rest_parts), masks, "wide")
    other_parts = exchange(rest_parts[:1], apart[-1], "wide")[1:]

    needed = columns + resident.shape[1]
    blocks_held = -(-needed // (PANEL * group))
    leading_parts = [leading_rows(index, lead_in, blocks_held * PANEL)]
    for masks in few:
        leading_parts = exchange(join(leading_parts), masks, "wide")
        if masks is few[0]:
            later_parts = exchange(tied(rest_parts[1:], *leading_parts), apart[-1], "wide")
    late = len(later_parts) // 2
    rest_parts = rest_parts + other_parts + later_parts[late:]
    rest_out = rest_products(
        my_index, order, a_rows, rest_parts, offsets_of(apart), packing, share // 2
    )
    rest_in = swap_rows(tied([rest_out], *leading_parts)[0], group)
    near, updated, pivots = updates(
        my_index,
        leading_parts,
        offsets_of(few),
        index,
        tied([lead_in], rest_out)[0],
        shift[None, :],
        resident,
        blocks_held,
        columns,
    )
    factored = formed_columns(index, rest_in, near, share // 2)
    return (factored, updated, pivots[0])


def solution(mesh):
    placed = (
        P(("parts", "wide"), None),
        P(("parts", "wide"), None),
        P(("parts", "wide"), None),
        P(("parts", "wide"), None),
        P(("parts", "wide"), None),
        P("parts"),
        P(("parts", "wide"), None),
    )
    return jax.shard_map(
        on_device,
        mesh=mesh,
        in_specs=placed,
        out_specs=(P(("parts", "wide"), None), P(("parts", "wide"), None), P("parts")),
        check_vma=False,
    )
```

```python
import functools

import jax
import jax.numpy as jnp
from jax import lax
from jax.experimental import pallas as pl
from jax.experimental.pallas import tpu as pltpu
from jax.sharding import PartitionSpec as P

PANEL = 64
LANES = 128
A_BLOCK = 640
DEEP_BLOCK = 256
F32 = jnp.float32
BF16 = jnp.bfloat16
MIB = 1024 * 1024


def params(mebibytes=12):
    return pltpu.CompilerParams(vmem_limit_bytes=mebibytes * MIB)


def in_hbm(x):
    return pltpu.with_memory_space_constraint(x, pltpu.HBM)


def lane_ids(shape):
    return lax.broadcasted_iota(jnp.int32, shape, len(shape) - 1)


def split(x, count):
    terms = []
    for _ in range(count):
        term = x.astype(BF16)
        terms.append(term)
        x = x - term.astype(F32)
    return terms


def swap_halves(x):
    return pltpu.roll(x, LANES // 2, 1)


def as_column(index_row):
    return jnp.transpose(jnp.broadcast_to(index_row, (LANES, LANES)))


def picks_of(at, width):
    lanes = lane_ids(at.shape)
    return jnp.concatenate(
        [(at == lanes + column).astype(F32).astype(BF16) for column in range(0, width, LANES)], axis=1
    )


def fill_picks(at_ref, picks_ref):
    rows, width = picks_ref.shape
    for start in range(0, rows, LANES):
        picks_ref[start : start + LANES, :] = picks_of(at_ref[start : start + LANES, :], width)


def one_hot(index_row, width):
    chunks = [
        picks_of(as_column(index_row[:, start : start + LANES]), width)
        for start in range(0, index_row.shape[1], LANES)
    ]
    return jnp.concatenate(chunks, axis=0) if len(chunks) > 1 else chunks[0]


def packed_order(share, half, slot):
    part = share // 2
    return (slot % share) // part * half + slot // share * part + slot % part


def fill_order(order_ref, at_ref, share):
    rows = order_ref.shape[1]
    height = 8
    for start in range(0, rows, LANES):
        column = as_column(order_ref[:, start : start + LANES])
        if not share:
            at_ref[start : start + LANES, :] = column
            continue
        for inner in range(0, LANES, height):
            place = packed_order(share, rows // 2, start + inner)
            at_ref[place : place + height, :] = column[inner : inner + height]


def exchange(held, masks, axis):
    size = lax.axis_size(axis)
    combined = [0]
    for mask in masks:
        combined += [other ^ mask for other in combined]
    parts = list(held)
    for mask in combined[1:]:
        parts += [lax.ppermute(part, axis, [(i, i ^ mask) for i in range(size)]) for part in held]
    return parts


def offsets_of(phases):
    offsets = [0]
    for masks in phases:
        combined = [0]
        for mask in masks:
            combined += [other ^ mask for other in combined]
        offsets = [offset ^ mask for mask in combined for offset in offsets]
    return offsets


def join(parts):
    return [jnp.concatenate(parts, axis=0)]


def phases_of(size):
    bits = [1 << bit for bit in reversed(range(size.bit_length() - 1))]
    return [bits[start : start + 2] for start in range(0, len(bits), 2)], [[bit] for bit in bits]


def tied(parts, *earlier):
    return list(lax.optimization_barrier((*parts, *earlier))[: len(parts)])


def picks_kernel(share, order_hbm, a_hbm, picks_ref, copy_ref, order_ref, at_ref, sems):
    fetch = pltpu.make_async_copy(order_hbm, order_ref, sems.at[0])
    copy = pltpu.make_async_copy(a_hbm, copy_ref, sems.at[1])
    fetch.start()
    copy.start()
    fetch.wait()
    fill_order(order_ref, at_ref, share)
    fill_picks(at_ref, picks_ref)
    copy.wait()


def order_picks(order, a_rows, share):
    rows, depth = a_rows.shape
    return pl.pallas_call(
        functools.partial(picks_kernel, share),
        in_specs=[pl.BlockSpec(memory_space=pltpu.HBM)] * 2,
        out_specs=[pl.BlockSpec(memory_space=pltpu.VMEM)] * 2,
        out_shape=[jax.ShapeDtypeStruct((rows, rows), BF16), jax.ShapeDtypeStruct((rows, depth), BF16)],
        scratch_shapes=[
            pltpu.VMEM((1, rows), jnp.int32),
            pltpu.VMEM((rows, LANES), jnp.int32),
            pltpu.SemaphoreType.DMA((2,)),
        ],
        compiler_params=params(),
        cost_estimate=pl.CostEstimate(flops=4 * rows * rows, bytes_accessed=4 * rows * depth, transcendentals=0),
        name="order_picks",
    )(in_hbm(order), in_hbm(a_rows))


def panels_kernel(my_ref, xa_hbm, za_hbm, lead_ref, rest_ref, xa_ref, za_ref, sems):
    copies = [
        pltpu.make_async_copy(xa_hbm, xa_ref, sems.at[0]),
        pltpu.make_async_copy(za_hbm, za_ref, sems.at[1]),
    ]
    for copy in copies:
        copy.start()
    for copy in copies:
        copy.wait()
    lead_ref[0] = jnp.concatenate([xa_ref[:, :PANEL], za_ref[:, :PANEL]], axis=1)
    rest_ref[0, :, :LANES] = jnp.concatenate([xa_ref[:, PANEL:LANES], za_ref[:, PANEL:LANES]], axis=1)
    rest_ref[0, :, LANES : 2 * LANES] = xa_ref[:, LANES:]
    rest_ref[0, :, 2 * LANES :] = za_ref[:, LANES:]


def split_panels(my_index, xa_panel, za_panel):
    depth, columns = xa_panel.shape
    return pl.pallas_call(
        panels_kernel,
        in_specs=[pl.BlockSpec(memory_space=pltpu.SMEM)] + [pl.BlockSpec(memory_space=pltpu.HBM)] * 2,
        out_shape=[
            jax.ShapeDtypeStruct((1, depth, LANES), BF16),
            jax.ShapeDtypeStruct((1, depth, 2 * columns - LANES), BF16),
        ],
        scratch_shapes=[
            pltpu.VMEM((depth, columns), BF16),
            pltpu.VMEM((depth, columns), BF16),
            pltpu.SemaphoreType.DMA((2,)),
        ],
        compiler_params=params(),
        name="split_panels",
    )(my_index, in_hbm(xa_panel), in_hbm(za_panel))


def assemble(my_index, offsets, parts, panel_ref):
    position = 0
    for part in parts:
        for number in range(part.shape[0]):
            depth = part.shape[1]
            start = pl.multiple_of((my_index ^ offsets[position]) * depth, depth)
            panel_ref[pl.ds(start, depth), :] = part[number]
            position += 1


def whole_sum(got):
    pair = got[:, :LANES]
    return (pair + swap_halves(pair)) + got[:, LANES:]


def store_rows(source, target, start, size, sem):
    rows = pl.ds(start, size)
    copy = pltpu.make_async_copy(source.at[rows, :], target.at[rows, :], sem)
    copy.start()
    return copy


def lead_product_kernel(offsets, my_ref, a_ref, picks_ref, *refs):
    parts, (out_hbm, panel_ref, terms_ref, out_ref, sems) = refs[:-5], refs[-5:]
    assemble(my_ref[0], offsets, parts, panel_ref)
    rows = a_ref.shape[0]
    for start in range(0, rows, DEEP_BLOCK):
        both = jnp.dot(a_ref[start : start + DEEP_BLOCK, :], panel_ref[...], preferred_element_type=F32)
        first, second, third = (term.astype(F32) for term in split(both * swap_halves(both), 3))
        near = lane_ids(both.shape) < PANEL
        terms_ref[start : start + DEEP_BLOCK, :LANES] = jnp.where(near, first, second).astype(BF16)
        terms_ref[start : start + DEEP_BLOCK, LANES:] = third.astype(BF16)
    half = rows // 2
    block = half // 2
    stores = []
    for number, start in enumerate(range(0, half, block)):
        low = jnp.dot(picks_ref[start : start + block, :], terms_ref[...], preferred_element_type=F32)
        high = jnp.dot(picks_ref[half + start : half + start + block, :], terms_ref[...], preferred_element_type=F32)
        low, high = whole_sum(low), whole_sum(high)
        out_ref[start : start + block, :] = jnp.where(lane_ids(low.shape) < PANEL, low, high)
        stores.append(store_rows(out_ref, out_hbm, start, block, sems.at[number]))
    for store in stores:
        store.wait()


def lead_products(my_index, a_rows, picks, parts, offsets):
    rows, depth = a_rows.shape
    return pl.pallas_call(
        functools.partial(lead_product_kernel, offsets),
        in_specs=[pl.BlockSpec(memory_space=pltpu.SMEM)] + [pl.BlockSpec(memory_space=pltpu.VMEM)] * (2 + len(parts)),
        out_specs=pl.BlockSpec(memory_space=pltpu.HBM),
        out_shape=pltpu.HBM((rows // 2, LANES), F32),
        scratch_shapes=[
            pltpu.VMEM((depth, LANES), BF16),
            pltpu.VMEM((rows, 2 * LANES), BF16),
            pltpu.VMEM((rows // 2, LANES), F32),
            pltpu.SemaphoreType.DMA((2,)),
        ],
        compiler_params=params(24),
        cost_estimate=pl.CostEstimate(
            flops=2 * rows * (depth + 2 * rows) * LANES, bytes_accessed=2 * rows * depth, transcendentals=0
        ),
        name="lead_products",
    )(my_index, a_rows, picks, *parts)


BIAS = 128
MARGIN = 0.9995
ROUNDER = 1.5 * 2.0**23


def tight_split(part):
    first = -(-part // 16) * 8
    return first if part % 8 == 0 and part <= PANEL and 2 * first - part >= 8 else 0


def words_shape(half, part):
    first = tight_split(part)
    return (half // part * (part + first), LANES) if first else (half, 2 * LANES)


def nearest(x):
    return (x + ROUNDER) - ROUNDER


def rest_product_kernel(offsets, share, part_rows, my_ref, order_ref, a_hbm, *refs):
    parts, (out_ref, a_ref, at_ref, picks_ref, panel_ref, terms_ref, sems) = refs[:-7], refs[-7:]
    rows = a_ref.shape[0]
    half = rows // 2
    block = DEEP_BLOCK
    starts = range(0, rows, block)
    copies = [
        pltpu.make_async_copy(a_hbm.at[pl.ds(start, block), :], a_ref.at[pl.ds(start, block), :], sems.at[i])
        for i, start in enumerate(starts)
    ]
    for copy in copies[:3]:
        copy.start()
    assemble(my_ref[0], offsets, parts, panel_ref)
    fill_order(order_ref, at_ref, share)
    fill_picks(at_ref, picks_ref)

    def product(i):
        copies[i].wait()
        if i + 3 < len(copies):
            copies[i + 3].start()
        return jnp.dot(a_ref[starts[i] : starts[i] + block, :], panel_ref[...], preferred_element_type=F32)

    low_lanes = lane_ids((block, LANES)) < PANEL
    later = product(0)
    for i, start in enumerate(starts):
        both = later
        if i + 1 < len(starts):
            later = product(i + 1)
        near = both[:, :LANES]
        near = near * swap_halves(near)
        far = both[:, LANES : 2 * LANES] * both[:, 2 * LANES :]
        largest = jnp.max(jnp.maximum(jnp.abs(near), jnp.abs(far)), axis=1, keepdims=True)
        exponent = jnp.floor(jnp.log2(jnp.maximum(largest, 1e-30))) + 1.0
        scale = jnp.exp2(15.0 - exponent) * MARGIN
        far = nearest(far * scale)
        near = nearest(near * scale)
        far_top = nearest(far * (1 / 256))
        near_top = nearest(near * (1 / 256))
        here = slice(start, start + block)
        terms_ref[here, :LANES] = far_top.astype(BF16)
        terms_ref[here, LANES : 2 * LANES] = (far - far_top * 256.0).astype(BF16)
        terms_ref[here, 2 * LANES : 3 * LANES] = jnp.where(low_lanes, near_top, near - near_top * 256.0).astype(BF16)
        terms_ref[here, 3 * LANES :] = jnp.broadcast_to(exponent, (block, LANES)).astype(BF16)

    def coded(start, size):
        got = jnp.dot(picks_ref[start : start + size, :], terms_ref[...], preferred_element_type=F32)
        far = got[:, :LANES] * 256.0 + got[:, LANES : 2 * LANES]
        pair = got[:, 2 * LANES : 3 * LANES]
        pair = jnp.where(lane_ids(pair.shape) < PANEL, pair * 256.0, pair)
        near = (pair + swap_halves(pair)).astype(jnp.int32)
        return far.astype(jnp.int32), near, got[:, 3 * LANES :]

    block = half // 2
    first = tight_split(part_rows)
    low_lanes = lane_ids((8, LANES)) < PANEL
    eights = lax.broadcasted_iota(jnp.int32, (8, LANES), 0)
    places = lax.broadcasted_iota(jnp.int32, (part_rows, LANES), 0) + PANEL
    for start in range(0, half, block):
        far_low, near_low, exponent_low = coded(start, block)
        far_high, near_high, exponent_high = coded(half + start, block)
        far = far_low * 65536 + (far_high & 65535)
        if not first:
            near = jnp.where(
                lane_ids(near_low.shape) < PANEL,
                near_low * 65536 + (exponent_low.astype(jnp.int32) + BIAS),
                near_high * 65536 + (exponent_high.astype(jnp.int32) + BIAS),
            )
            out_ref[start : start + block, :LANES] = far
            out_ref[start : start + block, LANES:] = near
            continue
        near = near_low * 65536 + (near_high & 65535)
        second = part_rows - first
        mine = lane_ids((part_rows, LANES)) == places
        for inner in range(0, block, part_rows):
            base = (start + inner) // part_rows * (part_rows + first)
            words = near[inner : inner + part_rows]
            rows = [
                jnp.sum(jnp.where(mine, exponent[inner : inner + part_rows], 0.0), axis=0, keepdims=True)
                for exponent in (exponent_low, exponent_high)
            ]
            rows = jnp.where(eights == 0, rows[0], jnp.where(eights == 1, rows[1], 0.0)).astype(jnp.int32)
            out_ref[base : base + part_rows, :] = far[inner : inner + part_rows]
            base += part_rows
            spare = [words[: first - second - 8]] if first > second + 8 else []
            both = jnp.concatenate([words[first:], rows, *spare], axis=0)
            out_ref[base : base + first, :] = jnp.where(lane_ids(both.shape) < PANEL, words[:first], both)


def rest_products(my_index, order, a_rows, parts, offsets, share, part_rows):
    rows, depth = a_rows.shape
    return pl.pallas_call(
        functools.partial(rest_product_kernel, offsets, share, part_rows),
        in_specs=[
            pl.BlockSpec(memory_space=pltpu.SMEM),
            pl.BlockSpec(memory_space=pltpu.VMEM),
            pl.BlockSpec(memory_space=pltpu.HBM),
        ]
        + [pl.BlockSpec(memory_space=pltpu.VMEM)] * len(parts),
        out_specs=pl.BlockSpec(memory_space=pltpu.VMEM),
        out_shape=jax.ShapeDtypeStruct(words_shape(rows // 2, part_rows), jnp.int32),
        scratch_shapes=[
            pltpu.VMEM((rows, depth), BF16),
            pltpu.VMEM((rows, LANES), jnp.int32),
            pltpu.VMEM((rows, rows), BF16),
            pltpu.VMEM((depth, 3 * LANES), BF16),
            pltpu.VMEM((rows, 4 * LANES), BF16),
            pltpu.SemaphoreType.DMA((rows // DEEP_BLOCK,)),
        ],
        compiler_params=params(32),
        cost_estimate=pl.CostEstimate(
            flops=2 * rows * (3 * depth + 4 * rows) * LANES, bytes_accessed=2 * rows * depth, transcendentals=0
        ),
        name="rest_products",
    )(my_index, order, in_hbm(a_rows), *parts)


def packed_terms(x, terms_ref, start):
    half = x.shape[0]
    first, second, third = (term.astype(F32) for term in split(x, 3))
    near = lane_ids(x.shape) < PANEL
    other = swap_halves(third)
    terms_ref[:half, start : start + LANES] = jnp.where(near, first, swap_halves(second)).astype(BF16)
    terms_ref[half:, start : start + LANES] = jnp.where(near, swap_halves(first), second).astype(BF16)
    terms_ref[:half, start + LANES : start + 2 * LANES] = jnp.where(near, third, other).astype(BF16)
    terms_ref[half:, start + LANES : start + 2 * LANES] = jnp.where(near, other, third).astype(BF16)


def leading_kernel(held, index_ref, arrived_ref, out_ref, terms_ref):
    packed_terms(arrived_ref[...], terms_ref, 0)
    width = -(-held // LANES) * LANES
    picks = one_hot(index_ref[:, :width], terms_ref.shape[0])
    got = whole_sum(jnp.dot(picks, terms_ref[...], preferred_element_type=F32))
    first, second = got[: held // 2], got[held // 2 : held]
    out_ref[0] = jnp.where(lane_ids(first.shape) < PANEL, first, second)


def leading_rows(index, arrived, held):
    rows = index.shape[1]
    return pl.pallas_call(
        functools.partial(leading_kernel, held),
        in_specs=[pl.BlockSpec(memory_space=pltpu.VMEM)] * 2,
        out_specs=pl.BlockSpec(memory_space=pltpu.VMEM),
        out_shape=jax.ShapeDtypeStruct((1, held // 2, LANES), F32),
        scratch_shapes=[pltpu.VMEM((rows, 2 * LANES), BF16)],
        compiler_params=params(),
        cost_estimate=pl.CostEstimate(
            flops=4 * held * rows * LANES, bytes_accessed=2 * rows * LANES, transcendentals=0
        ),
        name="leading_rows",
    )(index, arrived)


def eliminate(block, shift_row):
    rows = lax.broadcasted_iota(jnp.int32, (PANEL, PANEL), 0)
    columns = lax.broadcasted_iota(jnp.int32, (PANEL, PANEL), 1)
    flipped = jnp.transpose(block)
    mirrored = jnp.where(rows >= columns, block, flipped)
    diagonal = shift_row + jnp.sum(jnp.abs(mirrored), axis=0, keepdims=True)
    unit = (rows == columns).astype(F32)
    work = jnp.where(rows == columns, diagonal, mirrored)
    work = jnp.concatenate([work, unit], axis=1)
    height = 8
    groups = [work[start : start + height] for start in range(0, PANEL, height)]
    sublanes = lax.broadcasted_iota(jnp.int32, (height, LANES), 0)
    scaled_rows = []
    for k in range(PANEL):
        home, offset = divmod(k, height)
        row = groups[home][offset : offset + 1, :]
        row = row / row[:, k : k + 1]
        scaled_rows.append(row)
        for g in range(home, PANEL // height):
            column = jnp.broadcast_to(groups[g][:, k : k + 1], (height, LANES))
            if g == home:
                column = jnp.where(sublanes > offset, column, 0.0)
            groups[g] = groups[g] - column * row
    final = jnp.concatenate(groups, axis=0)
    scaled = jnp.concatenate(scaled_rows, axis=0)
    upper = jnp.where(columns >= rows, scaled[:, :PANEL], 0.0)
    pivots = jnp.sum(jnp.where(rows == columns, final[:, :PANEL], 0.0), axis=0, keepdims=True)
    return upper, final[:, PANEL:], pivots


def exact(lhs, rhs, dims):
    return lax.dot_general(lhs, rhs, (dims, ((), ())), precision=lax.Precision.HIGHEST, preferred_element_type=F32)


def update_kernel(offsets, blocks_held, columns, my_ref, index_ref, arrived_ref, shift_ref, resident_hbm, *refs):
    parts = refs[:-12]
    near_hbm, far_hbm, pivots_ref, leading_ref, tail_ref, resident_ref, terms_ref, lead_ref = refs[-12:-4]
    near_ref, far_ref, sem, sems = refs[-4:]
    fetch = pltpu.make_async_copy(resident_hbm, resident_ref, sem)
    fetch.start()
    my_index = my_ref[0]
    size = len(offsets)
    position = 0
    packed = blocks_held * PANEL // 2
    part_rows = PANEL // 2
    for part in parts:
        for number in range(part.shape[0]):
            owner = my_index ^ offsets[position]
            for start in range(0, blocks_held * PANEL, part_rows):
                held, inner = divmod(start, PANEL)
                if start < packed:
                    rows = part[number, start : start + part_rows, :PANEL]
                else:
                    rows = part[number, start - packed : start - packed + part_rows, PANEL:]
                target = pl.multiple_of((held * size + owner) * PANEL + inner, part_rows)
                leading_ref[pl.ds(target, part_rows), :] = rows
            position += 1
    upper, inverse, pivots = eliminate(leading_ref[:PANEL, :], shift_ref[...])
    pivots_ref[...] = pivots
    lower = jnp.transpose(upper)
    needed = tail_ref.shape[1]
    tail = exact(inverse, leading_ref[:needed, :], ((1,), (1,)))
    high, low = split(tail, 2)
    tail_ref[0:PANEL, :] = high
    tail_ref[PANEL : 2 * PANEL, :] = high
    tail_ref[2 * PANEL : 3 * PANEL, :] = low
    tail_ref[3 * PANEL :, :] = low

    block = A_BLOCK
    packed_terms(arrived_ref[...], terms_ref, 0)
    for start in range(0, lead_ref.shape[0], block):
        picks = one_hot(index_ref[:, start : start + block], lead_ref.shape[0])
        got = jnp.dot(picks, terms_ref[...], preferred_element_type=F32)
        lead_ref[start : start + block, :] = whole_sum(got)[:, :PANEL]
    fetch.wait()
    stores = []
    for number, start in enumerate(range(0, lead_ref.shape[0], block)):
        rows_here = slice(start, start + block)
        panel = exact(lead_ref[rows_here, :], inverse, ((1,), (1,))) / pivots
        shown = used = panel
        if start == 0:
            row_ids = lax.broadcasted_iota(jnp.int32, panel.shape, 0)
            top = jnp.logical_and(my_index == 0, row_ids < PANEL)
            used = jnp.where(top, 0.0, panel)
            filled = jnp.concatenate([lower, jnp.zeros((block - PANEL, PANEL), F32)], axis=0)
            shown = jnp.where(top, filled, panel)
        high, low = (term.astype(F32) for term in split(used, 2))
        pair = jnp.concatenate([high, low], axis=1).astype(BF16)
        factors = jnp.concatenate([pair, pair], axis=1)
        update = jnp.dot(factors, tail_ref[...], preferred_element_type=F32)
        shown = jnp.concatenate([shown, jnp.zeros_like(shown)], axis=1)
        near_ref[rows_here, :LANES] = jnp.where(lane_ids(shown.shape) < PANEL, shown, -update[:, :LANES])
        near_ref[rows_here, LANES:] = -update[:, LANES:columns]
        far_ref[rows_here, :] = (resident_ref[rows_here, :].astype(F32) - update[:, columns:]).astype(BF16)
        for which, (source, target) in enumerate(((near_ref, near_hbm), (far_ref, far_hbm))):
            store = pltpu.make_async_copy(
                source.at[pl.ds(start, block), :], target.at[pl.ds(start, block), :], sems.at[which, number]
            )
            store.start()
            stores.append(store)
    for store in stores:
        store.wait()


def updates(my_index, parts, offsets, index, arrived, shift, resident, blocks_held, columns):
    rows, width = resident.shape
    needed = columns + width
    held_rows = len(offsets) * blocks_held * PANEL
    vmem = pl.BlockSpec(memory_space=pltpu.VMEM)
    anywhere = pl.BlockSpec(memory_space=pltpu.HBM)
    return pl.pallas_call(
        functools.partial(update_kernel, offsets, blocks_held, columns),
        in_specs=[pl.BlockSpec(memory_space=pltpu.SMEM), vmem, vmem, vmem, anywhere] + [vmem] * len(parts),
        out_specs=[anywhere, anywhere, vmem],
        out_shape=[
            pltpu.HBM((rows, columns), F32),
            pltpu.HBM((rows, width), BF16),
            jax.ShapeDtypeStruct((1, PANEL), F32),
        ],
        scratch_shapes=[
            pltpu.VMEM((held_rows, PANEL), F32),
            pltpu.VMEM((4 * PANEL, needed), BF16),
            pltpu.VMEM((rows, width), BF16),
            pltpu.VMEM((rows, 2 * LANES), BF16),
            pltpu.VMEM((rows, PANEL), F32),
            pltpu.VMEM((rows, columns), F32),
            pltpu.VMEM((rows, width), BF16),
            pltpu.SemaphoreType.DMA,
            pltpu.SemaphoreType.DMA((2, rows // A_BLOCK)),
        ],
        compiler_params=params(32),
        cost_estimate=pl.CostEstimate(
            flops=2 * rows * needed * 4 * PANEL, bytes_accessed=4 * rows * (columns + width), transcendentals=0
        ),
        name="factor_and_update",
    )(my_index, index, arrived, shift, in_hbm(resident), *parts)


def upper_half(words):
    return (words >> 16).astype(F32)


def lower_half(words):
    return ((words << 16) >> 16).astype(F32)


def loose_values(arrived_ref):
    words = arrived_ref[:, LANES:]
    low_lanes = lane_ids(words.shape) < PANEL
    scale = jnp.exp2(((words & 255) - (BIAS + 15)).astype(F32)) * (1 / MARGIN)
    other = swap_halves(scale)
    near = upper_half(words) * scale
    words = arrived_ref[:, :LANES]
    low = upper_half(words) * jnp.where(low_lanes, scale, other)
    return low, lower_half(words) * jnp.where(low_lanes, other, scale), near


def tight_values(arrived_ref, part_rows, values_ref):
    first = tight_split(part_rows)
    second = part_rows - first
    step = part_rows + first
    sources = arrived_ref.shape[0] // step
    pairs = [arrived_ref[i * step + part_rows + second : i * step + part_rows + second + 2, :] for i in range(sources)]
    spare = jnp.zeros((LANES - 2 * sources, LANES), jnp.int32)
    exponents = jnp.concatenate([*pairs, spare], axis=0)
    scales = jnp.exp2(jnp.transpose(exponents.astype(F32)) - 15.0) * (1 / MARGIN)
    scales = scales[PANEL : PANEL + part_rows]
    low_lanes = lane_ids((part_rows, LANES)) < PANEL
    for i in range(sources):
        base = i * step
        here = slice(i * part_rows, (i + 1) * part_rows)
        low_scale = jnp.broadcast_to(scales[:, 2 * i : 2 * i + 1], (part_rows, LANES))
        high_scale = jnp.broadcast_to(scales[:, 2 * i + 1 : 2 * i + 2], (part_rows, LANES))
        words = arrived_ref[base : base + part_rows, :]
        values_ref[0, here, :] = upper_half(words) * low_scale
        values_ref[1, here, :] = lower_half(words) * high_scale
        words = arrived_ref[base + part_rows : base + step, :]
        words = jnp.concatenate([words, swap_halves(words[:second])], axis=0)
        words = jnp.where(low_lanes, words, swap_halves(words))
        values_ref[2, here, :] = jnp.where(low_lanes, upper_half(words) * low_scale, lower_half(words) * high_scale)
    return values_ref[0], values_ref[1], values_ref[2]


def formed_kernel(
    part_rows, index_ref, arrived_ref, near_hbm, out_hbm, near_ref, terms_ref, out_ref, values_ref, in_sems, out_sems
):
    half = terms_ref.shape[0] // 2
    first = tight_split(part_rows)
    block = A_BLOCK
    starts = range(0, near_ref.shape[0], block)

    def rows_of(ref, start):
        return ref.at[pl.ds(start, block), :]

    fetches = [
        pltpu.make_async_copy(rows_of(near_hbm, start), rows_of(near_ref, start), in_sems.at[i])
        for i, start in enumerate(starts)
    ]
    for fetch in fetches:
        fetch.start()
    low, high, near = loose_values(arrived_ref) if not first else tight_values(arrived_ref, part_rows, values_ref)
    for side, values in enumerate((low, high)):
        one, two = split(values, 2)
        terms_ref[side * half : (side + 1) * half, :LANES] = one
        terms_ref[side * half : (side + 1) * half, LANES : 2 * LANES] = two
    low_lanes = lane_ids(near.shape) < PANEL
    one, two = (term.astype(F32) for term in split(near, 2))
    terms_ref[:half, 2 * LANES :] = jnp.where(low_lanes, one, swap_halves(two)).astype(BF16)
    terms_ref[half:, 2 * LANES :] = jnp.where(low_lanes, swap_halves(one), two).astype(BF16)

    stores = []
    for i, start in enumerate(starts):
        rows_here = slice(start, start + block)
        picks = one_hot(index_ref[:, rows_here], terms_ref.shape[0])
        got = jnp.dot(picks, terms_ref[...], preferred_element_type=F32)
        pair = got[:, 2 * LANES :]
        fetches[i].wait()
        held = near_ref[rows_here, :LANES]
        out_ref[rows_here, :LANES] = jnp.where(
            lane_ids(held.shape) < PANEL, held, (pair + swap_halves(pair)) + held
        )
        out_ref[rows_here, LANES:] = (got[:, :LANES] + got[:, LANES : 2 * LANES]) + near_ref[rows_here, LANES:]
        store = pltpu.make_async_copy(rows_of(out_ref, start), rows_of(out_hbm, start), out_sems.at[i])
        store.start()
        stores.append(store)
    for store in stores:
        store.wait()


def formed_columns(index, arrived, near, part_rows):
    rows, columns = near.shape
    vmem = pl.BlockSpec(memory_space=pltpu.VMEM)
    anywhere = pl.BlockSpec(memory_space=pltpu.HBM)
    return pl.pallas_call(
        functools.partial(formed_kernel, part_rows),
        in_specs=[vmem, vmem, anywhere],
        out_specs=anywhere,
        out_shape=pltpu.HBM((rows, columns), F32),
        input_output_aliases={2: 0},
        scratch_shapes=[
            pltpu.VMEM((rows, columns), F32),
            pltpu.VMEM((rows, 3 * LANES), BF16),
            pltpu.VMEM((rows, columns), F32),
            pltpu.VMEM((3, rows // 2, LANES), F32),
            pltpu.SemaphoreType.DMA((rows // A_BLOCK,)),
            pltpu.SemaphoreType.DMA((rows // A_BLOCK,)),
        ],
        compiler_params=params(32),
        cost_estimate=pl.CostEstimate(
            flops=8 * rows * rows * LANES, bytes_accessed=8 * rows * columns, transcendentals=0
        ),
        name="formed_columns",
    )(index, arrived, near)


def swap_rows(x, group):
    rows, width = x.shape
    return lax.all_to_all(
        x.reshape(group, rows // group, width), "wide", split_axis=0, concat_axis=0, tiled=True
    ).reshape(rows, width)


def on_device(a_rows, xa_panel, za_panel, send_order, recv_order, shift, resident):
    rows = a_rows.shape[0]
    columns = xa_panel.shape[1]
    group = lax.axis_size("wide")
    my_index = lax.axis_index("wide").astype(jnp.int32).reshape(1)
    share = rows // group
    half = rows // 2
    few, apart = phases_of(group)

    order, packing = send_order, share
    if share % 16:
        order = send_order.reshape(group, 2, share // 2).transpose(1, 0, 2).reshape(1, rows)
        packing = 0
    source, slot = recv_order // share, recv_order % share
    index = (slot // (share // 2)) * half + source * (share // 2) + slot % (share // 2)

    lead_panel, rest_panel = split_panels(my_index, xa_panel, za_panel)
    send_picks, a_copy = order_picks(order, a_rows, packing)
    lead_parts = [lead_panel]
    for masks in few:
        lead_parts = exchange(join(lead_parts), masks, "wide")
    rest_parts = tied([rest_panel], send_picks)
    for number, masks in enumerate(apart[:-2]):
        rest_parts = exchange(join(rest_parts), masks, "wide")
        if number == 0:
            lead_parts = tied(lead_parts, *rest_parts)

    lead_out = lead_products(my_index, a_copy, send_picks, lead_parts, offsets_of(few))
    lead_in = swap_rows(tied([lead_out], *rest_parts)[0], group)
    rest_parts = exchange(join(rest_parts), apart[-2], "wide")
    other_parts = exchange(rest_parts[:1], apart[-1], "wide")[1:]

    needed = columns + resident.shape[1]
    blocks_held = -(-needed // (PANEL * group))
    leading_parts = [leading_rows(index, lead_in, blocks_held * PANEL)]
    for masks in few:
        leading_parts = exchange(join(leading_parts), masks, "wide")
        if masks is few[0]:
            later_parts = exchange(tied(rest_parts[1:], *leading_parts), apart[-1], "wide")
    late = len(later_parts) // 2
    rest_parts = rest_parts + other_parts + later_parts[late:]
    rest_out = rest_products(
        my_index, order, a_rows, rest_parts, offsets_of(apart), packing, share // 2
    )
    rest_in = swap_rows(tied([rest_out], *leading_parts)[0], group)
    near, updated, pivots = updates(
        my_index,
        leading_parts,
        offsets_of(few),
        index,
        tied([lead_in], rest_out)[0],
        shift[None, :],
        resident,
        blocks_held,
        columns,
    )
    factored = formed_columns(index, rest_in, near, share // 2)
    return (factored, updated, pivots[0])


def solution(mesh):
    placed = (
        P(("parts", "wide"), None),
        P(("parts", "wide"), None),
        P(("parts", "wide"), None),
        P(("parts", "wide"), None),
        P(("parts", "wide"), None),
        P("parts"),
        P(("parts", "wide"), None),
    )
    return jax.shard_map(
        on_device,
        mesh=mesh,
        in_specs=placed,
        out_specs=(P(("parts", "wide"), None), P(("parts", "wide"), None), P("parts")),
        check_vma=False,
    )
```
